32 devices in a mesh: tok: 8 (over y, x, core), head: 4 (over z).
Axes of the slice: x: 2, y: 2, z: 4, core: 2. Of those that a mesh axis runs over, the one named last changes fastest.
Arguments:
- tokens: bfloat16 [8192, 2048], P(('tok', 'head')), may hold values from -6 to 6
- cotangent: bfloat16 [8192, 2048], P(('tok', 'head')), may hold values from -6 to 6
- doc_lengths: int32 [4], replicated, may hold values from 1 to 4096, 8192 in all
- head_order: int32 [8], replicated, may hold values from 0 to 7, each once
- norm_gain: float32 [2048], replicated, may hold values from 0.5 to 1.5
- w_query: bfloat16 [2048, 2048], P('tok', 'head'), may hold values from -0.125 to 0.125
- w_key: bfloat16 [2048, 2048], P('tok', 'head'), may hold values from -0.125 to 0.125
- w_value: bfloat16 [2048, 4096], P('tok', 'head'), may hold values from -0.125 to 0.125
- w_gate: bfloat16 [2048, 4096], P('tok', 'head'), may hold values from -0.125 to 0.125
- group_gain: float32 [4096], P('head'), may hold values from 0.5 to 1.5
- w_out: bfloat16 [4096, 2048], P('head', 'tok'), may hold values from -0.1875 to 0.1875
- ffn_gain: float32 [2048], replicated, may hold values from 0.5 to 1.5
- w_up: bfloat16 [2048, 4096], P('tok', 'head'), may hold values from -0.125 to 0.125
- w_down: bfloat16 [4096, 2048], P('head', 'tok'), may hold values from -0.125 to 0.125
Outputs:
- layer_out: bfloat16 [8192, 2048], P(('tok', 'head'))
- tokens_grad: float32 [8192, 2048], P(('tok', 'head'))
- norm_gain_grad: float32 [2048], replicated
- w_query_grad: float32 [2048, 2048], P('tok', 'head')
- w_key_grad: float32 [2048, 2048], P('tok', 'head')
- w_value_grad: float32 [2048, 4096], P('tok', 'head')
- w_gate_grad: float32 [2048, 4096], P('tok', 'head')
- group_gain_grad: float32 [4096], P('head')
- w_out_grad: float32 [4096, 2048], P('head', 'tok')
- ffn_gain_grad: float32 [2048], replicated
- w_up_grad: float32 [2048, 4096], P('tok', 'head')
- w_down_grad: float32 [4096, 2048], P('head', 'tok')
The draws below stay inside these ranges and needn't reach their ends.
Inputs may be any that keep to these rules, and one draw needn't show every extreme that they name: `doc_lengths`: the 4 lengths add up to 8192, and the longest is exactly 4096. `head_order`: each of 0 to 7 appears once.
All inputs are finite; a program needn't handle non-finite values.
Results may differ from the reference program's by a relative error of at most 0.019.
Values may be sent and summed in bfloat16 or wider, within the bound.
A program may use at most 384 MiB of HBM per device.

```python
import math
import jax
import jax.numpy as jnp
import numpy as np
from jax import lax

D = 2048
HEADS = 8
KEY = 256
VAL = 512
FF = 4096
SPAN = 512
DOC_MOST = 4096
TOKENS = 8192
DOCS = 4


def block_levels(rng, dims, cuts, least, largest):
    loudness, own = 1.0, jax.random.fold_in(rng, 6)
    for dim, blocks in cuts:
        heights = jnp.exp(jax.random.uniform(jax.random.fold_in(own, dim), (blocks,), jnp.float32, least / len(cuts), largest / len(cuts)))
        loudness = loudness * jnp.repeat(heights, dims[dim] // blocks).reshape([-1 if axis == dim else 1 for axis in range(len(dims))])
    return loudness


def split_up(amount, total, reach, slope):
    portions = [(1 << 20) // math.isqrt(rank ** slope) + 1 for rank in range(2, amount + 1)]
    spare, counts = total - reach - (amount - 1), [1] * (amount - 1)
    while spare > 0:
        free = [i for i in range(amount - 1) if counts[i] < reach]
        whole, budget = sum([portions[i] for i in free]), spare
        for i in free:
            extra = min(reach - counts[i], max(1, budget * portions[i] // whole), spare)
            counts[i] = counts[i] + extra
            spare = spare - extra
    return np.array([reach] + counts)


def uneven(key, amount, total, bound, slope):
    if amount == 2:
        one = jax.random.randint(key, (), max(1, total - bound), min(bound, total - 1) + 1)
        return jnp.stack([one, total - one])
    sizes = jnp.asarray(split_up(amount, total, bound, slope), jnp.int32)
    twos = (amount - 1) // 2
    giver, receiver = sizes[1:1 + 2 * twos:2], sizes[2:2 + 2 * twos:2]
    room = jnp.minimum(giver - 1, bound - receiver)
    shifted = jax.random.randint(jax.random.fold_in(key, 1), (twos,), 0, 1 << 20) % (room + 1)
    sizes = sizes.at[1:1 + 2 * twos:2].set(giver - shifted).at[2:2 + 2 * twos:2].set(receiver + shifted)
    return sizes[jax.random.permutation(jax.random.fold_in(key, 2), amount)]


def normal_values(own_key, dims, spread, limit, split=(), kind=jnp.bfloat16):
    values = jax.random.normal(own_key, dims, jnp.float32) * spread
    if len(split) > 0:
        values = block_levels(own_key, dims, split, -0.22, 0.18) * values
    return jnp.clip(values, min=-limit, max=limit).astype(kind)


def setup_inputs(seed: int = 0) -> dict:
    key_of = jax.random.split(jax.random.key(seed), 15)
    return {
        "tokens": normal_values(key_of[0], (TOKENS, D), 1.0, 6.0, ((0, 32),)),
        "cotangent": normal_values(key_of[1], (TOKENS, D), 1.0, 6.0, ((0, 32),)),
        "doc_lengths": uneven(key_of[2], DOCS, TOKENS, DOC_MOST, 2).astype(jnp.int32),
        "head_order": jax.random.permutation(key_of[3], HEADS).astype(jnp.int32),
        "norm_gain": jnp.clip(1.0 + 0.1 * jax.random.normal(key_of[4], (D,), jnp.float32), 0.5, 1.5),
        "w_query": normal_values(key_of[5], (D, HEADS * KEY), D ** -0.5, 0.125, ((0, 8), (1, 4))),
        "w_key": normal_values(key_of[6], (D, HEADS * KEY), D ** -0.5, 0.125, ((0, 8), (1, 4))),
        "w_value": normal_values(key_of[7], (D, HEADS * VAL), D ** -0.5, 0.125, ((0, 8), (1, 4))),
        "w_gate": normal_values(key_of[8], (D, HEADS * VAL), D ** -0.5, 0.125, ((0, 8), (1, 4))),
        "group_gain": jnp.clip(1.0 + 0.1 * jax.random.normal(key_of[9], (HEADS * VAL,), jnp.float32), 0.5, 1.5),
        "w_out": normal_values(key_of[10], (HEADS * VAL, D), (HEADS * VAL // 4) ** -0.5, 0.1875, ((0, 4), (1, 8))),
        "ffn_gain": jnp.clip(1.0 + 0.1 * jax.random.normal(key_of[11], (D,), jnp.float32), 0.5, 1.5),
        "w_up": normal_values(key_of[12], (D, FF), D ** -0.5, 0.125, ((0, 8), (1, 4))),
        "w_down": normal_values(key_of[13], (FF, D), (FF // 2) ** -0.5, 0.125, ((0, 4), (1, 8))),
    }


@jax.custom_vjp
def low(v):
    return lax.optimization_barrier(v.astype(jnp.bfloat16)).astype(jnp.float32)

@jax.custom_vjp
def low_back(v):
    return v

def low_keep(v):
    return (low(v), None)

def low_pass(kept, grad):
    return (grad,)

def back_keep(v):
    return (v, None)

def back_low(kept, grad):
    return (low(grad),)
low.defvjp(low_keep, low_pass)
low_back.defvjp(back_keep, back_low)
EPS = 1e-05
TOP_PRECISION = lax.Precision.HIGHEST

def matmul(left, right):
    return jnp.dot(left, right, precision=TOP_PRECISION, preferred_element_type=jnp.float32)

def layer_norm(values, gain):
    mean = lax.optimization_barrier(jnp.mean(values, axis=-1, keepdims=True))
    centred = values - mean
    inverse = lax.rsqrt(lax.optimization_barrier(jnp.mean(centred * centred, axis=-1, keepdims=True)) + EPS)
    return centred * inverse * gain

def doc_index(row_ids, starts):
    return lax.optimization_barrier(jnp.sum((starts[None, :] <= row_ids[:, None]).astype(jnp.int32), axis=1)) - 1

def doc_position(row_ids, starts):
    first = lax.optimization_barrier(jnp.max(jnp.where(starts[None, :] <= row_ids[:, None], starts[None, :], 0), axis=1))
    return (row_ids - first).astype(jnp.int32)

def angles(position, half):
    freq = jnp.exp(-jnp.log(10000.0) * jnp.arange(half, dtype=jnp.float32) / half)
    turn = position.astype(jnp.float32)[:, None] * freq[None, :]
    return (jnp.cos(turn)[:, None, :], jnp.sin(turn)[:, None, :])

def rotate(values, cosine, sine):
    half = values.shape[-1] // 2
    first, second = (values[..., :half], values[..., half:])
    return jnp.concatenate([first * cosine - second * sine, first * sine + second * cosine], axis=-1)

def span_masks(doc_ids, before, log_decay):
    size = doc_ids.shape[0]
    place = jnp.arange(size, dtype=jnp.float32)
    lag = place[:, None] - place[None, :]
    same = (doc_ids[:, None] == doc_ids[None, :]) & (lag >= 0)
    decay = jnp.where(same[None], jnp.exp(jnp.maximum(lag, 0.0)[None] * log_decay[:, None, None]), 0.0)
    entry_decay = jnp.where((doc_ids == before)[:, None], jnp.exp((place + 1.0)[:, None] * log_decay[None, :]), 0.0)
    exit_decay = jnp.where((doc_ids == doc_ids[-1])[:, None], jnp.exp((size - 1.0 - place)[:, None] * log_decay[None, :]), 0.0)
    cross_span_output = jnp.where(doc_ids[-1] == before, jnp.exp(size * log_decay), 0.0)
    return (decay, entry_decay, exit_decay, cross_span_output)

def retention(queries, keys, values, doc_ids, log_decay):
    blocks = queries.shape[0] // SPAN
    query_blocks = queries.reshape(blocks, SPAN, HEADS, KEY)
    key_blocks = keys.reshape(blocks, SPAN, HEADS, KEY)
    value_blocks = values.reshape(blocks, SPAN, HEADS, VAL)
    doc_blocks = doc_ids.reshape(blocks, SPAN)
    before = jnp.concatenate([jnp.full((1,), -1, jnp.int32), doc_blocks[:-1, -1].astype(jnp.int32)])

    def step(carried_state, items):
        query_span_rows, key_span_rows, value_span_rows, doc_b, before_b = items
        decay, entry_decay, exit_decay, cross_span_output = span_masks(doc_b, before_b, log_decay)
        scores = low_back(jnp.einsum('ihk,jhk->hij', query_span_rows, key_span_rows, precision=TOP_PRECISION))
        probs = low(scores * decay)
        intra = jnp.einsum('hij,jhv->ihv', probs, value_span_rows, precision=TOP_PRECISION)
        between_span_term = jnp.einsum('djc,jcx->djx', query_span_rows, carried_state, precision=TOP_PRECISION) * entry_decay[:, :, None]
        new_state_term = cross_span_output[:, None, None] * carried_state + jnp.einsum('gpn,gps->pns', key_span_rows, value_span_rows * exit_decay[:, :, None], precision=TOP_PRECISION)
        return (new_state_term, intra + between_span_term)
    start = jnp.zeros((HEADS, KEY, VAL), jnp.float32)
    _, outputs = lax.scan(jax.checkpoint(step), start, (query_blocks, key_blocks, value_blocks, doc_blocks, before))
    return outputs.reshape(queries.shape[0], HEADS, VAL)

def forward(tokens, norm_gain, w_query, w_key, w_value, w_gate, group_gain, w_out, ffn_gain, w_up, w_down, doc_ids, position, log_decay):
    row_count = tokens.shape[0]
    cosine, sine = angles(position, KEY // 2)
    lifted = low(layer_norm(tokens, norm_gain))
    queries = low(rotate(low_back(matmul(lifted, w_query)).reshape(row_count, HEADS, KEY), cosine, sine))
    keys = low(rotate(low_back(matmul(lifted, w_key)).reshape(row_count, HEADS, KEY), cosine, sine))
    values = low(low_back(matmul(lifted, w_value))).reshape(row_count, HEADS, VAL)
    gate = low_back(matmul(lifted, w_gate)).reshape(row_count, HEADS, VAL)
    retained = low_back(retention(queries, keys, values, doc_ids, log_decay))
    grouped = layer_norm(retained, group_gain.reshape(HEADS, VAL))
    mixed = low(low_back(jax.nn.silu(gate) * grouped)).reshape(row_count, HEADS * VAL)
    resid = tokens + low_back(matmul(mixed, w_out))
    lifted2 = low(layer_norm(resid, ffn_gain))
    hidden = low(jax.nn.gelu(low_back(matmul(lifted2, w_up)), approximate=False))
    return resid + matmul(hidden, w_down)

def reference(tokens, cotangent, doc_lengths, head_order, norm_gain, w_query, w_key, w_value, w_gate, group_gain, w_out, ffn_gain, w_up, w_down):
    ends = jnp.cumsum(doc_lengths).astype(jnp.int32)
    starts = (ends - doc_lengths).astype(jnp.int32)
    row_ids = jnp.arange(TOKENS, dtype=jnp.int32)
    doc_ids = doc_index(row_ids, starts)
    position = doc_position(row_ids, starts)
    log_decay = jnp.log1p(-jnp.exp2(-(5.0 + head_order.astype(jnp.float32))))
    params = (tokens, norm_gain, w_query, w_key, w_value, w_gate, group_gain, w_out, ffn_gain, w_up, w_down)
    params = tuple((item.astype(jnp.float32) for item in params))

    def layer(*weights):
        return forward(*weights, doc_ids, position, log_decay)
    result, pull = jax.vjp(layer, *params)
    grads = pull(cotangent.astype(jnp.float32))
    return (result.astype(jnp.bfloat16), grads[0], grads[1], grads[2], grads[3], grads[4], grads[5], grads[6], grads[7], grads[8], grads[9], grads[10])
```

```python
import jax
import jax.numpy as jnp
from jax import lax
from jax.sharding import PartitionSpec as P

KEY = 256
VAL = 512
SPAN = 512

EPS = 1e-05
SQRT_HALF = 0.7071067811865476
INV_ROOT_TWO_PI = 0.3989422804014327
BF = jnp.bfloat16
F32 = jnp.float32


def mm(left, right):
    return jnp.dot(left, right, preferred_element_type=F32)


def mm_nt(left, right):
    return lax.dot_general(left, right, (((1,), (1,)), ((), ())), preferred_element_type=F32)


def mm_tn(left, right):
    return lax.dot_general(left, right, (((0,), (0,)), ((), ())), preferred_element_type=F32)


def swap(array, axis, bit):
    count = lax.axis_size(axis)
    return lax.ppermute(array, axis, [(i, i ^ bit) for i in range(count)])


def shift(array):
    count = lax.axis_size("head")
    return lax.ppermute(array, "head", [(i, (i + 1) % count) for i in range(count)])


def paired():
    return lax.axis_size("tok") == 8


def reorder(array):
    if not paired():
        return array
    me = lax.axis_index("tok")
    width = array.shape[-1] // 8
    return jnp.concatenate(
        [
            lax.dynamic_slice_in_dim(array, (me ^ r) * width, width, array.ndim - 1)
            for r in range(8)
        ],
        axis=-1,
    )


def halves(array):
    half = array.shape[0] // 2
    return array[:half], array[half:]


def tok_gather(shard, axis):
    if not paired():
        return lax.all_gather(shard, "tok", axis=axis, tiled=True)
    along_x = swap(shard, "tok", 2)
    along_y = swap(shard, "tok", 4)
    far = jnp.concatenate(
        [swap(halves(along_x)[0], "tok", 4), swap(halves(along_y)[1], "tok", 2)], axis=0
    )
    own = [shard, along_x, along_y, far]
    pieces = []
    for piece in own:
        pieces += [piece, swap(piece, "tok", 1)]
    return jnp.concatenate(pieces, axis=axis)


def tok_scatter(pieces):
    pieces = [p.astype(BF) for p in pieces]
    if not paired():
        return lax.psum_scatter(jnp.stack(pieces), "tok", scatter_dimension=0).astype(F32)
    kept = [
        pieces[r].astype(F32) + swap(pieces[r + 1], "tok", 1).astype(F32) for r in (0, 2, 4, 6)
    ]
    zero, two, four, six = kept
    six_a, six_b = halves(six.astype(BF))
    two_a, two_b = halves(two)
    four_a, four_b = halves(four)
    four_a = four_a + swap(six_a, "tok", 2).astype(F32)
    two_b = two_b + swap(six_b, "tok", 4).astype(F32)
    two = jnp.concatenate([two_a, two_b], axis=0).astype(BF)
    four = jnp.concatenate([four_a, four_b], axis=0).astype(BF)
    return zero + swap(two, "tok", 2).astype(F32) + swap(four, "tok", 4).astype(F32)


def head_gather(rows):
    count = lax.axis_size("head")
    me = lax.axis_index("head")
    size = rows.shape[0]
    whole = jnp.zeros((count * size,) + rows.shape[1:], rows.dtype)
    whole = lax.dynamic_update_slice_in_dim(whole, rows, me * size, 0)
    for step in range(1, count):
        rows = shift(rows)
        source = lax.rem(me - step + count, count)
        whole = lax.dynamic_update_slice_in_dim(whole, rows, source * size, 0)
    return whole


def head_scatter(term):
    count = lax.axis_size("head")
    me = lax.axis_index("head")
    total = term(lax.rem(me + count - 1, count))
    for step in range(1, count):
        arrived = shift(total.astype(BF))
        owner = lax.rem(me + 2 * count - 1 - step, count)
        total = term(owner) + arrived.astype(F32)
    return total


def rows_of(array, index, size):
    return lax.dynamic_slice_in_dim(array, index * size, size, 0)


def sum_small(vector, axis):
    count = lax.axis_size(axis)
    bit = 1
    while bit < count:
        vector = vector + swap(vector, axis, bit)
        bit *= 2
    return vector


def norm_forward(values, gain):
    mean = jnp.mean(values, axis=-1, keepdims=True)
    centred = values - mean
    inverse = lax.rsqrt(jnp.mean(centred * centred, axis=-1, keepdims=True) + EPS)
    unit = centred * inverse
    return (unit * gain, unit, inverse)


def norm_backward(grad_out, unit, inverse, gain):
    scaled = grad_out * gain
    first = jnp.mean(scaled, axis=-1, keepdims=True)
    second = jnp.mean(scaled * unit, axis=-1, keepdims=True)
    return (inverse * (scaled - first - unit * second), jnp.sum(grad_out * unit, axis=0))


def doc_index(row_ids, starts):
    return jnp.sum((starts[None, :] <= row_ids[:, None]).astype(jnp.int32), axis=1) - 1


def doc_position(row_ids, starts):
    first = jnp.max(jnp.where(starts[None, :] <= row_ids[:, None], starts[None, :], 0), axis=1)
    return row_ids - first


def angles(position, half):
    freq = jnp.exp(-jnp.log(10000.0) * jnp.arange(half, dtype=F32) / half)
    turn = position.astype(F32)[:, None] * freq[None, :]
    return (jnp.cos(turn), jnp.sin(turn))


def rotate(values, cosine, sine):
    half = values.shape[-1] // 2
    first, second = (values[..., :half], values[..., half:])
    return jnp.concatenate(
        [first * cosine - second * sine, first * sine + second * cosine], axis=-1
    )


def unrotate(grads, cosine, sine):
    return rotate(grads, cosine, -sine)


def span_masks(doc_ids, before, log_decay):
    size = doc_ids.shape[0]
    place = jnp.arange(size, dtype=F32)
    lag = place[:, None] - place[None, :]
    same = (doc_ids[:, None] == doc_ids[None, :]) & (lag >= 0)
    decay = jnp.where(same, jnp.exp(jnp.maximum(lag, 0.0) * log_decay), 0.0)
    reach = jnp.where(doc_ids == before, jnp.exp((place + 1.0) * log_decay), 0.0)[:, None]
    leave = jnp.where(doc_ids == doc_ids[-1], jnp.exp((size - 1.0 - place) * log_decay), 0.0)[
        :, None
    ]
    across = jnp.where(doc_ids[-1] == before, jnp.exp(size * log_decay), 0.0)
    return (decay, reach, leave, across)


def gelu_slope(hidden_pre):
    return (
        0.5 * (1.0 + lax.erf(hidden_pre * SQRT_HALF))
        + hidden_pre * jnp.exp(-0.5 * hidden_pre * hidden_pre) * INV_ROOT_TWO_PI
    )


def local(
    tokens,
    cotangent,
    doc_lengths,
    head_order,
    norm_gain,
    w_query,
    w_key,
    w_value,
    w_gate,
    group_gain,
    w_out,
    ffn_gain,
    w_up,
    w_down,
):
    heads = w_query.shape[1] // KEY
    head_count = lax.axis_size("head")
    tok_count = lax.axis_size("tok")
    z = lax.axis_index("head")
    tok = lax.axis_index("tok")
    rows = tokens.shape[0]
    group_rows = rows * head_count
    blocks = group_rows // SPAN
    width = tokens.shape[1]
    part = width // tok_count

    tokens_f = reorder(tokens).astype(F32)
    cot_own = reorder(cotangent)
    gain1 = reorder(norm_gain)
    gain2 = reorder(ffn_gain)
    normed1, unit1, inverse1 = norm_forward(tokens_f, gain1)
    group = head_gather(normed1.astype(BF))
    qkvg_full = tok_gather(jnp.concatenate([w_query, w_key, w_value, w_gate], axis=1), 0)
    qk = w_query.shape[1]
    vg = w_value.shape[1]
    query_full = qkvg_full[:, :qk]
    key_full = qkvg_full[:, qk : 2 * qk]
    value_full = qkvg_full[:, 2 * qk : 2 * qk + vg]
    gate_full = qkvg_full[:, 2 * qk + vg :]
    out_full = tok_gather(w_out, 1)
    up_two = jnp.concatenate([w_up, swap(w_up, "head", 2)], axis=1)
    down_two = jnp.concatenate([w_down, swap(w_down, "head", 2)], axis=0)
    up_full = tok_gather(up_two, 0)
    down_full = tok_gather(down_two, 1)
    cot_pair = jnp.concatenate([cot_own, swap(cot_own, "head", 1)], axis=0)

    ends = jnp.cumsum(doc_lengths)
    starts = ends - doc_lengths
    first_row = tok * group_rows
    row_ids = first_row + jnp.arange(group_rows, dtype=jnp.int32)
    doc_ids = doc_index(row_ids, starts)
    previous = doc_index(jnp.reshape(first_row - 1, (1,)), starts)[0]
    group_last = doc_index((jnp.arange(tok_count, dtype=jnp.int32) + 1) * group_rows - 1, starts)
    cosine, sine = angles(doc_position(row_ids, starts), KEY // 2)
    ranks = lax.dynamic_slice_in_dim(head_order, z * heads, heads)
    log_decay = jnp.log1p(-jnp.exp2(-(5.0 + ranks.astype(F32))))

    query_proj = mm(group, query_full)
    key_proj = mm(group, key_full)
    value_proj = mm(group, value_full)
    gate = mm(group, gate_full)

    def head_of(array, head, size):
        return array[:, head * size : (head + 1) * size]

    def block_of(array, block):
        return array[block * SPAN : (block + 1) * SPAN]

    q, k, v, masks = [], [], [], []
    for h in range(heads):
        q.append(rotate(head_of(query_proj, h, KEY), cosine, sine).astype(BF))
        k.append(rotate(head_of(key_proj, h, KEY), cosine, sine).astype(BF))
        v.append(head_of(value_proj, h, VAL).astype(BF))
        masks.append(
            [
                span_masks(
                    block_of(doc_ids, b),
                    previous if b == 0 else doc_ids[b * SPAN - 1],
                    log_decay[h],
                )
                for b in range(blocks)
            ]
        )

    group_order = jnp.arange(tok_count, dtype=jnp.int32)

    def weigh(lag, last, h):
        return jnp.where(
            (lag >= 0) & (group_last == last),
            jnp.exp(jnp.maximum(lag, 0).astype(F32) * group_rows * log_decay[h]),
            0.0,
        )

    ends_of = []
    added = []
    for h in range(heads):
        state = jnp.zeros((KEY, VAL), F32)
        terms = []
        for b in range(blocks):
            term = mm_tn(block_of(k[h], b), (block_of(v[h], b) * masks[h][b][2]).astype(BF))
            terms.append(term)
            state = masks[h][b][3] * state + term
        added.append(terms)
        ends_of.append(state.astype(BF))
    all_states = lax.all_gather(jnp.concatenate(ends_of, axis=0), "tok", axis=0)
    lag = tok - 1 - group_order
    states = []
    retained = []
    for h in range(heads):
        weights = weigh(lag, previous, h)
        state = jnp.sum(
            all_states[:, h * KEY : (h + 1) * KEY].astype(F32) * weights[:, None, None], axis=0
        )
        mine = []
        outs = []
        for b in range(blocks):
            mine.append(state.astype(BF))
            qb, kb, vb = block_of(q[h], b), block_of(k[h], b), block_of(v[h], b)
            decay, reach, leave, across = masks[h][b]
            probs = (mm_nt(qb, kb) * decay).astype(BF)
            outs.append(mm(probs, vb) + reach * mm(qb, mine[-1]))
            state = across * state + added[h][b]
        states.append(mine)
        retained.append(jnp.concatenate(outs, axis=0))

    mixed_parts, unit_g, inverse_g, grouped, swish, sigma = [], [], [], [], [], []
    for h in range(heads):
        g, u, i = norm_forward(retained[h], head_of(group_gain[None, :], h, VAL))
        gate_h = head_of(gate, h, VAL)
        s = jax.nn.sigmoid(gate_h)
        unit_g.append(u)
        inverse_g.append(i)
        grouped.append(g)
        sigma.append(s)
        swish.append(gate_h * s)
        mixed_parts.append((swish[-1] * g).astype(BF))
    mixed = jnp.concatenate(mixed_parts, axis=1)

    out_sum = head_scatter(lambda i: mm(rows_of(mixed, i, rows), out_full))
    resid = tokens_f + out_sum
    normed2, unit2, inverse2 = norm_forward(resid, gain2)
    lifted2 = normed2.astype(BF)
    lifted2_pair = jnp.concatenate([lifted2, swap(lifted2, "head", 1)], axis=0)
    hidden_pre = mm(lifted2_pair, up_full)
    hidden = jax.nn.gelu(hidden_pre, approximate=False).astype(BF)
    hidden_grad = mm_nt(cot_pair, down_full)
    pre_grad = (hidden_grad * gelu_slope(hidden_pre)).astype(BF)
    far_grad = mm_nt(pre_grad[rows:], up_full).astype(BF)
    lifted2_grad = mm_nt(pre_grad[:rows], up_full) + swap(far_grad, "head", 1).astype(F32)
    resid_part, ffn_gain_local = norm_backward(lifted2_grad, unit2, inverse2, gain2)
    resid_grad = cot_own.astype(F32) + resid_part
    branch_own = resid_grad.astype(BF)
    branch = head_gather(branch_own)

    far_out = mm(hidden[rows:], down_full).astype(BF)
    layer_out = reorder(
        (resid + mm(hidden[:rows], down_full) + swap(far_out, "head", 1).astype(F32)).astype(BF)
    )

    def piece(array, r):
        return array[:, r * part : (r + 1) * part]

    slots = range(tok_count)
    down_two_grad = tok_scatter([mm_tn(hidden, piece(cot_pair, r)) for r in slots])
    half = down_two_grad.shape[0] // 2
    w_down_grad = down_two_grad[:half] + swap(
        down_two_grad[half:].astype(BF), "head", 2
    ).astype(F32)
    up_two_grad = tok_scatter([mm_tn(piece(lifted2_pair, r), pre_grad) for r in slots])
    half = up_two_grad.shape[1] // 2
    w_up_grad = up_two_grad[:, :half] + swap(
        up_two_grad[:, half:].astype(BF), "head", 2
    ).astype(F32)

    mixed_grad = mm_nt(branch, out_full).astype(BF)
    w_out_grad = tok_scatter([mm_tn(mixed, piece(branch, r)) for r in slots])

    gate_parts, ret_grad, group_gain_parts = [], [], []
    for h in range(heads):
        head_grad = head_of(mixed_grad, h, VAL).astype(F32)
        gate_parts.append(
            (head_grad * grouped[h] * (sigma[h] + swish[h] * (1.0 - sigma[h]))).astype(BF)
        )
        back, gain_term = norm_backward(
            head_grad * swish[h], unit_g[h], inverse_g[h], head_of(group_gain[None, :], h, VAL)
        )
        ret_grad.append(back.astype(BF))
        group_gain_parts.append(gain_term)
    gate_grad = jnp.concatenate(gate_parts, axis=1)
    w_gate_grad = tok_scatter([mm_tn(piece(group, r), gate_grad) for r in slots])

    pending_of, pending_terms = [], []
    for h in range(heads):
        pending = jnp.zeros((KEY, VAL), F32)
        terms = [None] * blocks
        for b in reversed(range(blocks)):
            terms[b] = mm_tn(
                block_of(q[h], b), (block_of(ret_grad[h], b) * masks[h][b][1]).astype(BF)
            )
            pending = masks[h][b][3] * pending + terms[b]
        pending_terms.append(terms)
        pending_of.append(pending.astype(BF))
    all_pending = lax.all_gather(jnp.concatenate(pending_of, axis=0), "tok", axis=0)
    lag_back = group_order - 1 - tok
    shifted_last = doc_index(group_order * group_rows - 1, starts)
    q_parts, k_parts, v_parts = [], [], []
    for h in range(heads):
        weights = jnp.where(
            (lag_back >= 0) & (shifted_last == doc_ids[-1]),
            jnp.exp(jnp.maximum(lag_back, 0).astype(F32) * group_rows * log_decay[h]),
            0.0,
        )
        later = jnp.sum(
            all_pending[:, h * KEY : (h + 1) * KEY].astype(F32) * weights[:, None, None], axis=0
        )
        qg, kg, vg_ = [None] * blocks, [None] * blocks, [None] * blocks
        for b in reversed(range(blocks)):
            qb, kb, vb = block_of(q[h], b), block_of(k[h], b), block_of(v[h], b)
            rb = block_of(ret_grad[h], b)
            decay, reach, leave, across = masks[h][b]
            probs = (mm_nt(qb, kb) * decay).astype(BF)
            score_grad = (mm_nt(rb, vb) * decay).astype(BF)
            later_b = later.astype(BF)
            qg[b] = mm(score_grad, kb) + reach * mm_nt(rb, states[h][b])
            kg[b] = mm_tn(score_grad, qb) + leave * mm_nt(vb, later_b)
            vg_[b] = mm_tn(probs, rb) + leave * mm(kb, later_b)
            later = across * later + pending_terms[h][b]
        q_parts.append(unrotate(jnp.concatenate(qg, axis=0), cosine, sine).astype(BF))
        k_parts.append(unrotate(jnp.concatenate(kg, axis=0), cosine, sine).astype(BF))
        v_parts.append(jnp.concatenate(vg_, axis=0).astype(BF))
    all_grad = jnp.concatenate(q_parts + k_parts + v_parts + [gate_grad], axis=1)
    row_grad = head_scatter(lambda i: mm_nt(rows_of(all_grad, i, rows), qkvg_full))
    input_part, norm_gain_local = norm_backward(row_grad, unit1, inverse1, gain1)
    tokens_grad = reorder(resid_grad + input_part)
    qkv_grad = all_grad[:, : 2 * qk + vg]
    w_qkv_grad = tok_scatter([mm_tn(piece(group, r), qkv_grad) for r in slots])
    w_query_grad = w_qkv_grad[:, :qk]
    w_key_grad = w_qkv_grad[:, qk : 2 * qk]
    w_value_grad = w_qkv_grad[:, 2 * qk :]

    group_gain_grad = sum_small(jnp.concatenate(group_gain_parts, axis=0), "tok")
    ffn_sum = sum_small(sum_small(reorder(ffn_gain_local), "tok"), "head")
    norm_sum = sum_small(sum_small(reorder(norm_gain_local), "tok"), "head")
    return (
        layer_out,
        tokens_grad,
        norm_sum,
        w_query_grad,
        w_key_grad,
        w_value_grad,
        w_gate_grad,
        group_gain_grad,
        w_out_grad,
        ffn_sum,
        w_up_grad,
        w_down_grad,
    )


def solution(mesh):
    rows = P(("tok", "head"), None)
    inward = P("tok", "head")
    outward = P("head", "tok")
    return jax.shard_map(
        local,
        mesh=mesh,
        in_specs=(
            rows, rows, P(), P(), P(), inward, inward, inward, inward, P("head"),
            outward, P(), inward, outward,
        ),
        out_specs=(
            rows, rows, P(), inward, inward, inward, inward, P("head"),
            outward, P(), inward, outward,
        ),
        check_vma=False,
    )
```

```python
import jax
import jax.numpy as jnp
from jax import lax
from jax.experimental import pallas as pl
from jax.experimental.pallas import tpu as pltpu
from jax.sharding import PartitionSpec as P

KEY = 256
VAL = 512
SPAN = 512

EPS = 1e-05
SQRT_HALF = 0.7071067811865476
INV_ROOT_TWO_PI = 0.3989422804014327
BF = jnp.bfloat16
F32 = jnp.float32


def mm(left, right):
    return jnp.dot(left, right, preferred_element_type=F32)


def mm_nt(left, right):
    return lax.dot_general(left, right, (((1,), (1,)), ((), ())), preferred_element_type=F32)


def mm_tn(left, right):
    return lax.dot_general(left, right, (((0,), (0,)), ((), ())), preferred_element_type=F32)


def swap(array, axis, bit):
    count = lax.axis_size(axis)
    return lax.ppermute(array, axis, [(i, i ^ bit) for i in range(count)])


def shift(array):
    count = lax.axis_size("head")
    return lax.ppermute(array, "head", [(i, (i + 1) % count) for i in range(count)])


def paired():
    return lax.axis_size("tok") == 8


def reorder(array):
    if not paired():
        return array
    me = lax.axis_index("tok")
    width = array.shape[-1] // 8
    return jnp.concatenate(
        [
            lax.dynamic_slice_in_dim(array, (me ^ r) * width, width, array.ndim - 1)
            for r in range(8)
        ],
        axis=-1,
    )


def halves(array):
    half = array.shape[0] // 2
    return array[:half], array[half:]


def tok_gather(shard, axis):
    if not paired():
        return lax.all_gather(shard, "tok", axis=axis, tiled=True)
    along_x = swap(shard, "tok", 2)
    along_y = swap(shard, "tok", 4)
    far = jnp.concatenate(
        [swap(halves(along_x)[0], "tok", 4), swap(halves(along_y)[1], "tok", 2)], axis=0
    )
    own = [shard, along_x, along_y, far]
    pieces = []
    for piece in own:
        pieces += [piece, swap(piece, "tok", 1)]
    return jnp.concatenate(pieces, axis=axis)


def tok_scatter(pieces):
    pieces = [p.astype(BF) for p in pieces]
    if not paired():
        return lax.psum_scatter(jnp.stack(pieces), "tok", scatter_dimension=0).astype(F32)
    kept = [
        pieces[r].astype(F32) + swap(pieces[r + 1], "tok", 1).astype(F32) for r in (0, 2, 4, 6)
    ]
    zero, two, four, six = kept
    six_a, six_b = halves(six.astype(BF))
    two_a, two_b = halves(two)
    four_a, four_b = halves(four)
    four_a = four_a + swap(six_a, "tok", 2).astype(F32)
    two_b = two_b + swap(six_b, "tok", 4).astype(F32)
    two = jnp.concatenate([two_a, two_b], axis=0).astype(BF)
    four = jnp.concatenate([four_a, four_b], axis=0).astype(BF)
    return zero + swap(two, "tok", 2).astype(F32) + swap(four, "tok", 4).astype(F32)


def head_gather(rows):
    count = lax.axis_size("head")
    me = lax.axis_index("head")
    size = rows.shape[0]
    whole = jnp.zeros((count * size,) + rows.shape[1:], rows.dtype)
    whole = lax.dynamic_update_slice_in_dim(whole, rows, me * size, 0)
    for step in range(1, count):
        rows = shift(rows)
        source = lax.rem(me - step + count, count)
        whole = lax.dynamic_update_slice_in_dim(whole, rows, source * size, 0)
    return whole


def head_scatter(term):
    count = lax.axis_size("head")
    me = lax.axis_index("head")
    total = term(lax.rem(me + count - 1, count))
    for step in range(1, count):
        arrived = shift(total.astype(BF))
        owner = lax.rem(me + 2 * count - 1 - step, count)
        total = term(owner) + arrived.astype(F32)
    return total


def rows_of(array, index, size):
    return lax.dynamic_slice_in_dim(array, index * size, size, 0)


def sum_small(vector, axis):
    count = lax.axis_size(axis)
    bit = 1
    while bit < count:
        vector = vector + swap(vector, axis, bit)
        bit *= 2
    return vector


MESH = pl.DeviceIdType.MESH
ANY = pl.BlockSpec(memory_space=pl.ANY)
VMEM = pl.BlockSpec(memory_space=pltpu.VMEM)
LIMIT = 60 * 1024 * 1024


def flipped(index, bit):
    return index + bit - 2 * bit * lax.rem(lax.div(index, bit), 2)


def peers():
    tok = lax.axis_index("tok")
    z = lax.axis_index("head")
    count = lax.axis_size("head")
    return {
        "core": {"tok": flipped(tok, 1), "head": z},
        "x": {"tok": flipped(tok, 2), "head": z},
        "y": {"tok": flipped(tok, 4), "head": z},
        "up": {"tok": tok, "head": lax.rem(z + 1, count)},
        "down": {"tok": tok, "head": lax.rem(z + count - 1, count)},
        "pair": {"tok": tok, "head": flipped(z, 1)},
        "cross": {"tok": tok, "head": flipped(z, 2)},
    }


def greet(*devices):
    barrier = pltpu.get_barrier_semaphore()
    for device in devices:
        pl.semaphore_signal(barrier, inc=1, device_id=device, device_id_type=MESH)
    pl.semaphore_wait(barrier, len(devices))


class Moves:
    def __init__(self, send, recv):
        self.send, self.recv, self.made, self.over = send, recv, [], []

    def go(self, src, dst, device):
        n = len(self.made)
        copy = pltpu.make_async_remote_copy(
            src_ref=src,
            dst_ref=dst,
            send_sem=self.send.at[n],
            recv_sem=self.recv.at[n],
            device_id=device,
            device_id_type=MESH,
        )
        copy.start()
        self.made.append(copy)
        return copy

    def sent(self, copy):
        copy.wait_send()
        self.over.append(copy)

    def finish(self):
        for copy in self.made:
            if not any(copy is gone for gone in self.over):
                copy.wait_send()


class Gather:
    def __init__(self, moves, near, view):
        self.moves, self.near, self.view = moves, near, view

    def first(self):
        go, near, view = self.moves.go, self.near, self.view
        self.x = go(view(0), view(2), near["x"])
        self.y = go(view(0), view(4), near["y"])
        self.cores = [go(view(0), view(1), near["core"])]

    def second(self):
        go, near, view = self.moves.go, self.near, self.view
        self.x.wait_recv()
        self.far = [go(view(2, 0), view(6, 0), near["y"])]
        self.cores.append(go(view(2), view(3), near["core"]))
        self.y.wait_recv()
        self.far.append(go(view(4, 1), view(6, 1), near["x"]))
        self.cores.append(go(view(4), view(5), near["core"]))

    def third(self):
        go, near, view = self.moves.go, self.near, self.view
        for copy in self.far:
            copy.wait_recv()
        self.cores.append(go(view(6), view(7), near["core"]))

    def done(self):
        for copy in self.cores:
            copy.wait_recv()


def enter_kernel(
    tok_ref,
    gain_ref,
    cos_ref,
    sin_ref,
    wq_ref,
    wk_ref,
    wv_ref,
    wg_ref,
    wo_ref,
    turned_out,
    weights_out,
    out_full,
    qk_out,
    v_out,
    gate_out,
    turned,
    group,
    weights,
    send,
    recv,
    own_sem,
    keep_sem,
):
    near = peers()
    tok = lax.axis_index("tok")
    z = lax.axis_index("head")
    count = lax.axis_size("head")
    rows, width = tok_ref.shape
    part = width // 8
    cols = weights.shape[2]
    half = wq_ref.shape[1]

    own = [
        pltpu.make_async_copy(wq_ref, weights.at[0, pl.ds(0, part), pl.ds(0, half)], own_sem.at[0]),
        pltpu.make_async_copy(
            wk_ref, weights.at[0, pl.ds(0, part), pl.ds(half, half)], own_sem.at[1]
        ),
        pltpu.make_async_copy(wv_ref, weights.at[1, pl.ds(0, part), :], own_sem.at[2]),
        pltpu.make_async_copy(wg_ref, weights.at[2, pl.ds(0, part), :], own_sem.at[3]),
        pltpu.make_async_copy(wo_ref, out_full.at[:, pl.ds(0, part)], own_sem.at[4]),
    ]
    for copy in own:
        copy.start()
    greet(near["core"], near["x"], near["y"], near["up"], near["down"])
    moves = Moves(send, recv)

    def chunk_view(c):
        def view(r, side=None):
            if side is None:
                return weights.at[c, pl.ds(r * part, part), :]
            return weights.at[c, pl.ds(r * part + side * (part // 2), part // 2), :]

        return view

    def out_view(r, side=None):
        if side is None:
            return out_full.at[:, pl.ds(r * part, part)]
        size = out_full.shape[0] // 2
        return out_full.at[pl.ds(side * size, size), pl.ds(r * part, part)]

    chunks = [Gather(moves, near, chunk_view(c)) for c in range(3)]
    outward = Gather(moves, near, out_view)
    own[0].wait()
    own[1].wait()
    chunks[0].first()
    own[2].wait()
    chunks[1].first()
    own[3].wait()
    own[4].wait()

    @pl.loop(0, rows // 32)
    def _(i):
        at = pl.ds(pl.multiple_of(i * 32, 32), 32)
        values = jnp.concatenate(
            [
                tok_ref[at, pl.ds(pl.multiple_of(place * part, part), part)]
                for place in xor_places(tok)
            ],
            axis=1,
        ).astype(F32)
        mean = jnp.mean(values, axis=-1, keepdims=True)
        centred = values - mean
        inverse = lax.rsqrt(jnp.mean(centred * centred, axis=-1, keepdims=True) + EPS)
        lifted = (centred * inverse * gain_ref[...]).astype(BF)
        group[pl.ds(pl.multiple_of(z * rows + i * 32, 32), 32), :] = lifted

    def shard(step, side):
        owner = lax.rem(z - step + count, count)
        size = rows // 2
        return group.at[pl.ds(pl.multiple_of(owner * rows + side * size, size), size), :]

    ring = {}

    def pass_on(step, side):
        if step:
            ring[step - 1, side].wait_recv()
        if step < count - 1:
            ring[step, side] = moves.go(shard(step, side), shard(step, side), near["up"])

    def project(c, steps):
        first, number = steps

        @pl.loop(0, number * (cols // 256))
        def _(i):
            step = first + lax.div(i, cols // 256)
            tile = lax.rem(i, cols // 256)
            owner = lax.rem(z - step + count, count)
            at = pl.ds(pl.multiple_of(owner * rows, rows), rows)
            to = pl.ds(pl.multiple_of(tile * 256, 256), 256)
            found = jnp.dot(group[at, :], weights[c, :, to], preferred_element_type=F32)
            if c == 0:
                cosine, sine = cos_ref[at, :], sin_ref[at, :]
                one, two = found[:, :128], found[:, 128:]
                qk_out[at, to] = jnp.concatenate(
                    [one * cosine - two * sine, one * sine + two * cosine], axis=1
                ).astype(BF)
            elif c == 1:
                v_out[at, to] = found.astype(BF)
            else:
                gate_out[at, to] = found.astype(BF)

    def turn(step):
        owner = lax.rem(z - step + count, count)

        @pl.loop(0, width // 256)
        def _(i):
            at = pl.ds(pl.multiple_of(i * 256, 256), 256)
            to = pl.ds(pl.multiple_of(owner * rows, rows), rows)
            turned[at, to] = group[to, at].T

    kept = []

    def keep(c):
        copy = pltpu.make_async_copy(
            weights.at[c], weights_out.at[:, pl.ds(c * cols, cols)], keep_sem.at[c]
        )
        copy.start()
        kept.append(copy)

    pass_on(0, 0)
    pass_on(0, 1)
    chunks[0].second()
    chunks[2].first()
    pass_on(1, 0)
    chunks[1].second()
    outward.first()
    pass_on(1, 1)
    chunks[0].third()
    chunks[0].done()
    keep(0)
    project(0, (0, 2))
    pass_on(2, 0)
    turn(0)
    turn(1)
    chunks[2].second()
    pass_on(2, 1)
    chunks[1].third()
    chunks[1].done()
    keep(1)
    project(1, (0, 2))
    outward.second()
    project(0, (2, 1))
    project(1, (2, 1))
    turn(2)
    chunks[2].third()
    chunks[2].done()
    keep(2)
    pass_on(3, 0)
    outward.third()
    project(2, (0, 3))
    pass_on(3, 1)
    turn(3)
    copy = pltpu.make_async_copy(turned, turned_out, keep_sem.at[3])
    copy.start()
    kept.append(copy)
    project(0, (3, 1))
    project(1, (3, 1))
    project(2, (3, 1))
    outward.done()
    for copy in kept:
        copy.wait()
    moves.finish()


def xor_places(tok):
    places = []
    for r in range(8):
        place = tok
        for bit in (1, 2, 4):
            if r & bit:
                place = flipped(place, bit)
        places.append(place)
    return places


def enter(tokens, gain, cosine, sine, w_query, w_key, w_value, w_gate, w_out):
    rows, width = tokens.shape
    group_rows = rows * lax.axis_size("head")
    cols = w_value.shape[1]
    moves = 4 * 8 + 6
    return pl.pallas_call(
        enter_kernel,
        out_shape=(
            jax.ShapeDtypeStruct((width, group_rows), BF),
            jax.ShapeDtypeStruct((width, 3 * cols), BF),
            jax.ShapeDtypeStruct((w_out.shape[0], width), BF),
            jax.ShapeDtypeStruct((group_rows, cols), BF),
            jax.ShapeDtypeStruct((group_rows, cols), BF),
            jax.ShapeDtypeStruct((group_rows, cols), BF),
        ),
        in_specs=[VMEM] * 4 + [ANY] * 5,
        out_specs=[ANY] * 3 + [VMEM] * 3,
        scratch_shapes=[
            pltpu.VMEM((width, group_rows), BF),
            pltpu.VMEM((group_rows, width), BF),
            pltpu.VMEM((3, width, cols), BF),
            pltpu.SemaphoreType.DMA((moves,)),
            pltpu.SemaphoreType.DMA((moves,)),
            pltpu.SemaphoreType.DMA((5,)),
            pltpu.SemaphoreType.DMA((4,)),
        ],
        compiler_params=pltpu.CompilerParams(
            collective_id=0, has_side_effects=True, vmem_limit_bytes=LIMIT
        ),
        cost_estimate=pl.CostEstimate(
            flops=2 * group_rows * width * 3 * cols, bytes_accessed=40 << 20, transcendentals=0
        ),
    )(tokens, gain[None, :], cosine, sine, w_query, w_key, w_value, w_gate, w_out)


class Scatter:
    def __init__(self, moves, near, term, buffers, result):
        self.moves, self.near, self.term, self.result = moves, near, term, result
        self.odd_out, self.odd_in, self.far_out, self.far_in, self.near_out, self.near_in = buffers
        self.half = self.far_out.shape[0] // 2

    def odd(self, i):
        self.odd_out[i] = self.term(2 * i + 1).astype(BF)
        move = self.moves.go(self.odd_out.at[i], self.odd_in.at[i], self.near["core"])
        if i == 3:
            self.cores = {}
        self.cores[i] = move

    def folded(self, i):
        self.cores[i].wait_recv()
        return self.term(2 * i) + self.odd_in[i].astype(F32)

    def far(self):
        self.far_out[...] = self.folded(3).astype(BF)
        self.fars = [
            self.moves.go(
                self.far_out.at[pl.ds(side * self.half, self.half), :],
                self.far_in.at[side],
                self.near[way],
            )
            for side, way in ((0, "x"), (1, "y"))
        ]

    def close(self):
        half = self.half
        self.nears = []
        for i, side, way in ((1, 1, "x"), (2, 0, "y")):
            value = self.folded(i)
            self.fars[side].wait_recv()
            helped = value[side * half : (side + 1) * half] + self.far_in[side].astype(F32)
            other = value[(1 - side) * half : (2 - side) * half]
            self.near_out[i - 1, pl.ds(side * half, half), :] = helped.astype(BF)
            self.near_out[i - 1, pl.ds((1 - side) * half, half), :] = other.astype(BF)
            self.nears.append(
                self.moves.go(self.near_out.at[i - 1], self.near_in.at[i - 1], self.near[way])
            )

    def done(self):
        value = self.folded(0)
        for i in range(2):
            self.nears[i].wait_recv()
            value = value + self.near_in[i].astype(F32)
        self.result(value)


def leave_kernel(
    grads_ref,
    weights_ref,
    turned_ref,
    tok_ref,
    resid_ref,
    gain_ref,
    sums_ref,
    tokens_grad,
    wq_out,
    wk_out,
    wv_out,
    gains_out,
    grads,
    weights,
    turned,
    ring_out,
    ring_in,
    held,
    odd_out,
    odd_in,
    far_out,
    far_in,
    near_out,
    near_in,
    gains,
    gains_in,
    gains_z,
    send,
    recv,
    load_sem,
):
    near = peers()
    tok = lax.axis_index("tok")
    z = lax.axis_index("head")
    count = lax.axis_size("head")
    rows, width = tok_ref.shape
    part = width // 8
    side_rows = rows // 2
    cols = wv_out.shape[1]
    loads = [
        pltpu.make_async_copy(grads_ref, grads, load_sem.at[0]),
        pltpu.make_async_copy(weights_ref, weights, load_sem.at[1]),
        pltpu.make_async_copy(turned_ref, turned, load_sem.at[2]),
    ]
    for load in loads:
        load.start()
    others = [
        {"tok": tok, "head": lax.rem(z + step, count)} for step in range(1, count)
    ]
    greet(near["core"], near["x"], near["y"], *others)
    moves = Moves(send, recv)

    def ring_term(step):
        owner = lax.rem(z + 2 * count - 1 - step, count)
        at = pl.ds(pl.multiple_of(owner * rows, rows), rows)

        @pl.loop(0, width // 256)
        def _(i):
            to = pl.ds(pl.multiple_of(i * 256, 256), 256)
            held[:, to] = lax.dot_general(
                grads[at, :], weights[to, :], (((1,), (1,)), ((), ())), preferred_element_type=F32
            )

    ring = {}

    def ring_send(step, side):
        at = pl.ds(side * side_rows, side_rows)
        value = held[at, :]
        if step:
            ring[step - 1, side].wait_recv()
            value = value + ring_in[step - 1, at, :].astype(F32)
        ring_out[step, at, :] = value.astype(BF)
        ring[step, side] = moves.go(
            ring_out.at[step, at, :], ring_in.at[step, at, :], near["up"]
        )

    def chunk_term(c):
        def term(r):
            left = turned[pl.ds(r * part, part), :]
            return jnp.concatenate(
                [
                    jnp.dot(
                        left,
                        grads[:, c * cols + j * 256 : c * cols + (j + 1) * 256],
                        preferred_element_type=F32,
                    )
                    for j in range(cols // 256)
                ],
                axis=1,
            )

        return term

    def qk_result(value):
        wq_out[...] = value[:, : cols // 2]
        wk_out[...] = value[:, cols // 2 :]

    def v_result(value):
        wv_out[...] = value

    def buffers(c):
        return (
            odd_out.at[c], odd_in.at[c], far_out.at[c], far_in.at[c], near_out.at[c], near_in.at[c]
        )

    scatters = [
        Scatter(moves, near, chunk_term(c), buffers(c), result)
        for c, result in enumerate((qk_result, v_result))
    ]

    loads[0].wait()
    loads[1].wait()
    ring_term(0)
    ring_send(0, 0)
    ring_send(0, 1)
    loads[2].wait()
    for i in (3, 1, 2, 0):
        scatters[0].odd(i)
    ring_term(1)
    ring_send(1, 0)
    scatters[0].far()
    for i in (3, 1):
        scatters[1].odd(i)
    ring_send(1, 1)
    scatters[0].close()
    ring_term(2)
    for i in (2, 0):
        scatters[1].odd(i)
    ring_send(2, 0)
    scatters[1].far()
    ring_send(2, 1)
    scatters[1].close()
    scatters[0].done()
    ring_term(3)
    scatters[1].done()

    gains[...] = sums_ref[...]
    size = 32
    for side in range(2):
        ring[2, side].wait_recv()

        def block(i, total):
            at = pl.ds(pl.multiple_of(side * side_rows + i * size, size), size)
            values = jnp.concatenate(
                [
                    tok_ref[at, pl.ds(pl.multiple_of(place * part, part), part)]
                    for place in xor_places(tok)
                ],
                axis=1,
            ).astype(F32)
            mean = jnp.mean(values, axis=-1, keepdims=True)
            centred = values - mean
            inverse = lax.rsqrt(jnp.mean(centred * centred, axis=-1, keepdims=True) + EPS)
            unit = centred * inverse
            grad = held[at, :] + ring_in[2, at, :].astype(F32)
            scaled = grad * gain_ref[...]
            first = jnp.mean(scaled, axis=-1, keepdims=True)
            second = jnp.mean(scaled * unit, axis=-1, keepdims=True)
            found = resid_ref[at, :] + inverse * (scaled - first - unit * second)
            for r, place in enumerate(xor_places(tok)):
                tokens_grad[at, pl.ds(pl.multiple_of(place * part, part), part)] = found[
                    :, r * part : (r + 1) * part
                ]
            return total + jnp.sum(grad * unit, axis=0, keepdims=True)

        total = lax.fori_loop(
            0, side_rows // size, block, jnp.zeros((1, width), F32)
        )
        for r, place in enumerate(xor_places(tok)):
            at = pl.ds(pl.multiple_of(place * part, part), part)
            gains[pl.ds(0, 1), at] += total[:, r * part : (r + 1) * part]

    for i, way in enumerate(("core", "x", "y")):
        move = moves.go(gains, gains_in.at[i], near[way])
        move.wait_recv()
        moves.sent(move)
        gains[...] += gains_in[i]
    last = [moves.go(gains, gains_z.at[i], others[i]) for i in range(count - 1)]
    total = gains[...]
    gains_out[...] = total
    for i, move in enumerate(last):
        move.wait_recv()
        gains_out[pl.ds(0, 2), :] += gains_z[i, pl.ds(0, 2), :]
    moves.finish()


def depart(grads, weights, turned, tokens, resid_grad, gain, sums):
    rows, width = tokens.shape
    count = lax.axis_size("head")
    cols = grads.shape[1] // 3
    part = width // 8
    moves = 6 + 2 * 8 + 3 + count - 1
    return pl.pallas_call(
        leave_kernel,
        out_shape=(
            jax.ShapeDtypeStruct((rows, width), F32),
            jax.ShapeDtypeStruct((part, cols // 2), F32),
            jax.ShapeDtypeStruct((part, cols // 2), F32),
            jax.ShapeDtypeStruct((part, cols), F32),
            jax.ShapeDtypeStruct(sums.shape, F32),
        ),
        in_specs=[ANY] * 3 + [VMEM] * 4,
        out_specs=[VMEM] * 5,
        scratch_shapes=[
            pltpu.VMEM(grads.shape, BF),
            pltpu.VMEM(weights.shape, BF),
            pltpu.VMEM(turned.shape, BF),
            pltpu.VMEM((3, rows, width), BF),
            pltpu.VMEM((3, rows, width), BF),
            pltpu.VMEM((rows, width), F32),
            pltpu.VMEM((2, 4, part, cols), BF),
            pltpu.VMEM((2, 4, part, cols), BF),
            pltpu.VMEM((2, part, cols), BF),
            pltpu.VMEM((2, 2, part // 2, cols), BF),
            pltpu.VMEM((2, 2, part, cols), BF),
            pltpu.VMEM((2, 2, part, cols), BF),
            pltpu.VMEM(sums.shape, F32),
            pltpu.VMEM((3,) + sums.shape, F32),
            pltpu.VMEM((count - 1,) + sums.shape, F32),
            pltpu.SemaphoreType.DMA((moves,)),
            pltpu.SemaphoreType.DMA((moves,)),
            pltpu.SemaphoreType.DMA((3,)),
        ],
        compiler_params=pltpu.CompilerParams(
            collective_id=1, has_side_effects=True, vmem_limit_bytes=LIMIT
        ),
        cost_estimate=pl.CostEstimate(
            flops=2 * grads.shape[0] * width * 5 * cols, bytes_accessed=40 << 20, transcendentals=0
        ),
    )(grads, weights, turned, tokens, resid_grad, gain[None, :], sums)


def norm_forward(values, gain):
    mean = jnp.mean(values, axis=-1, keepdims=True)
    centred = values - mean
    inverse = lax.rsqrt(jnp.mean(centred * centred, axis=-1, keepdims=True) + EPS)
    unit = centred * inverse
    return (unit * gain, unit, inverse)


def norm_backward(grad_out, unit, inverse, gain):
    scaled = grad_out * gain
    first = jnp.mean(scaled, axis=-1, keepdims=True)
    second = jnp.mean(scaled * unit, axis=-1, keepdims=True)
    return (inverse * (scaled - first - unit * second), jnp.sum(grad_out * unit, axis=0))


def doc_index(row_ids, starts):
    return jnp.sum((starts[None, :] <= row_ids[:, None]).astype(jnp.int32), axis=1) - 1


def doc_position(row_ids, starts):
    first = jnp.max(jnp.where(starts[None, :] <= row_ids[:, None], starts[None, :], 0), axis=1)
    return row_ids - first


def angles(position, half):
    freq = jnp.exp(-jnp.log(10000.0) * jnp.arange(half, dtype=F32) / half)
    turn = position.astype(F32)[:, None] * freq[None, :]
    return (jnp.cos(turn), jnp.sin(turn))


def rotate(values, cosine, sine):
    half = values.shape[-1] // 2
    first, second = (values[..., :half], values[..., half:])
    return jnp.concatenate(
        [first * cosine - second * sine, first * sine + second * cosine], axis=-1
    )


def unrotate(grads, cosine, sine):
    return rotate(grads, cosine, -sine)


def span_masks(doc_ids, before, log_decay):
    size = doc_ids.shape[0]
    place = jnp.arange(size, dtype=F32)
    lag = place[:, None] - place[None, :]
    same = (doc_ids[:, None] == doc_ids[None, :]) & (lag >= 0)
    decay = jnp.where(same, jnp.exp(jnp.maximum(lag, 0.0) * log_decay), 0.0)
    reach = jnp.where(doc_ids == before, jnp.exp((place + 1.0) * log_decay), 0.0)[:, None]
    leave = jnp.where(doc_ids == doc_ids[-1], jnp.exp((size - 1.0 - place) * log_decay), 0.0)[
        :, None
    ]
    across = jnp.where(doc_ids[-1] == before, jnp.exp(size * log_decay), 0.0)
    return (decay, reach, leave, across)


def gelu_slope(hidden_pre):
    return (
        0.5 * (1.0 + lax.erf(hidden_pre * SQRT_HALF))
        + hidden_pre * jnp.exp(-0.5 * hidden_pre * hidden_pre) * INV_ROOT_TWO_PI
    )


def local(
    tokens,
    cotangent,
    doc_lengths,
    head_order,
    norm_gain,
    w_query,
    w_key,
    w_value,
    w_gate,
    group_gain,
    w_out,
    ffn_gain,
    w_up,
    w_down,
):
    heads = w_query.shape[1] // KEY
    head_count = lax.axis_size("head")
    tok_count = lax.axis_size("tok")
    z = lax.axis_index("head")
    tok = lax.axis_index("tok")
    rows = tokens.shape[0]
    group_rows = rows * head_count
    blocks = group_rows // SPAN
    width = tokens.shape[1]
    part = width // tok_count

    tokens_f = reorder(tokens).astype(F32)
    cot_own = reorder(cotangent)
    gain1 = reorder(norm_gain)
    gain2 = reorder(ffn_gain)
    normed1, unit1, inverse1 = norm_forward(tokens_f, gain1)
    qk = w_query.shape[1]
    vg = w_value.shape[1]
    up_two = jnp.concatenate([w_up, swap(w_up, "head", 2)], axis=1)
    down_two = jnp.concatenate([w_down, swap(w_down, "head", 2)], axis=0)
    up_full = tok_gather(up_two, 0)
    down_full = tok_gather(down_two, 1)
    cot_pair = jnp.concatenate([cot_own, swap(cot_own, "head", 1)], axis=0)

    ends = jnp.cumsum(doc_lengths)
    starts = ends - doc_lengths
    first_row = tok * group_rows
    row_ids = first_row + jnp.arange(group_rows, dtype=jnp.int32)
    doc_ids = doc_index(row_ids, starts)
    previous = doc_index(jnp.reshape(first_row - 1, (1,)), starts)[0]
    group_last = doc_index((jnp.arange(tok_count, dtype=jnp.int32) + 1) * group_rows - 1, starts)
    cosine, sine = angles(doc_position(row_ids, starts), KEY // 2)
    ranks = lax.dynamic_slice_in_dim(head_order, z * heads, heads)
    log_decay = jnp.log1p(-jnp.exp2(-(5.0 + ranks.astype(F32))))

    if paired():
        turned, qkvg_full, out_full, qk_rows, v_rows, gate = enter(
            tokens, gain1, cosine, sine, w_query, w_key, w_value, w_gate, w_out
        )
        gate = gate.astype(F32)
    else:
        group = head_gather(normed1.astype(BF))
        qkvg_full = tok_gather(jnp.concatenate([w_query, w_key, w_value, w_gate], axis=1), 0)
        out_full = tok_gather(w_out, 1)
        projected = mm(group, qkvg_full)
        qk_rows = jnp.concatenate(
            [
                rotate(projected[:, h * KEY : (h + 1) * KEY], cosine, sine).astype(BF)
                for h in range(2 * heads)
            ],
            axis=1,
        )
        v_rows = projected[:, 2 * qk : 2 * qk + vg].astype(BF)
        gate = projected[:, 2 * qk + vg :]

    def head_of(array, head, size):
        return array[:, head * size : (head + 1) * size]

    def block_of(array, block):
        return array[block * SPAN : (block + 1) * SPAN]

    q, k, v, masks = [], [], [], []
    for h in range(heads):
        q.append(head_of(qk_rows, h, KEY))
        k.append(head_of(qk_rows, heads + h, KEY))
        v.append(head_of(v_rows, h, VAL))
        masks.append(
            [
                span_masks(
                    block_of(doc_ids, b),
                    previous if b == 0 else doc_ids[b * SPAN - 1],
                    log_decay[h],
                )
                for b in range(blocks)
            ]
        )

    group_order = jnp.arange(tok_count, dtype=jnp.int32)

    def weigh(lag, last, h):
        return jnp.where(
            (lag >= 0) & (group_last == last),
            jnp.exp(jnp.maximum(lag, 0).astype(F32) * group_rows * log_decay[h]),
            0.0,
        )

    ends_of = []
    added = []
    for h in range(heads):
        state = jnp.zeros((KEY, VAL), F32)
        terms = []
        for b in range(blocks):
            term = mm_tn(block_of(k[h], b), (block_of(v[h], b) * masks[h][b][2]).astype(BF))
            terms.append(term)
            state = masks[h][b][3] * state + term
        added.append(terms)
        ends_of.append(state.astype(BF))
    all_states = lax.all_gather(jnp.concatenate(ends_of, axis=0), "tok", axis=0)
    lag = tok - 1 - group_order
    states = []
    retained = []
    for h in range(heads):
        weights = weigh(lag, previous, h)
        state = jnp.sum(
            all_states[:, h * KEY : (h + 1) * KEY].astype(F32) * weights[:, None, None], axis=0
        )
        mine = []
        outs = []
        for b in range(blocks):
            mine.append(state.astype(BF))
            qb, kb, vb = block_of(q[h], b), block_of(k[h], b), block_of(v[h], b)
            decay, reach, leave, across = masks[h][b]
            probs = (mm_nt(qb, kb) * decay).astype(BF)
            outs.append(mm(probs, vb) + reach * mm(qb, mine[-1]))
            state = across * state + added[h][b]
        states.append(mine)
        retained.append(jnp.concatenate(outs, axis=0))

    mixed_parts, unit_g, inverse_g, grouped, swish, sigma = [], [], [], [], [], []
    for h in range(heads):
        g, u, i = norm_forward(retained[h], head_of(group_gain[None, :], h, VAL))
        gate_h = head_of(gate, h, VAL)
        s = jax.nn.sigmoid(gate_h)
        unit_g.append(u)
        inverse_g.append(i)
        grouped.append(g)
        sigma.append(s)
        swish.append(gate_h * s)
        mixed_parts.append((swish[-1] * g).astype(BF))
    mixed = jnp.concatenate(mixed_parts, axis=1)

    out_sum = head_scatter(lambda i: mm(rows_of(mixed, i, rows), out_full))
    resid = tokens_f + out_sum
    normed2, unit2, inverse2 = norm_forward(resid, gain2)
    lifted2 = normed2.astype(BF)
    lifted2_pair = jnp.concatenate([lifted2, swap(lifted2, "head", 1)], axis=0)
    hidden_pre = mm(lifted2_pair, up_full)
    hidden = jax.nn.gelu(hidden_pre, approximate=False).astype(BF)
    hidden_grad = mm_nt(cot_pair, down_full)
    pre_grad = (hidden_grad * gelu_slope(hidden_pre)).astype(BF)
    far_grad = mm_nt(pre_grad[rows:], up_full).astype(BF)
    lifted2_grad = mm_nt(pre_grad[:rows], up_full) + swap(far_grad, "head", 1).astype(F32)
    resid_part, ffn_gain_local = norm_backward(lifted2_grad, unit2, inverse2, gain2)
    resid_grad = cot_own.astype(F32) + resid_part
    branch_own = resid_grad.astype(BF)
    branch = head_gather(branch_own)

    far_out = mm(hidden[rows:], down_full).astype(BF)
    layer_out = reorder(
        (resid + mm(hidden[:rows], down_full) + swap(far_out, "head", 1).astype(F32)).astype(BF)
    )

    def piece(array, r):
        return array[:, r * part : (r + 1) * part]

    slots = range(tok_count)
    down_two_grad = tok_scatter([mm_tn(hidden, piece(cot_pair, r)) for r in slots])
    half = down_two_grad.shape[0] // 2
    w_down_grad = down_two_grad[:half] + swap(
        down_two_grad[half:].astype(BF), "head", 2
    ).astype(F32)
    up_two_grad = tok_scatter([mm_tn(piece(lifted2_pair, r), pre_grad) for r in slots])
    half = up_two_grad.shape[1] // 2
    w_up_grad = up_two_grad[:, :half] + swap(
        up_two_grad[:, half:].astype(BF), "head", 2
    ).astype(F32)

    mixed_grad = mm_nt(branch, out_full).astype(BF)
    w_out_grad = tok_scatter([mm_tn(mixed, piece(branch, r)) for r in slots])

    gate_parts, ret_grad, group_gain_parts = [], [], []
    for h in range(heads):
        head_grad = head_of(mixed_grad, h, VAL).astype(F32)
        gate_parts.append(
            (head_grad * grouped[h] * (sigma[h] + swish[h] * (1.0 - sigma[h]))).astype(BF)
        )
        back, gain_term = norm_backward(
            head_grad * swish[h], unit_g[h], inverse_g[h], head_of(group_gain[None, :], h, VAL)
        )
        ret_grad.append(back.astype(BF))
        group_gain_parts.append(gain_term)
    gate_grad = jnp.concatenate(gate_parts, axis=1)
    if paired():
        w_gate_grad = tok_scatter(
            [mm(turned[r * part : (r + 1) * part], gate_grad) for r in slots]
        )
    else:
        w_gate_grad = tok_scatter([mm_tn(piece(group, r), gate_grad) for r in slots])

    pending_of, pending_terms = [], []
    for h in range(heads):
        pending = jnp.zeros((KEY, VAL), F32)
        terms = [None] * blocks
        for b in reversed(range(blocks)):
            terms[b] = mm_tn(
                block_of(q[h], b), (block_of(ret_grad[h], b) * masks[h][b][1]).astype(BF)
            )
            pending = masks[h][b][3] * pending + terms[b]
        pending_terms.append(terms)
        pending_of.append(pending.astype(BF))
    all_pending = lax.all_gather(jnp.concatenate(pending_of, axis=0), "tok", axis=0)
    lag_back = group_order - 1 - tok
    shifted_last = doc_index(group_order * group_rows - 1, starts)
    q_parts, k_parts, v_parts = [], [], []
    for h in range(heads):
        weights = jnp.where(
            (lag_back >= 0) & (shifted_last == doc_ids[-1]),
            jnp.exp(jnp.maximum(lag_back, 0).astype(F32) * group_rows * log_decay[h]),
            0.0,
        )
        later = jnp.sum(
            all_pending[:, h * KEY : (h + 1) * KEY].astype(F32) * weights[:, None, None], axis=0
        )
        qg, kg, vg_ = [None] * blocks, [None] * blocks, [None] * blocks
        for b in reversed(range(blocks)):
            qb, kb, vb = block_of(q[h], b), block_of(k[h], b), block_of(v[h], b)
            rb = block_of(ret_grad[h], b)
            decay, reach, leave, across = masks[h][b]
            probs = (mm_nt(qb, kb) * decay).astype(BF)
            score_grad = (mm_nt(rb, vb) * decay).astype(BF)
            later_b = later.astype(BF)
            qg[b] = mm(score_grad, kb) + reach * mm_nt(rb, states[h][b])
            kg[b] = mm_tn(score_grad, qb) + leave * mm_nt(vb, later_b)
            vg_[b] = mm_tn(probs, rb) + leave * mm(kb, later_b)
            later = across * later + pending_terms[h][b]
        q_parts.append(unrotate(jnp.concatenate(qg, axis=0), cosine, sine).astype(BF))
        k_parts.append(unrotate(jnp.concatenate(kg, axis=0), cosine, sine).astype(BF))
        v_parts.append(jnp.concatenate(vg_, axis=0).astype(BF))
    all_grad = jnp.concatenate(q_parts + k_parts + v_parts + [gate_grad], axis=1)
    group_terms = jnp.concatenate(group_gain_parts, axis=0)
    ffn_terms = reorder(ffn_gain_local)
    if paired():
        sums = jnp.concatenate(
            [
                jnp.zeros((1, width), F32),
                ffn_terms[None, :],
                jnp.concatenate([group_terms, jnp.zeros((width - vg,), F32)])[None, :],
                jnp.zeros((5, width), F32),
            ],
            axis=0,
        )
        tokens_grad, w_query_grad, w_key_grad, w_value_grad, sums = depart(
            all_grad, qkvg_full, turned, tokens, resid_grad, gain1, sums
        )
        norm_sum, ffn_sum, group_gain_grad = sums[0], sums[1], sums[2, :vg]
    else:
        row_grad = head_scatter(lambda i: mm_nt(rows_of(all_grad, i, rows), qkvg_full))
        input_part, norm_gain_local = norm_backward(row_grad, unit1, inverse1, gain1)
        tokens_grad = reorder(resid_grad + input_part)
        qkv_grad = all_grad[:, : 2 * qk + vg]
        w_qkv_grad = tok_scatter([mm_tn(piece(group, r), qkv_grad) for r in slots])
        w_query_grad = w_qkv_grad[:, :qk]
        w_key_grad = w_qkv_grad[:, qk : 2 * qk]
        w_value_grad = w_qkv_grad[:, 2 * qk :]
        group_gain_grad = sum_small(group_terms, "tok")
        ffn_sum = sum_small(sum_small(ffn_terms, "tok"), "head")
        norm_sum = sum_small(sum_small(reorder(norm_gain_local), "tok"), "head")
    return (
        layer_out,
        tokens_grad,
        norm_sum,
        w_query_grad,
        w_key_grad,
        w_value_grad,
        w_gate_grad,
        group_gain_grad,
        w_out_grad,
        ffn_sum,
        w_up_grad,
        w_down_grad,
    )


def solution(mesh):
    rows = P(("tok", "head"), None)
    inward = P("tok", "head")
    outward = P("head", "tok")
    return jax.shard_map(
        local,
        mesh=mesh,
        in_specs=(
            rows, rows, P(), P(), P(), inward, inward, inward, inward, P("head"),
            outward, P(), inward, outward,
        ),
        out_specs=(
            rows, rows, P(), inward, inward, inward, inward, P("head"),
            outward, P(), inward, outward,
        ),
        check_vma=False,
    )
```

```python
import jax
import jax.numpy as jnp
from jax import lax
from jax.experimental import pallas as pl
from jax.experimental.pallas import tpu as pltpu
from jax.sharding import PartitionSpec as P

KEY = 256
VAL = 512
SPAN = 512

EPS = 1e-05
SQRT_HALF = 0.7071067811865476
INV_ROOT_TWO_PI = 0.3989422804014327
BF = jnp.bfloat16
F32 = jnp.float32


def mm(left, right):
    return jnp.dot(left, right, preferred_element_type=F32)


def mm_nt(left, right):
    return lax.dot_general(left, right, (((1,), (1,)), ((), ())), preferred_element_type=F32)


def mm_tn(left, right):
    return lax.dot_general(left, right, (((0,), (0,)), ((), ())), preferred_element_type=F32)


def swap(array, axis, bit):
    count = lax.axis_size(axis)
    return lax.ppermute(array, axis, [(i, i ^ bit) for i in range(count)])


def shift(array):
    count = lax.axis_size("head")
    return lax.ppermute(array, "head", [(i, (i + 1) % count) for i in range(count)])


def paired():
    return lax.axis_size("tok") == 8


def reorder(array):
    if not paired():
        return array
    me = lax.axis_index("tok")
    width = array.shape[-1] // 8
    return jnp.concatenate(
        [
            lax.dynamic_slice_in_dim(array, (me ^ r) * width, width, array.ndim - 1)
            for r in range(8)
        ],
        axis=-1,
    )


def halves(array):
    half = array.shape[0] // 2
    return array[:half], array[half:]


def tok_gather(shard, axis):
    if not paired():
        return lax.all_gather(shard, "tok", axis=axis, tiled=True)
    along_x = swap(shard, "tok", 2)
    along_y = swap(shard, "tok", 4)
    far = jnp.concatenate(
        [swap(halves(along_x)[0], "tok", 4), swap(halves(along_y)[1], "tok", 2)], axis=0
    )
    own = [shard, along_x, along_y, far]
    pieces = []
    for piece in own:
        pieces += [piece, swap(piece, "tok", 1)]
    return jnp.concatenate(pieces, axis=axis)


def tok_scatter(pieces):
    pieces = [p.astype(BF) for p in pieces]
    if not paired():
        return lax.psum_scatter(jnp.stack(pieces), "tok", scatter_dimension=0).astype(F32)
    kept = [
        pieces[r].astype(F32) + swap(pieces[r + 1], "tok", 1).astype(F32) for r in (0, 2, 4, 6)
    ]
    zero, two, four, six = kept
    six_a, six_b = halves(six.astype(BF))
    two_a, two_b = halves(two)
    four_a, four_b = halves(four)
    four_a = four_a + swap(six_a, "tok", 2).astype(F32)
    two_b = two_b + swap(six_b, "tok", 4).astype(F32)
    two = jnp.concatenate([two_a, two_b], axis=0).astype(BF)
    four = jnp.concatenate([four_a, four_b], axis=0).astype(BF)
    return zero + swap(two, "tok", 2).astype(F32) + swap(four, "tok", 4).astype(F32)


def head_gather(rows):
    count = lax.axis_size("head")
    me = lax.axis_index("head")
    size = rows.shape[0]
    whole = jnp.zeros((count * size,) + rows.shape[1:], rows.dtype)
    whole = lax.dynamic_update_slice_in_dim(whole, rows, me * size, 0)
    for step in range(1, count):
        rows = shift(rows)
        source = lax.rem(me - step + count, count)
        whole = lax.dynamic_update_slice_in_dim(whole, rows, source * size, 0)
    return whole


def head_scatter(term):
    count = lax.axis_size("head")
    me = lax.axis_index("head")
    total = term(lax.rem(me + count - 1, count))
    for step in range(1, count):
        arrived = shift(total.astype(BF))
        owner = lax.rem(me + 2 * count - 1 - step, count)
        total = term(owner) + arrived.astype(F32)
    return total


def rows_of(array, index, size):
    return lax.dynamic_slice_in_dim(array, index * size, size, 0)


def sum_small(vector, axis):
    count = lax.axis_size(axis)
    bit = 1
    while bit < count:
        vector = vector + swap(vector, axis, bit)
        bit *= 2
    return vector


MESH = pl.DeviceIdType.MESH
ANY = pl.BlockSpec(memory_space=pl.ANY)
VMEM = pl.BlockSpec(memory_space=pltpu.VMEM)
LIMIT = 60 * 1024 * 1024


def flipped(index, bit):
    return index + bit - 2 * bit * lax.rem(lax.div(index, bit), 2)


def peers():
    tok = lax.axis_index("tok")
    z = lax.axis_index("head")
    count = lax.axis_size("head")
    return {
        "core": {"tok": flipped(tok, 1), "head": z},
        "x": {"tok": flipped(tok, 2), "head": z},
        "y": {"tok": flipped(tok, 4), "head": z},
        "up": {"tok": tok, "head": lax.rem(z + 1, count)},
        "down": {"tok": tok, "head": lax.rem(z + count - 1, count)},
        "pair": {"tok": tok, "head": flipped(z, 1)},
        "cross": {"tok": tok, "head": flipped(z, 2)},
    }


def everyone():
    near = peers()
    tok = lax.axis_index("tok")
    z = lax.axis_index("head")
    count = lax.axis_size("head")
    others = [{"tok": tok, "head": lax.rem(z + step, count)} for step in range(1, count)]
    return [near["core"], near["x"], near["y"], *others]


def greet(*devices):
    barrier = pltpu.get_barrier_semaphore()
    for device in devices:
        pl.semaphore_signal(barrier, inc=1, device_id=device, device_id_type=MESH)
    pl.semaphore_wait(barrier, len(devices))


class Moves:
    def __init__(self, send, recv):
        self.send, self.recv, self.made, self.over = send, recv, [], []

    def go(self, src, dst, device):
        n = len(self.made)
        copy = pltpu.make_async_remote_copy(
            src_ref=src,
            dst_ref=dst,
            send_sem=self.send.at[n],
            recv_sem=self.recv.at[n],
            device_id=device,
            device_id_type=MESH,
        )
        copy.start()
        self.made.append(copy)
        return copy

    def sent(self, copy):
        copy.wait_send()
        self.over.append(copy)

    def finish(self):
        for copy in self.made:
            if not any(copy is gone for gone in self.over):
                copy.wait_send()


class Gather:
    def __init__(self, moves, near, view):
        self.moves, self.near, self.view = moves, near, view

    def first(self):
        go, near, view = self.moves.go, self.near, self.view
        self.x = go(view(0), view(2), near["x"])
        self.y = go(view(0), view(4), near["y"])
        self.cores = [go(view(0), view(1), near["core"])]

    def second(self):
        go, near, view = self.moves.go, self.near, self.view
        self.x.wait_recv()
        self.far = [go(view(2, 0), view(6, 0), near["y"])]
        self.cores.append(go(view(2), view(3), near["core"]))
        self.y.wait_recv()
        self.far.append(go(view(4, 1), view(6, 1), near["x"]))
        self.cores.append(go(view(4), view(5), near["core"]))

    def third(self):
        go, near, view = self.moves.go, self.near, self.view
        for copy in self.far:
            copy.wait_recv()
        self.cores.append(go(view(6), view(7), near["core"]))

    def done(self):
        for copy in self.cores:
            copy.wait_recv()


def enter_kernel(
    tok_ref,
    gain_ref,
    cos_ref,
    sin_ref,
    wq_ref,
    wk_ref,
    wv_ref,
    wg_ref,
    wo_ref,
    turned_out,
    weights_out,
    out_full,
    qk_out,
    v_out,
    gate_out,
    turned,
    group,
    weights,
    send,
    recv,
    own_sem,
    keep_sem,
):
    near = peers()
    tok = lax.axis_index("tok")
    z = lax.axis_index("head")
    count = lax.axis_size("head")
    rows, width = tok_ref.shape
    part = width // 8
    cols = weights.shape[2]
    half = wq_ref.shape[1]

    own = [
        pltpu.make_async_copy(wq_ref, weights.at[0, pl.ds(0, part), pl.ds(0, half)], own_sem.at[0]),
        pltpu.make_async_copy(
            wk_ref, weights.at[0, pl.ds(0, part), pl.ds(half, half)], own_sem.at[1]
        ),
        pltpu.make_async_copy(wv_ref, weights.at[1, pl.ds(0, part), :], own_sem.at[2]),
        pltpu.make_async_copy(wg_ref, weights.at[2, pl.ds(0, part), :], own_sem.at[3]),
        pltpu.make_async_copy(wo_ref, out_full.at[:, pl.ds(0, part)], own_sem.at[4]),
    ]
    for copy in own:
        copy.start()
    greet(near["core"], near["x"], near["y"], near["up"], near["down"])
    moves = Moves(send, recv)

    def chunk_view(c):
        def view(r, side=None):
            if side is None:
                return weights.at[c, pl.ds(r * part, part), :]
            return weights.at[c, pl.ds(r * part + side * (part // 2), part // 2), :]

        return view

    def out_view(r, side=None):
        if side is None:
            return out_full.at[:, pl.ds(r * part, part)]
        size = out_full.shape[0] // 2
        return out_full.at[pl.ds(side * size, size), pl.ds(r * part, part)]

    chunks = [Gather(moves, near, chunk_view(c)) for c in range(3)]
    outward = Gather(moves, near, out_view)
    own[0].wait()
    own[1].wait()
    chunks[0].first()
    own[2].wait()
    chunks[1].first()
    own[3].wait()
    own[4].wait()

    @pl.loop(0, rows // 32)
    def _(i):
        at = pl.ds(pl.multiple_of(i * 32, 32), 32)
        values = jnp.concatenate(
            [
                tok_ref[at, pl.ds(pl.multiple_of(place * part, part), part)]
                for place in xor_places(tok)
            ],
            axis=1,
        ).astype(F32)
        mean = jnp.mean(values, axis=-1, keepdims=True)
        centred = values - mean
        inverse = lax.rsqrt(jnp.mean(centred * centred, axis=-1, keepdims=True) + EPS)
        lifted = (centred * inverse * gain_ref[...]).astype(BF)
        group[pl.ds(pl.multiple_of(z * rows + i * 32, 32), 32), :] = lifted

    def shard(step, side):
        owner = lax.rem(z - step + count, count)
        size = rows // 2
        return group.at[pl.ds(pl.multiple_of(owner * rows + side * size, size), size), :]

    ring = {}

    def pass_on(step, side):
        if step:
            ring[step - 1, side].wait_recv()
        if step < count - 1:
            ring[step, side] = moves.go(shard(step, side), shard(step, side), near["up"])

    def project(c, steps):
        first, number = steps

        @pl.loop(0, number * (cols // 256))
        def _(i):
            step = first + lax.div(i, cols // 256)
            tile = lax.rem(i, cols // 256)
            owner = lax.rem(z - step + count, count)
            at = pl.ds(pl.multiple_of(owner * rows, rows), rows)
            to = pl.ds(pl.multiple_of(tile * 256, 256), 256)
            found = jnp.dot(group[at, :], weights[c, :, to], preferred_element_type=F32)
            if c == 0:
                cosine, sine = cos_ref[at, :], sin_ref[at, :]
                one, two = found[:, :128], found[:, 128:]
                qk_out[at, to] = jnp.concatenate(
                    [one * cosine - two * sine, one * sine + two * cosine], axis=1
                ).astype(BF)
            elif c == 1:
                v_out[at, to] = found.astype(BF)
            else:
                gate_out[at, to] = found.astype(BF)

    def turn(step):
        owner = lax.rem(z - step + count, count)

        @pl.loop(0, width // 256)
        def _(i):
            at = pl.ds(pl.multiple_of(i * 256, 256), 256)
            to = pl.ds(pl.multiple_of(owner * rows, rows), rows)
            turned[at, to] = group[to, at].T

    kept = []

    def keep(c):
        copy = pltpu.make_async_copy(
            weights.at[c], weights_out.at[:, pl.ds(c * cols, cols)], keep_sem.at[c]
        )
        copy.start()
        kept.append(copy)

    pass_on(0, 0)
    pass_on(0, 1)
    chunks[0].second()
    chunks[2].first()
    pass_on(1, 0)
    chunks[1].second()
    outward.first()
    pass_on(1, 1)
    chunks[0].third()
    chunks[0].done()
    keep(0)
    project(0, (0, 2))
    pass_on(2, 0)
    turn(0)
    turn(1)
    chunks[2].second()
    pass_on(2, 1)
    chunks[1].third()
    chunks[1].done()
    keep(1)
    project(1, (0, 2))
    outward.second()
    project(0, (2, 1))
    project(1, (2, 1))
    turn(2)
    chunks[2].third()
    chunks[2].done()
    keep(2)
    pass_on(3, 0)
    outward.third()
    project(2, (0, 3))
    pass_on(3, 1)
    turn(3)
    copy = pltpu.make_async_copy(turned, turned_out, keep_sem.at[3])
    copy.start()
    kept.append(copy)
    project(0, (3, 1))
    project(1, (3, 1))
    project(2, (3, 1))
    outward.done()
    for copy in kept:
        copy.wait()
    moves.finish()


def xor_places(tok):
    places = []
    for r in range(8):
        place = tok
        for bit in (1, 2, 4):
            if r & bit:
                place = flipped(place, bit)
        places.append(place)
    return places


def enter(tokens, gain, cosine, sine, w_query, w_key, w_value, w_gate, w_out):
    rows, width = tokens.shape
    group_rows = rows * lax.axis_size("head")
    cols = w_value.shape[1]
    moves = 4 * 8 + 6
    return pl.pallas_call(
        enter_kernel,
        out_shape=(
            jax.ShapeDtypeStruct((width, group_rows), BF),
            jax.ShapeDtypeStruct((width, 3 * cols), BF),
            jax.ShapeDtypeStruct((w_out.shape[0], width), BF),
            jax.ShapeDtypeStruct((group_rows, cols), BF),
            jax.ShapeDtypeStruct((group_rows, cols), BF),
            jax.ShapeDtypeStruct((group_rows, cols), BF),
        ),
        in_specs=[VMEM] * 4 + [ANY] * 5,
        out_specs=[ANY] * 3 + [VMEM] * 3,
        scratch_shapes=[
            pltpu.VMEM((width, group_rows), BF),
            pltpu.VMEM((group_rows, width), BF),
            pltpu.VMEM((3, width, cols), BF),
            pltpu.SemaphoreType.DMA((moves,)),
            pltpu.SemaphoreType.DMA((moves,)),
            pltpu.SemaphoreType.DMA((5,)),
            pltpu.SemaphoreType.DMA((4,)),
        ],
        compiler_params=pltpu.CompilerParams(
            collective_id=0, has_side_effects=True, vmem_limit_bytes=LIMIT
        ),
        cost_estimate=pl.CostEstimate(
            flops=2 * group_rows * width * 3 * cols, bytes_accessed=40 << 20, transcendentals=0
        ),
    )(tokens, gain[None, :], cosine, sine, w_query, w_key, w_value, w_gate, w_out)


class Scatter:
    def __init__(self, moves, near, term, buffers, result, before=None, ready=None):
        self.moves, self.near, self.term, self.result = moves, near, term, result
        self.odd_out, self.odd_in, self.far_out, self.far_in, self.near_out, self.near_in = buffers
        self.half = self.far_out.shape[0] // 2
        self.before, self.ready, self.frees = before, ready, None
        self.cores = {}

    def odd(self, i):
        if self.before is not None:
            if not self.cores:
                pl.semaphore_wait(self.ready, 1)
            self.moves.sent(self.before.cores[i])
        self.odd_out[i] = self.term(2 * i + 1).astype(BF)
        self.cores[i] = self.moves.go(self.odd_out.at[i], self.odd_in.at[i], self.near["core"])

    def folded(self, i):
        self.cores[i].wait_recv()
        return self.term(2 * i) + self.odd_in[i].astype(F32)

    def far(self):
        value = self.folded(3).astype(BF)
        if self.before is not None:
            for move in self.before.fars:
                self.moves.sent(move)
        self.far_out[...] = value
        self.fars = [
            self.moves.go(
                self.far_out.at[pl.ds(side * self.half, self.half), :],
                self.far_in.at[side],
                self.near[way],
            )
            for side, way in ((0, "x"), (1, "y"))
        ]

    def close(self):
        half = self.half
        self.nears = []
        for i, side, way in ((1, 1, "x"), (2, 0, "y")):
            value = self.folded(i)
            self.fars[side].wait_recv()
            helped = value[side * half : (side + 1) * half] + self.far_in[side].astype(F32)
            other = value[(1 - side) * half : (2 - side) * half]
            if self.before is not None:
                self.moves.sent(self.before.nears[i - 1])
            self.near_out[i - 1, pl.ds(side * half, half), :] = helped.astype(BF)
            self.near_out[i - 1, pl.ds((1 - side) * half, half), :] = other.astype(BF)
            self.nears.append(
                self.moves.go(self.near_out.at[i - 1], self.near_in.at[i - 1], self.near[way])
            )
        self.result[...] = self.folded(0)
        if self.frees is not None:
            pl.semaphore_signal(
                self.frees, inc=1, device_id=self.near["core"], device_id_type=MESH
            )

    def done(self):
        for i in range(2):
            self.nears[i].wait_recv()
        self.result[...] += self.near_in[0].astype(F32) + self.near_in[1].astype(F32)


def leave_kernel(
    grads_ref,
    weights_ref,
    turned_ref,
    tok_ref,
    resid_ref,
    gain_ref,
    ffn_ref,
    group_ref,
    tokens_grad,
    wqk_out,
    wv_out,
    wg_out,
    gains_out,
    grads,
    weights,
    turned,
    ring_out,
    ring_in,
    held,
    odd_out,
    odd_in,
    far_out,
    far_in,
    near_out,
    near_in,
    gains,
    gains_in,
    gains_z,
    send,
    recv,
    load_sem,
    free_sem,
):
    near = peers()
    tok = lax.axis_index("tok")
    z = lax.axis_index("head")
    count = lax.axis_size("head")
    rows, width = tok_ref.shape
    part = width // 8
    side_rows = rows // 2
    cols = wv_out.shape[1]
    loads = [
        pltpu.make_async_copy(grads_ref, grads, load_sem.at[0]),
        pltpu.make_async_copy(weights_ref, weights, load_sem.at[1]),
        pltpu.make_async_copy(turned_ref, turned, load_sem.at[2]),
    ]
    for load in loads:
        load.start()
    others = [
        {"tok": tok, "head": lax.rem(z + step, count)} for step in range(1, count)
    ]
    greet(near["core"], near["x"], near["y"], *others)
    moves = Moves(send, recv)

    def ring_term(step):
        owner = lax.rem(z + 2 * count - 1 - step, count)
        at = pl.ds(pl.multiple_of(owner * rows, rows), rows)

        @pl.loop(0, width // 256)
        def _(i):
            to = pl.ds(pl.multiple_of(i * 256, 256), 256)
            held[:, to] = lax.dot_general(
                grads[at, :], weights[to, :], (((1,), (1,)), ((), ())), preferred_element_type=F32
            )

    ring = {}

    def ring_send(step, side):
        at = pl.ds(side * side_rows, side_rows)
        value = held[at, :]
        if step:
            ring[step - 1, side].wait_recv()
            value = value + ring_in[step - 1, at, :].astype(F32)
        ring_out[step, at, :] = value.astype(BF)
        ring[step, side] = moves.go(
            ring_out.at[step, at, :], ring_in.at[step, at, :], near["up"]
        )

    def chunk_term(c):
        def term(r):
            left = turned[pl.ds(r * part, part), :]
            return jnp.concatenate(
                [
                    jnp.dot(
                        left,
                        grads[:, c * cols + j * 256 : c * cols + (j + 1) * 256],
                        preferred_element_type=F32,
                    )
                    for j in range(cols // 256)
                ],
                axis=1,
            )

        return term

    def buffers(c):
        s = c % 2
        return (
            odd_out.at[s], odd_in.at[s], far_out.at[s], far_in.at[c], near_out.at[s], near_in.at[c]
        )

    scatters = [
        Scatter(moves, near, chunk_term(c), buffers(c), result)
        for c, result in enumerate((wqk_out, wv_out))
    ]
    scatters.append(
        Scatter(moves, near, chunk_term(2), buffers(2), wg_out, scatters[0], free_sem)
    )
    scatters[0].frees = free_sem

    loads[0].wait()
    loads[1].wait()
    ring_term(0)
    ring_send(0, 0)
    ring_send(0, 1)
    loads[2].wait()
    for i in (3, 1, 2, 0):
        scatters[0].odd(i)
    ring_term(1)
    ring_send(1, 0)
    scatters[0].far()
    for i in (3, 1):
        scatters[1].odd(i)
    ring_send(1, 1)
    scatters[0].close()
    for i in (2, 0):
        scatters[1].odd(i)
    ring_term(2)
    ring_send(2, 0)
    scatters[1].far()
    for i in (3, 1):
        scatters[2].odd(i)
    ring_send(2, 1)
    scatters[1].close()
    for i in (2, 0):
        scatters[2].odd(i)
    scatters[0].done()
    scatters[2].far()
    ring_term(3)
    scatters[1].done()
    scatters[2].close()
    scatters[2].done()

    gains[...] = jnp.zeros_like(gains)
    gains[pl.ds(2, 1), pl.ds(0, group_ref.shape[1])] = group_ref[pl.ds(0, 1), :]
    for r, place in enumerate(xor_places(tok)):
        at = pl.ds(pl.multiple_of(place * part, part), part)
        gains[pl.ds(1, 1), at] = (
            ffn_ref[pl.ds(0, 1), r * part : (r + 1) * part]
            + ffn_ref[pl.ds(1, 1), r * part : (r + 1) * part]
        )
    size = 32
    for side in range(2):
        ring[2, side].wait_recv()

        def block(i, total):
            at = pl.ds(pl.multiple_of(side * side_rows + i * size, size), size)
            values = jnp.concatenate(
                [
                    tok_ref[at, pl.ds(pl.multiple_of(place * part, part), part)]
                    for place in xor_places(tok)
                ],
                axis=1,
            ).astype(F32)
            mean = jnp.mean(values, axis=-1, keepdims=True)
            centred = values - mean
            inverse = lax.rsqrt(jnp.mean(centred * centred, axis=-1, keepdims=True) + EPS)
            unit = centred * inverse
            grad = held[at, :] + ring_in[2, at, :].astype(F32)
            scaled = grad * gain_ref[...]
            first = jnp.mean(scaled, axis=-1, keepdims=True)
            second = jnp.mean(scaled * unit, axis=-1, keepdims=True)
            found = resid_ref[at, :] + inverse * (scaled - first - unit * second)
            for r, place in enumerate(xor_places(tok)):
                tokens_grad[at, pl.ds(pl.multiple_of(place * part, part), part)] = found[
                    :, r * part : (r + 1) * part
                ]
            return total + jnp.sum(grad * unit, axis=0, keepdims=True)

        total = lax.fori_loop(
            0, side_rows // size, block, jnp.zeros((1, width), F32)
        )
        for r, place in enumerate(xor_places(tok)):
            at = pl.ds(pl.multiple_of(place * part, part), part)
            gains[pl.ds(0, 1), at] += total[:, r * part : (r + 1) * part]

    for i, way in enumerate(("core", "x", "y")):
        move = moves.go(gains, gains_in.at[i], near[way])
        move.wait_recv()
        moves.sent(move)
        gains[...] += gains_in[i]
    last = [moves.go(gains, gains_z.at[i], others[i]) for i in range(count - 1)]
    total = gains[...]
    gains_out[...] = total
    for i, move in enumerate(last):
        move.wait_recv()
        gains_out[pl.ds(0, 2), :] += gains_z[i, pl.ds(0, 2), :]
    moves.finish()


def depart(grads, weights, turned, tokens, resid_grad, gain, ffn_terms, group_terms):
    rows, width = tokens.shape
    count = lax.axis_size("head")
    cols = grads.shape[1] // 3
    part = width // 8
    moves = 6 + 3 * 8 + 3 + count - 1
    sums = (8, width)
    return pl.pallas_call(
        leave_kernel,
        out_shape=(
            jax.ShapeDtypeStruct((rows, width), F32),
            jax.ShapeDtypeStruct((part, cols), F32),
            jax.ShapeDtypeStruct((part, cols), F32),
            jax.ShapeDtypeStruct((part, cols), F32),
            jax.ShapeDtypeStruct(sums, F32),
        ),
        in_specs=[ANY] * 3 + [VMEM] * 5,
        out_specs=[VMEM] * 5,
        scratch_shapes=[
            pltpu.VMEM(grads.shape, BF),
            pltpu.VMEM(weights.shape, BF),
            pltpu.VMEM(turned.shape, BF),
            pltpu.VMEM((3, rows, width), BF),
            pltpu.VMEM((3, rows, width), BF),
            pltpu.VMEM((rows, width), F32),
            pltpu.VMEM((2, 4, part, cols), BF),
            pltpu.VMEM((2, 4, part, cols), BF),
            pltpu.VMEM((2, part, cols), BF),
            pltpu.VMEM((3, 2, part // 2, cols), BF),
            pltpu.VMEM((2, 2, part, cols), BF),
            pltpu.VMEM((3, 2, part, cols), BF),
            pltpu.VMEM(sums, F32),
            pltpu.VMEM((3,) + sums, F32),
            pltpu.VMEM((count - 1,) + sums, F32),
            pltpu.SemaphoreType.DMA((moves,)),
            pltpu.SemaphoreType.DMA((moves,)),
            pltpu.SemaphoreType.DMA((3,)),
            pltpu.SemaphoreType.REGULAR,
        ],
        compiler_params=pltpu.CompilerParams(
            collective_id=1, has_side_effects=True, vmem_limit_bytes=LIMIT
        ),
        cost_estimate=pl.CostEstimate(
            flops=2 * grads.shape[0] * width * 5 * cols, bytes_accessed=40 << 20, transcendentals=0
        ),
    )(
        grads, weights, turned, tokens, resid_grad, gain[None, :], ffn_terms, group_terms
    )


def dot_nt(left, right):
    return lax.dot_general(left, right, (((1,), (1,)), ((), ())), preferred_element_type=F32)


def dot_tn(left, right):
    return lax.dot_general(left, right, (((0,), (0,)), ((), ())), preferred_element_type=F32)


def dot_nn(left, right):
    return jnp.dot(left, right, preferred_element_type=F32)


def tile_decay(docs_col, docs_row, log_decay, first, tile, top):
    size = tile + top
    shape = (top, size)
    lag = (
        lax.broadcasted_iota(jnp.int32, shape, 0)
        + tile
        - lax.broadcasted_iota(jnp.int32, shape, 1)
    )
    same = docs_col[pl.ds(first + tile, top), :] == docs_row[:, pl.ds(first, size)]
    power = jnp.exp(jnp.maximum(lag, 0).astype(F32) * log_decay)
    return jnp.where(same & (lag >= 0), power, 0.0)


def retain_kernel(
    decay_ref,
    across_ref,
    fold_ref,
    docs_col,
    docs_row,
    scale_ref,
    gain_ref,
    qk_ref,
    v_ref,
    gate_ref,
    tok_ref,
    wo_ref,
    cot_ref,
    wu_ref,
    wd_ref,
    resid_out,
    unit_out,
    inverse_out,
    states_out,
    cot_pair,
    mixed_turned,
    up_full,
    down_full,
    mixed_out,
    out_weights,
    retained,
    terms,
    folded,
    gathered,
    held,
    ring_out,
    ring_in,
    cot_rows,
    send,
    recv,
    own_sem,
):
    near = peers()
    tok = lax.axis_index("tok")
    z = lax.axis_index("head")
    count = lax.axis_size("head")
    rows, width = tok_ref.shape
    group_rows = rows * count
    part = width // 8
    heads = v_ref.shape[1] // VAL
    blocks = group_rows // SPAN
    side_rows = rows // 2
    slice_ = wu_ref.shape[1]
    own = [
        pltpu.make_async_copy(
            wu_ref, up_full.at[pl.ds(0, part), pl.ds(0, slice_)], own_sem.at[0]
        ),
        pltpu.make_async_copy(
            wd_ref, down_full.at[pl.ds(0, slice_), pl.ds(0, part)], own_sem.at[1]
        ),
        pltpu.make_async_copy(wo_ref, out_weights, own_sem.at[2]),
    ]
    for copy in own:
        copy.start()
    greet(*everyone())
    moves = Moves(send, recv)
    far_up = moves.go(
        wu_ref, up_full.at[pl.ds(0, part), pl.ds(slice_, slice_)], near["cross"]
    )
    far_down = moves.go(
        wd_ref, down_full.at[pl.ds(slice_, slice_), pl.ds(0, part)], near["cross"]
    )

    def block_rows(b):
        return pl.ds(pl.multiple_of(b * SPAN, SPAN), SPAN)

    def q_cols(h):
        return pl.ds(h * KEY, KEY)

    def k_cols(h):
        return pl.ds((heads + h) * KEY, KEY)

    def v_cols(h):
        return pl.ds(h * VAL, VAL)

    for h in range(heads):
        total = jnp.zeros((KEY, VAL), F32)
        for b in range(blocks):
            weighed = v_ref[block_rows(b), v_cols(h)].astype(F32) * scale_ref[
                block_rows(b), heads + h : heads + h + 1
            ]
            term = dot_tn(qk_ref[block_rows(b), k_cols(h)], weighed.astype(BF))
            terms[b, pl.ds(h * KEY, KEY), :] = term
            total = across_ref[h, b] * total + term
        gathered[0, pl.ds(h * KEY, KEY), :] = total.astype(BF)

    def state_view(r, side=None):
        if side is None:
            return gathered.at[r]
        size = gathered.shape[1] // 2
        return gathered.at[r, pl.ds(side * size, size), :]

    def up_view(s):
        def view(r, side=None):
            if side is None:
                return up_full.at[pl.ds(r * part, part), pl.ds(s * slice_, slice_)]
            size = part // 2
            return up_full.at[
                pl.ds(r * part + side * size, size), pl.ds(s * slice_, slice_)
            ]

        return view

    def down_view(s):
        def view(r, side=None):
            if side is None:
                return down_full.at[pl.ds(s * slice_, slice_), pl.ds(r * part, part)]
            size = slice_ // 2
            return down_full.at[
                pl.ds(s * slice_ + side * size, size), pl.ds(r * part, part)
            ]

        return view

    states = Gather(moves, near, state_view)
    wide = [
        Gather(moves, near, view) for view in (up_view(0), down_view(0), up_view(1), down_view(1))
    ]
    states.first()
    own[0].wait()
    own[1].wait()
    wide[0].first()
    cot_move = moves.go(cot_ref, cot_rows, near["pair"])

    def intra(h):
        @pl.loop(0, blocks)
        def _(b):
            first = pl.multiple_of(b * SPAN, SPAN)
            for tile in range(0, SPAN, 128):
                at = pl.ds(first + tile, 128)
                seen = pl.ds(first, tile + 128)
                scores = dot_nt(qk_ref[at, q_cols(h)], qk_ref[seen, k_cols(h)])
                mask = tile_decay(docs_col, docs_row, decay_ref[h], first, tile, 128)
                probs = (scores * mask).astype(BF)
                retained[at, v_cols(h)] = dot_nn(probs, v_ref[seen, v_cols(h)])

    def finish_head(h):
        first = jnp.zeros((KEY, VAL), F32)
        for r in range(8):
            first = first + fold_ref[h, r] * gathered[r, pl.ds(h * KEY, KEY), :].astype(F32)
        for b in range(blocks):
            folded[b] = first.astype(BF)
            states_out[pl.ds((h * blocks + b) * KEY, KEY), :] = first.astype(BF)
            first = across_ref[h, b] * first + terms[b, pl.ds(h * KEY, KEY), :]

        @pl.loop(0, group_rows // 128)
        def _(i):
            at = pl.ds(pl.multiple_of(i * 128, 128), 128)
            b = lax.div(i, SPAN // 128)
            cross = dot_nn(qk_ref[at, q_cols(h)], folded[b])
            values = retained[at, v_cols(h)] + scale_ref[at, h : h + 1] * cross
            mean = jnp.mean(values, axis=-1, keepdims=True)
            centred = values - mean
            inverse = lax.rsqrt(jnp.mean(centred * centred, axis=-1, keepdims=True) + EPS)
            unit = centred * inverse
            gate = gate_ref[at, v_cols(h)].astype(F32)
            swish = gate / (1.0 + jnp.exp(-gate))
            unit_out[at, v_cols(h)] = unit.astype(BF)
            inverse_out[at, h : h + 1] = inverse
            mixed = (swish * unit * gain_ref[:, h * VAL : (h + 1) * VAL]).astype(BF)
            mixed_out[at, v_cols(h)] = mixed
            mixed_turned[v_cols(h), at] = mixed.T

    intra(0)
    states.second()
    wide[1].first()
    for h in range(1, heads):
        intra(h)
    states.third()
    wide[0].second()
    states.done()
    for h in range(heads):
        finish_head(h)

    def ring_term(step):
        owner = lax.rem(z + 2 * count - 1 - step, count)
        at = pl.ds(pl.multiple_of(owner * rows, rows), rows)

        @pl.loop(0, width // 256)
        def _(i):
            to = pl.ds(pl.multiple_of(i * 256, 256), 256)
            held[:, to] = dot_nn(mixed_out[at, :], out_weights[:, to])

    ring = {}

    def ring_send(step, side):
        at = pl.ds(side * side_rows, side_rows)
        value = held[at, :]
        if step:
            ring[step - 1, side].wait_recv()
            value = value + ring_in[step - 1, at, :].astype(F32)
        ring_out[step, at, :] = value.astype(BF)
        ring[step, side] = moves.go(
            ring_out.at[step, at, :], ring_in.at[step, at, :], near["up"]
        )

    own[2].wait()
    ring_term(0)
    ring_send(0, 0)
    ring_send(0, 1)
    wide[1].second()
    far_up.wait_recv()
    wide[2].first()
    wide[0].third()
    ring_term(1)
    ring_send(1, 0)
    far_down.wait_recv()
    wide[3].first()
    wide[1].third()
    ring_send(1, 1)
    ring_term(2)
    wide[2].second()
    ring_send(2, 0)
    wide[3].second()
    ring_send(2, 1)
    ring_term(3)
    wide[2].third()
    wide[3].third()
    size = 32
    for side in range(2):
        ring[2, side].wait_recv()

        @pl.loop(0, side_rows // size)
        def _(i):
            at = pl.ds(pl.multiple_of(side * side_rows + i * size, size), size)
            values = jnp.concatenate(
                [
                    tok_ref[at, pl.ds(pl.multiple_of(place * part, part), part)]
                    for place in xor_places(tok)
                ],
                axis=1,
            ).astype(F32)
            resid_out[at, :] = values + held[at, :] + ring_in[2, at, :].astype(F32)

    cot_move.wait_recv()
    for ref, first in ((cot_ref, 0), (cot_rows, rows)):
        for r, place in enumerate(xor_places(tok)):
            cot_pair[pl.ds(first, rows), pl.ds(r * part, part)] = ref[
                :, pl.ds(pl.multiple_of(place * part, part), part)
            ]
    for gather in wide:
        gather.done()
    moves.finish()


SMEM = pl.BlockSpec(memory_space=pltpu.SMEM)


def retain(
    decay, across, fold, docs, scales, gain, qk, v, gate, tokens, out_full, cotangent, w_up, w_down
):
    rows, width = tokens.shape
    count = lax.axis_size("head")
    group_rows = rows * count
    heads = v.shape[1] // VAL
    blocks = group_rows // SPAN
    wide = 2 * w_up.shape[1]
    moves = 3 + 5 * 8 + 6
    struct = jax.ShapeDtypeStruct
    return pl.pallas_call(
        retain_kernel,
        out_shape=(
            struct((rows, width), F32),
            struct(v.shape, BF),
            struct((group_rows, heads), F32),
            struct((heads * blocks * KEY, VAL), BF),
            struct((2 * rows, width), BF),
            struct((heads * VAL, group_rows), BF),
            struct((width, wide), BF),
            struct((wide, width), BF),
        ),
        in_specs=[SMEM] * 3 + [VMEM] * 8 + [ANY, VMEM] + [ANY] * 2,
        out_specs=[VMEM] * 6 + [ANY] * 2,
        scratch_shapes=[
            pltpu.VMEM(v.shape, BF),
            pltpu.VMEM(out_full.shape, BF),
            pltpu.VMEM((group_rows, heads * VAL), F32),
            pltpu.VMEM((blocks, heads * KEY, VAL), F32),
            pltpu.VMEM((blocks, KEY, VAL), BF),
            pltpu.VMEM((8, heads * KEY, VAL), BF),
            pltpu.VMEM((rows, width), F32),
            pltpu.VMEM((3, rows, width), BF),
            pltpu.VMEM((3, rows, width), BF),
            pltpu.VMEM((rows, width), BF),
            pltpu.SemaphoreType.DMA((moves,)),
            pltpu.SemaphoreType.DMA((moves,)),
            pltpu.SemaphoreType.DMA((3,)),
        ],
        compiler_params=pltpu.CompilerParams(
            collective_id=2, has_side_effects=True, vmem_limit_bytes=LIMIT
        ),
        cost_estimate=pl.CostEstimate(
            flops=12 << 30, bytes_accessed=40 << 20, transcendentals=0
        ),
    )(
        decay, across, fold, docs[:, None], docs[None, :], scales, gain[None, :], qk, v, gate,
        tokens, out_full, cotangent, w_up, w_down,
    )


def feed_kernel(
    resid_ref,
    gain_ref,
    cot_ref,
    up_ref,
    down_ref,
    layer_out,
    far_out,
    resid_grad,
    gain_out,
    up_own,
    up_far,
    down_own,
    down_far,
    branch,
    up,
    down,
    lifted,
    cot,
    hidden,
    turned,
    pre,
    back_out,
    back_in,
    staged,
    odd_out_d,
    odd_in_d,
    odd_out_u,
    odd_in_u,
    far_out_d,
    far_in_d,
    far_out_u,
    far_in_u,
    near_out_d,
    near_in_d,
    near_out_u,
    near_in_u,
    send,
    recv,
    load_sem,
    free_sem,
):
    near = peers()
    z = lax.axis_index("head")
    count = lax.axis_size("head")
    rows, width = resid_ref.shape
    part = width // 8
    side_rows = rows // 2
    wide = up.shape[1]
    slice_ = wide // 2
    loads = [
        pltpu.make_async_copy(cot_ref, cot, load_sem.at[0]),
        pltpu.make_async_copy(up_ref, up, load_sem.at[1]),
        pltpu.make_async_copy(down_ref, down, load_sem.at[2]),
    ]
    for load in loads:
        load.start()
    greet(*everyone())
    moves = Moves(send, recv)
    size = 32

    pairs = []
    for side in range(2):

        @pl.loop(0, side_rows // size)
        def _(i):
            at = pl.ds(pl.multiple_of(side * side_rows + i * size, size), size)
            values = resid_ref[at, :]
            mean = jnp.mean(values, axis=-1, keepdims=True)
            centred = values - mean
            inverse = lax.rsqrt(jnp.mean(centred * centred, axis=-1, keepdims=True) + EPS)
            lifted[at, :] = (centred * inverse * gain_ref[...]).astype(BF)

        pairs.append(
            moves.go(
                lifted.at[pl.ds(side * side_rows, side_rows), :],
                lifted.at[pl.ds(rows + side * side_rows, side_rows), :],
                near["pair"],
            )
        )

    def feed(first, number):
        @pl.loop(0, wide // 256)
        def _(i):
            to = pl.ds(pl.multiple_of(i * 256, 256), 256)
            at = pl.ds(first, number)
            hidden_pre = dot_nn(lifted[at, :], up[:, to])
            hidden_grad = dot_nt(cot[at, :], down[to, :])
            phi = 0.5 * (1.0 + lax.erf(hidden_pre * SQRT_HALF))
            made = (hidden_pre * phi).astype(BF)
            hidden[at, to] = made
            turned[to, at] = made.T
            slope = phi + hidden_pre * jnp.exp(-0.5 * hidden_pre * hidden_pre) * INV_ROOT_TWO_PI
            pre[at, to] = (hidden_grad * slope).astype(BF)

    for load in loads:
        load.wait()
    feed(0, rows)
    backs = []
    for side in range(2):
        pairs[side].wait_recv()
        feed(rows + side * side_rows, side_rows)

        @pl.loop(0, width // 256)
        def _(i):
            to = pl.ds(pl.multiple_of(i * 256, 256), 256)
            found = dot_nt(pre[pl.ds(rows + side * side_rows, side_rows), :], up[to, :])
            back_out[pl.ds(side * side_rows, side_rows), to] = found.astype(BF)

        at = pl.ds(side * side_rows, side_rows)
        backs.append(moves.go(back_out.at[at, :], back_in.at[at, :], near["pair"]))

    @pl.loop(0, width // 256)
    def _(i):
        to = pl.ds(pl.multiple_of(i * 256, 256), 256)
        resid_grad[:, to] = dot_nt(pre[pl.ds(0, rows), :], up[to, :])

    def down_term(s):
        def term(r):
            return dot_nn(turned[pl.ds(s * slice_, slice_), :], cot[:, r * part : (r + 1) * part])

        return term

    def up_term(s):
        def term(r):
            return dot_tn(
                lifted[:, r * part : (r + 1) * part], pre[:, s * slice_ : (s + 1) * slice_]
            )

        return term

    down_sets = [
        (odd_out_d, odd_in_d, far_out_d, far_in_d.at[s], near_out_d, near_in_d.at[s])
        for s in range(2)
    ]
    up_sets = [
        (odd_out_u, odd_in_u, far_out_u, far_in_u.at[s], near_out_u, near_in_u.at[s])
        for s in range(2)
    ]
    sums = [
        Scatter(moves, near, down_term(0), down_sets[0], down_own),
        Scatter(moves, near, up_term(0), up_sets[0], up_own),
    ]
    sums += [
        Scatter(moves, near, down_term(1), down_sets[1], down_far, sums[0], free_sem.at[0]),
        Scatter(moves, near, up_term(1), up_sets[1], up_far, sums[1], free_sem.at[1]),
    ]
    sums[0].frees = free_sem.at[0]
    sums[1].frees = free_sem.at[1]

    ring = {}

    def shard(step, side):
        owner = lax.rem(z - step + count, count)
        first = pl.multiple_of(owner * rows + side * side_rows, side_rows)
        return branch.at[pl.ds(first, side_rows), :]

    def pass_on(step, side):
        if step:
            ring[step - 1, side].wait_recv()
        if step < count - 1:
            here = staged.at[pl.ds(side * side_rows, side_rows), :] if step == 0 else shard(step, side)
            ring[step, side] = moves.go(here, shard(step, side), near["up"])

    def norm_back(side):
        backs[side].wait_recv()

        def block(i, total):
            at = pl.ds(pl.multiple_of(side * side_rows + i * size, size), size)
            values = resid_ref[at, :]
            mean = jnp.mean(values, axis=-1, keepdims=True)
            centred = values - mean
            inverse = lax.rsqrt(jnp.mean(centred * centred, axis=-1, keepdims=True) + EPS)
            unit = centred * inverse
            grad = resid_grad[at, :] + back_in[at, :].astype(F32)
            scaled = grad * gain_ref[...]
            first = jnp.mean(scaled, axis=-1, keepdims=True)
            second = jnp.mean(scaled * unit, axis=-1, keepdims=True)
            found = cot[at, :].astype(F32) + inverse * (scaled - first - unit * second)
            resid_grad[at, :] = found
            staged[at, :] = found.astype(BF)
            return total + jnp.sum(grad * unit, axis=0, keepdims=True)

        total = lax.fori_loop(0, side_rows // size, block, jnp.zeros((1, width), F32))
        gain_out[pl.ds(side, 1), :] = total

    norm_back(0)
    pass_on(0, 0)
    for i in (3, 1):
        sums[0].odd(i)
    norm_back(1)
    pass_on(0, 1)
    mine = pltpu.make_async_copy(
        staged, branch.at[pl.ds(pl.multiple_of(z * rows, rows), rows), :], load_sem.at[3]
    )
    mine.start()
    for i in (2, 0):
        sums[0].odd(i)
    pass_on(1, 0)
    sums[0].far()
    for i in (3, 1):
        sums[1].odd(i)

    @pl.loop(0, width // 256)
    def _(i):
        to = pl.ds(pl.multiple_of(i * 256, 256), 256)
        layer_out[:, to] = resid_ref[:, to] + dot_nn(hidden[pl.ds(0, rows), :], down[:, to])

    pass_on(1, 1)
    for i in (2, 0):
        sums[1].odd(i)
    sums[0].close()
    sums[1].far()
    pass_on(2, 0)
    for i in (3, 1):
        sums[2].odd(i)

    @pl.loop(0, width // 256)
    def _(i):
        to = pl.ds(pl.multiple_of(i * 256, 256), 256)
        far_out[:, to] = dot_nn(hidden[pl.ds(rows, rows), :], down[:, to]).astype(BF)

    sums[1].close()
    for i in (2, 0):
        sums[2].odd(i)
    pass_on(2, 1)
    sums[2].far()
    for i in (3, 1, 2, 0):
        sums[3].odd(i)
    sums[0].done()
    sums[3].far()
    sums[2].close()
    sums[1].done()
    sums[3].close()
    pass_on(3, 0)
    sums[2].done()
    sums[3].done()
    pass_on(3, 1)
    mine.wait()
    moves.finish()


def feed_forward(resid, gain, cot_pair, up_full, down_full):
    rows, width = resid.shape
    count = lax.axis_size("head")
    part = width // 8
    wide = up_full.shape[1]
    slice_ = wide // 2
    moves = 4 + 4 * 8 + 6
    struct = jax.ShapeDtypeStruct
    down_piece = (slice_, part)
    up_piece = (part, slice_)

    def sets(piece):
        half = (piece[0] // 2, piece[1])
        return [
            pltpu.VMEM(piece, BF),
            pltpu.VMEM((2, 2) + half, BF),
        ]

    def nears(piece):
        return [pltpu.VMEM((2,) + piece, BF), pltpu.VMEM((2, 2) + piece, BF)]

    def odds(piece):
        return [pltpu.VMEM((4,) + piece, BF)] * 2

    return pl.pallas_call(
        feed_kernel,
        out_shape=(
            struct((rows, width), F32),
            struct((rows, width), BF),
            struct((rows, width), F32),
            struct((8, width), F32),
            struct(up_piece, F32),
            struct(up_piece, F32),
            struct(down_piece, F32),
            struct(down_piece, F32),
            struct((count * rows, width), BF),
        ),
        in_specs=[VMEM] * 2 + [ANY] * 3,
        out_specs=[VMEM] * 8 + [ANY],
        scratch_shapes=[
            pltpu.VMEM((width, wide), BF),
            pltpu.VMEM((wide, width), BF),
            pltpu.VMEM((2 * rows, width), BF),
            pltpu.VMEM((2 * rows, width), BF),
            pltpu.VMEM((2 * rows, wide), BF),
            pltpu.VMEM((wide, 2 * rows), BF),
            pltpu.VMEM((2 * rows, wide), BF),
            pltpu.VMEM((rows, width), BF),
            pltpu.VMEM((rows, width), BF),
            pltpu.VMEM((rows, width), BF),
            *odds(down_piece),
            *odds(up_piece),
            *sets(down_piece),
            *sets(up_piece),
            *nears(down_piece),
            *nears(up_piece),
            pltpu.SemaphoreType.DMA((moves,)),
            pltpu.SemaphoreType.DMA((moves,)),
            pltpu.SemaphoreType.DMA((4,)),
            pltpu.SemaphoreType.REGULAR((2,)),
        ],
        compiler_params=pltpu.CompilerParams(
            collective_id=3, has_side_effects=True, vmem_limit_bytes=LIMIT
        ),
        cost_estimate=pl.CostEstimate(
            flops=26 << 30, bytes_accessed=40 << 20, transcendentals=0
        ),
    )(resid, gain[None, :], cot_pair, up_full, down_full)


def recall_kernel(
    decay_ref,
    across_ref,
    fold_ref,
    docs_col,
    docs_row,
    scale_ref,
    gain_ref,
    qk_ref,
    v_ref,
    gate_ref,
    unit_ref,
    inverse_ref,
    states_ref,
    cos_ref,
    sin_ref,
    turned_ref,
    branch_ref,
    wo_ref,
    far_ref,
    up_ref,
    down_ref,
    grads,
    wo_grad,
    gains,
    far_in,
    up_in,
    down_in,
    branch,
    out_weights,
    back,
    terms,
    gathered,
    folded,
    dqk,
    dv,
    odd_out,
    odd_in,
    out_far,
    in_far,
    out_near,
    in_near,
    send,
    recv,
    load_sem,
):
    near = peers()
    group_rows, cols = v_ref.shape
    heads = cols // VAL
    blocks = group_rows // SPAN
    width = branch.shape[1]
    part = width // 8
    loads = [
        pltpu.make_async_copy(branch_ref, branch, load_sem.at[0]),
        pltpu.make_async_copy(wo_ref, out_weights, load_sem.at[1]),
    ]
    for load in loads:
        load.start()
    greet(*everyone())
    moves = Moves(send, recv)
    swaps = [
        moves.go(far_ref, far_in, near["pair"]),
        moves.go(up_ref, up_in, near["cross"]),
        moves.go(down_ref, down_in, near["cross"]),
    ]

    def block_rows(b):
        return pl.ds(pl.multiple_of(b * SPAN, SPAN), SPAN)

    def q_cols(h):
        return pl.ds(h * KEY, KEY)

    def k_cols(h):
        return pl.ds((heads + h) * KEY, KEY)

    def v_cols(h):
        return pl.ds(h * VAL, VAL)

    for load in loads:
        load.wait()

    def tile_back(i, totals):
        at = pl.ds(pl.multiple_of(i * 128, 128), 128)
        sums = []
        for h in range(heads):
            grad = dot_nt(branch[at, :], out_weights[v_cols(h), :]).astype(BF).astype(F32)
            gate = gate_ref[at, v_cols(h)].astype(F32)
            sigma = 1.0 / (1.0 + jnp.exp(-gate))
            swish = gate * sigma
            unit = unit_ref[at, v_cols(h)].astype(F32)
            gain = gain_ref[:, h * VAL : (h + 1) * VAL]
            grads[at, pl.ds(2 * heads * KEY + cols + h * VAL, VAL)] = (
                grad * unit * gain * (sigma + swish * (1.0 - sigma))
            ).astype(BF)
            inner = grad * swish
            scaled = inner * gain
            first = jnp.mean(scaled, axis=-1, keepdims=True)
            second = jnp.mean(scaled * unit, axis=-1, keepdims=True)
            back[at, v_cols(h)] = (
                inverse_ref[at, h : h + 1] * (scaled - first - unit * second)
            ).astype(BF)
            sums.append(totals[h] + jnp.sum(inner * unit, axis=0, keepdims=True))
        return tuple(sums)

    totals = lax.fori_loop(
        0, group_rows // 128, tile_back, tuple(jnp.zeros((1, VAL), F32) for _ in range(heads))
    )
    gains[...] = jnp.zeros_like(gains)
    for h in range(heads):
        gains[pl.ds(0, 1), v_cols(h)] = totals[h]

    for h in range(heads):
        total = jnp.zeros((KEY, VAL), F32)
        for b in reversed(range(blocks)):
            weighed = back[block_rows(b), v_cols(h)].astype(F32) * scale_ref[
                block_rows(b), h : h + 1
            ]
            term = dot_tn(qk_ref[block_rows(b), q_cols(h)], weighed.astype(BF))
            terms[b, pl.ds(h * KEY, KEY), :] = term
            total = across_ref[h, b] * total + term
        gathered[0, pl.ds(h * KEY, KEY), :] = total.astype(BF)

    def state_view(r, side=None):
        if side is None:
            return gathered.at[r]
        size = gathered.shape[1] // 2
        return gathered.at[r, pl.ds(side * size, size), :]

    states = Gather(moves, near, state_view)
    states.first()

    def out_term(r):
        return dot_nn(turned_ref[...], branch[:, r * part : (r + 1) * part])

    outward = Scatter(
        moves, near, out_term, (odd_out, odd_in, out_far, in_far, out_near, in_near), wo_grad
    )

    def intra(h):
        @pl.loop(0, blocks)
        def _(b):
            first = pl.multiple_of(b * SPAN, SPAN)
            for tile in range(SPAN - 128, -1, -128):
                at = pl.ds(first + tile, 128)
                seen = pl.ds(first, tile + 128)
                mask = tile_decay(docs_col, docs_row, decay_ref[h], first, tile, 128)
                query = qk_ref[at, q_cols(h)]
                key = qk_ref[seen, k_cols(h)]
                ret = back[at, v_cols(h)]
                probs = (dot_nt(query, key) * mask).astype(BF)
                score = (dot_nt(ret, v_ref[seen, v_cols(h)]) * mask).astype(BF)
                dqk[at, q_cols(h)] = dot_nn(score, key)
                to_keys = dot_tn(score, query)
                to_values = dot_tn(probs, ret)
                if tile == SPAN - 128:
                    dqk[seen, k_cols(h)] = to_keys
                    dv[seen, v_cols(h)] = to_values
                else:
                    dqk[seen, k_cols(h)] += to_keys
                    dv[seen, v_cols(h)] += to_values

    def finish_head(h):
        later = jnp.zeros((KEY, VAL), F32)
        for r in range(8):
            later = later + fold_ref[h, r] * gathered[r, pl.ds(h * KEY, KEY), :].astype(F32)
        for b in reversed(range(blocks)):
            folded[b] = later.astype(BF)
            later = across_ref[h, b] * later + terms[b, pl.ds(h * KEY, KEY), :]

        @pl.loop(0, group_rows // 128)
        def _(i):
            at = pl.ds(pl.multiple_of(i * 128, 128), 128)
            b = lax.div(i, SPAN // 128)
            reach = scale_ref[at, h : h + 1]
            leave = scale_ref[at, heads + h : heads + h + 1]
            state = states_ref[pl.ds(pl.multiple_of((h * blocks + b) * KEY, KEY), KEY), :]
            cosine, sine = cos_ref[at, :], sin_ref[at, :]
            for found, to in (
                (
                    dqk[at, q_cols(h)] + reach * dot_nt(back[at, v_cols(h)], state),
                    q_cols(h),
                ),
                (
                    dqk[at, k_cols(h)] + leave * dot_nt(v_ref[at, v_cols(h)], folded[b]),
                    k_cols(h),
                ),
            ):
                one, two = found[:, : KEY // 2], found[:, KEY // 2 :]
                grads[at, to] = jnp.concatenate(
                    [one * cosine + two * sine, two * cosine - one * sine], axis=1
                ).astype(BF)
            found = dv[at, v_cols(h)] + leave * dot_nn(qk_ref[at, k_cols(h)], folded[b])
            grads[at, pl.ds(2 * heads * KEY + h * VAL, VAL)] = found.astype(BF)

    for i in (3, 1):
        outward.odd(i)
    intra(0)
    states.second()
    for i in (2, 0):
        outward.odd(i)
    for h in range(1, heads):
        intra(h)
    states.third()
    outward.far()
    states.done()
    finish_head(0)
    outward.close()
    for h in range(1, heads):
        finish_head(h)
    outward.done()
    for swap_ in swaps:
        swap_.wait_recv()
    moves.finish()


def recall(
    decay, across, fold, docs, scales, gain, qk, v, gate, unit, inverse, states, cosine, sine,
    mixed_turned, branch, out_full, far_out, up_far, down_far,
):
    group_rows, cols = v.shape
    heads = cols // VAL
    blocks = group_rows // SPAN
    width = branch.shape[1]
    part = width // 8
    piece = (cols, part)
    moves = 3 + 8 + 8
    struct = jax.ShapeDtypeStruct
    return pl.pallas_call(
        recall_kernel,
        out_shape=(
            struct((group_rows, 3 * cols), BF),
            struct(piece, F32),
            struct((8, cols), F32),
            struct(far_out.shape, BF),
            struct(up_far.shape, BF),
            struct(down_far.shape, BF),
        ),
        in_specs=[SMEM] * 3 + [VMEM] * 13 + [ANY] * 5,
        out_specs=[VMEM] * 3 + [ANY] * 3,
        scratch_shapes=[
            pltpu.VMEM(branch.shape, BF),
            pltpu.VMEM(out_full.shape, BF),
            pltpu.VMEM(v.shape, BF),
            pltpu.VMEM((blocks, heads * KEY, VAL), F32),
            pltpu.VMEM((8, heads * KEY, VAL), BF),
            pltpu.VMEM((blocks, KEY, VAL), BF),
            pltpu.VMEM((group_rows, 2 * heads * KEY), F32),
            pltpu.VMEM((group_rows, cols), F32),
            pltpu.VMEM((4,) + piece, BF),
            pltpu.VMEM((4,) + piece, BF),
            pltpu.VMEM(piece, BF),
            pltpu.VMEM((2, cols // 2, part), BF),
            pltpu.VMEM((2,) + piece, BF),
            pltpu.VMEM((2,) + piece, BF),
            pltpu.SemaphoreType.DMA((moves,)),
            pltpu.SemaphoreType.DMA((moves,)),
            pltpu.SemaphoreType.DMA((2,)),
        ],
        compiler_params=pltpu.CompilerParams(
            collective_id=4, has_side_effects=True, vmem_limit_bytes=LIMIT
        ),
        cost_estimate=pl.CostEstimate(
            flops=20 << 30, bytes_accessed=40 << 20, transcendentals=0
        ),
    )(
        decay, across, fold, docs[:, None], docs[None, :], scales, gain[None, :], qk, v, gate, unit,
        inverse, states, cosine, sine, mixed_turned, branch, out_full, far_out, up_far, down_far,
    )


def norm_forward(values, gain):
    mean = jnp.mean(values, axis=-1, keepdims=True)
    centred = values - mean
    inverse = lax.rsqrt(jnp.mean(centred * centred, axis=-1, keepdims=True) + EPS)
    unit = centred * inverse
    return (unit * gain, unit, inverse)


def norm_backward(grad_out, unit, inverse, gain):
    scaled = grad_out * gain
    first = jnp.mean(scaled, axis=-1, keepdims=True)
    second = jnp.mean(scaled * unit, axis=-1, keepdims=True)
    return (inverse * (scaled - first - unit * second), jnp.sum(grad_out * unit, axis=0))


def doc_index(row_ids, starts):
    return jnp.sum((starts[None, :] <= row_ids[:, None]).astype(jnp.int32), axis=1) - 1


def doc_position(row_ids, starts):
    first = jnp.max(jnp.where(starts[None, :] <= row_ids[:, None], starts[None, :], 0), axis=1)
    return row_ids - first


def angles(position, half):
    freq = jnp.exp(-jnp.log(10000.0) * jnp.arange(half, dtype=F32) / half)
    turn = position.astype(F32)[:, None] * freq[None, :]
    return (jnp.cos(turn), jnp.sin(turn))


def rotate(values, cosine, sine):
    half = values.shape[-1] // 2
    first, second = (values[..., :half], values[..., half:])
    return jnp.concatenate(
        [first * cosine - second * sine, first * sine + second * cosine], axis=-1
    )


def unrotate(grads, cosine, sine):
    return rotate(grads, cosine, -sine)


def span_masks(doc_ids, before, log_decay):
    size = doc_ids.shape[0]
    place = jnp.arange(size, dtype=F32)
    lag = place[:, None] - place[None, :]
    same = (doc_ids[:, None] == doc_ids[None, :]) & (lag >= 0)
    decay = jnp.where(same, jnp.exp(jnp.maximum(lag, 0.0) * log_decay), 0.0)
    reach = jnp.where(doc_ids == before, jnp.exp((place + 1.0) * log_decay), 0.0)[:, None]
    leave = jnp.where(doc_ids == doc_ids[-1], jnp.exp((size - 1.0 - place) * log_decay), 0.0)[
        :, None
    ]
    across = jnp.where(doc_ids[-1] == before, jnp.exp(size * log_decay), 0.0)
    return (decay, reach, leave, across)


def gelu_slope(hidden_pre):
    return (
        0.5 * (1.0 + lax.erf(hidden_pre * SQRT_HALF))
        + hidden_pre * jnp.exp(-0.5 * hidden_pre * hidden_pre) * INV_ROOT_TWO_PI
    )


def plain(
    tokens,
    cotangent,
    doc_lengths,
    head_order,
    norm_gain,
    w_query,
    w_key,
    w_value,
    w_gate,
    group_gain,
    w_out,
    ffn_gain,
    w_up,
    w_down,
):
    heads = w_query.shape[1] // KEY
    head_count = lax.axis_size("head")
    tok_count = lax.axis_size("tok")
    z = lax.axis_index("head")
    tok = lax.axis_index("tok")
    rows = tokens.shape[0]
    group_rows = rows * head_count
    blocks = group_rows // SPAN
    width = tokens.shape[1]
    part = width // tok_count

    tokens_f = reorder(tokens).astype(F32)
    cot_own = reorder(cotangent)
    gain1 = reorder(norm_gain)
    gain2 = reorder(ffn_gain)
    normed1, unit1, inverse1 = norm_forward(tokens_f, gain1)
    qk = w_query.shape[1]
    vg = w_value.shape[1]
    up_two = jnp.concatenate([w_up, swap(w_up, "head", 2)], axis=1)
    down_two = jnp.concatenate([w_down, swap(w_down, "head", 2)], axis=0)
    up_full = tok_gather(up_two, 0)
    down_full = tok_gather(down_two, 1)
    cot_pair = jnp.concatenate([cot_own, swap(cot_own, "head", 1)], axis=0)

    ends = jnp.cumsum(doc_lengths)
    starts = ends - doc_lengths
    first_row = tok * group_rows
    row_ids = first_row + jnp.arange(group_rows, dtype=jnp.int32)
    doc_ids = doc_index(row_ids, starts)
    previous = doc_index(jnp.reshape(first_row - 1, (1,)), starts)[0]
    group_last = doc_index((jnp.arange(tok_count, dtype=jnp.int32) + 1) * group_rows - 1, starts)
    cosine, sine = angles(doc_position(row_ids, starts), KEY // 2)
    ranks = lax.dynamic_slice_in_dim(head_order, z * heads, heads)
    log_decay = jnp.log1p(-jnp.exp2(-(5.0 + ranks.astype(F32))))

    group = head_gather(normed1.astype(BF))
    qkvg_full = tok_gather(jnp.concatenate([w_query, w_key, w_value, w_gate], axis=1), 0)
    out_full = tok_gather(w_out, 1)
    projected = mm(group, qkvg_full)
    qk_rows = jnp.concatenate(
        [
            rotate(projected[:, h * KEY : (h + 1) * KEY], cosine, sine).astype(BF)
            for h in range(2 * heads)
        ],
        axis=1,
    )
    v_rows = projected[:, 2 * qk : 2 * qk + vg].astype(BF)
    gate = projected[:, 2 * qk + vg :]

    def head_of(array, head, size):
        return array[:, head * size : (head + 1) * size]

    def block_of(array, block):
        return array[block * SPAN : (block + 1) * SPAN]

    q, k, v, masks = [], [], [], []
    for h in range(heads):
        q.append(head_of(qk_rows, h, KEY))
        k.append(head_of(qk_rows, heads + h, KEY))
        v.append(head_of(v_rows, h, VAL))
        masks.append(
            [
                span_masks(
                    block_of(doc_ids, b),
                    previous if b == 0 else doc_ids[b * SPAN - 1],
                    log_decay[h],
                )
                for b in range(blocks)
            ]
        )

    group_order = jnp.arange(tok_count, dtype=jnp.int32)

    def weigh(lag, last, h):
        return jnp.where(
            (lag >= 0) & (group_last == last),
            jnp.exp(jnp.maximum(lag, 0).astype(F32) * group_rows * log_decay[h]),
            0.0,
        )

    ends_of = []
    added = []
    for h in range(heads):
        state = jnp.zeros((KEY, VAL), F32)
        terms = []
        for b in range(blocks):
            term = mm_tn(block_of(k[h], b), (block_of(v[h], b) * masks[h][b][2]).astype(BF))
            terms.append(term)
            state = masks[h][b][3] * state + term
        added.append(terms)
        ends_of.append(state.astype(BF))
    all_states = lax.all_gather(jnp.concatenate(ends_of, axis=0), "tok", axis=0)
    lag = tok - 1 - group_order
    states = []
    retained = []
    for h in range(heads):
        weights = weigh(lag, previous, h)
        state = jnp.sum(
            all_states[:, h * KEY : (h + 1) * KEY].astype(F32) * weights[:, None, None], axis=0
        )
        mine = []
        outs = []
        for b in range(blocks):
            mine.append(state.astype(BF))
            qb, kb, vb = block_of(q[h], b), block_of(k[h], b), block_of(v[h], b)
            decay, reach, leave, across = masks[h][b]
            probs = (mm_nt(qb, kb) * decay).astype(BF)
            outs.append(mm(probs, vb) + reach * mm(qb, mine[-1]))
            state = across * state + added[h][b]
        states.append(mine)
        retained.append(jnp.concatenate(outs, axis=0))

    mixed_parts, unit_g, inverse_g, grouped, swish, sigma = [], [], [], [], [], []
    for h in range(heads):
        g, u, i = norm_forward(retained[h], head_of(group_gain[None, :], h, VAL))
        gate_h = head_of(gate, h, VAL)
        s = jax.nn.sigmoid(gate_h)
        unit_g.append(u)
        inverse_g.append(i)
        grouped.append(g)
        sigma.append(s)
        swish.append(gate_h * s)
        mixed_parts.append((swish[-1] * g).astype(BF))
    mixed = jnp.concatenate(mixed_parts, axis=1)

    out_sum = head_scatter(lambda i: mm(rows_of(mixed, i, rows), out_full))
    resid = tokens_f + out_sum
    normed2, unit2, inverse2 = norm_forward(resid, gain2)
    lifted2 = normed2.astype(BF)
    lifted2_pair = jnp.concatenate([lifted2, swap(lifted2, "head", 1)], axis=0)
    hidden_pre = mm(lifted2_pair, up_full)
    hidden = jax.nn.gelu(hidden_pre, approximate=False).astype(BF)
    hidden_grad = mm_nt(cot_pair, down_full)
    pre_grad = (hidden_grad * gelu_slope(hidden_pre)).astype(BF)
    far_grad = mm_nt(pre_grad[rows:], up_full).astype(BF)
    lifted2_grad = mm_nt(pre_grad[:rows], up_full) + swap(far_grad, "head", 1).astype(F32)
    resid_part, ffn_gain_local = norm_backward(lifted2_grad, unit2, inverse2, gain2)
    resid_grad = cot_own.astype(F32) + resid_part
    branch_own = resid_grad.astype(BF)
    branch = head_gather(branch_own)

    far_out = mm(hidden[rows:], down_full).astype(BF)
    layer_out = reorder(
        (resid + mm(hidden[:rows], down_full) + swap(far_out, "head", 1).astype(F32)).astype(BF)
    )

    def piece(array, r):
        return array[:, r * part : (r + 1) * part]

    slots = range(tok_count)
    down_two_grad = tok_scatter([mm_tn(hidden, piece(cot_pair, r)) for r in slots])
    half = down_two_grad.shape[0] // 2
    w_down_grad = down_two_grad[:half] + swap(
        down_two_grad[half:].astype(BF), "head", 2
    ).astype(F32)
    up_two_grad = tok_scatter([mm_tn(piece(lifted2_pair, r), pre_grad) for r in slots])
    half = up_two_grad.shape[1] // 2
    w_up_grad = up_two_grad[:, :half] + swap(
        up_two_grad[:, half:].astype(BF), "head", 2
    ).astype(F32)

    mixed_grad = mm_nt(branch, out_full).astype(BF)
    w_out_grad = tok_scatter([mm_tn(mixed, piece(branch, r)) for r in slots])

    gate_parts, ret_grad, group_gain_parts = [], [], []
    for h in range(heads):
        head_grad = head_of(mixed_grad, h, VAL).astype(F32)
        gate_parts.append(
            (head_grad * grouped[h] * (sigma[h] + swish[h] * (1.0 - sigma[h]))).astype(BF)
        )
        back, gain_term = norm_backward(
            head_grad * swish[h], unit_g[h], inverse_g[h], head_of(group_gain[None, :], h, VAL)
        )
        ret_grad.append(back.astype(BF))
        group_gain_parts.append(gain_term)
    gate_grad = jnp.concatenate(gate_parts, axis=1)
    w_gate_grad = tok_scatter([mm_tn(piece(group, r), gate_grad) for r in slots])

    pending_of, pending_terms = [], []
    for h in range(heads):
        pending = jnp.zeros((KEY, VAL), F32)
        terms = [None] * blocks
        for b in reversed(range(blocks)):
            terms[b] = mm_tn(
                block_of(q[h], b), (block_of(ret_grad[h], b) * masks[h][b][1]).astype(BF)
            )
            pending = masks[h][b][3] * pending + terms[b]
        pending_terms.append(terms)
        pending_of.append(pending.astype(BF))
    all_pending = lax.all_gather(jnp.concatenate(pending_of, axis=0), "tok", axis=0)
    lag_back = group_order - 1 - tok
    shifted_last = doc_index(group_order * group_rows - 1, starts)
    q_parts, k_parts, v_parts = [], [], []
    for h in range(heads):
        weights = jnp.where(
            (lag_back >= 0) & (shifted_last == doc_ids[-1]),
            jnp.exp(jnp.maximum(lag_back, 0).astype(F32) * group_rows * log_decay[h]),
            0.0,
        )
        later = jnp.sum(
            all_pending[:, h * KEY : (h + 1) * KEY].astype(F32) * weights[:, None, None], axis=0
        )
        qg, kg, vg_ = [None] * blocks, [None] * blocks, [None] * blocks
        for b in reversed(range(blocks)):
            qb, kb, vb = block_of(q[h], b), block_of(k[h], b), block_of(v[h], b)
            rb = block_of(ret_grad[h], b)
            decay, reach, leave, across = masks[h][b]
            probs = (mm_nt(qb, kb) * decay).astype(BF)
            score_grad = (mm_nt(rb, vb) * decay).astype(BF)
            later_b = later.astype(BF)
            qg[b] = mm(score_grad, kb) + reach * mm_nt(rb, states[h][b])
            kg[b] = mm_tn(score_grad, qb) + leave * mm_nt(vb, later_b)
            vg_[b] = mm_tn(probs, rb) + leave * mm(kb, later_b)
            later = across * later + pending_terms[h][b]
        q_parts.append(unrotate(jnp.concatenate(qg, axis=0), cosine, sine).astype(BF))
        k_parts.append(unrotate(jnp.concatenate(kg, axis=0), cosine, sine).astype(BF))
        v_parts.append(jnp.concatenate(vg_, axis=0).astype(BF))
    all_grad = jnp.concatenate(q_parts + k_parts + v_parts + [gate_grad], axis=1)
    group_terms = jnp.concatenate(group_gain_parts, axis=0)
    ffn_terms = reorder(ffn_gain_local)
    row_grad = head_scatter(lambda i: mm_nt(rows_of(all_grad, i, rows), qkvg_full))
    input_part, norm_gain_local = norm_backward(row_grad, unit1, inverse1, gain1)
    tokens_grad = reorder(resid_grad + input_part)
    qkv_grad = all_grad[:, : 2 * qk + vg]
    w_qkv_grad = tok_scatter([mm_tn(piece(group, r), qkv_grad) for r in slots])
    w_query_grad = w_qkv_grad[:, :qk]
    w_key_grad = w_qkv_grad[:, qk : 2 * qk]
    w_value_grad = w_qkv_grad[:, 2 * qk :]
    group_gain_grad = sum_small(group_terms, "tok")
    ffn_sum = sum_small(sum_small(ffn_terms, "tok"), "head")
    norm_sum = sum_small(sum_small(reorder(norm_gain_local), "tok"), "head")
    return (
        layer_out,
        tokens_grad,
        norm_sum,
        w_query_grad,
        w_key_grad,
        w_value_grad,
        w_gate_grad,
        group_gain_grad,
        w_out_grad,
        ffn_sum,
        w_up_grad,
        w_down_grad,
    )


def fused(
    tokens,
    cotangent,
    doc_lengths,
    head_order,
    norm_gain,
    w_query,
    w_key,
    w_value,
    w_gate,
    group_gain,
    w_out,
    ffn_gain,
    w_up,
    w_down,
):
    heads = w_query.shape[1] // KEY
    head_count = lax.axis_size("head")
    tok_count = lax.axis_size("tok")
    z = lax.axis_index("head")
    tok = lax.axis_index("tok")
    rows = tokens.shape[0]
    group_rows = rows * head_count
    qk = w_query.shape[1]
    vg = w_value.shape[1]

    gain1 = reorder(norm_gain)
    gain2 = reorder(ffn_gain)

    ends = jnp.cumsum(doc_lengths)
    starts = ends - doc_lengths
    first_row = tok * group_rows
    row_ids = first_row + jnp.arange(group_rows, dtype=jnp.int32)
    doc_ids = doc_index(row_ids, starts)
    cosine, sine = angles(doc_position(row_ids, starts), KEY // 2)
    ranks = lax.dynamic_slice_in_dim(head_order, z * heads, heads)
    log_decay = jnp.log1p(-jnp.exp2(-(5.0 + ranks.astype(F32))))
    place = row_ids % SPAN
    block_first = row_ids - place
    before = doc_index(block_first - 1, starts)
    last = doc_index(block_first + SPAN - 1, starts)
    reach = jnp.where(
        (doc_ids == before)[:, None], jnp.exp((place + 1).astype(F32)[:, None] * log_decay), 0.0
    )
    leave = jnp.where(
        (doc_ids == last)[:, None],
        jnp.exp((SPAN - 1 - place).astype(F32)[:, None] * log_decay),
        0.0,
    )
    scales = jnp.concatenate([reach, leave], axis=1)
    across = jnp.where(
        (before[::SPAN] == last[::SPAN])[None, :], jnp.exp(SPAN * log_decay)[:, None], 0.0
    )
    order = jnp.arange(tok_count, dtype=jnp.int32) ^ tok

    def weigh(lag, same):
        return jnp.where(
            ((lag >= 0) & same)[None, :],
            jnp.exp(jnp.maximum(lag, 0).astype(F32) * group_rows * log_decay[:, None]),
            0.0,
        )

    fold = weigh(
        tok - 1 - order, doc_index((order + 1) * group_rows - 1, starts) == before[0]
    )
    fold_back = weigh(
        order - 1 - tok, doc_index(order * group_rows - 1, starts) == doc_ids[-1]
    )

    turned, qkvg_full, out_full, qk_rows, v_rows, gate = enter(
        tokens, gain1, cosine, sine, w_query, w_key, w_value, w_gate, w_out
    )
    resid, unit_g, inverse_g, states, cot_pair, mixed_turned, up_full, down_full = retain(
        log_decay, across, fold, doc_ids, scales, group_gain, qk_rows, v_rows, gate, tokens,
        out_full, cotangent, w_up, w_down,
    )
    (
        layer_own, far_out, resid_grad, ffn_gain_parts, up_own, up_far, down_own, down_far, branch
    ) = feed_forward(resid, gain2, cot_pair, up_full, down_full)
    all_grad, w_out_grad, group_terms, far_in, up_in, down_in = recall(
        log_decay, across, fold_back, doc_ids, scales, group_gain, qk_rows, v_rows, gate, unit_g,
        inverse_g, states, cosine, sine, mixed_turned, branch, out_full, far_out,
        up_far.astype(BF), down_far.astype(BF),
    )
    layer_out = reorder((layer_own + far_in.astype(F32)).astype(BF))
    w_up_grad = up_own + up_in.astype(F32)
    w_down_grad = down_own + down_in.astype(F32)
    tokens_grad, w_qk_grad, w_value_grad, w_gate_grad, sums = depart(
        all_grad, qkvg_full, turned, tokens, resid_grad, gain1, ffn_gain_parts, group_terms
    )
    w_query_grad, w_key_grad = w_qk_grad[:, :qk], w_qk_grad[:, qk:]
    return (
        layer_out,
        tokens_grad,
        sums[0],
        w_query_grad,
        w_key_grad,
        w_value_grad,
        w_gate_grad,
        sums[2, :vg],
        w_out_grad,
        sums[1],
        w_up_grad,
        w_down_grad,
    )


def local(*arrays):
    return fused(*arrays) if paired() else plain(*arrays)


def solution(mesh):
    rows = P(("tok", "head"), None)
    inward = P("tok", "head")
    outward = P("head", "tok")
    return jax.shard_map(
        local,
        mesh=mesh,
        in_specs=(
            rows, rows, P(), P(), P(), inward, inward, inward, inward, P("head"),
            outward, P(), inward, outward,
        ),
        out_specs=(
            rows, rows, P(), inward, inward, inward, inward, P("head"),
            outward, P(), inward, outward,
        ),
        check_vma=False,
    )
```

```python
import jax
import jax.numpy as jnp
from jax import lax
from jax.experimental import pallas as pl
from jax.experimental.pallas import tpu as pltpu
from jax.sharding import PartitionSpec as P

KEY = 256
VAL = 512
SPAN = 512

EPS = 1e-05
SQRT_HALF = 0.7071067811865476
INV_ROOT_TWO_PI = 0.3989422804014327
BF = jnp.bfloat16
F32 = jnp.float32


def mm(left, right):
    return jnp.dot(left, right, preferred_element_type=F32)


def mm_nt(left, right):
    return lax.dot_general(left, right, (((1,), (1,)), ((), ())), preferred_element_type=F32)


def mm_tn(left, right):
    return lax.dot_general(left, right, (((0,), (0,)), ((), ())), preferred_element_type=F32)


def swap(array, axis, bit):
    count = lax.axis_size(axis)
    return lax.ppermute(array, axis, [(i, i ^ bit) for i in range(count)])


def shift(array):
    count = lax.axis_size("head")
    return lax.ppermute(array, "head", [(i, (i + 1) % count) for i in range(count)])


def paired():
    return lax.axis_size("tok") == 8


def reorder(array):
    if not paired():
        return array
    me = lax.axis_index("tok")
    width = array.shape[-1] // 8
    return jnp.concatenate(
        [
            lax.dynamic_slice_in_dim(array, (me ^ r) * width, width, array.ndim - 1)
            for r in range(8)
        ],
        axis=-1,
    )


def halves(array):
    half = array.shape[0] // 2
    return array[:half], array[half:]


def tok_gather(shard, axis):
    if not paired():
        return lax.all_gather(shard, "tok", axis=axis, tiled=True)
    along_x = swap(shard, "tok", 2)
    along_y = swap(shard, "tok", 4)
    far = jnp.concatenate(
        [swap(halves(along_x)[0], "tok", 4), swap(halves(along_y)[1], "tok", 2)], axis=0
    )
    own = [shard, along_x, along_y, far]
    pieces = []
    for piece in own:
        pieces += [piece, swap(piece, "tok", 1)]
    return jnp.concatenate(pieces, axis=axis)


def tok_scatter(pieces):
    pieces = [p.astype(BF) for p in pieces]
    if not paired():
        return lax.psum_scatter(jnp.stack(pieces), "tok", scatter_dimension=0).astype(F32)
    kept = [
        pieces[r].astype(F32) + swap(pieces[r + 1], "tok", 1).astype(F32) for r in (0, 2, 4, 6)
    ]
    zero, two, four, six = kept
    six_a, six_b = halves(six.astype(BF))
    two_a, two_b = halves(two)
    four_a, four_b = halves(four)
    four_a = four_a + swap(six_a, "tok", 2).astype(F32)
    two_b = two_b + swap(six_b, "tok", 4).astype(F32)
    two = jnp.concatenate([two_a, two_b], axis=0).astype(BF)
    four = jnp.concatenate([four_a, four_b], axis=0).astype(BF)
    return zero + swap(two, "tok", 2).astype(F32) + swap(four, "tok", 4).astype(F32)


def head_gather(rows):
    count = lax.axis_size("head")
    me = lax.axis_index("head")
    size = rows.shape[0]
    whole = jnp.zeros((count * size,) + rows.shape[1:], rows.dtype)
    whole = lax.dynamic_update_slice_in_dim(whole, rows, me * size, 0)
    for step in range(1, count):
        rows = shift(rows)
        source = lax.rem(me - step + count, count)
        whole = lax.dynamic_update_slice_in_dim(whole, rows, source * size, 0)
    return whole


def head_scatter(term):
    count = lax.axis_size("head")
    me = lax.axis_index("head")
    total = term(lax.rem(me + count - 1, count))
    for step in range(1, count):
        arrived = shift(total.astype(BF))
        owner = lax.rem(me + 2 * count - 1 - step, count)
        total = term(owner) + arrived.astype(F32)
    return total


def rows_of(array, index, size):
    return lax.dynamic_slice_in_dim(array, index * size, size, 0)


def sum_small(vector, axis):
    count = lax.axis_size(axis)
    bit = 1
    while bit < count:
        vector = vector + swap(vector, axis, bit)
        bit *= 2
    return vector


MESH = pl.DeviceIdType.MESH
ANY = pl.BlockSpec(memory_space=pl.ANY)
VMEM = pl.BlockSpec(memory_space=pltpu.VMEM)
SMEM = pl.BlockSpec(memory_space=pltpu.SMEM)
LIMIT = 60 * 1024 * 1024


def flipped(index, bit):
    return index + bit - 2 * bit * lax.rem(lax.div(index, bit), 2)


def peers():
    tok = lax.axis_index("tok")
    z = lax.axis_index("head")
    count = lax.axis_size("head")
    return {
        "core": {"tok": flipped(tok, 1), "head": z},
        "x": {"tok": flipped(tok, 2), "head": z},
        "y": {"tok": flipped(tok, 4), "head": z},
        "up": {"tok": tok, "head": lax.rem(z + 1, count)},
        "down": {"tok": tok, "head": lax.rem(z + count - 1, count)},
        "pair": {"tok": tok, "head": flipped(z, 1)},
        "cross": {"tok": tok, "head": flipped(z, 2)},
    }


def everyone():
    near = peers()
    tok = lax.axis_index("tok")
    z = lax.axis_index("head")
    count = lax.axis_size("head")
    others = [{"tok": tok, "head": lax.rem(z + step, count)} for step in range(1, count)]
    return [near["core"], near["x"], near["y"], *others]


def greet(*devices):
    barrier = pltpu.get_barrier_semaphore()
    for device in devices:
        pl.semaphore_signal(barrier, inc=1, device_id=device, device_id_type=MESH)
    pl.semaphore_wait(barrier, len(devices))


def doc_starts(lengths):
    starts, total = [], 0
    for d in range(lengths.shape[0]):
        starts.append(total)
        total = total + lengths[d]
    return starts


def doc_at(row, starts):
    return sum((start <= row).astype(jnp.int32) for start in starts) - 1


def doc_first(row, starts):
    first = jnp.zeros_like(row)
    for start in starts:
        first = jnp.maximum(first, jnp.where(start <= row, start, 0))
    return first


def decays(order, heads):
    z = lax.axis_index("head")
    found = []
    for h in range(heads):
        rank = jnp.full((1, 1), order[z * heads + h], jnp.int32).astype(F32)
        found.append(jnp.log1p(-jnp.exp2(-(5.0 + rank))))
    return found


def block_scales(lengths, log_decay, group_rows, scale, docs):
    heads = len(log_decay)
    starts = doc_starts(lengths)
    first_row = lax.axis_index("tok") * group_rows
    across = [[] for _ in range(heads)]
    for b in range(group_rows // SPAN):
        at = pl.ds(b * SPAN, SPAN)
        low = first_row + b * SPAN
        place = lax.broadcasted_iota(jnp.int32, (SPAN, 1), 0)
        doc = doc_at(low + place, starts)
        docs[at, :] = doc
        before = doc_at(low - 1, starts)
        last = doc_at(low + SPAN - 1, starts)
        where = place.astype(F32)
        for h in range(heads):
            scale[at, h : h + 1] = jnp.where(
                doc == before, jnp.exp((where + 1.0) * log_decay[h]), 0.0
            )
            scale[at, heads + h : heads + h + 1] = jnp.where(
                doc == last, jnp.exp((SPAN - 1.0 - where) * log_decay[h]), 0.0
            )
            across[h].append(jnp.where(last == before, jnp.exp(SPAN * log_decay[h]), 0.0))
    return across


def row_docs(lengths, group_rows):
    starts = doc_starts(lengths)
    first_row = lax.axis_index("tok") * group_rows
    return doc_at(first_row + lax.broadcasted_iota(jnp.int32, (8, group_rows), 1), starts)


def group_weights(lengths, log_decay, group_rows, backward):
    starts = doc_starts(lengths)
    tok = lax.axis_index("tok")
    first_row = tok * group_rows
    found = [[] for _ in log_decay]
    for other in xor_places(tok):
        if backward:
            lag = other - 1 - tok
            same = doc_at(other * group_rows - 1, starts) == doc_at(
                first_row + group_rows - 1, starts
            )
        else:
            lag = tok - 1 - other
            same = doc_at((other + 1) * group_rows - 1, starts) == doc_at(first_row - 1, starts)
        amount = (jnp.maximum(lag, 0) * group_rows).astype(F32)
        for h, rate in enumerate(log_decay):
            found[h].append(jnp.where((lag >= 0) & same, jnp.exp(amount * rate), 0.0))
    return found


class Moves:
    def __init__(self, send, recv):
        self.send, self.recv, self.made, self.over = send, recv, [], []

    def go(self, src, dst, device):
        n = len(self.made)
        copy = pltpu.make_async_remote_copy(
            src_ref=src,
            dst_ref=dst,
            send_sem=self.send.at[n],
            recv_sem=self.recv.at[n],
            device_id=device,
            device_id_type=MESH,
        )
        copy.start()
        self.made.append(copy)
        return copy

    def sent(self, copy):
        copy.wait_send()
        self.over.append(copy)

    def finish(self):
        for copy in self.made:
            if not any(copy is gone for gone in self.over):
                copy.wait_send()


class Gather:
    def __init__(self, moves, near, view):
        self.moves, self.near, self.view = moves, near, view

    def first(self):
        go, near, view = self.moves.go, self.near, self.view
        self.x = go(view(0), view(2), near["x"])
        self.y = go(view(0), view(4), near["y"])
        self.cores = [go(view(0), view(1), near["core"])]

    def second(self):
        go, near, view = self.moves.go, self.near, self.view
        self.x.wait_recv()
        self.far = [go(view(2, 0), view(6, 0), near["y"])]
        self.cores.append(go(view(2), view(3), near["core"]))
        self.y.wait_recv()
        self.far.append(go(view(4, 1), view(6, 1), near["x"]))
        self.cores.append(go(view(4), view(5), near["core"]))

    def third(self):
        go, near, view = self.moves.go, self.near, self.view
        for copy in self.far:
            copy.wait_recv()
        self.cores.append(go(view(6), view(7), near["core"]))

    def done(self):
        for copy in self.cores:
            copy.wait_recv()


def enter_kernel(
    tok_ref,
    gain_ref,
    lengths_ref,
    wq_ref,
    wk_ref,
    wv_ref,
    wg_ref,
    wo_ref,
    turned_out,
    weights_out,
    out_full,
    qk_out,
    v_out,
    gate_out,
    cos_ref,
    sin_ref,
    turned,
    group,
    weights,
    own_out,
    gain,
    send,
    recv,
    own_sem,
    keep_sem,
):
    near = peers()
    tok = lax.axis_index("tok")
    z = lax.axis_index("head")
    count = lax.axis_size("head")
    rows, width = tok_ref.shape
    part = width // 8
    cols = weights.shape[2]
    half = wq_ref.shape[1]

    own = [
        pltpu.make_async_copy(wq_ref, weights.at[0, pl.ds(0, part), pl.ds(0, half)], own_sem.at[0]),
        pltpu.make_async_copy(
            wk_ref, weights.at[0, pl.ds(0, part), pl.ds(half, half)], own_sem.at[1]
        ),
        pltpu.make_async_copy(wv_ref, weights.at[1, pl.ds(0, part), :], own_sem.at[2]),
        pltpu.make_async_copy(wg_ref, weights.at[2, pl.ds(0, part), :], own_sem.at[3]),
        pltpu.make_async_copy(wo_ref, own_out, own_sem.at[4]),
    ]
    for copy in own:
        copy.start()
    greet(near["core"], near["x"], near["y"], near["up"], near["down"])
    moves = Moves(send, recv)

    def chunk_view(c):
        def view(r, side=None):
            if side is None:
                return weights.at[c, pl.ds(r * part, part), :]
            return weights.at[c, pl.ds(r * part + side * (part // 2), part // 2), :]

        return view

    def out_view(r, side=None):
        if r == 0:
            return own_out
        if side is None:
            return out_full.at[:, pl.ds(r * part, part)]
        size = out_full.shape[0] // 2
        return out_full.at[pl.ds(side * size, size), pl.ds(r * part, part)]

    chunks = [Gather(moves, near, chunk_view(c)) for c in range(3)]
    outward = Gather(moves, near, out_view)
    own[0].wait()
    own[1].wait()
    chunks[0].first()
    own[2].wait()
    chunks[1].first()
    own[3].wait()
    own[4].wait()
    kept = [pltpu.make_async_copy(own_out, out_full.at[:, pl.ds(0, part)], keep_sem.at[4])]
    kept[0].start()
    gain[...] = arranged(gain_ref, tok)

    @pl.loop(0, rows // 16)
    def _(i):
        at = pl.ds(pl.multiple_of(i * 16, 16), 16)
        values = jnp.concatenate(
            [
                tok_ref[at, pl.ds(pl.multiple_of(place * part, part), part)]
                for place in xor_places(tok)
            ],
            axis=1,
        ).astype(F32)
        mean = jnp.mean(values, axis=-1, keepdims=True)
        centred = values - mean
        inverse = lax.rsqrt(jnp.mean(centred * centred, axis=-1, keepdims=True) + EPS)
        lifted = (centred * inverse * gain[...]).astype(BF)
        group[pl.ds(pl.multiple_of(z * rows + i * 16, 16), 16), :] = lifted

    def shard(step, side):
        owner = lax.rem(z - step + count, count)
        size = rows // 2
        return group.at[pl.ds(pl.multiple_of(owner * rows + side * size, size), size), :]

    ring = {}

    def pass_on(step, side):
        if step:
            ring[step - 1, side].wait_recv()
        if step < count - 1:
            ring[step, side] = moves.go(shard(step, side), shard(step, side), near["up"])

    def project(c, steps):
        first, number = steps

        @pl.loop(0, number * (cols // 256))
        def _(i):
            step = first + lax.div(i, cols // 256)
            tile = lax.rem(i, cols // 256)
            owner = lax.rem(z - step + count, count)
            at = pl.ds(pl.multiple_of(owner * rows, rows), rows)
            to = pl.ds(pl.multiple_of(tile * 256, 256), 256)
            found = jnp.dot(group[at, :], weights[c, :, to], preferred_element_type=F32)
            if c == 0:
                cosine, sine = cos_ref[at, :], sin_ref[at, :]
                one, two = found[:, :128], found[:, 128:]
                qk_out[at, to] = jnp.concatenate(
                    [one * cosine - two * sine, one * sine + two * cosine], axis=1
                ).astype(BF)
            elif c == 1:
                v_out[at, to] = found.astype(BF)
            else:
                gate_out[at, to] = found.astype(BF)

    def turn(step):
        owner = lax.rem(z - step + count, count)

        @pl.loop(0, width // 256)
        def _(i):
            at = pl.ds(pl.multiple_of(i * 256, 256), 256)
            to = pl.ds(pl.multiple_of(owner * rows, rows), rows)
            turned[at, to] = group[to, at].T

    def keep(c):
        copy = pltpu.make_async_copy(
            weights.at[c], weights_out.at[:, pl.ds(c * cols, cols)], keep_sem.at[c]
        )
        copy.start()
        kept.append(copy)

    pass_on(0, 0)
    pass_on(0, 1)
    group_rows = rows * count
    starts = doc_starts(lengths_ref)
    index = lax.broadcasted_iota(jnp.int32, (1, KEY // 2), 1).astype(F32)
    freq = jnp.exp(-jnp.log(10000.0) * index / (KEY // 2))

    @pl.loop(0, group_rows // 64)
    def _(i):
        at = pl.ds(pl.multiple_of(i * 64, 64), 64)
        row = tok * group_rows + i * 64 + lax.broadcasted_iota(jnp.int32, (64, KEY // 2), 0)
        turn = (row - doc_first(row, starts)).astype(F32) * freq
        cos_ref[at, :] = jnp.cos(turn)
        sin_ref[at, :] = jnp.sin(turn)

    chunks[0].second()
    chunks[2].first()
    pass_on(1, 0)
    chunks[1].second()
    outward.first()
    pass_on(1, 1)
    chunks[0].third()
    chunks[0].done()
    keep(0)
    project(0, (0, 2))
    pass_on(2, 0)
    turn(0)
    turn(1)
    chunks[2].second()
    pass_on(2, 1)
    chunks[1].third()
    chunks[1].done()
    keep(1)
    project(1, (0, 2))
    outward.second()
    project(0, (2, 1))
    project(1, (2, 1))
    turn(2)
    chunks[2].third()
    chunks[2].done()
    keep(2)
    pass_on(3, 0)
    outward.third()
    project(2, (0, 3))
    pass_on(3, 1)
    turn(3)
    copy = pltpu.make_async_copy(turned, turned_out, keep_sem.at[3])
    copy.start()
    kept.append(copy)
    project(0, (3, 1))
    project(1, (3, 1))
    project(2, (3, 1))
    outward.done()
    for copy in kept:
        copy.wait()
    moves.finish()


def arranged(ref, tok):
    part = ref.shape[-1] // 8
    return jnp.concatenate(
        [ref[:, pl.ds(pl.multiple_of(place * part, part), part)] for place in xor_places(tok)],
        axis=1,
    )


def xor_places(tok):
    places = []
    for r in range(8):
        place = tok
        for bit in (1, 2, 4):
            if r & bit:
                place = flipped(place, bit)
        places.append(place)
    return places


def enter(tokens, gain, doc_lengths, w_query, w_key, w_value, w_gate, w_out):
    rows, width = tokens.shape
    group_rows = rows * lax.axis_size("head")
    cols = w_value.shape[1]
    moves = 4 * 8 + 6
    return pl.pallas_call(
        enter_kernel,
        out_shape=(
            jax.ShapeDtypeStruct((width, group_rows), BF),
            jax.ShapeDtypeStruct((width, 3 * cols), BF),
            jax.ShapeDtypeStruct((w_out.shape[0], width), BF),
            jax.ShapeDtypeStruct((group_rows, cols), BF),
            jax.ShapeDtypeStruct((group_rows, cols), BF),
            jax.ShapeDtypeStruct((group_rows, cols), BF),
            jax.ShapeDtypeStruct((group_rows, KEY // 2), F32),
            jax.ShapeDtypeStruct((group_rows, KEY // 2), F32),
        ),
        in_specs=[VMEM] * 2 + [SMEM] + [ANY] * 5,
        out_specs=[ANY] * 3 + [VMEM] * 5,
        scratch_shapes=[
            pltpu.VMEM((width, group_rows), BF),
            pltpu.VMEM((group_rows, width), BF),
            pltpu.VMEM((3, width, cols), BF),
            pltpu.VMEM(w_out.shape, BF),
            pltpu.VMEM((1, width), F32),
            pltpu.SemaphoreType.DMA((moves,)),
            pltpu.SemaphoreType.DMA((moves,)),
            pltpu.SemaphoreType.DMA((5,)),
            pltpu.SemaphoreType.DMA((5,)),
        ],
        compiler_params=pltpu.CompilerParams(
            collective_id=0, has_side_effects=True, vmem_limit_bytes=LIMIT
        ),
        cost_estimate=pl.CostEstimate(
            flops=2 * group_rows * width * 3 * cols, bytes_accessed=40 << 20, transcendentals=0
        ),
    )(tokens, gain[None, :], doc_lengths, w_query, w_key, w_value, w_gate, w_out)


class Scatter:
    def __init__(self, moves, near, term, buffers, result, before=None, ready=None):
        self.moves, self.near, self.term, self.result = moves, near, term, result
        self.odd_out, self.odd_in, self.far_out, self.far_in, self.near_out, self.near_in = buffers
        self.half = self.far_out.shape[0] // 2
        self.before, self.ready, self.frees = before, ready, None
        self.cores = {}

    def odd(self, i):
        if self.before is not None:
            if not self.cores:
                pl.semaphore_wait(self.ready, 1)
            self.moves.sent(self.before.cores[i])
        self.odd_out[i] = self.term(2 * i + 1).astype(BF)
        self.cores[i] = self.moves.go(self.odd_out.at[i], self.odd_in.at[i], self.near["core"])

    def folded(self, i):
        self.cores[i].wait_recv()
        return self.term(2 * i) + self.odd_in[i].astype(F32)

    def far(self):
        value = self.folded(3).astype(BF)
        if self.before is not None:
            for move in self.before.fars:
                self.moves.sent(move)
        self.far_out[...] = value
        self.fars = [
            self.moves.go(
                self.far_out.at[pl.ds(side * self.half, self.half), :],
                self.far_in.at[side],
                self.near[way],
            )
            for side, way in ((0, "x"), (1, "y"))
        ]

    def close(self):
        half = self.half
        self.nears = []
        for i, side, way in ((1, 1, "x"), (2, 0, "y")):
            value = self.folded(i)
            self.fars[side].wait_recv()
            helped = value[side * half : (side + 1) * half] + self.far_in[side].astype(F32)
            other = value[(1 - side) * half : (2 - side) * half]
            if self.before is not None:
                self.moves.sent(self.before.nears[i - 1])
            self.near_out[i - 1, pl.ds(side * half, half), :] = helped.astype(BF)
            self.near_out[i - 1, pl.ds((1 - side) * half, half), :] = other.astype(BF)
            self.nears.append(
                self.moves.go(self.near_out.at[i - 1], self.near_in.at[i - 1], self.near[way])
            )
        self.result[...] = self.folded(0)
        if self.frees is not None:
            pl.semaphore_signal(
                self.frees, inc=1, device_id=self.near["core"], device_id_type=MESH
            )

    def done(self):
        for i in range(2):
            self.nears[i].wait_recv()
        self.result[...] += self.near_in[0].astype(F32) + self.near_in[1].astype(F32)


class Beside:
    def __init__(self, left, right):
        self.refs, self.size = (left, right), left.shape[1]

    def __getitem__(self, index):
        return jnp.concatenate([ref[...] for ref in self.refs], axis=1)

    def __setitem__(self, index, value):
        for i, ref in enumerate(self.refs):
            ref[...] = value[:, i * self.size : (i + 1) * self.size]


def leave_kernel(
    grads_ref,
    weights_ref,
    turned_ref,
    tok_ref,
    resid_ref,
    gain_ref,
    ffn_ref,
    group_ref,
    tokens_grad,
    wq_out,
    wk_out,
    wv_out,
    wg_out,
    gains_out,
    grads,
    weights,
    turned,
    ring_out,
    ring_in,
    held,
    odd_out,
    odd_in,
    far_out,
    far_in,
    near_out,
    near_in,
    gains,
    gains_in,
    gains_z,
    gain,
    send,
    recv,
    load_sem,
    free_sem,
):
    near = peers()
    tok = lax.axis_index("tok")
    z = lax.axis_index("head")
    count = lax.axis_size("head")
    rows, width = tok_ref.shape
    part = width // 8
    gain[...] = arranged(gain_ref, tok)
    cols = wv_out.shape[1]
    strip = width // 4

    def owned(step):
        owner = lax.rem(z + 2 * count - 1 - step, count)
        return pl.ds(pl.multiple_of(owner * rows, rows), rows)

    grad_loads = [
        pltpu.make_async_copy(
            grads_ref.at[owned(step), :], grads.at[owned(step), :], load_sem.at[step]
        )
        for step in range(count)
    ]
    strip_loads = [
        pltpu.make_async_copy(
            weights_ref.at[pl.ds(n * strip, strip), :],
            weights.at[pl.ds(n * strip, strip), :],
            load_sem.at[count + n],
        )
        for n in range(4)
    ]
    turned_load = pltpu.make_async_copy(turned_ref, turned, load_sem.at[count + 4])
    loads = [grad_loads[0], *strip_loads, *grad_loads[1:], turned_load]
    for load in loads:
        load.start()
    others = [
        {"tok": tok, "head": lax.rem(z + step, count)} for step in range(1, count)
    ]
    greet(near["core"], near["x"], near["y"], *others)
    moves = Moves(send, recv)

    def ring_term(step, side):
        @pl.loop(side * (width // 512), (side + 1) * (width // 512))
        def _(i):
            to = pl.ds(pl.multiple_of(i * 256, 256), 256)
            held[:, to] = dot_nt(grads[owned(step), :], weights[to, :])

    ring = {}
    half = width // 2

    def ring_send(step, side):
        at = pl.ds(side * half, half)
        value = held[:, at]
        if step:
            ring[step - 1, side].wait_recv()
            value = value + ring_in[step - 1, :, at].astype(F32)
        ring_out[step, :, at] = value.astype(BF)
        ring[step, side] = moves.go(
            ring_out.at[step, :, at], ring_in.at[step, :, at], near["up"]
        )

    def chunk_term(c):
        def term(r):
            left = turned[pl.ds(r * part, part), :]
            return jnp.concatenate(
                [
                    jnp.dot(
                        left,
                        grads[:, c * cols + j * 256 : c * cols + (j + 1) * 256],
                        preferred_element_type=F32,
                    )
                    for j in range(cols // 256)
                ],
                axis=1,
            )

        return term

    def buffers(c):
        s = c % 2
        return (
            odd_out.at[s], odd_in.at[s], far_out.at[s], far_in.at[c], near_out.at[s], near_in.at[c]
        )

    scatters = [
        Scatter(moves, near, chunk_term(c), buffers(c), result)
        for c, result in enumerate((Beside(wq_out, wk_out), wv_out))
    ]
    scatters.append(
        Scatter(moves, near, chunk_term(2), buffers(2), wg_out, scatters[0], free_sem)
    )
    scatters[0].frees = free_sem

    grad_loads[0].wait()
    for side in range(2):
        strip_loads[2 * side].wait()
        strip_loads[2 * side + 1].wait()
        ring_term(0, side)
        ring_send(0, side)
    for load in grad_loads[1:]:
        load.wait()
    turned_load.wait()
    ring_term(1, 0)
    ring_term(1, 1)
    for i in (3, 1, 2, 0):
        scatters[0].odd(i)
    ring_send(1, 0)
    scatters[0].far()
    for i in (3, 1):
        scatters[1].odd(i)
    ring_send(1, 1)
    for i in (2, 0):
        scatters[1].odd(i)
    ring_term(2, 0)
    scatters[0].close()
    ring_term(2, 1)
    ring_send(2, 0)
    scatters[1].far()
    for i in (3, 1):
        scatters[2].odd(i)
    ring_send(2, 1)
    scatters[1].close()
    for i in (2, 0):
        scatters[2].odd(i)
    scatters[0].done()
    scatters[2].far()
    ring_term(3, 0)
    ring_term(3, 1)
    scatters[1].done()
    scatters[2].close()
    scatters[2].done()

    gains[...] = jnp.zeros_like(gains)
    gains[pl.ds(2, 1), pl.ds(0, group_ref.shape[1])] = group_ref[pl.ds(0, 1), :]
    for r, place in enumerate(xor_places(tok)):
        at = pl.ds(pl.multiple_of(place * part, part), part)
        gains[pl.ds(1, 1), at] = (
            ffn_ref[pl.ds(0, 1), r * part : (r + 1) * part]
            + ffn_ref[pl.ds(1, 1), r * part : (r + 1) * part]
        )
    size = 16
    for side in range(2):
        ring[2, side].wait_recv()

    def block(i, total):
        at = pl.ds(pl.multiple_of(i * size, size), size)
        values = arranged(tok_ref.at[at, :], tok).astype(F32)
        mean = jnp.mean(values, axis=-1, keepdims=True)
        centred = values - mean
        inverse = lax.rsqrt(jnp.mean(centred * centred, axis=-1, keepdims=True) + EPS)
        unit = centred * inverse
        grad = held[at, :] + ring_in[2, at, :].astype(F32)
        scaled = grad * gain[...]
        first = jnp.mean(scaled, axis=-1, keepdims=True)
        second = jnp.mean(scaled * unit, axis=-1, keepdims=True)
        found = resid_ref[at, :] + inverse * (scaled - first - unit * second)
        for r, place in enumerate(xor_places(tok)):
            tokens_grad[at, pl.ds(pl.multiple_of(place * part, part), part)] = found[
                :, r * part : (r + 1) * part
            ]
        return total + jnp.sum(grad * unit, axis=0, keepdims=True)

    total = lax.fori_loop(0, rows // size, block, jnp.zeros((1, width), F32))
    for r, place in enumerate(xor_places(tok)):
        at = pl.ds(pl.multiple_of(place * part, part), part)
        gains[pl.ds(0, 1), at] = total[:, r * part : (r + 1) * part]

    for i, way in enumerate(("core", "x", "y")):
        move = moves.go(gains, gains_in.at[i], near[way])
        move.wait_recv()
        moves.sent(move)
        gains[...] += gains_in[i]
    last = [moves.go(gains, gains_z.at[i], others[i]) for i in range(count - 1)]
    total = gains[...]
    gains_out[...] = total
    for i, move in enumerate(last):
        move.wait_recv()
        gains_out[pl.ds(0, 2), :] += gains_z[i, pl.ds(0, 2), :]
    moves.finish()


def depart(grads, weights, turned, tokens, resid_grad, gain, ffn_terms, group_terms):
    rows, width = tokens.shape
    count = lax.axis_size("head")
    cols = grads.shape[1] // 3
    part = width // 8
    moves = 6 + 3 * 8 + 3 + count - 1
    sums = (8, width)
    return pl.pallas_call(
        leave_kernel,
        out_shape=(
            jax.ShapeDtypeStruct((rows, width), F32),
            jax.ShapeDtypeStruct((part, cols // 2), F32),
            jax.ShapeDtypeStruct((part, cols // 2), F32),
            jax.ShapeDtypeStruct((part, cols), F32),
            jax.ShapeDtypeStruct((part, cols), F32),
            jax.ShapeDtypeStruct(sums, F32),
        ),
        in_specs=[ANY] * 3 + [VMEM] * 5,
        out_specs=[VMEM] * 6,
        scratch_shapes=[
            pltpu.VMEM(grads.shape, BF),
            pltpu.VMEM(weights.shape, BF),
            pltpu.VMEM(turned.shape, BF),
            pltpu.VMEM((3, rows, width), BF),
            pltpu.VMEM((3, rows, width), BF),
            pltpu.VMEM((rows, width), F32),
            pltpu.VMEM((2, 4, part, cols), BF),
            pltpu.VMEM((2, 4, part, cols), BF),
            pltpu.VMEM((2, part, cols), BF),
            pltpu.VMEM((3, 2, part // 2, cols), BF),
            pltpu.VMEM((2, 2, part, cols), BF),
            pltpu.VMEM((3, 2, part, cols), BF),
            pltpu.VMEM(sums, F32),
            pltpu.VMEM((3,) + sums, F32),
            pltpu.VMEM((count - 1,) + sums, F32),
            pltpu.VMEM((1, width), F32),
            pltpu.SemaphoreType.DMA((moves,)),
            pltpu.SemaphoreType.DMA((moves,)),
            pltpu.SemaphoreType.DMA((count + 5,)),
            pltpu.SemaphoreType.REGULAR,
        ],
        compiler_params=pltpu.CompilerParams(
            collective_id=1, has_side_effects=True, vmem_limit_bytes=LIMIT
        ),
        cost_estimate=pl.CostEstimate(
            flops=2 * grads.shape[0] * width * 5 * cols, bytes_accessed=40 << 20, transcendentals=0
        ),
    )(
        grads, weights, turned, tokens, resid_grad, gain[None, :], ffn_terms, group_terms
    )


def dot_nt(left, right):
    return lax.dot_general(left, right, (((1,), (1,)), ((), ())), preferred_element_type=F32)


def dot_tn(left, right):
    return lax.dot_general(left, right, (((0,), (0,)), ((), ())), preferred_element_type=F32)


def dot_nn(left, right):
    return jnp.dot(left, right, preferred_element_type=F32)


def tile_decay(docs_col, docs_row, log_decay, first, tile, top):
    size = tile + top
    shape = (top, size)
    lag = (
        lax.broadcasted_iota(jnp.int32, shape, 0)
        + tile
        - lax.broadcasted_iota(jnp.int32, shape, 1)
    )
    same = docs_col[pl.ds(first + tile, top), :] == docs_row[pl.ds(0, 1), pl.ds(first, size)]
    power = jnp.exp(jnp.maximum(lag, 0).astype(F32) * log_decay)
    return jnp.where(same & (lag >= 0), power, 0.0)


def retain_kernel(
    lengths_ref,
    order_ref,
    gain_ref,
    qk_ref,
    v_ref,
    gate_ref,
    tok_ref,
    wo_ref,
    cot_ref,
    wu_ref,
    wd_ref,
    resid_out,
    unit_out,
    inverse_out,
    states_out,
    cot_pair,
    mixed_turned,
    up_full,
    down_full,
    mixed_out,
    out_weights,
    retained,
    terms,
    folded,
    gathered,
    held,
    ring_out,
    ring_in,
    cot_rows,
    docs_col,
    docs_row,
    scale_ref,
    send,
    recv,
    own_sem,
):
    near = peers()
    tok = lax.axis_index("tok")
    z = lax.axis_index("head")
    count = lax.axis_size("head")
    rows, width = tok_ref.shape
    group_rows = rows * count
    part = width // 8
    heads = v_ref.shape[1] // VAL
    blocks = group_rows // SPAN
    side_rows = rows // 2
    slice_ = wu_ref.shape[1]
    own = [
        pltpu.make_async_copy(
            wu_ref, up_full.at[pl.ds(0, part), pl.ds(0, slice_)], own_sem.at[0]
        ),
        pltpu.make_async_copy(
            wd_ref, down_full.at[pl.ds(0, slice_), pl.ds(0, part)], own_sem.at[1]
        ),
        pltpu.make_async_copy(wo_ref, out_weights, own_sem.at[2]),
    ]
    for copy in own:
        copy.start()
    greet(*everyone())
    moves = Moves(send, recv)
    far_up = moves.go(
        wu_ref, up_full.at[pl.ds(0, part), pl.ds(slice_, slice_)], near["cross"]
    )
    far_down = moves.go(
        wd_ref, down_full.at[pl.ds(slice_, slice_), pl.ds(0, part)], near["cross"]
    )

    def block_rows(b):
        return pl.ds(pl.multiple_of(b * SPAN, SPAN), SPAN)

    rate = decays(order_ref, heads)
    across = block_scales(lengths_ref, rate, group_rows, scale_ref, docs_col)
    docs_row[...] = row_docs(lengths_ref, group_rows)
    fold = group_weights(lengths_ref, rate, group_rows, False)

    def q_cols(h):
        return pl.ds(h * KEY, KEY)

    def k_cols(h):
        return pl.ds((heads + h) * KEY, KEY)

    def v_cols(h):
        return pl.ds(h * VAL, VAL)

    for h in range(heads):
        total = jnp.zeros((KEY, VAL), F32)
        for b in range(blocks):
            weighed = v_ref[block_rows(b), v_cols(h)].astype(F32) * scale_ref[
                block_rows(b), heads + h : heads + h + 1
            ]
            term = dot_tn(qk_ref[block_rows(b), k_cols(h)], weighed.astype(BF))
            terms[b, pl.ds(h * KEY, KEY), :] = term
            total = across[h][b] * total + term
        gathered[0, pl.ds(h * KEY, KEY), :] = total.astype(BF)

    def state_view(r, side=None):
        if side is None:
            return gathered.at[r]
        size = gathered.shape[1] // 2
        return gathered.at[r, pl.ds(side * size, size), :]

    def up_view(s):
        def view(r, side=None):
            if r == 0 and s == 0:
                return wu_ref
            if side is None:
                return up_full.at[pl.ds(r * part, part), pl.ds(s * slice_, slice_)]
            size = part // 2
            return up_full.at[
                pl.ds(r * part + side * size, size), pl.ds(s * slice_, slice_)
            ]

        return view

    def down_view(s):
        def view(r, side=None):
            if r == 0 and s == 0:
                return wd_ref
            if side is None:
                return down_full.at[pl.ds(s * slice_, slice_), pl.ds(r * part, part)]
            size = slice_ // 2
            return down_full.at[
                pl.ds(s * slice_ + side * size, size), pl.ds(r * part, part)
            ]

        return view

    states = Gather(moves, near, state_view)
    wide = [
        Gather(moves, near, view) for view in (up_view(0), down_view(0), up_view(1), down_view(1))
    ]
    states.first()
    wide[0].first()
    cot_move = moves.go(cot_ref, cot_rows, near["pair"])

    def intra(h):
        @pl.loop(0, blocks)
        def _(b):
            first = pl.multiple_of(b * SPAN, SPAN)
            for tile in range(0, SPAN, 128):
                at = pl.ds(first + tile, 128)
                seen = pl.ds(first, tile + 128)
                scores = dot_nt(qk_ref[at, q_cols(h)], qk_ref[seen, k_cols(h)])
                mask = tile_decay(docs_col, docs_row, rate[h], first, tile, 128)
                probs = (scores * mask).astype(BF)
                retained[at, v_cols(h)] = dot_nn(probs, v_ref[seen, v_cols(h)])

    def finish_head(h):
        first = jnp.zeros((KEY, VAL), F32)
        for r in range(8):
            first = first + fold[h][r] * gathered[r, pl.ds(h * KEY, KEY), :].astype(F32)
        for b in range(blocks):
            folded[b] = first.astype(BF)
            states_out[pl.ds((h * blocks + b) * KEY, KEY), :] = first.astype(BF)
            first = across[h][b] * first + terms[b, pl.ds(h * KEY, KEY), :]

        @pl.loop(0, group_rows // 128)
        def _(i):
            at = pl.ds(pl.multiple_of(i * 128, 128), 128)
            b = lax.div(i, SPAN // 128)
            cross = dot_nn(qk_ref[at, q_cols(h)], folded[b])
            values = retained[at, v_cols(h)] + scale_ref[at, h : h + 1] * cross
            mean = jnp.mean(values, axis=-1, keepdims=True)
            centred = values - mean
            inverse = lax.rsqrt(jnp.mean(centred * centred, axis=-1, keepdims=True) + EPS)
            unit = centred * inverse
            gate = gate_ref[at, v_cols(h)].astype(F32)
            swish = gate / (1.0 + jnp.exp(-gate))
            unit_out[at, v_cols(h)] = unit.astype(BF)
            inverse_out[at, h : h + 1] = inverse
            mixed = (swish * unit * gain_ref[:, h * VAL : (h + 1) * VAL]).astype(BF)
            mixed_out[at, v_cols(h)] = mixed
            mixed_turned[v_cols(h), at] = mixed.T

    intra(0)
    states.second()
    wide[1].first()
    for h in range(1, heads):
        intra(h)
    states.third()
    wide[0].second()
    states.done()
    for h in range(heads):
        finish_head(h)

    def ring_term(step):
        owner = lax.rem(z + 2 * count - 1 - step, count)
        at = pl.ds(pl.multiple_of(owner * rows, rows), rows)

        @pl.loop(0, width // 256)
        def _(i):
            to = pl.ds(pl.multiple_of(i * 256, 256), 256)
            held[:, to] = dot_nn(mixed_out[at, :], out_weights[:, to])

    ring = {}

    def ring_send(step, side):
        at = pl.ds(side * side_rows, side_rows)
        value = held[at, :]
        if step:
            ring[step - 1, side].wait_recv()
            value = value + ring_in[step - 1, at, :].astype(F32)
        ring_out[step, at, :] = value.astype(BF)
        ring[step, side] = moves.go(
            ring_out.at[step, at, :], ring_in.at[step, at, :], near["up"]
        )

    own[2].wait()
    ring_term(0)
    ring_send(0, 0)
    ring_send(0, 1)
    wide[1].second()
    far_up.wait_recv()
    wide[2].first()
    wide[0].third()
    ring_term(1)
    ring_send(1, 0)
    far_down.wait_recv()
    wide[3].first()
    wide[1].third()
    ring_send(1, 1)
    ring_term(2)
    wide[2].second()
    ring_send(2, 0)
    wide[3].second()
    ring_send(2, 1)
    ring_term(3)
    wide[2].third()
    wide[3].third()
    size = 32
    for side in range(2):
        ring[2, side].wait_recv()

        @pl.loop(0, side_rows // size)
        def _(i):
            at = pl.ds(pl.multiple_of(side * side_rows + i * size, size), size)
            values = jnp.concatenate(
                [
                    tok_ref[at, pl.ds(pl.multiple_of(place * part, part), part)]
                    for place in xor_places(tok)
                ],
                axis=1,
            ).astype(F32)
            resid_out[at, :] = values + held[at, :] + ring_in[2, at, :].astype(F32)

    cot_move.wait_recv()
    for ref, first in ((cot_ref, 0), (cot_rows, rows)):
        for r, place in enumerate(xor_places(tok)):
            cot_pair[pl.ds(first, rows), pl.ds(r * part, part)] = ref[
                :, pl.ds(pl.multiple_of(place * part, part), part)
            ]
    for gather in wide:
        gather.done()
    own[0].wait()
    own[1].wait()
    moves.finish()


def retain(
    doc_lengths, head_order, gain, qk, v, gate, tokens, out_full, cotangent, w_up, w_down
):
    rows, width = tokens.shape
    count = lax.axis_size("head")
    group_rows = rows * count
    heads = v.shape[1] // VAL
    blocks = group_rows // SPAN
    wide = 2 * w_up.shape[1]
    moves = 3 + 5 * 8 + 6
    struct = jax.ShapeDtypeStruct
    return pl.pallas_call(
        retain_kernel,
        out_shape=(
            struct((rows, width), F32),
            struct(v.shape, BF),
            struct((group_rows, heads), F32),
            struct((heads * blocks * KEY, VAL), BF),
            struct((2 * rows, width), BF),
            struct((heads * VAL, group_rows), BF),
            struct((width, wide), BF),
            struct((wide, width), BF),
        ),
        in_specs=[SMEM] * 2 + [VMEM] * 5 + [ANY] + [VMEM] * 3,
        out_specs=[VMEM] * 6 + [ANY] * 2,
        scratch_shapes=[
            pltpu.VMEM(v.shape, BF),
            pltpu.VMEM(out_full.shape, BF),
            pltpu.VMEM((group_rows, heads * VAL), F32),
            pltpu.VMEM((blocks, heads * KEY, VAL), F32),
            pltpu.VMEM((blocks, KEY, VAL), BF),
            pltpu.VMEM((8, heads * KEY, VAL), BF),
            pltpu.VMEM((rows, width), F32),
            pltpu.VMEM((3, rows, width), BF),
            pltpu.VMEM((3, rows, width), BF),
            pltpu.VMEM((rows, width), BF),
            pltpu.VMEM((group_rows, 1), jnp.int32),
            pltpu.VMEM((8, group_rows), jnp.int32),
            pltpu.VMEM((group_rows, 2 * heads), F32),
            pltpu.SemaphoreType.DMA((moves,)),
            pltpu.SemaphoreType.DMA((moves,)),
            pltpu.SemaphoreType.DMA((3,)),
        ],
        compiler_params=pltpu.CompilerParams(
            collective_id=2, has_side_effects=True, vmem_limit_bytes=LIMIT
        ),
        cost_estimate=pl.CostEstimate(
            flops=12 << 30, bytes_accessed=40 << 20, transcendentals=0
        ),
    )(
        doc_lengths, head_order, gain[None, :], qk, v, gate, tokens, out_full, cotangent, w_up,
        w_down,
    )


def feed_kernel(
    resid_ref,
    gain_ref,
    cot_ref,
    up_ref,
    down_ref,
    layer_out,
    far_out,
    resid_grad,
    gain_out,
    up_own,
    up_far,
    down_own,
    down_far,
    branch,
    up,
    down,
    lifted,
    cot,
    hidden,
    turned,
    pre,
    back_out,
    back_in,
    odd_out_d,
    odd_in_d,
    odd_out_u,
    odd_in_u,
    far_out_d,
    far_in_d,
    far_out_u,
    far_in_u,
    near_out_d,
    near_in_d,
    near_out_u,
    near_in_u,
    up_sum,
    down_sum,
    gain,
    send,
    recv,
    load_sem,
    free_sem,
):
    near = peers()
    gain[...] = arranged(gain_ref, lax.axis_index("tok"))
    z = lax.axis_index("head")
    count = lax.axis_size("head")
    rows, width = resid_ref.shape
    part = width // 8
    side_rows = rows // 2
    wide = up.shape[1]
    slice_ = wide // 2
    loads = [
        pltpu.make_async_copy(cot_ref, cot, load_sem.at[0]),
        pltpu.make_async_copy(up_ref, up, load_sem.at[1]),
        pltpu.make_async_copy(down_ref, down, load_sem.at[2]),
    ]
    for load in loads:
        load.start()
    greet(*everyone())
    moves = Moves(send, recv)
    size = 16

    pairs = []
    for side in range(2):

        @pl.loop(0, side_rows // size)
        def _(i):
            at = pl.ds(pl.multiple_of(side * side_rows + i * size, size), size)
            values = resid_ref[at, :]
            mean = jnp.mean(values, axis=-1, keepdims=True)
            centred = values - mean
            inverse = lax.rsqrt(jnp.mean(centred * centred, axis=-1, keepdims=True) + EPS)
            lifted[at, :] = (centred * inverse * gain[...]).astype(BF)

        pairs.append(
            moves.go(
                lifted.at[pl.ds(side * side_rows, side_rows), :],
                lifted.at[pl.ds(rows + side * side_rows, side_rows), :],
                near["pair"],
            )
        )

    def feed(first, number):
        @pl.loop(0, wide // 256)
        def _(i):
            to = pl.ds(pl.multiple_of(i * 256, 256), 256)
            at = pl.ds(first, number)
            hidden_pre = dot_nn(lifted[at, :], up[:, to])
            hidden_grad = dot_nt(cot[at, :], down[to, :])
            phi = 0.5 * (1.0 + lax.erf(hidden_pre * SQRT_HALF))
            made = (hidden_pre * phi).astype(BF)
            hidden[at, to] = made
            turned[to, at] = made.T
            slope = phi + hidden_pre * jnp.exp(-0.5 * hidden_pre * hidden_pre) * INV_ROOT_TWO_PI
            pre[at, to] = (hidden_grad * slope).astype(BF)

    for load in loads:
        load.wait()
    feed(0, rows)
    backs = []
    for side in range(2):
        if side:

            @pl.loop(0, width // 256)
            def _(i):
                to = pl.ds(pl.multiple_of(i * 256, 256), 256)
                resid_grad[:, to] = dot_nt(pre[pl.ds(0, rows), :], up[to, :])

        pairs[side].wait_recv()
        feed(rows + side * side_rows, side_rows)

        @pl.loop(0, width // 256)
        def _(i):
            to = pl.ds(pl.multiple_of(i * 256, 256), 256)
            found = dot_nt(pre[pl.ds(rows + side * side_rows, side_rows), :], up[to, :])
            back_out[pl.ds(side * side_rows, side_rows), to] = found.astype(BF)

        at = pl.ds(side * side_rows, side_rows)
        backs.append(moves.go(back_out.at[at, :], back_in.at[at, :], near["pair"]))

    def down_term(s):
        def term(r):
            return dot_nn(turned[pl.ds(s * slice_, slice_), :], cot[:, r * part : (r + 1) * part])

        return term

    def up_term(s):
        def term(r):
            return dot_tn(
                lifted[:, r * part : (r + 1) * part], pre[:, s * slice_ : (s + 1) * slice_]
            )

        return term

    down_sets = [
        (odd_out_d, odd_in_d, far_out_d, far_in_d.at[s], near_out_d, near_in_d.at[s])
        for s in range(2)
    ]
    up_sets = [
        (odd_out_u, odd_in_u, far_out_u, far_in_u.at[s], near_out_u, near_in_u.at[s])
        for s in range(2)
    ]
    sums = [
        Scatter(moves, near, down_term(0), down_sets[0], down_own),
        Scatter(moves, near, up_term(0), up_sets[0], up_own),
    ]
    sums += [
        Scatter(moves, near, down_term(1), down_sets[1], down_sum, sums[0], free_sem.at[0]),
        Scatter(moves, near, up_term(1), up_sets[1], up_sum, sums[1], free_sem.at[1]),
    ]
    sums[0].frees = free_sem.at[0]
    sums[1].frees = free_sem.at[1]

    ring = {}

    def shard(step, side):
        owner = lax.rem(z - step + count, count)
        first = pl.multiple_of(owner * rows + side * side_rows, side_rows)
        return branch.at[pl.ds(first, side_rows), :]

    def pass_on(step, side):
        if step:
            ring[step - 1, side].wait_recv()
        if step < count - 1:
            here = back_in.at[pl.ds(side * side_rows, side_rows), :] if step == 0 else shard(step, side)
            ring[step, side] = moves.go(here, shard(step, side), near["up"])

    def norm_back(side):
        backs[side].wait_recv()

        def block(i, total):
            at = pl.ds(pl.multiple_of(side * side_rows + i * size, size), size)
            values = resid_ref[at, :]
            mean = jnp.mean(values, axis=-1, keepdims=True)
            centred = values - mean
            inverse = lax.rsqrt(jnp.mean(centred * centred, axis=-1, keepdims=True) + EPS)
            unit = centred * inverse
            grad = resid_grad[at, :] + back_in[at, :].astype(F32)
            scaled = grad * gain[...]
            first = jnp.mean(scaled, axis=-1, keepdims=True)
            second = jnp.mean(scaled * unit, axis=-1, keepdims=True)
            found = cot[at, :].astype(F32) + inverse * (scaled - first - unit * second)
            resid_grad[at, :] = found
            back_in[at, :] = found.astype(BF)
            return total + jnp.sum(grad * unit, axis=0, keepdims=True)

        total = lax.fori_loop(0, side_rows // size, block, jnp.zeros((1, width), F32))
        gain_out[pl.ds(side, 1), :] = total

    norm_back(0)
    pass_on(0, 0)
    for i in (3, 1, 2, 0):
        sums[0].odd(i)
    for i in (3, 1):
        sums[1].odd(i)
    norm_back(1)
    pass_on(0, 1)
    mine = pltpu.make_async_copy(
        back_in, branch.at[pl.ds(pl.multiple_of(z * rows, rows), rows), :], load_sem.at[3]
    )
    mine.start()
    sums[0].far()
    for i in (2, 0):
        sums[1].odd(i)
    pass_on(1, 0)
    sums[1].far()
    sums[0].close()
    pass_on(1, 1)
    for i in (3, 1, 2, 0):
        sums[2].odd(i)
    sums[1].close()
    sums[2].far()
    pass_on(2, 0)

    @pl.loop(0, width // 256)
    def _(i):
        to = pl.ds(pl.multiple_of(i * 256, 256), 256)
        layer_out[:, to] = resid_ref[:, to] + dot_nn(hidden[pl.ds(0, rows), :], down[:, to])

    for i in (3, 1, 2, 0):
        sums[3].odd(i)
    pass_on(2, 1)
    sums[2].close()
    sums[3].far()
    sums[0].done()
    sums[1].done()

    @pl.loop(0, width // 256)
    def _(i):
        to = pl.ds(pl.multiple_of(i * 256, 256), 256)
        far_out[:, to] = dot_nn(hidden[pl.ds(rows, rows), :], down[:, to]).astype(BF)

    sums[3].close()
    pass_on(3, 0)
    sums[2].done()
    down_far[...] = down_sum[...].astype(BF)
    sums[3].done()
    up_far[...] = up_sum[...].astype(BF)
    pass_on(3, 1)
    mine.wait()
    moves.finish()


def feed_forward(resid, gain, cot_pair, up_full, down_full):
    rows, width = resid.shape
    count = lax.axis_size("head")
    part = width // 8
    wide = up_full.shape[1]
    slice_ = wide // 2
    moves = 4 + 4 * 8 + 6
    struct = jax.ShapeDtypeStruct
    down_piece = (slice_, part)
    up_piece = (part, slice_)

    def sets(piece):
        half = (piece[0] // 2, piece[1])
        return [
            pltpu.VMEM(piece, BF),
            pltpu.VMEM((2, 2) + half, BF),
        ]

    def nears(piece):
        return [pltpu.VMEM((2,) + piece, BF), pltpu.VMEM((2, 2) + piece, BF)]

    def odds(piece):
        return [pltpu.VMEM((4,) + piece, BF)] * 2

    return pl.pallas_call(
        feed_kernel,
        out_shape=(
            struct((rows, width), F32),
            struct((rows, width), BF),
            struct((rows, width), F32),
            struct((8, width), F32),
            struct(up_piece, F32),
            struct(up_piece, BF),
            struct(down_piece, F32),
            struct(down_piece, BF),
            struct((count * rows, width), BF),
        ),
        in_specs=[VMEM] * 2 + [ANY] * 3,
        out_specs=[VMEM] * 8 + [ANY],
        scratch_shapes=[
            pltpu.VMEM((width, wide), BF),
            pltpu.VMEM((wide, width), BF),
            pltpu.VMEM((2 * rows, width), BF),
            pltpu.VMEM((2 * rows, width), BF),
            pltpu.VMEM((2 * rows, wide), BF),
            pltpu.VMEM((wide, 2 * rows), BF),
            pltpu.VMEM((2 * rows, wide), BF),
            pltpu.VMEM((rows, width), BF),
            pltpu.VMEM((rows, width), BF),
            *odds(down_piece),
            *odds(up_piece),
            *sets(down_piece),
            *sets(up_piece),
            *nears(down_piece),
            *nears(up_piece),
            pltpu.VMEM(up_piece, F32),
            pltpu.VMEM(down_piece, F32),
            pltpu.VMEM((1, width), F32),
            pltpu.SemaphoreType.DMA((moves,)),
            pltpu.SemaphoreType.DMA((moves,)),
            pltpu.SemaphoreType.DMA((4,)),
            pltpu.SemaphoreType.REGULAR((2,)),
        ],
        compiler_params=pltpu.CompilerParams(
            collective_id=3, has_side_effects=True, vmem_limit_bytes=LIMIT
        ),
        cost_estimate=pl.CostEstimate(
            flops=26 << 30, bytes_accessed=40 << 20, transcendentals=0
        ),
    )(resid, gain[None, :], cot_pair, up_full, down_full)


def recall_kernel(
    lengths_ref,
    order_ref,
    gain_ref,
    wo_hbm,
    branch_hbm,
    gate_hbm,
    unit_hbm,
    inverse_hbm,
    qk_hbm,
    v_hbm,
    turned_hbm,
    states_hbm,
    cos_hbm,
    sin_hbm,
    own_hbm,
    far_ref,
    up_ref,
    down_ref,
    wo_grad,
    gains,
    layer_out,
    grads_out,
    up_in,
    down_in,
    out_weights,
    branch,
    gate_ref,
    unit_ref,
    inverse_ref,
    qk_ref,
    v_ref,
    turned_ref,
    states_ref,
    cos_ref,
    sin_ref,
    own_ref,
    far_in,
    grads,
    docs_col,
    docs_row,
    scale_ref,
    back,
    terms,
    gathered,
    folded,
    dqk,
    dv,
    odd_out,
    odd_in,
    out_far,
    in_far,
    out_near,
    in_near,
    send,
    recv,
    load_sem,
    keep_sem,
):
    near = peers()
    tok = lax.axis_index("tok")
    group_rows, cols = v_ref.shape
    heads = cols // VAL
    blocks = group_rows // SPAN
    width = branch.shape[1]
    part = width // 8
    loads = [
        pltpu.make_async_copy(source, target, load_sem.at[n])
        for n, (source, target) in enumerate(
            (
                (wo_hbm, out_weights),
                (branch_hbm, branch),
                (gate_hbm, gate_ref),
                (unit_hbm, unit_ref),
                (inverse_hbm, inverse_ref),
                (qk_hbm, qk_ref),
                (v_hbm, v_ref),
                (turned_hbm, turned_ref),
                (states_hbm, states_ref),
                (cos_hbm, cos_ref),
                (sin_hbm, sin_ref),
                (own_hbm, own_ref),
            )
        )
    ]
    for load in loads:
        load.start()
    greet(*everyone())
    moves = Moves(send, recv)
    swaps = [
        moves.go(far_ref, far_in, near["pair"]),
        moves.go(up_ref, up_in, near["cross"]),
        moves.go(down_ref, down_in, near["cross"]),
    ]

    def block_rows(b):
        return pl.ds(pl.multiple_of(b * SPAN, SPAN), SPAN)

    def q_cols(h):
        return pl.ds(h * KEY, KEY)

    def k_cols(h):
        return pl.ds((heads + h) * KEY, KEY)

    def v_cols(h):
        return pl.ds(h * VAL, VAL)

    rate = decays(order_ref, heads)
    across = block_scales(lengths_ref, rate, group_rows, scale_ref, docs_col)
    docs_row[...] = row_docs(lengths_ref, group_rows)
    fold = group_weights(lengths_ref, rate, group_rows, True)
    for load in loads[:5]:
        load.wait()

    def tile_back(i, totals):
        at = pl.ds(pl.multiple_of(i * 128, 128), 128)
        sums = []
        for h in range(heads):
            grad = dot_nt(branch[at, :], out_weights[v_cols(h), :]).astype(BF).astype(F32)
            gate = gate_ref[at, v_cols(h)].astype(F32)
            sigma = 1.0 / (1.0 + jnp.exp(-gate))
            swish = gate * sigma
            unit = unit_ref[at, v_cols(h)].astype(F32)
            gain = gain_ref[:, h * VAL : (h + 1) * VAL]
            grads[at, pl.ds(2 * heads * KEY + cols + h * VAL, VAL)] = (
                grad * unit * gain * (sigma + swish * (1.0 - sigma))
            ).astype(BF)
            inner = grad * swish
            scaled = inner * gain
            first = jnp.mean(scaled, axis=-1, keepdims=True)
            second = jnp.mean(scaled * unit, axis=-1, keepdims=True)
            back[at, v_cols(h)] = (
                inverse_ref[at, h : h + 1] * (scaled - first - unit * second)
            ).astype(BF)
            sums.append(totals[h] + jnp.sum(inner * unit, axis=0, keepdims=True))
        return tuple(sums)

    totals = lax.fori_loop(
        0, group_rows // 128, tile_back, tuple(jnp.zeros((1, VAL), F32) for _ in range(heads))
    )
    gains[...] = jnp.zeros_like(gains)
    for h in range(heads):
        gains[pl.ds(0, 1), v_cols(h)] = totals[h]
    first_gate = 2 * heads * KEY + cols
    kept = [
        pltpu.make_async_copy(
            grads.at[:, pl.ds(first_gate, cols)],
            grads_out.at[:, pl.ds(first_gate, cols)],
            keep_sem.at[0],
        ),
        pltpu.make_async_copy(
            grads.at[:, pl.ds(0, first_gate)], grads_out.at[:, pl.ds(0, first_gate)], keep_sem.at[1]
        ),
    ]
    kept[0].start()
    for load in loads[5:]:
        load.wait()

    for h in range(heads):
        total = jnp.zeros((KEY, VAL), F32)
        for b in reversed(range(blocks)):
            weighed = back[block_rows(b), v_cols(h)].astype(F32) * scale_ref[
                block_rows(b), h : h + 1
            ]
            term = dot_tn(qk_ref[block_rows(b), q_cols(h)], weighed.astype(BF))
            terms[b, pl.ds(h * KEY, KEY), :] = term
            total = across[h][b] * total + term
        gathered[0, pl.ds(h * KEY, KEY), :] = total.astype(BF)

    def state_view(r, side=None):
        if side is None:
            return gathered.at[r]
        size = gathered.shape[1] // 2
        return gathered.at[r, pl.ds(side * size, size), :]

    states = Gather(moves, near, state_view)
    states.first()

    def out_term(r):
        return dot_nn(turned_ref[...], branch[:, r * part : (r + 1) * part])

    outward = Scatter(
        moves, near, out_term, (odd_out, odd_in, out_far, in_far, out_near, in_near), wo_grad
    )

    def intra(h):
        @pl.loop(0, blocks)
        def _(b):
            first = pl.multiple_of(b * SPAN, SPAN)
            for tile in range(SPAN - 128, -1, -128):
                at = pl.ds(first + tile, 128)
                seen = pl.ds(first, tile + 128)
                mask = tile_decay(docs_col, docs_row, rate[h], first, tile, 128)
                query = qk_ref[at, q_cols(h)]
                key = qk_ref[seen, k_cols(h)]
                ret = back[at, v_cols(h)]
                probs = (dot_nt(query, key) * mask).astype(BF)
                score = (dot_nt(ret, v_ref[seen, v_cols(h)]) * mask).astype(BF)
                dqk[at, q_cols(h)] = dot_nn(score, key)
                to_keys = dot_tn(score, query)
                to_values = dot_tn(probs, ret)
                if tile == SPAN - 128:
                    dqk[seen, k_cols(h)] = to_keys
                    dv[seen, v_cols(h)] = to_values
                else:
                    dqk[seen, k_cols(h)] += to_keys
                    dv[seen, v_cols(h)] += to_values

    def finish_head(h):
        later = jnp.zeros((KEY, VAL), F32)
        for r in range(8):
            later = later + fold[h][r] * gathered[r, pl.ds(h * KEY, KEY), :].astype(F32)
        for b in reversed(range(blocks)):
            folded[b] = later.astype(BF)
            later = across[h][b] * later + terms[b, pl.ds(h * KEY, KEY), :]

        @pl.loop(0, group_rows // 128)
        def _(i):
            at = pl.ds(pl.multiple_of(i * 128, 128), 128)
            b = lax.div(i, SPAN // 128)
            reach = scale_ref[at, h : h + 1]
            leave = scale_ref[at, heads + h : heads + h + 1]
            state = states_ref[pl.ds(pl.multiple_of((h * blocks + b) * KEY, KEY), KEY), :]
            cosine, sine = cos_ref[at, :], sin_ref[at, :]
            for found, to in (
                (
                    dqk[at, q_cols(h)] + reach * dot_nt(back[at, v_cols(h)], state),
                    q_cols(h),
                ),
                (
                    dqk[at, k_cols(h)] + leave * dot_nt(v_ref[at, v_cols(h)], folded[b]),
                    k_cols(h),
                ),
            ):
                one, two = found[:, : KEY // 2], found[:, KEY // 2 :]
                grads[at, to] = jnp.concatenate(
                    [one * cosine + two * sine, two * cosine - one * sine], axis=1
                ).astype(BF)
            found = dv[at, v_cols(h)] + leave * dot_nn(qk_ref[at, k_cols(h)], folded[b])
            grads[at, pl.ds(2 * heads * KEY + h * VAL, VAL)] = found.astype(BF)

    for i in (3, 1):
        outward.odd(i)
    intra(0)
    states.second()
    for i in (2, 0):
        outward.odd(i)
    for h in range(1, heads):
        intra(h)
    states.third()
    outward.far()
    states.done()
    finish_head(0)
    outward.close()
    for h in range(1, heads):
        finish_head(h)
    kept[1].start()
    swaps[0].wait_recv()
    for r, place in enumerate(xor_places(tok)):
        at = pl.ds(r * part, part)
        layer_out[:, pl.ds(pl.multiple_of(place * part, part), part)] = (
            own_ref[:, at] + far_in[:, at].astype(F32)
        ).astype(BF)
    outward.done()
    for swap_ in swaps[1:]:
        swap_.wait_recv()
    for copy in kept:
        copy.wait()
    moves.finish()


def recall(
    doc_lengths, head_order, gain, qk, v, gate, unit, inverse, states, cosine, sine, mixed_turned,
    branch, out_full, layer_own, far_out, up_far, down_far,
):
    group_rows, cols = v.shape
    heads = cols // VAL
    blocks = group_rows // SPAN
    width = branch.shape[1]
    part = width // 8
    piece = (cols, part)
    moves = 3 + 8 + 8
    struct = jax.ShapeDtypeStruct
    loaded = (
        out_full, branch, gate, unit, inverse, qk, v, mixed_turned, states, cosine, sine, layer_own
    )
    return pl.pallas_call(
        recall_kernel,
        out_shape=(
            struct(piece, F32),
            struct((8, cols), F32),
            struct(far_out.shape, BF),
            struct((group_rows, 3 * cols), BF),
            struct(up_far.shape, BF),
            struct(down_far.shape, BF),
        ),
        in_specs=[SMEM] * 2 + [VMEM] + [ANY] * 15,
        out_specs=[VMEM] * 3 + [ANY] * 3,
        scratch_shapes=[
            *[pltpu.VMEM(array.shape, array.dtype) for array in loaded],
            pltpu.VMEM(far_out.shape, BF),
            pltpu.VMEM((group_rows, 3 * cols), BF),
            pltpu.VMEM((group_rows, 1), jnp.int32),
            pltpu.VMEM((8, group_rows), jnp.int32),
            pltpu.VMEM((group_rows, 2 * heads), F32),
            pltpu.VMEM(v.shape, BF),
            pltpu.VMEM((blocks, heads * KEY, VAL), F32),
            pltpu.VMEM((8, heads * KEY, VAL), BF),
            pltpu.VMEM((blocks, KEY, VAL), BF),
            pltpu.VMEM((group_rows, 2 * heads * KEY), F32),
            pltpu.VMEM((group_rows, cols), F32),
            pltpu.VMEM((4,) + piece, BF),
            pltpu.VMEM((4,) + piece, BF),
            pltpu.VMEM(piece, BF),
            pltpu.VMEM((2, cols // 2, part), BF),
            pltpu.VMEM((2,) + piece, BF),
            pltpu.VMEM((2,) + piece, BF),
            pltpu.SemaphoreType.DMA((moves,)),
            pltpu.SemaphoreType.DMA((moves,)),
            pltpu.SemaphoreType.DMA((len(loaded),)),
            pltpu.SemaphoreType.DMA((2,)),
        ],
        compiler_params=pltpu.CompilerParams(
            collective_id=4, has_side_effects=True, vmem_limit_bytes=LIMIT
        ),
        cost_estimate=pl.CostEstimate(
            flops=20 << 30, bytes_accessed=40 << 20, transcendentals=0
        ),
    )(doc_lengths, head_order, gain[None, :], *loaded, far_out, up_far, down_far)


def norm_forward(values, gain):
    mean = jnp.mean(values, axis=-1, keepdims=True)
    centred = values - mean
    inverse = lax.rsqrt(jnp.mean(centred * centred, axis=-1, keepdims=True) + EPS)
    unit = centred * inverse
    return (unit * gain, unit, inverse)


def norm_backward(grad_out, unit, inverse, gain):
    scaled = grad_out * gain
    first = jnp.mean(scaled, axis=-1, keepdims=True)
    second = jnp.mean(scaled * unit, axis=-1, keepdims=True)
    return (inverse * (scaled - first - unit * second), jnp.sum(grad_out * unit, axis=0))


def doc_index(row_ids, starts):
    return jnp.sum((starts[None, :] <= row_ids[:, None]).astype(jnp.int32), axis=1) - 1


def doc_position(row_ids, starts):
    first = jnp.max(jnp.where(starts[None, :] <= row_ids[:, None], starts[None, :], 0), axis=1)
    return row_ids - first


def angles(position, half):
    freq = jnp.exp(-jnp.log(10000.0) * jnp.arange(half, dtype=F32) / half)
    turn = position.astype(F32)[:, None] * freq[None, :]
    return (jnp.cos(turn), jnp.sin(turn))


def rotate(values, cosine, sine):
    half = values.shape[-1] // 2
    first, second = (values[..., :half], values[..., half:])
    return jnp.concatenate(
        [first * cosine - second * sine, first * sine + second * cosine], axis=-1
    )


def unrotate(grads, cosine, sine):
    return rotate(grads, cosine, -sine)


def span_masks(doc_ids, before, log_decay):
    size = doc_ids.shape[0]
    place = jnp.arange(size, dtype=F32)
    lag = place[:, None] - place[None, :]
    same = (doc_ids[:, None] == doc_ids[None, :]) & (lag >= 0)
    decay = jnp.where(same, jnp.exp(jnp.maximum(lag, 0.0) * log_decay), 0.0)
    reach = jnp.where(doc_ids == before, jnp.exp((place + 1.0) * log_decay), 0.0)[:, None]
    leave = jnp.where(doc_ids == doc_ids[-1], jnp.exp((size - 1.0 - place) * log_decay), 0.0)[
        :, None
    ]
    across = jnp.where(doc_ids[-1] == before, jnp.exp(size * log_decay), 0.0)
    return (decay, reach, leave, across)


def gelu_slope(hidden_pre):
    return (
        0.5 * (1.0 + lax.erf(hidden_pre * SQRT_HALF))
        + hidden_pre * jnp.exp(-0.5 * hidden_pre * hidden_pre) * INV_ROOT_TWO_PI
    )


def plain(
    tokens,
    cotangent,
    doc_lengths,
    head_order,
    norm_gain,
    w_query,
    w_key,
    w_value,
    w_gate,
    group_gain,
    w_out,
    ffn_gain,
    w_up,
    w_down,
):
    heads = w_query.shape[1] // KEY
    head_count = lax.axis_size("head")
    tok_count = lax.axis_size("tok")
    z = lax.axis_index("head")
    tok = lax.axis_index("tok")
    rows = tokens.shape[0]
    group_rows = rows * head_count
    blocks = group_rows // SPAN
    width = tokens.shape[1]
    part = width // tok_count

    tokens_f = reorder(tokens).astype(F32)
    cot_own = reorder(cotangent)
    gain1 = reorder(norm_gain)
    gain2 = reorder(ffn_gain)
    normed1, unit1, inverse1 = norm_forward(tokens_f, gain1)
    qk = w_query.shape[1]
    vg = w_value.shape[1]
    up_two = jnp.concatenate([w_up, swap(w_up, "head", 2)], axis=1)
    down_two = jnp.concatenate([w_down, swap(w_down, "head", 2)], axis=0)
    up_full = tok_gather(up_two, 0)
    down_full = tok_gather(down_two, 1)
    cot_pair = jnp.concatenate([cot_own, swap(cot_own, "head", 1)], axis=0)

    ends = jnp.cumsum(doc_lengths)
    starts = ends - doc_lengths
    first_row = tok * group_rows
    row_ids = first_row + jnp.arange(group_rows, dtype=jnp.int32)
    doc_ids = doc_index(row_ids, starts)
    previous = doc_index(jnp.reshape(first_row - 1, (1,)), starts)[0]
    group_last = doc_index((jnp.arange(tok_count, dtype=jnp.int32) + 1) * group_rows - 1, starts)
    cosine, sine = angles(doc_position(row_ids, starts), KEY // 2)
    ranks = lax.dynamic_slice_in_dim(head_order, z * heads, heads)
    log_decay = jnp.log1p(-jnp.exp2(-(5.0 + ranks.astype(F32))))

    group = head_gather(normed1.astype(BF))
    qkvg_full = tok_gather(jnp.concatenate([w_query, w_key, w_value, w_gate], axis=1), 0)
    out_full = tok_gather(w_out, 1)
    projected = mm(group, qkvg_full)
    qk_rows = jnp.concatenate(
        [
            rotate(projected[:, h * KEY : (h + 1) * KEY], cosine, sine).astype(BF)
            for h in range(2 * heads)
        ],
        axis=1,
    )
    v_rows = projected[:, 2 * qk : 2 * qk + vg].astype(BF)
    gate = projected[:, 2 * qk + vg :]

    def head_of(array, head, size):
        return array[:, head * size : (head + 1) * size]

    def block_of(array, block):
        return array[block * SPAN : (block + 1) * SPAN]

    q, k, v, masks = [], [], [], []
    for h in range(heads):
        q.append(head_of(qk_rows, h, KEY))
        k.append(head_of(qk_rows, heads + h, KEY))
        v.append(head_of(v_rows, h, VAL))
        masks.append(
            [
                span_masks(
                    block_of(doc_ids, b),
                    previous if b == 0 else doc_ids[b * SPAN - 1],
                    log_decay[h],
                )
                for b in range(blocks)
            ]
        )

    group_order = jnp.arange(tok_count, dtype=jnp.int32)

    def weigh(lag, last, h):
        return jnp.where(
            (lag >= 0) & (group_last == last),
            jnp.exp(jnp.maximum(lag, 0).astype(F32) * group_rows * log_decay[h]),
            0.0,
        )

    ends_of = []
    added = []
    for h in range(heads):
        state = jnp.zeros((KEY, VAL), F32)
        terms = []
        for b in range(blocks):
            term = mm_tn(block_of(k[h], b), (block_of(v[h], b) * masks[h][b][2]).astype(BF))
            terms.append(term)
            state = masks[h][b][3] * state + term
        added.append(terms)
        ends_of.append(state.astype(BF))
    all_states = lax.all_gather(jnp.concatenate(ends_of, axis=0), "tok", axis=0)
    lag = tok - 1 - group_order
    states = []
    retained = []
    for h in range(heads):
        weights = weigh(lag, previous, h)
        state = jnp.sum(
            all_states[:, h * KEY : (h + 1) * KEY].astype(F32) * weights[:, None, None], axis=0
        )
        mine = []
        outs = []
        for b in range(blocks):
            mine.append(state.astype(BF))
            qb, kb, vb = block_of(q[h], b), block_of(k[h], b), block_of(v[h], b)
            decay, reach, leave, across = masks[h][b]
            probs = (mm_nt(qb, kb) * decay).astype(BF)
            outs.append(mm(probs, vb) + reach * mm(qb, mine[-1]))
            state = across * state + added[h][b]
        states.append(mine)
        retained.append(jnp.concatenate(outs, axis=0))

    mixed_parts, unit_g, inverse_g, grouped, swish, sigma = [], [], [], [], [], []
    for h in range(heads):
        g, u, i = norm_forward(retained[h], head_of(group_gain[None, :], h, VAL))
        gate_h = head_of(gate, h, VAL)
        s = jax.nn.sigmoid(gate_h)
        unit_g.append(u)
        inverse_g.append(i)
        grouped.append(g)
        sigma.append(s)
        swish.append(gate_h * s)
        mixed_parts.append((swish[-1] * g).astype(BF))
    mixed = jnp.concatenate(mixed_parts, axis=1)

    out_sum = head_scatter(lambda i: mm(rows_of(mixed, i, rows), out_full))
    resid = tokens_f + out_sum
    normed2, unit2, inverse2 = norm_forward(resid, gain2)
    lifted2 = normed2.astype(BF)
    lifted2_pair = jnp.concatenate([lifted2, swap(lifted2, "head", 1)], axis=0)
    hidden_pre = mm(lifted2_pair, up_full)
    hidden = jax.nn.gelu(hidden_pre, approximate=False).astype(BF)
    hidden_grad = mm_nt(cot_pair, down_full)
    pre_grad = (hidden_grad * gelu_slope(hidden_pre)).astype(BF)
    far_grad = mm_nt(pre_grad[rows:], up_full).astype(BF)
    lifted2_grad = mm_nt(pre_grad[:rows], up_full) + swap(far_grad, "head", 1).astype(F32)
    resid_part, ffn_gain_local = norm_backward(lifted2_grad, unit2, inverse2, gain2)
    resid_grad = cot_own.astype(F32) + resid_part
    branch_own = resid_grad.astype(BF)
    branch = head_gather(branch_own)

    far_out = mm(hidden[rows:], down_full).astype(BF)
    layer_out = reorder(
        (resid + mm(hidden[:rows], down_full) + swap(far_out, "head", 1).astype(F32)).astype(BF)
    )

    def piece(array, r):
        return array[:, r * part : (r + 1) * part]

    slots = range(tok_count)
    down_two_grad = tok_scatter([mm_tn(hidden, piece(cot_pair, r)) for r in slots])
    half = down_two_grad.shape[0] // 2
    w_down_grad = down_two_grad[:half] + swap(
        down_two_grad[half:].astype(BF), "head", 2
    ).astype(F32)
    up_two_grad = tok_scatter([mm_tn(piece(lifted2_pair, r), pre_grad) for r in slots])
    half = up_two_grad.shape[1] // 2
    w_up_grad = up_two_grad[:, :half] + swap(
        up_two_grad[:, half:].astype(BF), "head", 2
    ).astype(F32)

    mixed_grad = mm_nt(branch, out_full).astype(BF)
    w_out_grad = tok_scatter([mm_tn(mixed, piece(branch, r)) for r in slots])

    gate_parts, ret_grad, group_gain_parts = [], [], []
    for h in range(heads):
        head_grad = head_of(mixed_grad, h, VAL).astype(F32)
        gate_parts.append(
            (head_grad * grouped[h] * (sigma[h] + swish[h] * (1.0 - sigma[h]))).astype(BF)
        )
        back, gain_term = norm_backward(
            head_grad * swish[h], unit_g[h], inverse_g[h], head_of(group_gain[None, :], h, VAL)
        )
        ret_grad.append(back.astype(BF))
        group_gain_parts.append(gain_term)
    gate_grad = jnp.concatenate(gate_parts, axis=1)
    w_gate_grad = tok_scatter([mm_tn(piece(group, r), gate_grad) for r in slots])

    pending_of, pending_terms = [], []
    for h in range(heads):
        pending = jnp.zeros((KEY, VAL), F32)
        terms = [None] * blocks
        for b in reversed(range(blocks)):
            terms[b] = mm_tn(
                block_of(q[h], b), (block_of(ret_grad[h], b) * masks[h][b][1]).astype(BF)
            )
            pending = masks[h][b][3] * pending + terms[b]
        pending_terms.append(terms)
        pending_of.append(pending.astype(BF))
    all_pending = lax.all_gather(jnp.concatenate(pending_of, axis=0), "tok", axis=0)
    lag_back = group_order - 1 - tok
    shifted_last = doc_index(group_order * group_rows - 1, starts)
    q_parts, k_parts, v_parts = [], [], []
    for h in range(heads):
        weights = jnp.where(
            (lag_back >= 0) & (shifted_last == doc_ids[-1]),
            jnp.exp(jnp.maximum(lag_back, 0).astype(F32) * group_rows * log_decay[h]),
            0.0,
        )
        later = jnp.sum(
            all_pending[:, h * KEY : (h + 1) * KEY].astype(F32) * weights[:, None, None], axis=0
        )
        qg, kg, vg_ = [None] * blocks, [None] * blocks, [None] * blocks
        for b in reversed(range(blocks)):
            qb, kb, vb = block_of(q[h], b), block_of(k[h], b), block_of(v[h], b)
            rb = block_of(ret_grad[h], b)
            decay, reach, leave, across = masks[h][b]
            probs = (mm_nt(qb, kb) * decay).astype(BF)
            score_grad = (mm_nt(rb, vb) * decay).astype(BF)
            later_b = later.astype(BF)
            qg[b] = mm(score_grad, kb) + reach * mm_nt(rb, states[h][b])
            kg[b] = mm_tn(score_grad, qb) + leave * mm_nt(vb, later_b)
            vg_[b] = mm_tn(probs, rb) + leave * mm(kb, later_b)
            later = across * later + pending_terms[h][b]
        q_parts.append(unrotate(jnp.concatenate(qg, axis=0), cosine, sine).astype(BF))
        k_parts.append(unrotate(jnp.concatenate(kg, axis=0), cosine, sine).astype(BF))
        v_parts.append(jnp.concatenate(vg_, axis=0).astype(BF))
    all_grad = jnp.concatenate(q_parts + k_parts + v_parts + [gate_grad], axis=1)
    group_terms = jnp.concatenate(group_gain_parts, axis=0)
    ffn_terms = reorder(ffn_gain_local)
    row_grad = head_scatter(lambda i: mm_nt(rows_of(all_grad, i, rows), qkvg_full))
    input_part, norm_gain_local = norm_backward(row_grad, unit1, inverse1, gain1)
    tokens_grad = reorder(resid_grad + input_part)
    qkv_grad = all_grad[:, : 2 * qk + vg]
    w_qkv_grad = tok_scatter([mm_tn(piece(group, r), qkv_grad) for r in slots])
    w_query_grad = w_qkv_grad[:, :qk]
    w_key_grad = w_qkv_grad[:, qk : 2 * qk]
    w_value_grad = w_qkv_grad[:, 2 * qk :]
    group_gain_grad = sum_small(group_terms, "tok")
    ffn_sum = sum_small(sum_small(ffn_terms, "tok"), "head")
    norm_sum = sum_small(sum_small(reorder(norm_gain_local), "tok"), "head")
    return (
        layer_out,
        tokens_grad,
        norm_sum,
        w_query_grad,
        w_key_grad,
        w_value_grad,
        w_gate_grad,
        group_gain_grad,
        w_out_grad,
        ffn_sum,
        w_up_grad,
        w_down_grad,
    )


def fused(
    tokens,
    cotangent,
    doc_lengths,
    head_order,
    norm_gain,
    w_query,
    w_key,
    w_value,
    w_gate,
    group_gain,
    w_out,
    ffn_gain,
    w_up,
    w_down,
):
    turned, qkvg_full, out_full, qk_rows, v_rows, gate, cosine, sine = enter(
        tokens, norm_gain, doc_lengths, w_query, w_key, w_value, w_gate, w_out
    )
    resid, unit_g, inverse_g, states, cot_pair, mixed_turned, up_full, down_full = retain(
        doc_lengths, head_order, group_gain, qk_rows, v_rows, gate, tokens, out_full, cotangent,
        w_up, w_down,
    )
    (
        layer_own, far_out, resid_grad, ffn_terms, up_own, up_far, down_own, down_far, branch
    ) = feed_forward(resid, ffn_gain, cot_pair, up_full, down_full)
    w_out_grad, group_terms, layer_out, all_grad, up_in, down_in = recall(
        doc_lengths, head_order, group_gain, qk_rows, v_rows, gate, unit_g, inverse_g, states,
        cosine, sine, mixed_turned, branch, out_full, layer_own, far_out, up_far, down_far,
    )
    w_up_grad = up_own + up_in.astype(F32)
    w_down_grad = down_own + down_in.astype(F32)
    tokens_grad, w_query_grad, w_key_grad, w_value_grad, w_gate_grad, sums = depart(
        all_grad, qkvg_full, turned, tokens, resid_grad, norm_gain, ffn_terms, group_terms
    )
    return (
        layer_out,
        tokens_grad,
        sums[0],
        w_query_grad,
        w_key_grad,
        w_value_grad,
        w_gate_grad,
        sums[2, : group_gain.shape[0]],
        w_out_grad,
        sums[1],
        w_up_grad,
        w_down_grad,
    )


def local(*arrays):
    return fused(*arrays) if paired() else plain(*arrays)


def solution(mesh):
    rows = P(("tok", "head"), None)
    inward = P("tok", "head")
    outward = P("head", "tok")
    return jax.shard_map(
        local,
        mesh=mesh,
        in_specs=(
            rows, rows, P(), P(), P(), inward, inward, inward, inward, P("head"),
            outward, P(), inward, outward,
        ),
        out_specs=(
            rows, rows, P(), inward, inward, inward, inward, P("head"),
            outward, P(), inward, outward,
        ),
        check_vma=False,
    )
```

```python
import jax
import jax.numpy as jnp
from jax import lax
from jax.experimental import pallas as pl
from jax.experimental.pallas import tpu as pltpu
from jax.sharding import PartitionSpec as P

KEY = 256
VAL = 512
SPAN = 512

EPS = 1e-05
SQRT_HALF = 0.7071067811865476
INV_ROOT_TWO_PI = 0.3989422804014327
BF = jnp.bfloat16
F32 = jnp.float32


def mm(left, right):
    return jnp.dot(left, right, preferred_element_type=F32)


def mm_nt(left, right):
    return lax.dot_general(left, right, (((1,), (1,)), ((), ())), preferred_element_type=F32)


def mm_tn(left, right):
    return lax.dot_general(left, right, (((0,), (0,)), ((), ())), preferred_element_type=F32)


def swap(array, axis, bit):
    count = lax.axis_size(axis)
    return lax.ppermute(array, axis, [(i, i ^ bit) for i in range(count)])


def shift(array):
    count = lax.axis_size("head")
    return lax.ppermute(array, "head", [(i, (i + 1) % count) for i in range(count)])


def paired():
    return lax.axis_size("tok") == 8


def reorder(array):
    if not paired():
        return array
    me = lax.axis_index("tok")
    width = array.shape[-1] // 8
    return jnp.concatenate(
        [
            lax.dynamic_slice_in_dim(array, (me ^ r) * width, width, array.ndim - 1)
            for r in range(8)
        ],
        axis=-1,
    )


def halves(array):
    half = array.shape[0] // 2
    return array[:half], array[half:]


def tok_gather(shard, axis):
    if not paired():
        return lax.all_gather(shard, "tok", axis=axis, tiled=True)
    along_x = swap(shard, "tok", 2)
    along_y = swap(shard, "tok", 4)
    far = jnp.concatenate(
        [swap(halves(along_x)[0], "tok", 4), swap(halves(along_y)[1], "tok", 2)], axis=0
    )
    own = [shard, along_x, along_y, far]
    pieces = []
    for piece in own:
        pieces += [piece, swap(piece, "tok", 1)]
    return jnp.concatenate(pieces, axis=axis)


def tok_scatter(pieces):
    pieces = [p.astype(BF) for p in pieces]
    if not paired():
        return lax.psum_scatter(jnp.stack(pieces), "tok", scatter_dimension=0).astype(F32)
    kept = [
        pieces[r].astype(F32) + swap(pieces[r + 1], "tok", 1).astype(F32) for r in (0, 2, 4, 6)
    ]
    zero, two, four, six = kept
    six_a, six_b = halves(six.astype(BF))
    two_a, two_b = halves(two)
    four_a, four_b = halves(four)
    four_a = four_a + swap(six_a, "tok", 2).astype(F32)
    two_b = two_b + swap(six_b, "tok", 4).astype(F32)
    two = jnp.concatenate([two_a, two_b], axis=0).astype(BF)
    four = jnp.concatenate([four_a, four_b], axis=0).astype(BF)
    return zero + swap(two, "tok", 2).astype(F32) + swap(four, "tok", 4).astype(F32)


def head_gather(rows):
    count = lax.axis_size("head")
    me = lax.axis_index("head")
    size = rows.shape[0]
    whole = jnp.zeros((count * size,) + rows.shape[1:], rows.dtype)
    whole = lax.dynamic_update_slice_in_dim(whole, rows, me * size, 0)
    for step in range(1, count):
        rows = shift(rows)
        source = lax.rem(me - step + count, count)
        whole = lax.dynamic_update_slice_in_dim(whole, rows, source * size, 0)
    return whole


def head_scatter(term):
    count = lax.axis_size("head")
    me = lax.axis_index("head")
    total = term(lax.rem(me + count - 1, count))
    for step in range(1, count):
        arrived = shift(total.astype(BF))
        owner = lax.rem(me + 2 * count - 1 - step, count)
        total = term(owner) + arrived.astype(F32)
    return total


def rows_of(array, index, size):
    return lax.dynamic_slice_in_dim(array, index * size, size, 0)


def sum_small(vector, axis):
    count = lax.axis_size(axis)
    bit = 1
    while bit < count:
        vector = vector + swap(vector, axis, bit)
        bit *= 2
    return vector


MESH = pl.DeviceIdType.MESH
ANY = pl.BlockSpec(memory_space=pl.ANY)
VMEM = pl.BlockSpec(memory_space=pltpu.VMEM)
SMEM = pl.BlockSpec(memory_space=pltpu.SMEM)
LIMIT = 60 * 1024 * 1024


def flipped(index, bit):
    return index + bit - 2 * bit * lax.rem(lax.div(index, bit), 2)


def peers():
    tok = lax.axis_index("tok")
    z = lax.axis_index("head")
    count = lax.axis_size("head")
    return {
        "core": {"tok": flipped(tok, 1), "head": z},
        "x": {"tok": flipped(tok, 2), "head": z},
        "y": {"tok": flipped(tok, 4), "head": z},
        "up": {"tok": tok, "head": lax.rem(z + 1, count)},
        "down": {"tok": tok, "head": lax.rem(z + count - 1, count)},
        "pair": {"tok": tok, "head": flipped(z, 1)},
        "cross": {"tok": tok, "head": flipped(z, 2)},
    }


def everyone():
    near = peers()
    tok = lax.axis_index("tok")
    z = lax.axis_index("head")
    count = lax.axis_size("head")
    others = [{"tok": tok, "head": lax.rem(z + step, count)} for step in range(1, count)]
    return [near["core"], near["x"], near["y"], *others]


def greet(*devices):
    barrier = pltpu.get_barrier_semaphore()
    for device in devices:
        pl.semaphore_signal(barrier, inc=1, device_id=device, device_id_type=MESH)
    pl.semaphore_wait(barrier, len(devices))


def doc_starts(lengths):
    starts, total = [], 0
    for d in range(lengths.shape[0]):
        starts.append(total)
        total = total + lengths[d]
    return starts


def doc_at(row, starts):
    return sum((start <= row).astype(jnp.int32) for start in starts) - 1


def doc_first(row, starts):
    first = jnp.zeros_like(row)
    for start in starts:
        first = jnp.maximum(first, jnp.where(start <= row, start, 0))
    return first


def decays(order, heads):
    z = lax.axis_index("head")
    found = []
    for h in range(heads):
        rank = jnp.full((1, 1), order[z * heads + h], jnp.int32).astype(F32)
        found.append(jnp.log1p(-jnp.exp2(-(5.0 + rank))))
    return found


def block_scales(lengths, log_decay, group_rows, scale, docs):
    heads = len(log_decay)
    starts = doc_starts(lengths)
    first_row = lax.axis_index("tok") * group_rows
    across = [[] for _ in range(heads)]
    for b in range(group_rows // SPAN):
        at = pl.ds(b * SPAN, SPAN)
        low = first_row + b * SPAN
        place = lax.broadcasted_iota(jnp.int32, (SPAN, 1), 0)
        doc = doc_at(low + place, starts)
        docs[at, :] = doc
        before = doc_at(low - 1, starts)
        last = doc_at(low + SPAN - 1, starts)
        where = place.astype(F32)
        for h in range(heads):
            scale[at, h : h + 1] = jnp.where(
                doc == before, jnp.exp((where + 1.0) * log_decay[h]), 0.0
            )
            scale[at, heads + h : heads + h + 1] = jnp.where(
                doc == last, jnp.exp((SPAN - 1.0 - where) * log_decay[h]), 0.0
            )
            across[h].append(jnp.where(last == before, jnp.exp(SPAN * log_decay[h]), 0.0))
    return across


def row_docs(lengths, group_rows):
    starts = doc_starts(lengths)
    first_row = lax.axis_index("tok") * group_rows
    return doc_at(first_row + lax.broadcasted_iota(jnp.int32, (8, group_rows), 1), starts)


def group_weights(lengths, log_decay, group_rows, backward):
    starts = doc_starts(lengths)
    tok = lax.axis_index("tok")
    first_row = tok * group_rows
    found = [[] for _ in log_decay]
    for other in xor_places(tok):
        if backward:
            lag = other - 1 - tok
            same = doc_at(other * group_rows - 1, starts) == doc_at(
                first_row + group_rows - 1, starts
            )
        else:
            lag = tok - 1 - other
            same = doc_at((other + 1) * group_rows - 1, starts) == doc_at(first_row - 1, starts)
        amount = (jnp.maximum(lag, 0) * group_rows).astype(F32)
        for h, rate in enumerate(log_decay):
            found[h].append(jnp.where((lag >= 0) & same, jnp.exp(amount * rate), 0.0))
    return found


def state_view(gathered, h):
    def view(r, side=None):
        if side is None:
            return gathered.at[r, pl.ds(h * KEY, KEY), :]
        return gathered.at[r, pl.ds(h * KEY + side * (KEY // 2), KEY // 2), :]

    return view


class Moves:
    def __init__(self, send, recv):
        self.send, self.recv, self.made, self.over = send, recv, [], []

    def go(self, src, dst, device):
        n = len(self.made)
        copy = pltpu.make_async_remote_copy(
            src_ref=src,
            dst_ref=dst,
            send_sem=self.send.at[n],
            recv_sem=self.recv.at[n],
            device_id=device,
            device_id_type=MESH,
        )
        copy.start()
        self.made.append(copy)
        return copy

    def sent(self, copy):
        copy.wait_send()
        self.over.append(copy)

    def finish(self):
        for copy in self.made:
            if not any(copy is gone for gone in self.over):
                copy.wait_send()


class Gather:
    def __init__(self, moves, near, view):
        self.moves, self.near, self.view = moves, near, view

    def first(self):
        go, near, view = self.moves.go, self.near, self.view
        self.x = go(view(0), view(2), near["x"])
        self.y = go(view(0), view(4), near["y"])
        self.cores = [go(view(0), view(1), near["core"])]

    def second(self):
        go, near, view = self.moves.go, self.near, self.view
        self.x.wait_recv()
        self.far = [go(view(2, 0), view(6, 0), near["y"])]
        self.cores.append(go(view(2), view(3), near["core"]))
        self.y.wait_recv()
        self.far.append(go(view(4, 1), view(6, 1), near["x"]))
        self.cores.append(go(view(4), view(5), near["core"]))

    def third(self):
        go, near, view = self.moves.go, self.near, self.view
        for copy in self.far:
            copy.wait_recv()
        self.cores.append(go(view(6), view(7), near["core"]))

    def done(self):
        for copy in self.cores:
            copy.wait_recv()


def enter_kernel(
    tok_ref,
    gain_ref,
    lengths_ref,
    wq_ref,
    wk_ref,
    wv_ref,
    wg_ref,
    wo_ref,
    turned_out,
    weights_out,
    out_full,
    qk_out,
    v_out,
    gate_out,
    cos_ref,
    sin_ref,
    turned,
    group,
    weights,
    own_out,
    gain,
    send,
    recv,
    own_sem,
    keep_sem,
):
    near = peers()
    tok = lax.axis_index("tok")
    z = lax.axis_index("head")
    count = lax.axis_size("head")
    rows, width = tok_ref.shape
    part = width // 8
    cols = weights.shape[2]
    half = wq_ref.shape[1]

    own = [
        pltpu.make_async_copy(wq_ref, weights.at[0, pl.ds(0, part), pl.ds(0, half)], own_sem.at[0]),
        pltpu.make_async_copy(
            wk_ref, weights.at[0, pl.ds(0, part), pl.ds(half, half)], own_sem.at[1]
        ),
        pltpu.make_async_copy(wv_ref, weights.at[1, pl.ds(0, part), :], own_sem.at[2]),
        pltpu.make_async_copy(wg_ref, weights.at[2, pl.ds(0, part), :], own_sem.at[3]),
        pltpu.make_async_copy(wo_ref, own_out, own_sem.at[4]),
    ]
    for copy in own:
        copy.start()
    greet(*everyone())
    moves = Moves(send, recv)

    def chunk_view(c):
        def view(r, side=None):
            if side is None:
                return weights.at[c, pl.ds(r * part, part), :]
            return weights.at[c, pl.ds(r * part + side * (part // 2), part // 2), :]

        return view

    def out_view(r, side=None):
        if r == 0:
            return own_out
        if side is None:
            return out_full.at[:, pl.ds(r * part, part)]
        size = out_full.shape[0] // 2
        return out_full.at[pl.ds(side * size, size), pl.ds(r * part, part)]

    chunks = [Gather(moves, near, chunk_view(c)) for c in range(3)]
    outward = Gather(moves, near, out_view)
    own[0].wait()
    own[1].wait()
    chunks[0].first()
    own[2].wait()
    chunks[1].first()
    own[3].wait()
    own[4].wait()
    kept = [pltpu.make_async_copy(own_out, out_full.at[:, pl.ds(0, part)], keep_sem.at[4])]
    kept[0].start()
    gain[...] = arranged(gain_ref, tok)

    @pl.loop(0, rows // 16)
    def _(i):
        at = pl.ds(pl.multiple_of(i * 16, 16), 16)
        values = jnp.concatenate(
            [
                tok_ref[at, pl.ds(pl.multiple_of(place * part, part), part)]
                for place in xor_places(tok)
            ],
            axis=1,
        ).astype(F32)
        mean = jnp.mean(values, axis=-1, keepdims=True)
        centred = values - mean
        inverse = lax.rsqrt(jnp.mean(centred * centred, axis=-1, keepdims=True) + EPS)
        lifted = (centred * inverse * gain[...]).astype(BF)
        group[pl.ds(pl.multiple_of(z * rows + i * 16, 16), 16), :] = lifted

    def shard(step, side):
        owner = lax.rem(z - step + count, count)
        size = rows // 2
        return group.at[pl.ds(pl.multiple_of(owner * rows + side * size, size), size), :]

    ring = {}

    def pass_on(step, side):
        if step:
            ring[step - 1, side].wait_recv()
        if step < count - 1:
            ring[step, side] = moves.go(shard(step, side), shard(step, side), near["up"])

    def project(c, steps):
        first, number = steps

        @pl.loop(0, number * (cols // 256))
        def _(i):
            step = first + lax.div(i, cols // 256)
            tile = lax.rem(i, cols // 256)
            owner = lax.rem(z - step + count, count)
            at = pl.ds(pl.multiple_of(owner * rows, rows), rows)
            to = pl.ds(pl.multiple_of(tile * 256, 256), 256)
            found = jnp.dot(group[at, :], weights[c, :, to], preferred_element_type=F32)
            if c == 0:
                cosine, sine = cos_ref[at, :], sin_ref[at, :]
                one, two = found[:, :128], found[:, 128:]
                qk_out[at, to] = jnp.concatenate(
                    [one * cosine - two * sine, one * sine + two * cosine], axis=1
                ).astype(BF)
            elif c == 1:
                v_out[at, to] = found.astype(BF)
            else:
                gate_out[at, to] = found.astype(BF)

    def turn(step):
        owner = lax.rem(z - step + count, count)

        @pl.loop(0, width // 256)
        def _(i):
            at = pl.ds(pl.multiple_of(i * 256, 256), 256)
            to = pl.ds(pl.multiple_of(owner * rows, rows), rows)
            turned[at, to] = group[to, at].T

    def keep(c):
        copy = pltpu.make_async_copy(
            weights.at[c], weights_out.at[:, pl.ds(c * cols, cols)], keep_sem.at[c]
        )
        copy.start()
        kept.append(copy)

    pass_on(0, 0)
    pass_on(0, 1)
    group_rows = rows * count
    starts = doc_starts(lengths_ref)
    index = lax.broadcasted_iota(jnp.int32, (1, KEY // 2), 1).astype(F32)
    freq = jnp.exp(-jnp.log(10000.0) * index / (KEY // 2))

    @pl.loop(0, group_rows // 64)
    def _(i):
        at = pl.ds(pl.multiple_of(i * 64, 64), 64)
        row = tok * group_rows + i * 64 + lax.broadcasted_iota(jnp.int32, (64, KEY // 2), 0)
        turn = (row - doc_first(row, starts)).astype(F32) * freq
        cos_ref[at, :] = jnp.cos(turn)
        sin_ref[at, :] = jnp.sin(turn)

    chunks[0].second()
    chunks[2].first()
    pass_on(1, 0)
    chunks[1].second()
    outward.first()
    pass_on(1, 1)
    chunks[0].third()
    chunks[0].done()
    keep(0)
    project(0, (0, 2))
    pass_on(2, 0)
    turn(0)
    turn(1)
    chunks[2].second()
    pass_on(2, 1)
    chunks[1].third()
    chunks[1].done()
    keep(1)
    project(1, (0, 2))
    outward.second()
    project(0, (2, 1))
    project(1, (2, 1))
    turn(2)
    chunks[2].third()
    chunks[2].done()
    keep(2)
    pass_on(3, 0)
    outward.third()
    project(2, (0, 3))
    pass_on(3, 1)
    turn(3)
    copy = pltpu.make_async_copy(turned, turned_out, keep_sem.at[3])
    copy.start()
    kept.append(copy)
    project(0, (3, 1))
    project(1, (3, 1))
    project(2, (3, 1))
    outward.done()
    for copy in kept:
        copy.wait()
    moves.finish()


def arranged(ref, tok):
    part = ref.shape[-1] // 8
    return jnp.concatenate(
        [ref[:, pl.ds(pl.multiple_of(place * part, part), part)] for place in xor_places(tok)],
        axis=1,
    )


def xor_places(tok):
    places = []
    for r in range(8):
        place = tok
        for bit in (1, 2, 4):
            if r & bit:
                place = flipped(place, bit)
        places.append(place)
    return places


def enter(tokens, gain, doc_lengths, w_query, w_key, w_value, w_gate, w_out):
    rows, width = tokens.shape
    group_rows = rows * lax.axis_size("head")
    cols = w_value.shape[1]
    moves = 4 * 8 + 6
    return pl.pallas_call(
        enter_kernel,
        out_shape=(
            jax.ShapeDtypeStruct((width, group_rows), BF),
            jax.ShapeDtypeStruct((width, 3 * cols), BF),
            jax.ShapeDtypeStruct((w_out.shape[0], width), BF),
            jax.ShapeDtypeStruct((group_rows, cols), BF),
            jax.ShapeDtypeStruct((group_rows, cols), BF),
            jax.ShapeDtypeStruct((group_rows, cols), BF),
            jax.ShapeDtypeStruct((group_rows, KEY // 2), F32),
            jax.ShapeDtypeStruct((group_rows, KEY // 2), F32),
        ),
        in_specs=[VMEM] * 2 + [SMEM] + [ANY] * 5,
        out_specs=[ANY] * 3 + [VMEM] * 5,
        scratch_shapes=[
            pltpu.VMEM((width, group_rows), BF),
            pltpu.VMEM((group_rows, width), BF),
            pltpu.VMEM((3, width, cols), BF),
            pltpu.VMEM(w_out.shape, BF),
            pltpu.VMEM((1, width), F32),
            pltpu.SemaphoreType.DMA((moves,)),
            pltpu.SemaphoreType.DMA((moves,)),
            pltpu.SemaphoreType.DMA((5,)),
            pltpu.SemaphoreType.DMA((5,)),
        ],
        compiler_params=pltpu.CompilerParams(
            collective_id=0, has_side_effects=True, vmem_limit_bytes=LIMIT
        ),
        cost_estimate=pl.CostEstimate(
            flops=2 * group_rows * width * 3 * cols, bytes_accessed=40 << 20, transcendentals=0
        ),
    )(tokens, gain[None, :], doc_lengths, w_query, w_key, w_value, w_gate, w_out)


class Scatter:
    def __init__(self, moves, near, term, buffers, result, before=None, ready=None):
        self.moves, self.near, self.term, self.result = moves, near, term, result
        self.odd_out, self.odd_in, self.far_out, self.far_in, self.near_out, self.near_in = buffers
        self.half = self.far_out.shape[0] // 2
        self.before, self.ready, self.frees = before, ready, None
        self.cores = {}

    def odd(self, i):
        if self.before is not None:
            if not self.cores:
                pl.semaphore_wait(self.ready, 1)
            self.moves.sent(self.before.cores[i])
        self.odd_out[i] = self.term(2 * i + 1).astype(BF)
        self.cores[i] = self.moves.go(self.odd_out.at[i], self.odd_in.at[i], self.near["core"])

    def folded(self, i):
        self.cores[i].wait_recv()
        return self.term(2 * i) + self.odd_in[i].astype(F32)

    def far(self):
        value = self.folded(3).astype(BF)
        if self.before is not None:
            for move in self.before.fars:
                self.moves.sent(move)
        self.far_out[...] = value
        self.fars = [
            self.moves.go(
                self.far_out.at[pl.ds(side * self.half, self.half), :],
                self.far_in.at[side],
                self.near[way],
            )
            for side, way in ((0, "x"), (1, "y"))
        ]

    def close(self):
        half = self.half
        self.nears = []
        for i, side, way in ((1, 1, "x"), (2, 0, "y")):
            value = self.folded(i)
            self.fars[side].wait_recv()
            helped = value[side * half : (side + 1) * half] + self.far_in[side].astype(F32)
            other = value[(1 - side) * half : (2 - side) * half]
            if self.before is not None:
                self.moves.sent(self.before.nears[i - 1])
            self.near_out[i - 1, pl.ds(side * half, half), :] = helped.astype(BF)
            self.near_out[i - 1, pl.ds((1 - side) * half, half), :] = other.astype(BF)
            self.nears.append(
                self.moves.go(self.near_out.at[i - 1], self.near_in.at[i - 1], self.near[way])
            )
        self.result[...] = self.folded(0)
        if self.frees is not None:
            pl.semaphore_signal(
                self.frees, inc=1, device_id=self.near["core"], device_id_type=MESH
            )

    def done(self):
        for i in range(2):
            self.nears[i].wait_recv()
        self.result[...] += self.near_in[0].astype(F32) + self.near_in[1].astype(F32)


class Beside:
    def __init__(self, left, right):
        self.refs, self.size = (left, right), left.shape[1]

    def __getitem__(self, index):
        return jnp.concatenate([ref[...] for ref in self.refs], axis=1)

    def __setitem__(self, index, value):
        for i, ref in enumerate(self.refs):
            ref[...] = value[:, i * self.size : (i + 1) * self.size]


class AllSum:
    def __init__(self, moves, vector, slots, others):
        self.moves, self.vector, self.slots, self.others = moves, vector, slots, others

    def start(self):
        self.made = [
            self.moves.go(self.vector, self.slots.at[n], device)
            for n, device in enumerate(self.others)
        ]

    def total(self):
        total = self.vector[...]
        for n, move in enumerate(self.made):
            move.wait_recv()
            total = total + self.slots[n]
        return total


def leave_kernel(
    grads_ref,
    weights_ref,
    turned_ref,
    tok_ref,
    resid_ref,
    gain_ref,
    ffn_ref,
    group_ref,
    tokens_grad,
    wq_out,
    wk_out,
    wv_out,
    wg_out,
    norm_out,
    ffn_out,
    group_out,
    grads,
    weights,
    turned,
    ring_out,
    ring_in,
    held,
    odd_out,
    odd_in,
    far_out,
    far_in,
    near_out,
    near_in,
    norm_vec,
    norm_vec2,
    norm_slots_z,
    norm_slots,
    ffn_vec,
    ffn_vec2,
    ffn_slots_z,
    ffn_slots,
    group_vec,
    group_slots,
    gain,
    send,
    recv,
    load_sem,
    free_sem,
):
    near = peers()
    tok = lax.axis_index("tok")
    z = lax.axis_index("head")
    count = lax.axis_size("head")
    rows, width = tok_ref.shape
    part = width // 8
    gain[...] = arranged(gain_ref, tok)
    cols = wv_out.shape[1]
    strip = width // 4

    def owned(step):
        owner = lax.rem(z + 2 * count - 1 - step, count)
        return pl.ds(pl.multiple_of(owner * rows, rows), rows)

    grad_loads = [
        pltpu.make_async_copy(
            grads_ref.at[owned(step), :], grads.at[owned(step), :], load_sem.at[step]
        )
        for step in range(count)
    ]
    strip_loads = [
        pltpu.make_async_copy(
            weights_ref.at[pl.ds(n * strip, strip), :],
            weights.at[pl.ds(n * strip, strip), :],
            load_sem.at[count + n],
        )
        for n in range(4)
    ]
    turned_load = pltpu.make_async_copy(turned_ref, turned, load_sem.at[count + 4])
    loads = [grad_loads[0], *strip_loads, *grad_loads[1:], turned_load]
    for load in loads:
        load.start()
    z_others = [{"tok": tok, "head": lax.rem(z + step, count)} for step in range(1, count)]
    tok_others = [{"tok": place, "head": z} for place in xor_places(tok)[1:]]
    greet(*z_others, *tok_others)
    moves = Moves(send, recv)

    def ring_term(step, side):
        @pl.loop(side * (width // 512), (side + 1) * (width // 512))
        def _(i):
            to = pl.ds(pl.multiple_of(i * 256, 256), 256)
            held[:, to] = dot_nt(grads[owned(step), :], weights[to, :])

    ring = {}
    half = width // 2

    def ring_send(step, side):
        at = pl.ds(side * half, half)
        value = held[:, at]
        if step:
            ring[step - 1, side].wait_recv()
            value = value + ring_in[step - 1, :, at].astype(F32)
        ring_out[step, :, at] = value.astype(BF)
        ring[step, side] = moves.go(
            ring_out.at[step, :, at], ring_in.at[step, :, at], near["up"]
        )

    def chunk_term(c):
        def term(r):
            left = turned[pl.ds(r * part, part), :]
            return jnp.concatenate(
                [
                    jnp.dot(
                        left,
                        grads[:, c * cols + j * 256 : c * cols + (j + 1) * 256],
                        preferred_element_type=F32,
                    )
                    for j in range(cols // 256)
                ],
                axis=1,
            )

        return term

    def buffers(c):
        s = c % 2
        return (
            odd_out.at[s], odd_in.at[s], far_out.at[s], far_in.at[c], near_out.at[s], near_in.at[c]
        )

    scatters = [
        Scatter(moves, near, chunk_term(c), buffers(c), result)
        for c, result in enumerate((Beside(wq_out, wk_out), wv_out))
    ]
    scatters.append(
        Scatter(moves, near, chunk_term(2), buffers(2), wg_out, scatters[0], free_sem)
    )
    scatters[0].frees = free_sem

    ffn_vec[...] = jnp.zeros_like(ffn_vec)
    group_vec[...] = jnp.zeros_like(group_vec)
    for r, place in enumerate(xor_places(tok)):
        ffn_vec[pl.ds(place, 1), :] = (
            ffn_ref[pl.ds(0, 1), r * part : (r + 1) * part]
            + ffn_ref[pl.ds(1, 1), r * part : (r + 1) * part]
        )
    for n in range(cols // part):
        group_vec[pl.ds(n, 1), :] = group_ref[pl.ds(0, 1), n * part : (n + 1) * part]
    ffn_z = AllSum(moves, ffn_vec, ffn_slots_z, z_others)
    group_tok = AllSum(moves, group_vec, group_slots, tok_others)
    ffn_z.start()
    group_tok.start()
    grad_loads[0].wait()
    for side in range(2):
        strip_loads[2 * side].wait()
        strip_loads[2 * side + 1].wait()
        ring_term(0, side)
        ring_send(0, side)
    for load in grad_loads[1:]:
        load.wait()
    turned_load.wait()
    ring_term(1, 0)
    ring_term(1, 1)
    for i in (3, 1, 2, 0):
        scatters[0].odd(i)
    group_out[...] = group_tok.total()
    ffn_vec2[...] = ffn_z.total()
    ffn_tok = AllSum(moves, ffn_vec2, ffn_slots, tok_others)
    ffn_tok.start()
    ring_send(1, 0)
    scatters[0].far()
    for i in (3, 1):
        scatters[1].odd(i)
    ring_send(1, 1)
    for i in (2, 0):
        scatters[1].odd(i)
    ring_term(2, 0)
    scatters[0].close()
    ring_term(2, 1)
    ring_send(2, 0)
    scatters[1].far()
    for i in (3, 1):
        scatters[2].odd(i)
    ring_send(2, 1)
    scatters[1].close()
    for i in (2, 0):
        scatters[2].odd(i)
    scatters[0].done()
    scatters[2].far()
    ffn_out[...] = ffn_tok.total()
    ring_term(3, 0)
    ring_term(3, 1)
    scatters[1].done()
    scatters[2].close()
    scatters[2].done()

    size = 16
    for side in range(2):
        ring[2, side].wait_recv()

    def block(i, total):
        at = pl.ds(pl.multiple_of(i * size, size), size)
        values = arranged(tok_ref.at[at, :], tok).astype(F32)
        mean = jnp.mean(values, axis=-1, keepdims=True)
        centred = values - mean
        inverse = lax.rsqrt(jnp.mean(centred * centred, axis=-1, keepdims=True) + EPS)
        unit = centred * inverse
        grad = held[at, :] + ring_in[2, at, :].astype(F32)
        scaled = grad * gain[...]
        first = jnp.mean(scaled, axis=-1, keepdims=True)
        second = jnp.mean(scaled * unit, axis=-1, keepdims=True)
        found = resid_ref[at, :] + inverse * (scaled - first - unit * second)
        for r, place in enumerate(xor_places(tok)):
            tokens_grad[at, pl.ds(pl.multiple_of(place * part, part), part)] = found[
                :, r * part : (r + 1) * part
            ]
        return total + jnp.sum(grad * unit, axis=0, keepdims=True)

    total = lax.fori_loop(0, rows // size, block, jnp.zeros((1, width), F32))
    for r, place in enumerate(xor_places(tok)):
        norm_vec[pl.ds(place, 1), :] = total[:, r * part : (r + 1) * part]
    norm_z = AllSum(moves, norm_vec, norm_slots_z, z_others)
    norm_z.start()
    norm_vec2[...] = norm_z.total()
    norm_tok = AllSum(moves, norm_vec2, norm_slots, tok_others)
    norm_tok.start()
    norm_out[...] = norm_tok.total()
    moves.finish()


def depart(grads, weights, turned, tokens, resid_grad, gain, ffn_terms, group_terms):
    rows, width = tokens.shape
    count = lax.axis_size("head")
    cols = grads.shape[1] // 3
    part = width // 8
    moves = 6 + 3 * 8 + 2 * (count - 1) + 3 * 7
    vector = (8, part)
    return pl.pallas_call(
        leave_kernel,
        out_shape=(
            jax.ShapeDtypeStruct((rows, width), F32),
            jax.ShapeDtypeStruct((part, cols // 2), F32),
            jax.ShapeDtypeStruct((part, cols // 2), F32),
            jax.ShapeDtypeStruct((part, cols), F32),
            jax.ShapeDtypeStruct((part, cols), F32),
            jax.ShapeDtypeStruct(vector, F32),
            jax.ShapeDtypeStruct(vector, F32),
            jax.ShapeDtypeStruct(vector, F32),
        ),
        in_specs=[ANY] * 3 + [VMEM] * 5,
        out_specs=[VMEM] * 8,
        scratch_shapes=[
            pltpu.VMEM(grads.shape, BF),
            pltpu.VMEM(weights.shape, BF),
            pltpu.VMEM(turned.shape, BF),
            pltpu.VMEM((3, rows, width), BF),
            pltpu.VMEM((3, rows, width), BF),
            pltpu.VMEM((rows, width), F32),
            pltpu.VMEM((2, 4, part, cols), BF),
            pltpu.VMEM((2, 4, part, cols), BF),
            pltpu.VMEM((2, part, cols), BF),
            pltpu.VMEM((3, 2, part // 2, cols), BF),
            pltpu.VMEM((2, 2, part, cols), BF),
            pltpu.VMEM((3, 2, part, cols), BF),
            pltpu.VMEM(vector, F32),
            pltpu.VMEM(vector, F32),
            pltpu.VMEM((count - 1,) + vector, F32),
            pltpu.VMEM((7,) + vector, F32),
            pltpu.VMEM(vector, F32),
            pltpu.VMEM(vector, F32),
            pltpu.VMEM((count - 1,) + vector, F32),
            pltpu.VMEM((7,) + vector, F32),
            pltpu.VMEM(vector, F32),
            pltpu.VMEM((7,) + vector, F32),
            pltpu.VMEM((1, width), F32),
            pltpu.SemaphoreType.DMA((moves,)),
            pltpu.SemaphoreType.DMA((moves,)),
            pltpu.SemaphoreType.DMA((count + 5,)),
            pltpu.SemaphoreType.REGULAR,
        ],
        compiler_params=pltpu.CompilerParams(
            collective_id=1, has_side_effects=True, vmem_limit_bytes=LIMIT
        ),
        cost_estimate=pl.CostEstimate(
            flops=2 * grads.shape[0] * width * 5 * cols, bytes_accessed=40 << 20, transcendentals=0
        ),
    )(
        grads, weights, turned, tokens, resid_grad, gain[None, :], ffn_terms, group_terms
    )


def dot_nt(left, right):
    return lax.dot_general(left, right, (((1,), (1,)), ((), ())), preferred_element_type=F32)


def dot_tn(left, right):
    return lax.dot_general(left, right, (((0,), (0,)), ((), ())), preferred_element_type=F32)


def dot_nn(left, right):
    return jnp.dot(left, right, preferred_element_type=F32)


def tile_decay(docs_col, docs_row, log_decay, first, tile, top):
    size = tile + top
    shape = (top, size)
    lag = (
        lax.broadcasted_iota(jnp.int32, shape, 0)
        + tile
        - lax.broadcasted_iota(jnp.int32, shape, 1)
    )
    same = docs_col[pl.ds(first + tile, top), :] == docs_row[pl.ds(0, 1), pl.ds(first, size)]
    power = jnp.exp(jnp.maximum(lag, 0).astype(F32) * log_decay)
    return jnp.where(same & (lag >= 0), power, 0.0)


def retain_kernel(
    lengths_ref,
    order_ref,
    gain_ref,
    qk_ref,
    v_ref,
    wu_ref,
    wd_ref,
    gate_hbm,
    tok_hbm,
    cot_hbm,
    wo_ref,
    resid_out,
    inverse_out,
    unit_hbm,
    states_hbm,
    cot_out,
    turned_hbm,
    up_full,
    down_full,
    gate_ref,
    tok_ref,
    cot_ref,
    cot_rows,
    unit_out,
    states_out,
    cot_pair,
    mixed_turned,
    mixed_out,
    out_weights,
    retained,
    terms,
    folded,
    gathered,
    held,
    ring_out,
    ring_in,
    docs_col,
    docs_row,
    scale_ref,
    send,
    recv,
    own_sem,
):
    near = peers()
    tok = lax.axis_index("tok")
    z = lax.axis_index("head")
    count = lax.axis_size("head")
    rows, width = tok_hbm.shape
    group_rows = rows * count
    part = width // 8
    heads = v_ref.shape[1] // VAL
    blocks = group_rows // SPAN
    slice_ = wu_ref.shape[1]
    own = [
        pltpu.make_async_copy(
            wu_ref, up_full.at[pl.ds(0, part), pl.ds(0, slice_)], own_sem.at[0]
        ),
        pltpu.make_async_copy(
            wd_ref, down_full.at[pl.ds(0, slice_), pl.ds(0, part)], own_sem.at[1]
        ),
        pltpu.make_async_copy(wo_ref, out_weights, own_sem.at[2]),
        pltpu.make_async_copy(gate_hbm, gate_ref, own_sem.at[3]),
        pltpu.make_async_copy(tok_hbm, tok_ref, own_sem.at[4]),
        pltpu.make_async_copy(cot_hbm, cot_ref, own_sem.at[5]),
    ]
    keeps = [
        pltpu.make_async_copy(unit_out, unit_hbm, own_sem.at[7]),
        pltpu.make_async_copy(states_out, states_hbm, own_sem.at[8]),
        pltpu.make_async_copy(mixed_turned, turned_hbm, own_sem.at[9]),
        pltpu.make_async_copy(cot_pair, cot_out, own_sem.at[10]),
    ]
    for copy in own:
        copy.start()
    greet(*everyone())
    moves = Moves(send, recv)
    far_up = moves.go(
        wu_ref, up_full.at[pl.ds(0, part), pl.ds(slice_, slice_)], near["cross"]
    )
    far_down = moves.go(
        wd_ref, down_full.at[pl.ds(slice_, slice_), pl.ds(0, part)], near["cross"]
    )

    def block_rows(b):
        return pl.ds(pl.multiple_of(b * SPAN, SPAN), SPAN)

    rate = decays(order_ref, heads)
    across = block_scales(lengths_ref, rate, group_rows, scale_ref, docs_col)
    docs_row[...] = row_docs(lengths_ref, group_rows)
    fold = group_weights(lengths_ref, rate, group_rows, False)

    def q_cols(h):
        return pl.ds(h * KEY, KEY)

    def k_cols(h):
        return pl.ds((heads + h) * KEY, KEY)

    def v_cols(h):
        return pl.ds(h * VAL, VAL)

    def up_view(s):
        def view(r, side=None):
            if r == 0 and s == 0:
                return wu_ref
            if side is None:
                return up_full.at[pl.ds(r * part, part), pl.ds(s * slice_, slice_)]
            size = part // 2
            return up_full.at[
                pl.ds(r * part + side * size, size), pl.ds(s * slice_, slice_)
            ]

        return view

    def down_view(s):
        def view(r, side=None):
            if r == 0 and s == 0:
                return wd_ref
            if side is None:
                return down_full.at[pl.ds(s * slice_, slice_), pl.ds(r * part, part)]
            size = slice_ // 2
            return down_full.at[
                pl.ds(s * slice_ + side * size, size), pl.ds(r * part, part)
            ]

        return view

    wide = [
        Gather(moves, near, view) for view in (up_view(0), down_view(0), up_view(1), down_view(1))
    ]

    states = [Gather(moves, near, state_view(gathered, h)) for h in range(heads)]
    for h in range(heads):
        total = jnp.zeros((KEY, VAL), F32)
        for b in range(blocks):
            weighed = v_ref[block_rows(b), v_cols(h)].astype(F32) * scale_ref[
                block_rows(b), heads + h : heads + h + 1
            ]
            term = dot_tn(qk_ref[block_rows(b), k_cols(h)], weighed.astype(BF))
            terms[b, pl.ds(h * KEY, KEY), :] = term
            total = across[h][b] * total + term
        gathered[0, pl.ds(h * KEY, KEY), :] = total.astype(BF)
        states[h].first()
    wide[0].first()
    own[5].wait()
    cot_move = moves.go(cot_ref, cot_rows, near["pair"])

    def intra(h):
        @pl.loop(0, blocks)
        def _(b):
            first = pl.multiple_of(b * SPAN, SPAN)
            for tile in range(0, SPAN, 128):
                at = pl.ds(first + tile, 128)
                seen = pl.ds(first, tile + 128)
                scores = dot_nt(qk_ref[at, q_cols(h)], qk_ref[seen, k_cols(h)])
                mask = tile_decay(docs_col, docs_row, rate[h], first, tile, 128)
                probs = (scores * mask).astype(BF)
                retained[at, v_cols(h)] = dot_nn(probs, v_ref[seen, v_cols(h)])

    def finish_head(h):
        first = jnp.zeros((KEY, VAL), F32)
        for r in range(8):
            first = first + fold[h][r] * gathered[r, pl.ds(h * KEY, KEY), :].astype(F32)
        for b in range(blocks):
            folded[b] = first.astype(BF)
            states_out[pl.ds((h * blocks + b) * KEY, KEY), :] = first.astype(BF)
            first = across[h][b] * first + terms[b, pl.ds(h * KEY, KEY), :]

        @pl.loop(0, group_rows // 128)
        def _(i):
            at = pl.ds(pl.multiple_of(i * 128, 128), 128)
            b = lax.div(i, SPAN // 128)
            cross = dot_nn(qk_ref[at, q_cols(h)], folded[b])
            values = retained[at, v_cols(h)] + scale_ref[at, h : h + 1] * cross
            mean = jnp.mean(values, axis=-1, keepdims=True)
            centred = values - mean
            inverse = lax.rsqrt(jnp.mean(centred * centred, axis=-1, keepdims=True) + EPS)
            unit = centred * inverse
            gate = gate_ref[at, v_cols(h)].astype(F32)
            swish = gate / (1.0 + jnp.exp(-gate))
            unit_out[at, v_cols(h)] = unit.astype(BF)
            inverse_out[at, h : h + 1] = inverse
            mixed = (swish * unit * gain_ref[:, h * VAL : (h + 1) * VAL]).astype(BF)
            mixed_out[at, v_cols(h)] = mixed
            mixed_turned[v_cols(h), at] = mixed.T

    for h in range(heads):
        intra(h)
        states[h].second()
    wide[1].first()
    for h in range(heads):
        states[h].third()
    wide[0].second()
    own[3].wait()
    for h in range(heads):
        states[h].done()
        finish_head(h)
    for keep in keeps[:3]:
        keep.start()

    def ring_term(step, side):
        owner = lax.rem(z + 2 * count - 1 - step, count)
        at = pl.ds(pl.multiple_of(owner * rows, rows), rows)

        @pl.loop(side * (width // 512), (side + 1) * (width // 512))
        def _(i):
            to = pl.ds(pl.multiple_of(i * 256, 256), 256)
            held[:, to] = dot_nn(mixed_out[at, :], out_weights[:, to])

    ring = {}
    half = width // 2

    def ring_send(step, side):
        at = pl.ds(side * half, half)
        value = held[:, at]
        if step:
            ring[step - 1, side].wait_recv()
            value = value + ring_in[step - 1, :, at].astype(F32)
        ring_out[step, :, at] = value.astype(BF)
        ring[step, side] = moves.go(
            ring_out.at[step, :, at], ring_in.at[step, :, at], near["up"]
        )

    own[2].wait()
    for side in range(2):
        ring_term(0, side)
        ring_send(0, side)
    wide[1].second()
    ring_term(1, 0)
    ring_term(1, 1)
    far_up.wait_recv()
    wide[2].first()
    wide[0].third()
    ring_send(1, 0)
    far_down.wait_recv()
    wide[3].first()
    wide[1].third()
    ring_send(1, 1)
    ring_term(2, 0)
    ring_term(2, 1)
    wide[2].second()
    ring_send(2, 0)
    wide[3].second()
    ring_send(2, 1)
    ring_term(3, 0)
    ring_term(3, 1)
    wide[2].third()
    wide[3].third()
    own[4].wait()
    cot_move.wait_recv()
    for ref, first in ((cot_ref, 0), (cot_rows, rows)):
        for r, place in enumerate(xor_places(tok)):
            cot_pair[pl.ds(first, rows), pl.ds(r * part, part)] = ref[
                :, pl.ds(pl.multiple_of(place * part, part), part)
            ]
    keeps[3].start()
    for side in range(2):
        ring[2, side].wait_recv()
        for n in range(4):
            r = side * 4 + n
            place = xor_places(tok)[r]
            at = pl.ds(r * part, part)
            values = tok_ref[:, pl.ds(pl.multiple_of(place * part, part), part)].astype(F32)
            resid_out[:, at] = values + held[:, at] + ring_in[2, :, at].astype(F32)
    for gather in wide:
        gather.done()
    own[0].wait()
    own[1].wait()
    for keep in keeps:
        keep.wait()
    moves.finish()


def retain(
    doc_lengths, head_order, gain, qk, v, gate, tokens, out_full, cotangent, w_up, w_down
):
    rows, width = tokens.shape
    count = lax.axis_size("head")
    group_rows = rows * count
    heads = v.shape[1] // VAL
    blocks = group_rows // SPAN
    wide = 2 * w_up.shape[1]
    moves = 3 + (4 + heads) * 8 + 6
    struct = jax.ShapeDtypeStruct
    kept = (
        struct(v.shape, BF),
        struct((heads * blocks * KEY, VAL), BF),
        struct((2 * rows, width), BF),
        struct((heads * VAL, group_rows), BF),
    )
    return pl.pallas_call(
        retain_kernel,
        out_shape=(
            struct((rows, width), F32),
            struct((group_rows, heads), F32),
            *kept,
            struct((width, wide), BF),
            struct((wide, width), BF),
        ),
        in_specs=[SMEM] * 2 + [VMEM] * 5 + [ANY] * 4,
        out_specs=[VMEM] * 2 + [ANY] * 6,
        scratch_shapes=[
            pltpu.VMEM(gate.shape, BF),
            *[pltpu.VMEM(tokens.shape, BF)] * 3,
            *[pltpu.VMEM(array.shape, BF) for array in kept],
            pltpu.VMEM(v.shape, BF),
            pltpu.VMEM(out_full.shape, BF),
            pltpu.VMEM((group_rows, heads * VAL), F32),
            pltpu.VMEM((blocks, heads * KEY, VAL), F32),
            pltpu.VMEM((blocks, KEY, VAL), BF),
            pltpu.VMEM((8, heads * KEY, VAL), BF),
            pltpu.VMEM((rows, width), F32),
            pltpu.VMEM((3, rows, width), BF),
            pltpu.VMEM((3, rows, width), BF),
            pltpu.VMEM((group_rows, 1), jnp.int32),
            pltpu.VMEM((8, group_rows), jnp.int32),
            pltpu.VMEM((group_rows, 2 * heads), F32),
            pltpu.SemaphoreType.DMA((moves,)),
            pltpu.SemaphoreType.DMA((moves,)),
            pltpu.SemaphoreType.DMA((11,)),
        ],
        compiler_params=pltpu.CompilerParams(
            collective_id=2, has_side_effects=True, vmem_limit_bytes=LIMIT
        ),
        cost_estimate=pl.CostEstimate(
            flops=12 << 30, bytes_accessed=40 << 20, transcendentals=0
        ),
    )(
        doc_lengths, head_order, gain[None, :], qk, v, w_up, w_down, gate, tokens, cotangent,
        out_full,
    )


def feed_kernel(
    resid_ref,
    gain_ref,
    cot_ref,
    up_ref,
    down_ref,
    layer_out,
    far_out,
    resid_grad,
    gain_out,
    up_own,
    up_far,
    down_own,
    down_far,
    branch,
    up,
    down,
    lifted,
    cot,
    hidden,
    turned,
    pre,
    back_out,
    back_in,
    odd_out_d,
    odd_in_d,
    odd_out_u,
    odd_in_u,
    far_out_d,
    far_in_d,
    far_out_u,
    far_in_u,
    near_out_d,
    near_in_d,
    near_out_u,
    near_in_u,
    up_sum,
    down_sum,
    gain,
    send,
    recv,
    load_sem,
    free_sem,
):
    near = peers()
    gain[...] = arranged(gain_ref, lax.axis_index("tok"))
    z = lax.axis_index("head")
    count = lax.axis_size("head")
    rows, width = resid_ref.shape
    part = width // 8
    side_rows = rows // 2
    wide = up.shape[1]
    slice_ = wide // 2
    loads = [
        pltpu.make_async_copy(cot_ref, cot, load_sem.at[0]),
        pltpu.make_async_copy(up_ref, up, load_sem.at[1]),
        pltpu.make_async_copy(down_ref, down, load_sem.at[2]),
    ]
    for load in loads:
        load.start()
    greet(*everyone())
    moves = Moves(send, recv)
    size = 16

    pairs = []
    for side in range(2):

        @pl.loop(0, side_rows // size)
        def _(i):
            at = pl.ds(pl.multiple_of(side * side_rows + i * size, size), size)
            values = resid_ref[at, :]
            mean = jnp.mean(values, axis=-1, keepdims=True)
            centred = values - mean
            inverse = lax.rsqrt(jnp.mean(centred * centred, axis=-1, keepdims=True) + EPS)
            lifted[at, :] = (centred * inverse * gain[...]).astype(BF)

        pairs.append(
            moves.go(
                lifted.at[pl.ds(side * side_rows, side_rows), :],
                lifted.at[pl.ds(rows + side * side_rows, side_rows), :],
                near["pair"],
            )
        )

    def feed(first, number):
        @pl.loop(0, wide // 256)
        def _(i):
            to = pl.ds(pl.multiple_of(i * 256, 256), 256)
            at = pl.ds(first, number)
            hidden_pre = dot_nn(lifted[at, :], up[:, to])
            hidden_grad = dot_nt(cot[at, :], down[to, :])
            phi = 0.5 * (1.0 + lax.erf(hidden_pre * SQRT_HALF))
            made = (hidden_pre * phi).astype(BF)
            hidden[at, to] = made
            turned[to, at] = made.T
            slope = phi + hidden_pre * jnp.exp(-0.5 * hidden_pre * hidden_pre) * INV_ROOT_TWO_PI
            pre[at, to] = (hidden_grad * slope).astype(BF)

    for load in loads:
        load.wait()
    feed(0, rows)
    backs = []
    for side in range(2):
        if side:

            @pl.loop(0, width // 256)
            def _(i):
                to = pl.ds(pl.multiple_of(i * 256, 256), 256)
                resid_grad[:, to] = dot_nt(pre[pl.ds(0, rows), :], up[to, :])

        pairs[side].wait_recv()
        feed(rows + side * side_rows, side_rows)

        @pl.loop(0, width // 256)
        def _(i):
            to = pl.ds(pl.multiple_of(i * 256, 256), 256)
            found = dot_nt(pre[pl.ds(rows + side * side_rows, side_rows), :], up[to, :])
            back_out[pl.ds(side * side_rows, side_rows), to] = found.astype(BF)

        at = pl.ds(side * side_rows, side_rows)
        backs.append(moves.go(back_out.at[at, :], back_in.at[at, :], near["pair"]))

    def down_term(s):
        def term(r):
            return dot_nn(turned[pl.ds(s * slice_, slice_), :], cot[:, r * part : (r + 1) * part])

        return term

    def up_term(s):
        def term(r):
            return dot_tn(
                lifted[:, r * part : (r + 1) * part], pre[:, s * slice_ : (s + 1) * slice_]
            )

        return term

    down_sets = [
        (odd_out_d, odd_in_d, far_out_d, far_in_d.at[s], near_out_d, near_in_d.at[s])
        for s in range(2)
    ]
    up_sets = [
        (odd_out_u, odd_in_u, far_out_u, far_in_u.at[s], near_out_u, near_in_u.at[s])
        for s in range(2)
    ]
    sums = [
        Scatter(moves, near, down_term(0), down_sets[0], down_own),
        Scatter(moves, near, up_term(0), up_sets[0], up_own),
    ]
    sums += [
        Scatter(moves, near, down_term(1), down_sets[1], down_sum, sums[0], free_sem.at[0]),
        Scatter(moves, near, up_term(1), up_sets[1], up_sum, sums[1], free_sem.at[1]),
    ]
    sums[0].frees = free_sem.at[0]
    sums[1].frees = free_sem.at[1]

    ring = {}

    def shard(step, side):
        owner = lax.rem(z - step + count, count)
        first = pl.multiple_of(owner * rows + side * side_rows, side_rows)
        return branch.at[pl.ds(first, side_rows), :]

    def pass_on(step, side):
        if step:
            ring[step - 1, side].wait_recv()
        if step < count - 1:
            here = back_in.at[pl.ds(side * side_rows, side_rows), :] if step == 0 else shard(step, side)
            ring[step, side] = moves.go(here, shard(step, side), near["up"])

    def norm_back(side):
        backs[side].wait_recv()

        def block(i, total):
            at = pl.ds(pl.multiple_of(side * side_rows + i * size, size), size)
            values = resid_ref[at, :]
            mean = jnp.mean(values, axis=-1, keepdims=True)
            centred = values - mean
            inverse = lax.rsqrt(jnp.mean(centred * centred, axis=-1, keepdims=True) + EPS)
            unit = centred * inverse
            grad = resid_grad[at, :] + back_in[at, :].astype(F32)
            scaled = grad * gain[...]
            first = jnp.mean(scaled, axis=-1, keepdims=True)
            second = jnp.mean(scaled * unit, axis=-1, keepdims=True)
            found = cot[at, :].astype(F32) + inverse * (scaled - first - unit * second)
            resid_grad[at, :] = found
            back_in[at, :] = found.astype(BF)
            return total + jnp.sum(grad * unit, axis=0, keepdims=True)

        total = lax.fori_loop(0, side_rows // size, block, jnp.zeros((1, width), F32))
        gain_out[pl.ds(side, 1), :] = total

    norm_back(0)
    pass_on(0, 0)
    for i in (3, 1, 2, 0):
        sums[0].odd(i)
    for i in (3, 1):
        sums[1].odd(i)
    norm_back(1)
    pass_on(0, 1)
    mine = pltpu.make_async_copy(
        back_in, branch.at[pl.ds(pl.multiple_of(z * rows, rows), rows), :], load_sem.at[3]
    )
    mine.start()
    sums[0].far()
    for i in (2, 0):
        sums[1].odd(i)
    pass_on(1, 0)
    sums[1].far()
    sums[0].close()
    pass_on(1, 1)
    for i in (3, 1, 2, 0):
        sums[2].odd(i)
    sums[1].close()
    sums[2].far()
    pass_on(2, 0)

    @pl.loop(0, width // 256)
    def _(i):
        to = pl.ds(pl.multiple_of(i * 256, 256), 256)
        layer_out[:, to] = resid_ref[:, to] + dot_nn(hidden[pl.ds(0, rows), :], down[:, to])

    for i in (3, 1, 2, 0):
        sums[3].odd(i)
    pass_on(2, 1)
    sums[2].close()
    sums[3].far()
    sums[0].done()
    sums[1].done()

    @pl.loop(0, width // 256)
    def _(i):
        to = pl.ds(pl.multiple_of(i * 256, 256), 256)
        far_out[:, to] = dot_nn(hidden[pl.ds(rows, rows), :], down[:, to]).astype(BF)

    sums[3].close()
    pass_on(3, 0)
    sums[2].done()
    down_far[...] = down_sum[...].astype(BF)
    sums[3].done()
    up_far[...] = up_sum[...].astype(BF)
    pass_on(3, 1)
    mine.wait()
    moves.finish()


def feed_forward(resid, gain, cot_pair, up_full, down_full):
    rows, width = resid.shape
    count = lax.axis_size("head")
    part = width // 8
    wide = up_full.shape[1]
    slice_ = wide // 2
    moves = 4 + 4 * 8 + 6
    struct = jax.ShapeDtypeStruct
    down_piece = (slice_, part)
    up_piece = (part, slice_)

    def sets(piece):
        half = (piece[0] // 2, piece[1])
        return [
            pltpu.VMEM(piece, BF),
            pltpu.VMEM((2, 2) + half, BF),
        ]

    def nears(piece):
        return [pltpu.VMEM((2,) + piece, BF), pltpu.VMEM((2, 2) + piece, BF)]

    def odds(piece):
        return [pltpu.VMEM((4,) + piece, BF)] * 2

    return pl.pallas_call(
        feed_kernel,
        out_shape=(
            struct((rows, width), F32),
            struct((rows, width), BF),
            struct((rows, width), F32),
            struct((8, width), F32),
            struct(up_piece, F32),
            struct(up_piece, BF),
            struct(down_piece, F32),
            struct(down_piece, BF),
            struct((count * rows, width), BF),
        ),
        in_specs=[VMEM] * 2 + [ANY] * 3,
        out_specs=[VMEM] * 8 + [ANY],
        scratch_shapes=[
            pltpu.VMEM((width, wide), BF),
            pltpu.VMEM((wide, width), BF),
            pltpu.VMEM((2 * rows, width), BF),
            pltpu.VMEM((2 * rows, width), BF),
            pltpu.VMEM((2 * rows, wide), BF),
            pltpu.VMEM((wide, 2 * rows), BF),
            pltpu.VMEM((2 * rows, wide), BF),
            pltpu.VMEM((rows, width), BF),
            pltpu.VMEM((rows, width), BF),
            *odds(down_piece),
            *odds(up_piece),
            *sets(down_piece),
            *sets(up_piece),
            *nears(down_piece),
            *nears(up_piece),
            pltpu.VMEM(up_piece, F32),
            pltpu.VMEM(down_piece, F32),
            pltpu.VMEM((1, width), F32),
            pltpu.SemaphoreType.DMA((moves,)),
            pltpu.SemaphoreType.DMA((moves,)),
            pltpu.SemaphoreType.DMA((4,)),
            pltpu.SemaphoreType.REGULAR((2,)),
        ],
        compiler_params=pltpu.CompilerParams(
            collective_id=3, has_side_effects=True, vmem_limit_bytes=LIMIT
        ),
        cost_estimate=pl.CostEstimate(
            flops=26 << 30, bytes_accessed=40 << 20, transcendentals=0
        ),
    )(resid, gain[None, :], cot_pair, up_full, down_full)


def recall_kernel(
    lengths_ref,
    order_ref,
    gain_ref,
    wo_hbm,
    branch_hbm,
    gate_hbm,
    unit_hbm,
    inverse_hbm,
    qk_hbm,
    v_hbm,
    turned_hbm,
    states_hbm,
    cos_hbm,
    sin_hbm,
    own_hbm,
    far_ref,
    up_ref,
    down_ref,
    wo_grad,
    gains,
    layer_out,
    grads_out,
    up_in,
    down_in,
    out_weights,
    branch,
    gate_ref,
    unit_ref,
    inverse_ref,
    qk_ref,
    v_ref,
    turned_ref,
    states_ref,
    cos_ref,
    sin_ref,
    own_ref,
    far_in,
    grads,
    docs_col,
    docs_row,
    scale_ref,
    back,
    terms,
    gathered,
    folded,
    dqk,
    dv,
    odd_out,
    odd_in,
    out_far,
    in_far,
    out_near,
    in_near,
    send,
    recv,
    load_sem,
    keep_sem,
):
    near = peers()
    tok = lax.axis_index("tok")
    group_rows, cols = v_ref.shape
    heads = cols // VAL
    blocks = group_rows // SPAN
    width = branch.shape[1]
    part = width // 8
    loads = [
        pltpu.make_async_copy(source, target, load_sem.at[n])
        for n, (source, target) in enumerate(
            (
                (wo_hbm, out_weights),
                (branch_hbm, branch),
                (gate_hbm, gate_ref),
                (unit_hbm, unit_ref),
                (inverse_hbm, inverse_ref),
                (qk_hbm, qk_ref),
                (v_hbm, v_ref),
                (turned_hbm, turned_ref),
                (states_hbm, states_ref),
                (cos_hbm, cos_ref),
                (sin_hbm, sin_ref),
                (own_hbm, own_ref),
            )
        )
    ]
    for load in loads:
        load.start()
    greet(*everyone())
    moves = Moves(send, recv)
    swaps = [
        moves.go(far_ref, far_in, near["pair"]),
        moves.go(up_ref, up_in, near["cross"]),
        moves.go(down_ref, down_in, near["cross"]),
    ]

    def block_rows(b):
        return pl.ds(pl.multiple_of(b * SPAN, SPAN), SPAN)

    def q_cols(h):
        return pl.ds(h * KEY, KEY)

    def k_cols(h):
        return pl.ds((heads + h) * KEY, KEY)

    def v_cols(h):
        return pl.ds(h * VAL, VAL)

    rate = decays(order_ref, heads)
    across = block_scales(lengths_ref, rate, group_rows, scale_ref, docs_col)
    docs_row[...] = row_docs(lengths_ref, group_rows)
    fold = group_weights(lengths_ref, rate, group_rows, True)
    for load in loads[:5]:
        load.wait()

    first_gate = 2 * heads * KEY + cols
    states = [Gather(moves, near, state_view(gathered, h)) for h in range(heads)]
    gains[...] = jnp.zeros_like(gains)
    kept = [
        pltpu.make_async_copy(
            grads.at[:, pl.ds(first_gate, cols)],
            grads_out.at[:, pl.ds(first_gate, cols)],
            keep_sem.at[0],
        ),
        pltpu.make_async_copy(
            grads.at[:, pl.ds(0, first_gate)], grads_out.at[:, pl.ds(0, first_gate)], keep_sem.at[1]
        ),
    ]
    for h in range(heads):
        gain = gain_ref[:, h * VAL : (h + 1) * VAL]

        def tile_back(i, total):
            at = pl.ds(pl.multiple_of(i * 128, 128), 128)
            grad = dot_nt(branch[at, :], out_weights[v_cols(h), :]).astype(BF).astype(F32)
            gate = gate_ref[at, v_cols(h)].astype(F32)
            sigma = 1.0 / (1.0 + jnp.exp(-gate))
            swish = gate * sigma
            unit = unit_ref[at, v_cols(h)].astype(F32)
            grads[at, pl.ds(first_gate + h * VAL, VAL)] = (
                grad * unit * gain * (sigma + swish * (1.0 - sigma))
            ).astype(BF)
            inner = grad * swish
            scaled = inner * gain
            first = jnp.mean(scaled, axis=-1, keepdims=True)
            second = jnp.mean(scaled * unit, axis=-1, keepdims=True)
            back[at, v_cols(h)] = (
                inverse_ref[at, h : h + 1] * (scaled - first - unit * second)
            ).astype(BF)
            return total + jnp.sum(inner * unit, axis=0, keepdims=True)

        gains[pl.ds(0, 1), v_cols(h)] = lax.fori_loop(
            0, group_rows // 128, tile_back, jnp.zeros((1, VAL), F32)
        )
        if h == 0:
            for load in loads[5:]:
                load.wait()
        total = jnp.zeros((KEY, VAL), F32)
        for b in reversed(range(blocks)):
            weighed = back[block_rows(b), v_cols(h)].astype(F32) * scale_ref[
                block_rows(b), h : h + 1
            ]
            term = dot_tn(qk_ref[block_rows(b), q_cols(h)], weighed.astype(BF))
            terms[b, pl.ds(h * KEY, KEY), :] = term
            total = across[h][b] * total + term
        gathered[0, pl.ds(h * KEY, KEY), :] = total.astype(BF)
        states[h].first()
    kept[0].start()

    def out_term(r):
        return dot_nn(turned_ref[...], branch[:, r * part : (r + 1) * part])

    outward = Scatter(
        moves, near, out_term, (odd_out, odd_in, out_far, in_far, out_near, in_near), wo_grad
    )

    def intra(h):
        @pl.loop(0, blocks)
        def _(b):
            first = pl.multiple_of(b * SPAN, SPAN)
            for tile in range(SPAN - 128, -1, -128):
                at = pl.ds(first + tile, 128)
                seen = pl.ds(first, tile + 128)
                mask = tile_decay(docs_col, docs_row, rate[h], first, tile, 128)
                query = qk_ref[at, q_cols(h)]
                key = qk_ref[seen, k_cols(h)]
                ret = back[at, v_cols(h)]
                probs = (dot_nt(query, key) * mask).astype(BF)
                score = (dot_nt(ret, v_ref[seen, v_cols(h)]) * mask).astype(BF)
                dqk[at, q_cols(h)] = dot_nn(score, key)
                to_keys = dot_tn(score, query)
                to_values = dot_tn(probs, ret)
                if tile == SPAN - 128:
                    dqk[seen, k_cols(h)] = to_keys
                    dv[seen, v_cols(h)] = to_values
                else:
                    dqk[seen, k_cols(h)] += to_keys
                    dv[seen, v_cols(h)] += to_values

    def finish_head(h):
        later = jnp.zeros((KEY, VAL), F32)
        for r in range(8):
            later = later + fold[h][r] * gathered[r, pl.ds(h * KEY, KEY), :].astype(F32)
        for b in reversed(range(blocks)):
            folded[b] = later.astype(BF)
            later = across[h][b] * later + terms[b, pl.ds(h * KEY, KEY), :]

        @pl.loop(0, group_rows // 128)
        def _(i):
            at = pl.ds(pl.multiple_of(i * 128, 128), 128)
            b = lax.div(i, SPAN // 128)
            reach = scale_ref[at, h : h + 1]
            leave = scale_ref[at, heads + h : heads + h + 1]
            state = states_ref[pl.ds(pl.multiple_of((h * blocks + b) * KEY, KEY), KEY), :]
            cosine, sine = cos_ref[at, :], sin_ref[at, :]
            for found, to in (
                (
                    dqk[at, q_cols(h)] + reach * dot_nt(back[at, v_cols(h)], state),
                    q_cols(h),
                ),
                (
                    dqk[at, k_cols(h)] + leave * dot_nt(v_ref[at, v_cols(h)], folded[b]),
                    k_cols(h),
                ),
            ):
                one, two = found[:, : KEY // 2], found[:, KEY // 2 :]
                grads[at, to] = jnp.concatenate(
                    [one * cosine + two * sine, two * cosine - one * sine], axis=1
                ).astype(BF)
            found = dv[at, v_cols(h)] + leave * dot_nn(qk_ref[at, k_cols(h)], folded[b])
            grads[at, pl.ds(2 * heads * KEY + h * VAL, VAL)] = found.astype(BF)

    intra(0)
    states[0].second()
    for i in (3, 1, 2, 0):
        outward.odd(i)
    for h in range(1, heads):
        states[h].second()
        intra(h)
    outward.far()
    states[0].third()
    for h in range(1, heads):
        states[h].third()
    states[0].done()
    finish_head(0)
    outward.close()
    for h in range(1, heads):
        states[h].done()
        finish_head(h)
    kept[1].start()
    swaps[0].wait_recv()
    for r, place in enumerate(xor_places(tok)):
        at = pl.ds(r * part, part)
        layer_out[:, pl.ds(pl.multiple_of(place * part, part), part)] = (
            own_ref[:, at] + far_in[:, at].astype(F32)
        ).astype(BF)
    outward.done()
    for swap_ in swaps[1:]:
        swap_.wait_recv()
    for copy in kept:
        copy.wait()
    moves.finish()


def recall(
    doc_lengths, head_order, gain, qk, v, gate, unit, inverse, states, cosine, sine, mixed_turned,
    branch, out_full, layer_own, far_out, up_far, down_far,
):
    group_rows, cols = v.shape
    heads = cols // VAL
    blocks = group_rows // SPAN
    width = branch.shape[1]
    part = width // 8
    piece = (cols, part)
    moves = 3 + 8 + 8 * heads
    struct = jax.ShapeDtypeStruct
    loaded = (
        out_full, branch, gate, unit, inverse, qk, v, mixed_turned, states, cosine, sine, layer_own
    )
    return pl.pallas_call(
        recall_kernel,
        out_shape=(
            struct(piece, F32),
            struct((8, cols), F32),
            struct(far_out.shape, BF),
            struct((group_rows, 3 * cols), BF),
            struct(up_far.shape, BF),
            struct(down_far.shape, BF),
        ),
        in_specs=[SMEM] * 2 + [VMEM] + [ANY] * 15,
        out_specs=[VMEM] * 3 + [ANY] * 3,
        scratch_shapes=[
            *[pltpu.VMEM(array.shape, array.dtype) for array in loaded],
            pltpu.VMEM(far_out.shape, BF),
            pltpu.VMEM((group_rows, 3 * cols), BF),
            pltpu.VMEM((group_rows, 1), jnp.int32),
            pltpu.VMEM((8, group_rows), jnp.int32),
            pltpu.VMEM((group_rows, 2 * heads), F32),
            pltpu.VMEM(v.shape, BF),
            pltpu.VMEM((blocks, heads * KEY, VAL), F32),
            pltpu.VMEM((8, heads * KEY, VAL), BF),
            pltpu.VMEM((blocks, KEY, VAL), BF),
            pltpu.VMEM((group_rows, 2 * heads * KEY), F32),
            pltpu.VMEM((group_rows, cols), F32),
            pltpu.VMEM((4,) + piece, BF),
            pltpu.VMEM((4,) + piece, BF),
            pltpu.VMEM(piece, BF),
            pltpu.VMEM((2, cols // 2, part), BF),
            pltpu.VMEM((2,) + piece, BF),
            pltpu.VMEM((2,) + piece, BF),
            pltpu.SemaphoreType.DMA((moves,)),
            pltpu.SemaphoreType.DMA((moves,)),
            pltpu.SemaphoreType.DMA((len(loaded),)),
            pltpu.SemaphoreType.DMA((2,)),
        ],
        compiler_params=pltpu.CompilerParams(
            collective_id=4, has_side_effects=True, vmem_limit_bytes=LIMIT
        ),
        cost_estimate=pl.CostEstimate(
            flops=20 << 30, bytes_accessed=40 << 20, transcendentals=0
        ),
    )(doc_lengths, head_order, gain[None, :], *loaded, far_out, up_far, down_far)


def norm_forward(values, gain):
    mean = jnp.mean(values, axis=-1, keepdims=True)
    centred = values - mean
    inverse = lax.rsqrt(jnp.mean(centred * centred, axis=-1, keepdims=True) + EPS)
    unit = centred * inverse
    return (unit * gain, unit, inverse)


def norm_backward(grad_out, unit, inverse, gain):
    scaled = grad_out * gain
    first = jnp.mean(scaled, axis=-1, keepdims=True)
    second = jnp.mean(scaled * unit, axis=-1, keepdims=True)
    return (inverse * (scaled - first - unit * second), jnp.sum(grad_out * unit, axis=0))


def doc_index(row_ids, starts):
    return jnp.sum((starts[None, :] <= row_ids[:, None]).astype(jnp.int32), axis=1) - 1


def doc_position(row_ids, starts):
    first = jnp.max(jnp.where(starts[None, :] <= row_ids[:, None], starts[None, :], 0), axis=1)
    return row_ids - first


def angles(position, half):
    freq = jnp.exp(-jnp.log(10000.0) * jnp.arange(half, dtype=F32) / half)
    turn = position.astype(F32)[:, None] * freq[None, :]
    return (jnp.cos(turn), jnp.sin(turn))


def rotate(values, cosine, sine):
    half = values.shape[-1] // 2
    first, second = (values[..., :half], values[..., half:])
    return jnp.concatenate(
        [first * cosine - second * sine, first * sine + second * cosine], axis=-1
    )


def unrotate(grads, cosine, sine):
    return rotate(grads, cosine, -sine)


def span_masks(doc_ids, before, log_decay):
    size = doc_ids.shape[0]
    place = jnp.arange(size, dtype=F32)
    lag = place[:, None] - place[None, :]
    same = (doc_ids[:, None] == doc_ids[None, :]) & (lag >= 0)
    decay = jnp.where(same, jnp.exp(jnp.maximum(lag, 0.0) * log_decay), 0.0)
    reach = jnp.where(doc_ids == before, jnp.exp((place + 1.0) * log_decay), 0.0)[:, None]
    leave = jnp.where(doc_ids == doc_ids[-1], jnp.exp((size - 1.0 - place) * log_decay), 0.0)[
        :, None
    ]
    across = jnp.where(doc_ids[-1] == before, jnp.exp(size * log_decay), 0.0)
    return (decay, reach, leave, across)


def gelu_slope(hidden_pre):
    return (
        0.5 * (1.0 + lax.erf(hidden_pre * SQRT_HALF))
        + hidden_pre * jnp.exp(-0.5 * hidden_pre * hidden_pre) * INV_ROOT_TWO_PI
    )


def plain(
    tokens,
    cotangent,
    doc_lengths,
    head_order,
    norm_gain,
    w_query,
    w_key,
    w_value,
    w_gate,
    group_gain,
    w_out,
    ffn_gain,
    w_up,
    w_down,
):
    heads = w_query.shape[1] // KEY
    head_count = lax.axis_size("head")
    tok_count = lax.axis_size("tok")
    z = lax.axis_index("head")
    tok = lax.axis_index("tok")
    rows = tokens.shape[0]
    group_rows = rows * head_count
    blocks = group_rows // SPAN
    width = tokens.shape[1]
    part = width // tok_count

    tokens_f = reorder(tokens).astype(F32)
    cot_own = reorder(cotangent)
    gain1 = reorder(norm_gain)
    gain2 = reorder(ffn_gain)
    normed1, unit1, inverse1 = norm_forward(tokens_f, gain1)
    qk = w_query.shape[1]
    vg = w_value.shape[1]
    up_two = jnp.concatenate([w_up, swap(w_up, "head", 2)], axis=1)
    down_two = jnp.concatenate([w_down, swap(w_down, "head", 2)], axis=0)
    up_full = tok_gather(up_two, 0)
    down_full = tok_gather(down_two, 1)
    cot_pair = jnp.concatenate([cot_own, swap(cot_own, "head", 1)], axis=0)

    ends = jnp.cumsum(doc_lengths)
    starts = ends - doc_lengths
    first_row = tok * group_rows
    row_ids = first_row + jnp.arange(group_rows, dtype=jnp.int32)
    doc_ids = doc_index(row_ids, starts)
    previous = doc_index(jnp.reshape(first_row - 1, (1,)), starts)[0]
    group_last = doc_index((jnp.arange(tok_count, dtype=jnp.int32) + 1) * group_rows - 1, starts)
    cosine, sine = angles(doc_position(row_ids, starts), KEY // 2)
    ranks = lax.dynamic_slice_in_dim(head_order, z * heads, heads)
    log_decay = jnp.log1p(-jnp.exp2(-(5.0 + ranks.astype(F32))))

    group = head_gather(normed1.astype(BF))
    qkvg_full = tok_gather(jnp.concatenate([w_query, w_key, w_value, w_gate], axis=1), 0)
    out_full = tok_gather(w_out, 1)
    projected = mm(group, qkvg_full)
    qk_rows = jnp.concatenate(
        [
            rotate(projected[:, h * KEY : (h + 1) * KEY], cosine, sine).astype(BF)
            for h in range(2 * heads)
        ],
        axis=1,
    )
    v_rows = projected[:, 2 * qk : 2 * qk + vg].astype(BF)
    gate = projected[:, 2 * qk + vg :]

    def head_of(array, head, size):
        return array[:, head * size : (head + 1) * size]

    def block_of(array, block):
        return array[block * SPAN : (block + 1) * SPAN]

    q, k, v, masks = [], [], [], []
    for h in range(heads):
        q.append(head_of(qk_rows, h, KEY))
        k.append(head_of(qk_rows, heads + h, KEY))
        v.append(head_of(v_rows, h, VAL))
        masks.append(
            [
                span_masks(
                    block_of(doc_ids, b),
                    previous if b == 0 else doc_ids[b * SPAN - 1],
                    log_decay[h],
                )
                for b in range(blocks)
            ]
        )

    group_order = jnp.arange(tok_count, dtype=jnp.int32)

    def weigh(lag, last, h):
        return jnp.where(
            (lag >= 0) & (group_last == last),
            jnp.exp(jnp.maximum(lag, 0).astype(F32) * group_rows * log_decay[h]),
            0.0,
        )

    ends_of = []
    added = []
    for h in range(heads):
        state = jnp.zeros((KEY, VAL), F32)
        terms = []
        for b in range(blocks):
            term = mm_tn(block_of(k[h], b), (block_of(v[h], b) * masks[h][b][2]).astype(BF))
            terms.append(term)
            state = masks[h][b][3] * state + term
        added.append(terms)
        ends_of.append(state.astype(BF))
    all_states = lax.all_gather(jnp.concatenate(ends_of, axis=0), "tok", axis=0)
    lag = tok - 1 - group_order
    states = []
    retained = []
    for h in range(heads):
        weights = weigh(lag, previous, h)
        state = jnp.sum(
            all_states[:, h * KEY : (h + 1) * KEY].astype(F32) * weights[:, None, None], axis=0
        )
        mine = []
        outs = []
        for b in range(blocks):
            mine.append(state.astype(BF))
            qb, kb, vb = block_of(q[h], b), block_of(k[h], b), block_of(v[h], b)
            decay, reach, leave, across = masks[h][b]
            probs = (mm_nt(qb, kb) * decay).astype(BF)
            outs.append(mm(probs, vb) + reach * mm(qb, mine[-1]))
            state = across * state + added[h][b]
        states.append(mine)
        retained.append(jnp.concatenate(outs, axis=0))

    mixed_parts, unit_g, inverse_g, grouped, swish, sigma = [], [], [], [], [], []
    for h in range(heads):
        g, u, i = norm_forward(retained[h], head_of(group_gain[None, :], h, VAL))
        gate_h = head_of(gate, h, VAL)
        s = jax.nn.sigmoid(gate_h)
        unit_g.append(u)
        inverse_g.append(i)
        grouped.append(g)
        sigma.append(s)
        swish.append(gate_h * s)
        mixed_parts.append((swish[-1] * g).astype(BF))
    mixed = jnp.concatenate(mixed_parts, axis=1)

    out_sum = head_scatter(lambda i: mm(rows_of(mixed, i, rows), out_full))
    resid = tokens_f + out_sum
    normed2, unit2, inverse2 = norm_forward(resid, gain2)
    lifted2 = normed2.astype(BF)
    lifted2_pair = jnp.concatenate([lifted2, swap(lifted2, "head", 1)], axis=0)
    hidden_pre = mm(lifted2_pair, up_full)
    hidden = jax.nn.gelu(hidden_pre, approximate=False).astype(BF)
    hidden_grad = mm_nt(cot_pair, down_full)
    pre_grad = (hidden_grad * gelu_slope(hidden_pre)).astype(BF)
    far_grad = mm_nt(pre_grad[rows:], up_full).astype(BF)
    lifted2_grad = mm_nt(pre_grad[:rows], up_full) + swap(far_grad, "head", 1).astype(F32)
    resid_part, ffn_gain_local = norm_backward(lifted2_grad, unit2, inverse2, gain2)
    resid_grad = cot_own.astype(F32) + resid_part
    branch_own = resid_grad.astype(BF)
    branch = head_gather(branch_own)

    far_out = mm(hidden[rows:], down_full).astype(BF)
    layer_out = reorder(
        (resid + mm(hidden[:rows], down_full) + swap(far_out, "head", 1).astype(F32)).astype(BF)
    )

    def piece(array, r):
        return array[:, r * part : (r + 1) * part]

    slots = range(tok_count)
    down_two_grad = tok_scatter([mm_tn(hidden, piece(cot_pair, r)) for r in slots])
    half = down_two_grad.shape[0] // 2
    w_down_grad = down_two_grad[:half] + swap(
        down_two_grad[half:].astype(BF), "head", 2
    ).astype(F32)
    up_two_grad = tok_scatter([mm_tn(piece(lifted2_pair, r), pre_grad) for r in slots])
    half = up_two_grad.shape[1] // 2
    w_up_grad = up_two_grad[:, :half] + swap(
        up_two_grad[:, half:].astype(BF), "head", 2
    ).astype(F32)

    mixed_grad = mm_nt(branch, out_full).astype(BF)
    w_out_grad = tok_scatter([mm_tn(mixed, piece(branch, r)) for r in slots])

    gate_parts, ret_grad, group_gain_parts = [], [], []
    for h in range(heads):
        head_grad = head_of(mixed_grad, h, VAL).astype(F32)
        gate_parts.append(
            (head_grad * grouped[h] * (sigma[h] + swish[h] * (1.0 - sigma[h]))).astype(BF)
        )
        back, gain_term = norm_backward(
            head_grad * swish[h], unit_g[h], inverse_g[h], head_of(group_gain[None, :], h, VAL)
        )
        ret_grad.append(back.astype(BF))
        group_gain_parts.append(gain_term)
    gate_grad = jnp.concatenate(gate_parts, axis=1)
    w_gate_grad = tok_scatter([mm_tn(piece(group, r), gate_grad) for r in slots])

    pending_of, pending_terms = [], []
    for h in range(heads):
        pending = jnp.zeros((KEY, VAL), F32)
        terms = [None] * blocks
        for b in reversed(range(blocks)):
            terms[b] = mm_tn(
                block_of(q[h], b), (block_of(ret_grad[h], b) * masks[h][b][1]).astype(BF)
            )
            pending = masks[h][b][3] * pending + terms[b]
        pending_terms.append(terms)
        pending_of.append(pending.astype(BF))
    all_pending = lax.all_gather(jnp.concatenate(pending_of, axis=0), "tok", axis=0)
    lag_back = group_order - 1 - tok
    shifted_last = doc_index(group_order * group_rows - 1, starts)
    q_parts, k_parts, v_parts = [], [], []
    for h in range(heads):
        weights = jnp.where(
            (lag_back >= 0) & (shifted_last == doc_ids[-1]),
            jnp.exp(jnp.maximum(lag_back, 0).astype(F32) * group_rows * log_decay[h]),
            0.0,
        )
        later = jnp.sum(
            all_pending[:, h * KEY : (h + 1) * KEY].astype(F32) * weights[:, None, None], axis=0
        )
        qg, kg, vg_ = [None] * blocks, [None] * blocks, [None] * blocks
        for b in reversed(range(blocks)):
            qb, kb, vb = block_of(q[h], b), block_of(k[h], b), block_of(v[h], b)
            rb = block_of(ret_grad[h], b)
            decay, reach, leave, across = masks[h][b]
            probs = (mm_nt(qb, kb) * decay).astype(BF)
            score_grad = (mm_nt(rb, vb) * decay).astype(BF)
            later_b = later.astype(BF)
            qg[b] = mm(score_grad, kb) + reach * mm_nt(rb, states[h][b])
            kg[b] = mm_tn(score_grad, qb) + leave * mm_nt(vb, later_b)
            vg_[b] = mm_tn(probs, rb) + leave * mm(kb, later_b)
            later = across * later + pending_terms[h][b]
        q_parts.append(unrotate(jnp.concatenate(qg, axis=0), cosine, sine).astype(BF))
        k_parts.append(unrotate(jnp.concatenate(kg, axis=0), cosine, sine).astype(BF))
        v_parts.append(jnp.concatenate(vg_, axis=0).astype(BF))
    all_grad = jnp.concatenate(q_parts + k_parts + v_parts + [gate_grad], axis=1)
    group_terms = jnp.concatenate(group_gain_parts, axis=0)
    ffn_terms = reorder(ffn_gain_local)
    row_grad = head_scatter(lambda i: mm_nt(rows_of(all_grad, i, rows), qkvg_full))
    input_part, norm_gain_local = norm_backward(row_grad, unit1, inverse1, gain1)
    tokens_grad = reorder(resid_grad + input_part)
    qkv_grad = all_grad[:, : 2 * qk + vg]
    w_qkv_grad = tok_scatter([mm_tn(piece(group, r), qkv_grad) for r in slots])
    w_query_grad = w_qkv_grad[:, :qk]
    w_key_grad = w_qkv_grad[:, qk : 2 * qk]
    w_value_grad = w_qkv_grad[:, 2 * qk :]
    group_gain_grad = sum_small(group_terms, "tok")
    ffn_sum = sum_small(sum_small(ffn_terms, "tok"), "head")
    norm_sum = sum_small(sum_small(reorder(norm_gain_local), "tok"), "head")
    return (
        layer_out,
        tokens_grad,
        norm_sum,
        w_query_grad,
        w_key_grad,
        w_value_grad,
        w_gate_grad,
        group_gain_grad,
        w_out_grad,
        ffn_sum,
        w_up_grad,
        w_down_grad,
    )


def fused(
    tokens,
    cotangent,
    doc_lengths,
    head_order,
    norm_gain,
    w_query,
    w_key,
    w_value,
    w_gate,
    group_gain,
    w_out,
    ffn_gain,
    w_up,
    w_down,
):
    turned, qkvg_full, out_full, qk_rows, v_rows, gate, cosine, sine = enter(
        tokens, norm_gain, doc_lengths, w_query, w_key, w_value, w_gate, w_out
    )
    resid, inverse_g, unit_g, states, cot_pair, mixed_turned, up_full, down_full = retain(
        doc_lengths, head_order, group_gain, qk_rows, v_rows, gate, tokens, out_full, cotangent,
        w_up, w_down,
    )
    (
        layer_own, far_out, resid_grad, ffn_terms, up_own, up_far, down_own, down_far, branch
    ) = feed_forward(resid, ffn_gain, cot_pair, up_full, down_full)
    w_out_grad, group_terms, layer_out, all_grad, up_in, down_in = recall(
        doc_lengths, head_order, group_gain, qk_rows, v_rows, gate, unit_g, inverse_g, states,
        cosine, sine, mixed_turned, branch, out_full, layer_own, far_out, up_far, down_far,
    )
    w_up_grad = up_own + up_in.astype(F32)
    w_down_grad = down_own + down_in.astype(F32)
    (
        tokens_grad, w_query_grad, w_key_grad, w_value_grad, w_gate_grad, norm_sum, ffn_sum, group_sum
    ) = depart(all_grad, qkvg_full, turned, tokens, resid_grad, norm_gain, ffn_terms, group_terms)
    return (
        layer_out,
        tokens_grad,
        norm_sum.reshape(-1),
        w_query_grad,
        w_key_grad,
        w_value_grad,
        w_gate_grad,
        group_sum.reshape(-1)[: group_gain.shape[0]],
        w_out_grad,
        ffn_sum.reshape(-1),
        w_up_grad,
        w_down_grad,
    )


def local(*arrays):
    return fused(*arrays) if paired() else plain(*arrays)


def solution(mesh):
    rows = P(("tok", "head"), None)
    inward = P("tok", "head")
    outward = P("head", "tok")
    return jax.shard_map(
        local,
        mesh=mesh,
        in_specs=(
            rows, rows, P(), P(), P(), inward, inward, inward, inward, P("head"),
            outward, P(), inward, outward,
        ),
        out_specs=(
            rows, rows, P(), inward, inward, inward, inward, P("head"),
            outward, P(), inward, outward,
        ),
        check_vma=False,
    )
```

```python
import jax
import jax.numpy as jnp
from jax import lax
from jax.experimental import pallas as pl
from jax.experimental.pallas import tpu as pltpu
from jax.sharding import PartitionSpec as P

KEY = 256
VAL = 512
SPAN = 512

EPS = 1e-05
SQRT_HALF = 0.7071067811865476
INV_ROOT_TWO_PI = 0.3989422804014327
BF = jnp.bfloat16
F32 = jnp.float32


def mm(left, right):
    return jnp.dot(left, right, preferred_element_type=F32)


def mm_nt(left, right):
    return lax.dot_general(left, right, (((1,), (1,)), ((), ())), preferred_element_type=F32)


def mm_tn(left, right):
    return lax.dot_general(left, right, (((0,), (0,)), ((), ())), preferred_element_type=F32)


def swap(array, axis, bit):
    count = lax.axis_size(axis)
    return lax.ppermute(array, axis, [(i, i ^ bit) for i in range(count)])


def shift(array):
    count = lax.axis_size("head")
    return lax.ppermute(array, "head", [(i, (i + 1) % count) for i in range(count)])


def paired():
    return lax.axis_size("tok") == 8


def reorder(array):
    if not paired():
        return array
    me = lax.axis_index("tok")
    width = array.shape[-1] // 8
    return jnp.concatenate(
        [
            lax.dynamic_slice_in_dim(array, (me ^ r) * width, width, array.ndim - 1)
            for r in range(8)
        ],
        axis=-1,
    )


def halves(array):
    half = array.shape[0] // 2
    return array[:half], array[half:]


def tok_gather(shard, axis):
    if not paired():
        return lax.all_gather(shard, "tok", axis=axis, tiled=True)
    along_x = swap(shard, "tok", 2)
    along_y = swap(shard, "tok", 4)
    far = jnp.concatenate(
        [swap(halves(along_x)[0], "tok", 4), swap(halves(along_y)[1], "tok", 2)], axis=0
    )
    own = [shard, along_x, along_y, far]
    pieces = []
    for piece in own:
        pieces += [piece, swap(piece, "tok", 1)]
    return jnp.concatenate(pieces, axis=axis)


def tok_scatter(pieces):
    pieces = [p.astype(BF) for p in pieces]
    if not paired():
        return lax.psum_scatter(jnp.stack(pieces), "tok", scatter_dimension=0).astype(F32)
    kept = [
        pieces[r].astype(F32) + swap(pieces[r + 1], "tok", 1).astype(F32) for r in (0, 2, 4, 6)
    ]
    zero, two, four, six = kept
    six_a, six_b = halves(six.astype(BF))
    two_a, two_b = halves(two)
    four_a, four_b = halves(four)
    four_a = four_a + swap(six_a, "tok", 2).astype(F32)
    two_b = two_b + swap(six_b, "tok", 4).astype(F32)
    two = jnp.concatenate([two_a, two_b], axis=0).astype(BF)
    four = jnp.concatenate([four_a, four_b], axis=0).astype(BF)
    return zero + swap(two, "tok", 2).astype(F32) + swap(four, "tok", 4).astype(F32)


def head_gather(rows):
    count = lax.axis_size("head")
    me = lax.axis_index("head")
    size = rows.shape[0]
    whole = jnp.zeros((count * size,) + rows.shape[1:], rows.dtype)
    whole = lax.dynamic_update_slice_in_dim(whole, rows, me * size, 0)
    for step in range(1, count):
        rows = shift(rows)
        source = lax.rem(me - step + count, count)
        whole = lax.dynamic_update_slice_in_dim(whole, rows, source * size, 0)
    return whole


def head_scatter(term):
    count = lax.axis_size("head")
    me = lax.axis_index("head")
    total = term(lax.rem(me + count - 1, count))
    for step in range(1, count):
        arrived = shift(total.astype(BF))
        owner = lax.rem(me + 2 * count - 1 - step, count)
        total = term(owner) + arrived.astype(F32)
    return total


def rows_of(array, index, size):
    return lax.dynamic_slice_in_dim(array, index * size, size, 0)


def sum_small(vector, axis):
    count = lax.axis_size(axis)
    bit = 1
    while bit < count:
        vector = vector + swap(vector, axis, bit)
        bit *= 2
    return vector


MESH = pl.DeviceIdType.MESH
ANY = pl.BlockSpec(memory_space=pl.ANY)
VMEM = pl.BlockSpec(memory_space=pltpu.VMEM)
SMEM = pl.BlockSpec(memory_space=pltpu.SMEM)
LIMIT = 60 * 1024 * 1024


def flipped(index, bit):
    return index + bit - 2 * bit * lax.rem(lax.div(index, bit), 2)


def peers():
    tok = lax.axis_index("tok")
    z = lax.axis_index("head")
    count = lax.axis_size("head")
    return {
        "core": {"tok": flipped(tok, 1), "head": z},
        "x": {"tok": flipped(tok, 2), "head": z},
        "y": {"tok": flipped(tok, 4), "head": z},
        "up": {"tok": tok, "head": lax.rem(z + 1, count)},
        "down": {"tok": tok, "head": lax.rem(z + count - 1, count)},
        "pair": {"tok": tok, "head": flipped(z, 1)},
        "cross": {"tok": tok, "head": flipped(z, 2)},
    }


def everyone():
    near = peers()
    tok = lax.axis_index("tok")
    z = lax.axis_index("head")
    count = lax.axis_size("head")
    others = [{"tok": tok, "head": lax.rem(z + step, count)} for step in range(1, count)]
    return [near["core"], near["x"], near["y"], *others]


def greet(*devices):
    barrier = pltpu.get_barrier_semaphore()
    for device in devices:
        pl.semaphore_signal(barrier, inc=1, device_id=device, device_id_type=MESH)


def greeted(*devices):
    pl.semaphore_wait(pltpu.get_barrier_semaphore(), len(devices))


def doc_starts(lengths):
    starts, total = [], 0
    for d in range(lengths.shape[0]):
        starts.append(total)
        total = total + lengths[d]
    return starts


def doc_at(row, starts):
    return sum((start <= row).astype(jnp.int32) for start in starts) - 1


def doc_first(row, starts):
    first = jnp.zeros_like(row)
    for start in starts:
        first = jnp.maximum(first, jnp.where(start <= row, start, 0))
    return first


def decays(order, heads):
    z = lax.axis_index("head")
    found = []
    for h in range(heads):
        rank = jnp.full((1, 1), order[z * heads + h], jnp.int32).astype(F32)
        found.append(jnp.log1p(-jnp.exp2(-(5.0 + rank))))
    return found


def block_scales(lengths, log_decay, group_rows, scale, docs):
    heads = len(log_decay)
    starts = doc_starts(lengths)
    first_row = lax.axis_index("tok") * group_rows
    across = [[] for _ in range(heads)]
    for b in range(group_rows // SPAN):
        at = pl.ds(b * SPAN, SPAN)
        low = first_row + b * SPAN
        place = lax.broadcasted_iota(jnp.int32, (SPAN, 1), 0)
        doc = doc_at(low + place, starts)
        docs[at, :] = doc
        before = doc_at(low - 1, starts)
        last = doc_at(low + SPAN - 1, starts)
        where = place.astype(F32)
        for h in range(heads):
            scale[at, h : h + 1] = jnp.where(
                doc == before, jnp.exp((where + 1.0) * log_decay[h]), 0.0
            )
            scale[at, heads + h : heads + h + 1] = jnp.where(
                doc == last, jnp.exp((SPAN - 1.0 - where) * log_decay[h]), 0.0
            )
            across[h].append(jnp.where(last == before, jnp.exp(SPAN * log_decay[h]), 0.0))
    return across


def row_docs(lengths, group_rows):
    starts = doc_starts(lengths)
    first_row = lax.axis_index("tok") * group_rows
    return doc_at(first_row + lax.broadcasted_iota(jnp.int32, (8, group_rows), 1), starts)


def group_weights(lengths, log_decay, group_rows, backward):
    starts = doc_starts(lengths)
    tok = lax.axis_index("tok")
    first_row = tok * group_rows
    found = [[] for _ in log_decay]
    for other in xor_places(tok):
        if backward:
            lag = other - 1 - tok
            same = doc_at(other * group_rows - 1, starts) == doc_at(
                first_row + group_rows - 1, starts
            )
        else:
            lag = tok - 1 - other
            same = doc_at((other + 1) * group_rows - 1, starts) == doc_at(first_row - 1, starts)
        amount = (jnp.maximum(lag, 0) * group_rows).astype(F32)
        for h, rate in enumerate(log_decay):
            found[h].append(jnp.where((lag >= 0) & same, jnp.exp(amount * rate), 0.0))
    return found


def state_view(gathered, h):
    def view(r, side=None):
        if side is None:
            return gathered.at[r, pl.ds(h * KEY, KEY), :]
        return gathered.at[r, pl.ds(h * KEY + side * (KEY // 2), KEY // 2), :]

    return view


class Moves:
    def __init__(self, send, recv):
        self.send, self.recv, self.made, self.over = send, recv, [], []

    def go(self, src, dst, device):
        n = len(self.made)
        copy = pltpu.make_async_remote_copy(
            src_ref=src,
            dst_ref=dst,
            send_sem=self.send.at[n],
            recv_sem=self.recv.at[n],
            device_id=device,
            device_id_type=MESH,
        )
        copy.start()
        self.made.append(copy)
        return copy

    def sent(self, copy):
        copy.wait_send()
        self.over.append(copy)

    def finish(self):
        for copy in self.made:
            if not any(copy is gone for gone in self.over):
                copy.wait_send()


class Gather:
    def __init__(self, moves, near, view):
        self.moves, self.near, self.view = moves, near, view

    def first(self):
        go, near, view = self.moves.go, self.near, self.view
        self.x = go(view(0), view(2), near["x"])
        self.y = go(view(0), view(4), near["y"])
        self.cores = [go(view(0), view(1), near["core"])]

    def second(self):
        go, near, view = self.moves.go, self.near, self.view
        self.x.wait_recv()
        self.far = [go(view(2, 0), view(6, 0), near["y"])]
        self.cores.append(go(view(2), view(3), near["core"]))
        self.y.wait_recv()
        self.far.append(go(view(4, 1), view(6, 1), near["x"]))
        self.cores.append(go(view(4), view(5), near["core"]))

    def third(self):
        go, near, view = self.moves.go, self.near, self.view
        for copy in self.far:
            copy.wait_recv()
        self.cores.append(go(view(6), view(7), near["core"]))

    def done(self):
        for copy in self.cores:
            copy.wait_recv()


def enter_kernel(
    tok_ref,
    gain_ref,
    lengths_ref,
    wq_ref,
    wk_ref,
    wv_ref,
    wg_ref,
    wo_ref,
    turned_out,
    weights_out,
    out_full,
    qk_hbm,
    v_hbm,
    gate_hbm,
    cos_hbm,
    sin_hbm,
    qk_out,
    v_out,
    gate_out,
    cos_ref,
    sin_ref,
    turned,
    group,
    weights,
    own_out,
    gain,
    send,
    recv,
    own_sem,
    keep_sem,
    rows_sem,
):
    near = peers()
    tok = lax.axis_index("tok")
    z = lax.axis_index("head")
    count = lax.axis_size("head")
    rows, width = tok_ref.shape
    part = width // 8
    cols = weights.shape[2]
    half = wq_ref.shape[1]

    own = [
        pltpu.make_async_copy(wq_ref, weights.at[0, pl.ds(0, part), pl.ds(0, half)], own_sem.at[0]),
        pltpu.make_async_copy(
            wk_ref, weights.at[0, pl.ds(0, part), pl.ds(half, half)], own_sem.at[1]
        ),
        pltpu.make_async_copy(wv_ref, weights.at[1, pl.ds(0, part), :], own_sem.at[2]),
        pltpu.make_async_copy(wg_ref, weights.at[2, pl.ds(0, part), :], own_sem.at[3]),
        pltpu.make_async_copy(wo_ref, own_out, own_sem.at[4]),
    ]
    for copy in own:
        copy.start()
    reached = everyone()
    greet(*reached)
    gain[...] = arranged(gain_ref, tok)
    moves = Moves(send, recv)

    def chunk_view(c):
        def view(r, side=None):
            if side is None:
                return weights.at[c, pl.ds(r * part, part), :]
            return weights.at[c, pl.ds(r * part + side * (part // 2), part // 2), :]

        return view

    def out_view(r, side=None):
        if r == 0:
            return own_out
        if side is None:
            return out_full.at[:, pl.ds(r * part, part)]
        size = out_full.shape[0] // 2
        return out_full.at[pl.ds(side * size, size), pl.ds(r * part, part)]

    chunks = [Gather(moves, near, chunk_view(c)) for c in range(3)]
    outward = Gather(moves, near, out_view)
    def lift(side):
        @pl.loop(side * (rows // 32), (side + 1) * (rows // 32))
        def _(i):
            at = pl.ds(pl.multiple_of(i * 16, 16), 16)
            values = arranged(tok_ref.at[at, :], tok).astype(F32)
            mean = jnp.mean(values, axis=-1, keepdims=True)
            centred = values - mean
            inverse = lax.rsqrt(jnp.mean(centred * centred, axis=-1, keepdims=True) + EPS)
            lifted = (centred * inverse * gain[...]).astype(BF)
            group[pl.ds(pl.multiple_of(z * rows + i * 16, 16), 16), :] = lifted

    def shard(step, side):
        owner = lax.rem(z - step + count, count)
        size = rows // 2
        return group.at[pl.ds(pl.multiple_of(owner * rows + side * size, size), size), :]

    ring = {}

    def pass_on(step, side):
        if step:
            ring[step - 1, side].wait_recv()
        if step < count - 1:
            ring[step, side] = moves.go(shard(step, side), shard(step, side), near["up"])

    def keep_rows(step):
        owner = lax.rem(z - step + count, count)
        at = pl.ds(pl.multiple_of(owner * rows, rows), rows)
        for n, (source, target) in enumerate(
            ((qk_out, qk_hbm), (v_out, v_hbm), (gate_out, gate_hbm))
        ):
            copy = pltpu.make_async_copy(
                source.at[at, :], target.at[at, :], rows_sem.at[3 * step + n]
            )
            copy.start()
            kept.append(copy)

    def project(c, steps, part_rows=None):
        first, number = steps
        offset, size = part_rows or (0, rows)

        @pl.loop(0, number * (cols // 256))
        def _(i):
            step = first + lax.div(i, cols // 256)
            tile = lax.rem(i, cols // 256)
            owner = lax.rem(z - step + count, count)
            at = pl.ds(pl.multiple_of(owner * rows + offset, size), size)
            to = pl.ds(pl.multiple_of(tile * 256, 256), 256)
            found = jnp.dot(group[at, :], weights[c, :, to], preferred_element_type=F32)
            if c == 0:
                cosine, sine = cos_ref[at, :], sin_ref[at, :]
                one, two = found[:, :128], found[:, 128:]
                qk_out[at, to] = jnp.concatenate(
                    [one * cosine - two * sine, one * sine + two * cosine], axis=1
                ).astype(BF)
            elif c == 1:
                v_out[at, to] = found.astype(BF)
            else:
                gate_out[at, to] = found.astype(BF)

    def turn(step):
        owner = lax.rem(z - step + count, count)

        @pl.loop(0, width // 256)
        def _(i):
            at = pl.ds(pl.multiple_of(i * 256, 256), 256)
            to = pl.ds(pl.multiple_of(owner * rows, rows), rows)
            turned[at, to] = group[to, at].T

    def keep(c):
        copy = pltpu.make_async_copy(
            weights.at[c], weights_out.at[:, pl.ds(c * cols, cols)], keep_sem.at[c]
        )
        copy.start()
        kept.append(copy)

    lift(0)
    greeted(*reached)
    pass_on(0, 0)
    own[0].wait()
    own[1].wait()
    chunks[0].first()
    own[2].wait()
    chunks[1].first()
    lift(1)
    pass_on(0, 1)
    own[3].wait()
    own[4].wait()
    kept = [pltpu.make_async_copy(own_out, out_full.at[:, pl.ds(0, part)], keep_sem.at[4])]
    kept[0].start()
    group_rows = rows * count
    starts = doc_starts(lengths_ref)
    index = lax.broadcasted_iota(jnp.int32, (1, KEY // 2), 1).astype(F32)
    freq = jnp.exp(-jnp.log(10000.0) * index / (KEY // 2))

    @pl.loop(0, group_rows // 64)
    def _(i):
        at = pl.ds(pl.multiple_of(i * 64, 64), 64)
        row = tok * group_rows + i * 64 + lax.broadcasted_iota(jnp.int32, (64, KEY // 2), 0)
        turn = (row - doc_first(row, starts)).astype(F32) * freq
        cos_ref[at, :] = jnp.cos(turn)
        sin_ref[at, :] = jnp.sin(turn)

    for n, (source, target) in enumerate(((cos_ref, cos_hbm), (sin_ref, sin_hbm))):
        copy = pltpu.make_async_copy(source, target, keep_sem.at[5 + n])
        copy.start()
        kept.append(copy)

    chunks[0].second()
    chunks[2].first()
    pass_on(1, 0)
    chunks[1].second()
    outward.first()
    pass_on(1, 1)
    chunks[0].third()
    chunks[0].done()
    keep(0)
    project(0, (0, 2))
    pass_on(2, 0)
    turn(0)
    turn(1)
    chunks[2].second()
    pass_on(2, 1)
    chunks[1].third()
    chunks[1].done()
    keep(1)
    project(1, (0, 2))
    outward.second()
    project(0, (2, 1))
    project(1, (2, 1))
    turn(2)
    chunks[2].third()
    chunks[2].done()
    keep(2)
    project(2, (0, 3))
    for step in range(3):
        keep_rows(step)
    outward.third()
    pass_on(3, 0)
    for c in range(3):
        project(c, (3, 1), (0, rows // 2))
    pass_on(3, 1)
    for c in range(3):
        project(c, (3, 1), (rows // 2, rows // 2))
    keep_rows(3)
    turn(3)
    copy = pltpu.make_async_copy(turned, turned_out, keep_sem.at[3])
    copy.start()
    kept.append(copy)
    outward.done()
    for copy in kept:
        copy.wait()
    moves.finish()


def arranged(ref, tok):
    part = ref.shape[-1] // 8
    return jnp.concatenate(
        [ref[:, pl.ds(pl.multiple_of(place * part, part), part)] for place in xor_places(tok)],
        axis=1,
    )


def xor_places(tok):
    places = []
    for r in range(8):
        place = tok
        for bit in (1, 2, 4):
            if r & bit:
                place = flipped(place, bit)
        places.append(place)
    return places


def enter(tokens, gain, doc_lengths, w_query, w_key, w_value, w_gate, w_out):
    rows, width = tokens.shape
    group_rows = rows * lax.axis_size("head")
    cols = w_value.shape[1]
    moves = 4 * 8 + 6
    return pl.pallas_call(
        enter_kernel,
        out_shape=(
            jax.ShapeDtypeStruct((width, group_rows), BF),
            jax.ShapeDtypeStruct((width, 3 * cols), BF),
            jax.ShapeDtypeStruct((w_out.shape[0], width), BF),
            jax.ShapeDtypeStruct((group_rows, cols), BF),
            jax.ShapeDtypeStruct((group_rows, cols), BF),
            jax.ShapeDtypeStruct((group_rows, cols), BF),
            jax.ShapeDtypeStruct((group_rows, KEY // 2), F32),
            jax.ShapeDtypeStruct((group_rows, KEY // 2), F32),
        ),
        in_specs=[VMEM] * 2 + [SMEM] + [ANY] * 5,
        out_specs=[ANY] * 8,
        scratch_shapes=[
            *[pltpu.VMEM((group_rows, cols), BF)] * 3,
            *[pltpu.VMEM((group_rows, KEY // 2), F32)] * 2,
            pltpu.VMEM((width, group_rows), BF),
            pltpu.VMEM((group_rows, width), BF),
            pltpu.VMEM((3, width, cols), BF),
            pltpu.VMEM(w_out.shape, BF),
            pltpu.VMEM((1, width), F32),
            pltpu.SemaphoreType.DMA((moves,)),
            pltpu.SemaphoreType.DMA((moves,)),
            pltpu.SemaphoreType.DMA((5,)),
            pltpu.SemaphoreType.DMA((7,)),
            pltpu.SemaphoreType.DMA((12,)),
        ],
        compiler_params=pltpu.CompilerParams(
            collective_id=0, has_side_effects=True, vmem_limit_bytes=LIMIT
        ),
        cost_estimate=pl.CostEstimate(
            flops=2 * group_rows * width * 3 * cols, bytes_accessed=40 << 20, transcendentals=0
        ),
    )(tokens, gain[None, :], doc_lengths, w_query, w_key, w_value, w_gate, w_out)


class Scatter:
    def __init__(self, moves, near, term, buffers, result, before=None, ready=None):
        self.moves, self.near, self.term, self.result = moves, near, term, result
        self.odd_out, self.odd_in, self.far_out, self.far_in, self.near_out, self.near_in = buffers
        self.half = self.far_out.shape[0] // 2
        self.before, self.ready, self.frees = before, ready, None
        self.cores = {}

    def odd(self, i):
        if self.before is not None:
            if not self.cores:
                pl.semaphore_wait(self.ready, 1)
            self.moves.sent(self.before.cores[i])
        self.odd_out[i] = self.term(2 * i + 1).astype(BF)
        self.cores[i] = self.moves.go(self.odd_out.at[i], self.odd_in.at[i], self.near["core"])

    def folded(self, i):
        self.cores[i].wait_recv()
        return self.term(2 * i) + self.odd_in[i].astype(F32)

    def far(self):
        value = self.folded(3).astype(BF)
        if self.before is not None:
            for move in self.before.fars:
                self.moves.sent(move)
        self.far_out[...] = value
        self.fars = [
            self.moves.go(
                self.far_out.at[pl.ds(side * self.half, self.half), :],
                self.far_in.at[side],
                self.near[way],
            )
            for side, way in ((0, "x"), (1, "y"))
        ]

    def close(self):
        half = self.half
        self.nears = []
        for i, side, way in ((1, 1, "x"), (2, 0, "y")):
            value = self.folded(i)
            self.fars[side].wait_recv()
            helped = value[side * half : (side + 1) * half] + self.far_in[side].astype(F32)
            other = value[(1 - side) * half : (2 - side) * half]
            if self.before is not None:
                self.moves.sent(self.before.nears[i - 1])
            self.near_out[i - 1, pl.ds(side * half, half), :] = helped.astype(BF)
            self.near_out[i - 1, pl.ds((1 - side) * half, half), :] = other.astype(BF)
            self.nears.append(
                self.moves.go(self.near_out.at[i - 1], self.near_in.at[i - 1], self.near[way])
            )
        self.result[...] = self.folded(0)
        if self.frees is not None:
            pl.semaphore_signal(
                self.frees, inc=1, device_id=self.near["core"], device_id_type=MESH
            )

    def done(self):
        for i in range(2):
            self.nears[i].wait_recv()
        self.result[...] += self.near_in[0].astype(F32) + self.near_in[1].astype(F32)


class Beside:
    def __init__(self, left, right):
        self.refs, self.size = (left, right), left.shape[1]

    def __getitem__(self, index):
        return jnp.concatenate([ref[...] for ref in self.refs], axis=1)

    def __setitem__(self, index, value):
        for i, ref in enumerate(self.refs):
            ref[...] = value[:, i * self.size : (i + 1) * self.size]


class AllSum:
    def __init__(self, moves, vector, slots, others):
        self.moves, self.vector, self.slots, self.others = moves, vector, slots, others

    def start(self):
        self.made = [
            self.moves.go(self.vector, self.slots.at[n], device)
            for n, device in enumerate(self.others)
        ]

    def total(self):
        total = self.vector[...]
        for n, move in enumerate(self.made):
            move.wait_recv()
            total = total + self.slots[n]
        return total


def leave_kernel(
    grads_ref,
    weights_ref,
    turned_ref,
    tok_ref,
    resid_ref,
    gain_ref,
    ffn_ref,
    group_ref,
    wq_out,
    wk_out,
    wv_out,
    wg_out,
    norm_out,
    ffn_out,
    group_out,
    tokens_hbm,
    tokens_grad,
    units,
    spreads,
    grads,
    weights,
    turned,
    ring_out,
    ring_in,
    held,
    odd_out,
    odd_in,
    far_out,
    far_in,
    near_out,
    near_in,
    norm_vec,
    norm_vec2,
    norm_slots_z,
    norm_slots,
    ffn_vec,
    ffn_vec2,
    ffn_slots_z,
    ffn_slots,
    group_vec,
    group_slots,
    gain,
    send,
    recv,
    load_sem,
    free_sem,
):
    near = peers()
    tok = lax.axis_index("tok")
    z = lax.axis_index("head")
    count = lax.axis_size("head")
    rows, width = tok_ref.shape
    part = width // 8
    gain[...] = arranged(gain_ref, tok)
    cols = wv_out.shape[1]
    strip = width // 4

    def owned(step):
        owner = lax.rem(z + 2 * count - 1 - step, count)
        return pl.ds(pl.multiple_of(owner * rows, rows), rows)

    grad_loads = [
        pltpu.make_async_copy(
            grads_ref.at[owned(step), :], grads.at[owned(step), :], load_sem.at[step]
        )
        for step in range(count)
    ]
    strip_loads = [
        pltpu.make_async_copy(
            weights_ref.at[pl.ds(n * strip, strip), :],
            weights.at[pl.ds(n * strip, strip), :],
            load_sem.at[count + n],
        )
        for n in range(4)
    ]
    turned_load = pltpu.make_async_copy(turned_ref, turned, load_sem.at[count + 4])
    loads = [grad_loads[0], *strip_loads, *grad_loads[1:], turned_load]
    for load in loads:
        load.start()
    z_others = [{"tok": tok, "head": lax.rem(z + step, count)} for step in range(1, count)]
    tok_others = [{"tok": place, "head": z} for place in xor_places(tok)[1:]]
    greet(*z_others, *tok_others)
    gain[...] = arranged(gain_ref, tok)
    moves = Moves(send, recv)

    def ring_term(step, side):
        @pl.loop(side * (width // 512), (side + 1) * (width // 512))
        def _(i):
            to = pl.ds(pl.multiple_of(i * 256, 256), 256)
            held[:, to] = dot_nt(grads[owned(step), :], weights[to, :])

    ring = {}
    half = width // 2

    def ring_send(step, side):
        at = pl.ds(side * half, half)
        value = held[:, at]
        if step:
            ring[step - 1, side].wait_recv()
            value = value + ring_in[step - 1, :, at].astype(F32)
        ring_out[step, :, at] = value.astype(BF)
        ring[step, side] = moves.go(
            ring_out.at[step, :, at], ring_in.at[step, :, at], near["up"]
        )

    def chunk_term(c):
        def term(r):
            left = turned[pl.ds(r * part, part), :]
            return jnp.concatenate(
                [
                    jnp.dot(
                        left,
                        grads[:, c * cols + j * 256 : c * cols + (j + 1) * 256],
                        preferred_element_type=F32,
                    )
                    for j in range(cols // 256)
                ],
                axis=1,
            )

        return term

    def buffers(c):
        s = c % 2
        return (
            odd_out.at[s], odd_in.at[s], far_out.at[s], far_in.at[c], near_out.at[s], near_in.at[c]
        )

    scatters = [
        Scatter(moves, near, chunk_term(c), buffers(c), result)
        for c, result in enumerate((Beside(wq_out, wk_out), wv_out))
    ]
    scatters.append(
        Scatter(moves, near, chunk_term(2), buffers(2), wg_out, scatters[0], free_sem)
    )
    scatters[0].frees = free_sem

    def spread(ref, value):
        for n in range(8):
            ref[:, n * part : (n + 1) * part] = value[n : n + 1, :]

    ffn_vec[...] = jnp.zeros_like(ffn_vec)
    group_vec[...] = jnp.zeros_like(group_vec)
    for r, place in enumerate(xor_places(tok)):
        ffn_vec[pl.ds(place, 1), :] = (
            ffn_ref[pl.ds(0, 1), r * part : (r + 1) * part]
            + ffn_ref[pl.ds(1, 1), r * part : (r + 1) * part]
        )
    for n in range(cols // part):
        group_vec[pl.ds(n, 1), :] = group_ref[pl.ds(0, 1), n * part : (n + 1) * part]
    ffn_z = AllSum(moves, ffn_vec, ffn_slots_z, z_others)
    group_tok = AllSum(moves, group_vec, group_slots, tok_others)
    grad_loads[0].wait()
    strip_loads[0].wait()
    strip_loads[1].wait()
    ring_term(0, 0)
    greeted(*z_others, *tok_others)
    ring_send(0, 0)
    strip_loads[2].wait()
    strip_loads[3].wait()
    ring_term(0, 1)
    ring_send(0, 1)
    for load in grad_loads[1:]:
        load.wait()
    turned_load.wait()
    for i in (3, 1, 2, 0):
        scatters[0].odd(i)
    for i in (3, 1):
        scatters[1].odd(i)
    scatters[0].far()
    ring_term(1, 0)
    ring_term(1, 1)
    ring_send(1, 0)
    for i in (2, 0):
        scatters[1].odd(i)
    scatters[1].far()
    ring_send(1, 1)
    scatters[0].close()
    ring_term(2, 0)
    ring_term(2, 1)
    for i in (3, 1):
        scatters[2].odd(i)
    ring_send(2, 0)
    for i in (2, 0):
        scatters[2].odd(i)
    scatters[2].far()
    scatters[1].close()
    ring_send(2, 1)
    scatters[0].done()
    ring_term(3, 0)
    ring_term(3, 1)
    scatters[2].close()
    size = 16

    @pl.loop(0, rows // size)
    def _(i):
        at = pl.ds(pl.multiple_of(i * size, size), size)
        values = arranged(tok_ref.at[at, :], tok).astype(F32)
        mean = jnp.mean(values, axis=-1, keepdims=True)
        centred = values - mean
        inverse = lax.rsqrt(jnp.mean(centred * centred, axis=-1, keepdims=True) + EPS)
        units[at, :] = centred * inverse
        spreads[at, :] = inverse

    scatters[1].done()
    scatters[2].done()
    for side in range(2):
        ring[2, side].wait_recv()
    ffn_z.start()
    group_tok.start()

    def block(i, total):
        at = pl.ds(pl.multiple_of(i * size, size), size)
        unit = units[at, :]
        grad = held[at, :] + ring_in[2, at, :].astype(F32)
        scaled = grad * gain[...]
        first = jnp.mean(scaled, axis=-1, keepdims=True)
        second = jnp.mean(scaled * unit, axis=-1, keepdims=True)
        found = resid_ref[at, :] + spreads[at, :] * (scaled - first - unit * second)
        for r, place in enumerate(xor_places(tok)):
            tokens_grad[at, pl.ds(pl.multiple_of(place * part, part), part)] = found[
                :, r * part : (r + 1) * part
            ]
        return total + jnp.sum(grad * unit, axis=0, keepdims=True)

    total = lax.fori_loop(0, rows // size, block, jnp.zeros((1, width), F32))
    keep = pltpu.make_async_copy(tokens_grad, tokens_hbm, load_sem.at[count + 5])
    keep.start()
    for r, place in enumerate(xor_places(tok)):
        norm_vec[pl.ds(place, 1), :] = total[:, r * part : (r + 1) * part]
    norm_z = AllSum(moves, norm_vec, norm_slots_z, z_others)
    norm_z.start()
    ffn_vec2[...] = ffn_z.total()
    ffn_tok = AllSum(moves, ffn_vec2, ffn_slots, tok_others)
    ffn_tok.start()
    norm_vec2[...] = norm_z.total()
    norm_tok = AllSum(moves, norm_vec2, norm_slots, tok_others)
    norm_tok.start()
    spread(group_out, group_tok.total())
    spread(ffn_out, ffn_tok.total())
    spread(norm_out, norm_tok.total())
    keep.wait()
    moves.finish()


def depart(grads, weights, turned, tokens, resid_grad, gain, ffn_terms, group_terms):
    rows, width = tokens.shape
    count = lax.axis_size("head")
    cols = grads.shape[1] // 3
    part = width // 8
    moves = 6 + 3 * 8 + 2 * (count - 1) + 3 * 7
    vector = (8, part)
    return pl.pallas_call(
        leave_kernel,
        out_shape=(
            jax.ShapeDtypeStruct((part, cols // 2), F32),
            jax.ShapeDtypeStruct((part, cols // 2), F32),
            jax.ShapeDtypeStruct((part, cols), F32),
            jax.ShapeDtypeStruct((part, cols), F32),
            jax.ShapeDtypeStruct((1, width), F32),
            jax.ShapeDtypeStruct((1, width), F32),
            jax.ShapeDtypeStruct((1, width), F32),
            jax.ShapeDtypeStruct((rows, width), F32),
        ),
        in_specs=[ANY] * 3 + [VMEM] * 5,
        out_specs=[VMEM] * 7 + [ANY],
        scratch_shapes=[
            pltpu.VMEM((rows, width), F32),
            pltpu.VMEM((rows, width), F32),
            pltpu.VMEM((rows, 1), F32),
            pltpu.VMEM(grads.shape, BF),
            pltpu.VMEM(weights.shape, BF),
            pltpu.VMEM(turned.shape, BF),
            pltpu.VMEM((3, rows, width), BF),
            pltpu.VMEM((3, rows, width), BF),
            pltpu.VMEM((rows, width), F32),
            pltpu.VMEM((2, 4, part, cols), BF),
            pltpu.VMEM((2, 4, part, cols), BF),
            pltpu.VMEM((2, part, cols), BF),
            pltpu.VMEM((3, 2, part // 2, cols), BF),
            pltpu.VMEM((2, 2, part, cols), BF),
            pltpu.VMEM((3, 2, part, cols), BF),
            pltpu.VMEM(vector, F32),
            pltpu.VMEM(vector, F32),
            pltpu.VMEM((count - 1,) + vector, F32),
            pltpu.VMEM((7,) + vector, F32),
            pltpu.VMEM(vector, F32),
            pltpu.VMEM(vector, F32),
            pltpu.VMEM((count - 1,) + vector, F32),
            pltpu.VMEM((7,) + vector, F32),
            pltpu.VMEM(vector, F32),
            pltpu.VMEM((7,) + vector, F32),
            pltpu.VMEM((1, width), F32),
            pltpu.SemaphoreType.DMA((moves,)),
            pltpu.SemaphoreType.DMA((moves,)),
            pltpu.SemaphoreType.DMA((count + 6,)),
            pltpu.SemaphoreType.REGULAR,
        ],
        compiler_params=pltpu.CompilerParams(
            collective_id=1, has_side_effects=True, vmem_limit_bytes=LIMIT
        ),
        cost_estimate=pl.CostEstimate(
            flops=2 * grads.shape[0] * width * 5 * cols, bytes_accessed=40 << 20, transcendentals=0
        ),
    )(
        grads, weights, turned, tokens, resid_grad, gain[None, :], ffn_terms, group_terms
    )


def dot_nt(left, right):
    return lax.dot_general(left, right, (((1,), (1,)), ((), ())), preferred_element_type=F32)


def dot_tn(left, right):
    return lax.dot_general(left, right, (((0,), (0,)), ((), ())), preferred_element_type=F32)


def dot_nn(left, right):
    return jnp.dot(left, right, preferred_element_type=F32)


def tile_decay(docs_col, docs_row, log_decay, first, tile, top):
    size = tile + top
    shape = (top, size)
    lag = (
        lax.broadcasted_iota(jnp.int32, shape, 0)
        + tile
        - lax.broadcasted_iota(jnp.int32, shape, 1)
    )
    same = docs_col[pl.ds(first + tile, top), :] == docs_row[pl.ds(0, 1), pl.ds(first, size)]
    power = jnp.exp(jnp.maximum(lag, 0).astype(F32) * log_decay)
    return jnp.where(same & (lag >= 0), power, 0.0)


def retain_kernel(
    lengths_ref,
    order_ref,
    gain_ref,
    qk_ref,
    v_ref,
    wu_ref,
    wd_ref,
    gate_hbm,
    tok_hbm,
    cot_hbm,
    wo_ref,
    resid_out,
    inverse_out,
    unit_hbm,
    states_hbm,
    cot_out,
    turned_hbm,
    up_full,
    down_full,
    gate_ref,
    tok_ref,
    cot_ref,
    cot_rows,
    unit_out,
    states_out,
    cot_pair,
    mixed_turned,
    mixed_out,
    out_weights,
    retained,
    terms,
    folded,
    gathered,
    held,
    ring_out,
    ring_in,
    docs_col,
    docs_row,
    scale_ref,
    send,
    recv,
    own_sem,
):
    near = peers()
    tok = lax.axis_index("tok")
    z = lax.axis_index("head")
    count = lax.axis_size("head")
    rows, width = tok_hbm.shape
    group_rows = rows * count
    part = width // 8
    heads = v_ref.shape[1] // VAL
    blocks = group_rows // SPAN
    slice_ = wu_ref.shape[1]
    own = [
        pltpu.make_async_copy(
            wu_ref, up_full.at[pl.ds(0, part), pl.ds(0, slice_)], own_sem.at[0]
        ),
        pltpu.make_async_copy(
            wd_ref, down_full.at[pl.ds(0, slice_), pl.ds(0, part)], own_sem.at[1]
        ),
        pltpu.make_async_copy(wo_ref, out_weights, own_sem.at[2]),
        pltpu.make_async_copy(gate_hbm, gate_ref, own_sem.at[3]),
        pltpu.make_async_copy(tok_hbm, tok_ref, own_sem.at[4]),
        pltpu.make_async_copy(cot_hbm, cot_ref, own_sem.at[5]),
    ]
    keeps = [
        pltpu.make_async_copy(unit_out, unit_hbm, own_sem.at[7]),
        pltpu.make_async_copy(states_out, states_hbm, own_sem.at[8]),
        pltpu.make_async_copy(mixed_turned, turned_hbm, own_sem.at[9]),
        pltpu.make_async_copy(cot_pair, cot_out, own_sem.at[10]),
    ]
    for copy in own:
        copy.start()
    reached = everyone()
    greet(*reached)
    rate = decays(order_ref, heads)
    across = block_scales(lengths_ref, rate, group_rows, scale_ref, docs_col)
    docs_row[...] = row_docs(lengths_ref, group_rows)
    fold = group_weights(lengths_ref, rate, group_rows, False)
    greeted(*reached)
    moves = Moves(send, recv)
    far_up = moves.go(
        wu_ref, up_full.at[pl.ds(0, part), pl.ds(slice_, slice_)], near["cross"]
    )
    far_down = moves.go(
        wd_ref, down_full.at[pl.ds(slice_, slice_), pl.ds(0, part)], near["cross"]
    )

    def block_rows(b):
        return pl.ds(pl.multiple_of(b * SPAN, SPAN), SPAN)


    def q_cols(h):
        return pl.ds(h * KEY, KEY)

    def k_cols(h):
        return pl.ds((heads + h) * KEY, KEY)

    def v_cols(h):
        return pl.ds(h * VAL, VAL)

    def up_view(s):
        def view(r, side=None):
            if r == 0 and s == 0:
                return wu_ref
            if side is None:
                return up_full.at[pl.ds(r * part, part), pl.ds(s * slice_, slice_)]
            size = part // 2
            return up_full.at[
                pl.ds(r * part + side * size, size), pl.ds(s * slice_, slice_)
            ]

        return view

    def down_view(s):
        def view(r, side=None):
            if r == 0 and s == 0:
                return wd_ref
            if side is None:
                return down_full.at[pl.ds(s * slice_, slice_), pl.ds(r * part, part)]
            size = slice_ // 2
            return down_full.at[
                pl.ds(s * slice_ + side * size, size), pl.ds(r * part, part)
            ]

        return view

    wide = [
        Gather(moves, near, view) for view in (up_view(0), down_view(0), up_view(1), down_view(1))
    ]

    states = [Gather(moves, near, state_view(gathered, h)) for h in range(heads)]
    for h in range(heads):
        total = jnp.zeros((KEY, VAL), F32)
        for b in range(blocks):
            weighed = v_ref[block_rows(b), v_cols(h)].astype(F32) * scale_ref[
                block_rows(b), heads + h : heads + h + 1
            ]
            term = dot_tn(qk_ref[block_rows(b), k_cols(h)], weighed.astype(BF))
            terms[b, pl.ds(h * KEY, KEY), :] = term
            total = across[h][b] * total + term
        gathered[0, pl.ds(h * KEY, KEY), :] = total.astype(BF)
        states[h].first()
    wide[0].first()
    own[5].wait()
    cot_move = moves.go(cot_ref, cot_rows, near["pair"])

    def intra(h):
        @pl.loop(0, blocks)
        def _(b):
            first = pl.multiple_of(b * SPAN, SPAN)
            for tile in range(0, SPAN, 128):
                at = pl.ds(first + tile, 128)
                seen = pl.ds(first, tile + 128)
                scores = dot_nt(qk_ref[at, q_cols(h)], qk_ref[seen, k_cols(h)])
                mask = tile_decay(docs_col, docs_row, rate[h], first, tile, 128)
                probs = (scores * mask).astype(BF)
                retained[at, v_cols(h)] = dot_nn(probs, v_ref[seen, v_cols(h)])

    def finish_head(h):
        first = jnp.zeros((KEY, VAL), F32)
        for r in range(8):
            first = first + fold[h][r] * gathered[r, pl.ds(h * KEY, KEY), :].astype(F32)
        for b in range(blocks):
            folded[b] = first.astype(BF)
            states_out[pl.ds((h * blocks + b) * KEY, KEY), :] = first.astype(BF)
            first = across[h][b] * first + terms[b, pl.ds(h * KEY, KEY), :]

        @pl.loop(0, group_rows // 128)
        def _(i):
            at = pl.ds(pl.multiple_of(i * 128, 128), 128)
            b = lax.div(i, SPAN // 128)
            cross = dot_nn(qk_ref[at, q_cols(h)], folded[b])
            values = retained[at, v_cols(h)] + scale_ref[at, h : h + 1] * cross
            mean = jnp.mean(values, axis=-1, keepdims=True)
            centred = values - mean
            inverse = lax.rsqrt(jnp.mean(centred * centred, axis=-1, keepdims=True) + EPS)
            unit = centred * inverse
            gate = gate_ref[at, v_cols(h)].astype(F32)
            swish = gate / (1.0 + jnp.exp(-gate))
            unit_out[at, v_cols(h)] = unit.astype(BF)
            inverse_out[at, h : h + 1] = inverse
            mixed = (swish * unit * gain_ref[:, h * VAL : (h + 1) * VAL]).astype(BF)
            mixed_out[at, v_cols(h)] = mixed
            mixed_turned[v_cols(h), at] = mixed.T

    for h in range(heads):
        intra(h)
        states[h].second()
    wide[1].first()
    for h in range(heads):
        states[h].third()
    wide[0].second()
    own[3].wait()
    for h in range(heads):
        states[h].done()
        finish_head(h)
    for keep in keeps[:3]:
        keep.start()

    def ring_term(step, side):
        owner = lax.rem(z + 2 * count - 1 - step, count)
        at = pl.ds(pl.multiple_of(owner * rows, rows), rows)

        @pl.loop(side * (width // 512), (side + 1) * (width // 512))
        def _(i):
            to = pl.ds(pl.multiple_of(i * 256, 256), 256)
            held[:, to] = dot_nn(mixed_out[at, :], out_weights[:, to])

    ring = {}
    half = width // 2

    def ring_send(step, side):
        at = pl.ds(side * half, half)
        value = held[:, at]
        if step:
            ring[step - 1, side].wait_recv()
            value = value + ring_in[step - 1, :, at].astype(F32)
        ring_out[step, :, at] = value.astype(BF)
        ring[step, side] = moves.go(
            ring_out.at[step, :, at], ring_in.at[step, :, at], near["up"]
        )

    own[2].wait()
    for side in range(2):
        ring_term(0, side)
        ring_send(0, side)
    wide[1].second()
    ring_term(1, 0)
    ring_term(1, 1)
    far_up.wait_recv()
    wide[2].first()
    wide[0].third()
    ring_send(1, 0)
    far_down.wait_recv()
    wide[3].first()
    wide[1].third()
    ring_send(1, 1)
    ring_term(2, 0)
    ring_term(2, 1)
    wide[2].second()
    ring_send(2, 0)
    wide[3].second()
    ring_send(2, 1)
    ring_term(3, 0)
    ring_term(3, 1)
    wide[2].third()
    wide[3].third()
    own[4].wait()
    cot_move.wait_recv()
    for ref, first in ((cot_ref, 0), (cot_rows, rows)):
        for r, place in enumerate(xor_places(tok)):
            cot_pair[pl.ds(first, rows), pl.ds(r * part, part)] = ref[
                :, pl.ds(pl.multiple_of(place * part, part), part)
            ]
    keeps[3].start()
    for side in range(2):
        ring[2, side].wait_recv()
        for n in range(4):
            r = side * 4 + n
            place = xor_places(tok)[r]
            at = pl.ds(r * part, part)
            values = tok_ref[:, pl.ds(pl.multiple_of(place * part, part), part)].astype(F32)
            resid_out[:, at] = values + held[:, at] + ring_in[2, :, at].astype(F32)
    for gather in wide:
        gather.done()
    own[0].wait()
    own[1].wait()
    for keep in keeps:
        keep.wait()
    moves.finish()


def retain(
    doc_lengths, head_order, gain, qk, v, gate, tokens, out_full, cotangent, w_up, w_down
):
    rows, width = tokens.shape
    count = lax.axis_size("head")
    group_rows = rows * count
    heads = v.shape[1] // VAL
    blocks = group_rows // SPAN
    wide = 2 * w_up.shape[1]
    moves = 3 + (4 + heads) * 8 + 6
    struct = jax.ShapeDtypeStruct
    kept = (
        struct(v.shape, BF),
        struct((heads * blocks * KEY, VAL), BF),
        struct((2 * rows, width), BF),
        struct((heads * VAL, group_rows), BF),
    )
    return pl.pallas_call(
        retain_kernel,
        out_shape=(
            struct((rows, width), F32),
            struct((group_rows, heads), F32),
            *kept,
            struct((width, wide), BF),
            struct((wide, width), BF),
        ),
        in_specs=[SMEM] * 2 + [VMEM] * 5 + [ANY] * 4,
        out_specs=[VMEM] * 2 + [ANY] * 6,
        scratch_shapes=[
            pltpu.VMEM(gate.shape, BF),
            *[pltpu.VMEM(tokens.shape, BF)] * 3,
            *[pltpu.VMEM(array.shape, BF) for array in kept],
            pltpu.VMEM(v.shape, BF),
            pltpu.VMEM(out_full.shape, BF),
            pltpu.VMEM((group_rows, heads * VAL), F32),
            pltpu.VMEM((blocks, heads * KEY, VAL), F32),
            pltpu.VMEM((blocks, KEY, VAL), BF),
            pltpu.VMEM((8, heads * KEY, VAL), BF),
            pltpu.VMEM((rows, width), F32),
            pltpu.VMEM((3, rows, width), BF),
            pltpu.VMEM((3, rows, width), BF),
            pltpu.VMEM((group_rows, 1), jnp.int32),
            pltpu.VMEM((8, group_rows), jnp.int32),
            pltpu.VMEM((group_rows, 2 * heads), F32),
            pltpu.SemaphoreType.DMA((moves,)),
            pltpu.SemaphoreType.DMA((moves,)),
            pltpu.SemaphoreType.DMA((11,)),
        ],
        compiler_params=pltpu.CompilerParams(
            collective_id=2, has_side_effects=True, vmem_limit_bytes=LIMIT
        ),
        cost_estimate=pl.CostEstimate(
            flops=12 << 30, bytes_accessed=40 << 20, transcendentals=0
        ),
    )(
        doc_lengths, head_order, gain[None, :], qk, v, w_up, w_down, gate, tokens, cotangent,
        out_full,
    )


def feed_kernel(
    resid_ref,
    gain_ref,
    cot_ref,
    up_ref,
    down_ref,
    gain_out,
    up_own,
    up_far,
    down_own,
    down_far,
    layer_hbm,
    far_hbm,
    resid_hbm,
    branch,
    layer_out,
    far_out,
    resid_grad,
    up,
    down,
    lifted,
    cot,
    hidden,
    turned,
    pre,
    back_out,
    back_in,
    odd_out_d,
    odd_in_d,
    odd_out_u,
    odd_in_u,
    far_out_d,
    far_in_d,
    far_out_u,
    far_in_u,
    near_out_d,
    near_in_d,
    near_out_u,
    near_in_u,
    up_sum,
    down_sum,
    gain,
    send,
    recv,
    load_sem,
    free_sem,
):
    near = peers()
    z = lax.axis_index("head")
    count = lax.axis_size("head")
    rows, width = resid_ref.shape
    part = width // 8
    side_rows = rows // 2
    wide = up.shape[1]
    slice_ = wide // 2
    loads = [
        pltpu.make_async_copy(cot_ref, cot, load_sem.at[0]),
        pltpu.make_async_copy(up_ref, up, load_sem.at[1]),
        pltpu.make_async_copy(down_ref, down, load_sem.at[2]),
    ]
    for load in loads:
        load.start()
    reached = everyone()
    greet(*reached)
    gain[...] = arranged(gain_ref, lax.axis_index("tok"))
    moves = Moves(send, recv)
    size = 16

    pairs = []
    for side in range(2):

        @pl.loop(0, side_rows // size)
        def _(i):
            at = pl.ds(pl.multiple_of(side * side_rows + i * size, size), size)
            values = resid_ref[at, :]
            mean = jnp.mean(values, axis=-1, keepdims=True)
            centred = values - mean
            inverse = lax.rsqrt(jnp.mean(centred * centred, axis=-1, keepdims=True) + EPS)
            lifted[at, :] = (centred * inverse * gain[...]).astype(BF)

        if side == 0:
            greeted(*reached)
        pairs.append(
            moves.go(
                lifted.at[pl.ds(side * side_rows, side_rows), :],
                lifted.at[pl.ds(rows + side * side_rows, side_rows), :],
                near["pair"],
            )
        )

    def feed(first, number):
        @pl.loop(0, wide // 256)
        def _(i):
            to = pl.ds(pl.multiple_of(i * 256, 256), 256)
            at = pl.ds(first, number)
            hidden_pre = dot_nn(lifted[at, :], up[:, to])
            hidden_grad = dot_nt(cot[at, :], down[to, :])
            phi = 0.5 * (1.0 + lax.erf(hidden_pre * SQRT_HALF))
            made = (hidden_pre * phi).astype(BF)
            hidden[at, to] = made
            turned[to, at] = made.T
            slope = phi + hidden_pre * jnp.exp(-0.5 * hidden_pre * hidden_pre) * INV_ROOT_TWO_PI
            pre[at, to] = (hidden_grad * slope).astype(BF)

    for load in loads:
        load.wait()
    feed(0, rows)
    backs = []
    for side in range(2):
        if side:

            @pl.loop(0, width // 256)
            def _(i):
                to = pl.ds(pl.multiple_of(i * 256, 256), 256)
                resid_grad[:, to] = dot_nt(pre[pl.ds(0, rows), :], up[to, :])

        pairs[side].wait_recv()
        feed(rows + side * side_rows, side_rows)

        @pl.loop(0, width // 256)
        def _(i):
            to = pl.ds(pl.multiple_of(i * 256, 256), 256)
            found = dot_nt(pre[pl.ds(rows + side * side_rows, side_rows), :], up[to, :])
            back_out[pl.ds(side * side_rows, side_rows), to] = found.astype(BF)

        at = pl.ds(side * side_rows, side_rows)
        backs.append(moves.go(back_out.at[at, :], back_in.at[at, :], near["pair"]))

    def down_term(s):
        def term(r):
            return dot_nn(turned[pl.ds(s * slice_, slice_), :], cot[:, r * part : (r + 1) * part])

        return term

    def up_term(s):
        def term(r):
            return dot_tn(
                lifted[:, r * part : (r + 1) * part], pre[:, s * slice_ : (s + 1) * slice_]
            )

        return term

    down_sets = [
        (odd_out_d, odd_in_d, far_out_d, far_in_d.at[s], near_out_d, near_in_d.at[s])
        for s in range(2)
    ]
    up_sets = [
        (odd_out_u, odd_in_u, far_out_u, far_in_u.at[s], near_out_u, near_in_u.at[s])
        for s in range(2)
    ]
    sums = [
        Scatter(moves, near, down_term(0), down_sets[0], down_own),
        Scatter(moves, near, up_term(0), up_sets[0], up_own),
    ]
    sums += [
        Scatter(moves, near, down_term(1), down_sets[1], down_sum, sums[0], free_sem.at[0]),
        Scatter(moves, near, up_term(1), up_sets[1], up_sum, sums[1], free_sem.at[1]),
    ]
    sums[0].frees = free_sem.at[0]
    sums[1].frees = free_sem.at[1]

    ring = {}

    def shard(step, side):
        owner = lax.rem(z - step + count, count)
        first = pl.multiple_of(owner * rows + side * side_rows, side_rows)
        return branch.at[pl.ds(first, side_rows), :]

    def pass_on(step, side):
        if step:
            ring[step - 1, side].wait_recv()
        if step < count - 1:
            here = back_in.at[pl.ds(side * side_rows, side_rows), :] if step == 0 else shard(step, side)
            ring[step, side] = moves.go(here, shard(step, side), near["up"])

    def norm_back(side):
        backs[side].wait_recv()

        def block(i, total):
            at = pl.ds(pl.multiple_of(side * side_rows + i * size, size), size)
            values = resid_ref[at, :]
            mean = jnp.mean(values, axis=-1, keepdims=True)
            centred = values - mean
            inverse = lax.rsqrt(jnp.mean(centred * centred, axis=-1, keepdims=True) + EPS)
            unit = centred * inverse
            grad = resid_grad[at, :] + back_in[at, :].astype(F32)
            scaled = grad * gain[...]
            first = jnp.mean(scaled, axis=-1, keepdims=True)
            second = jnp.mean(scaled * unit, axis=-1, keepdims=True)
            found = cot[at, :].astype(F32) + inverse * (scaled - first - unit * second)
            resid_grad[at, :] = found
            back_in[at, :] = found.astype(BF)
            return total + jnp.sum(grad * unit, axis=0, keepdims=True)

        total = lax.fori_loop(0, side_rows // size, block, jnp.zeros((1, width), F32))
        gain_out[pl.ds(side, 1), :] = total

    norm_back(0)
    pass_on(0, 0)
    for i in (3, 1, 2, 0):
        sums[0].odd(i)
    for i in (3, 1):
        sums[1].odd(i)
    norm_back(1)
    pass_on(0, 1)
    mine = pltpu.make_async_copy(
        back_in, branch.at[pl.ds(pl.multiple_of(z * rows, rows), rows), :], load_sem.at[3]
    )
    mine.start()
    keeps = [pltpu.make_async_copy(resid_grad, resid_hbm, load_sem.at[4])]
    keeps[0].start()
    sums[0].far()
    for i in (2, 0):
        sums[1].odd(i)
    sums[1].far()
    pass_on(1, 0)
    sums[0].close()
    for i in (3, 1, 2, 0):
        sums[2].odd(i)
    sums[2].far()
    pass_on(1, 1)
    sums[1].close()
    for i in (3, 1, 2, 0):
        sums[3].odd(i)
    sums[3].far()
    pass_on(2, 0)
    sums[2].close()

    @pl.loop(0, width // 256)
    def _(i):
        to = pl.ds(pl.multiple_of(i * 256, 256), 256)
        layer_out[:, to] = resid_ref[:, to] + dot_nn(hidden[pl.ds(0, rows), :], down[:, to])

    keeps.append(pltpu.make_async_copy(layer_out, layer_hbm, load_sem.at[5]))
    keeps[-1].start()
    pass_on(2, 1)

    @pl.loop(0, width // 256)
    def _(i):
        to = pl.ds(pl.multiple_of(i * 256, 256), 256)
        far_out[:, to] = dot_nn(hidden[pl.ds(rows, rows), :], down[:, to]).astype(BF)

    keeps.append(pltpu.make_async_copy(far_out, far_hbm, load_sem.at[6]))
    keeps[-1].start()
    sums[0].done()
    sums[1].done()
    sums[3].close()
    pass_on(3, 0)
    sums[2].done()
    down_far[...] = down_sum[...].astype(BF)
    pass_on(3, 1)
    sums[3].done()
    up_far[...] = up_sum[...].astype(BF)
    mine.wait()
    for keep in keeps:
        keep.wait()
    moves.finish()


def feed_forward(resid, gain, cot_pair, up_full, down_full):
    rows, width = resid.shape
    count = lax.axis_size("head")
    part = width // 8
    wide = up_full.shape[1]
    slice_ = wide // 2
    moves = 4 + 4 * 8 + 6
    struct = jax.ShapeDtypeStruct
    down_piece = (slice_, part)
    up_piece = (part, slice_)

    def sets(piece):
        half = (piece[0] // 2, piece[1])
        return [
            pltpu.VMEM(piece, BF),
            pltpu.VMEM((2, 2) + half, BF),
        ]

    def nears(piece):
        return [pltpu.VMEM((2,) + piece, BF), pltpu.VMEM((2, 2) + piece, BF)]

    def odds(piece):
        return [pltpu.VMEM((4,) + piece, BF)] * 2

    return pl.pallas_call(
        feed_kernel,
        out_shape=(
            struct((8, width), F32),
            struct(up_piece, F32),
            struct(up_piece, BF),
            struct(down_piece, F32),
            struct(down_piece, BF),
            struct((rows, width), F32),
            struct((rows, width), BF),
            struct((rows, width), F32),
            struct((count * rows, width), BF),
        ),
        in_specs=[VMEM] * 2 + [ANY] * 3,
        out_specs=[VMEM] * 5 + [ANY] * 4,
        scratch_shapes=[
            pltpu.VMEM((rows, width), F32),
            pltpu.VMEM((rows, width), BF),
            pltpu.VMEM((rows, width), F32),
            pltpu.VMEM((width, wide), BF),
            pltpu.VMEM((wide, width), BF),
            pltpu.VMEM((2 * rows, width), BF),
            pltpu.VMEM((2 * rows, width), BF),
            pltpu.VMEM((2 * rows, wide), BF),
            pltpu.VMEM((wide, 2 * rows), BF),
            pltpu.VMEM((2 * rows, wide), BF),
            pltpu.VMEM((rows, width), BF),
            pltpu.VMEM((rows, width), BF),
            *odds(down_piece),
            *odds(up_piece),
            *sets(down_piece),
            *sets(up_piece),
            *nears(down_piece),
            *nears(up_piece),
            pltpu.VMEM(up_piece, F32),
            pltpu.VMEM(down_piece, F32),
            pltpu.VMEM((1, width), F32),
            pltpu.SemaphoreType.DMA((moves,)),
            pltpu.SemaphoreType.DMA((moves,)),
            pltpu.SemaphoreType.DMA((7,)),
            pltpu.SemaphoreType.REGULAR((2,)),
        ],
        compiler_params=pltpu.CompilerParams(
            collective_id=3, has_side_effects=True, vmem_limit_bytes=LIMIT
        ),
        cost_estimate=pl.CostEstimate(
            flops=26 << 30, bytes_accessed=40 << 20, transcendentals=0
        ),
    )(resid, gain[None, :], cot_pair, up_full, down_full)


def recall_kernel(
    lengths_ref,
    order_ref,
    gain_ref,
    wo_hbm,
    branch_hbm,
    gate_hbm,
    unit_hbm,
    inverse_hbm,
    qk_hbm,
    v_hbm,
    turned_hbm,
    states_hbm,
    cos_hbm,
    sin_hbm,
    own_hbm,
    far_ref,
    up_ref,
    down_ref,
    wo_grad,
    gains,
    layer_out,
    grads_out,
    up_in,
    down_in,
    out_weights,
    branch,
    gate_ref,
    unit_ref,
    inverse_ref,
    qk_ref,
    v_ref,
    turned_ref,
    states_ref,
    cos_ref,
    sin_ref,
    own_ref,
    far_in,
    grads,
    docs_col,
    docs_row,
    scale_ref,
    back,
    terms,
    gathered,
    folded,
    dqk,
    dv,
    odd_out,
    odd_in,
    out_far,
    in_far,
    out_near,
    in_near,
    send,
    recv,
    load_sem,
    keep_sem,
):
    near = peers()
    tok = lax.axis_index("tok")
    group_rows, cols = v_ref.shape
    heads = cols // VAL
    blocks = group_rows // SPAN
    width = branch.shape[1]
    part = width // 8
    loads = [
        pltpu.make_async_copy(source, target, load_sem.at[n])
        for n, (source, target) in enumerate(
            (
                (wo_hbm, out_weights),
                (branch_hbm, branch),
                (gate_hbm, gate_ref),
                (unit_hbm, unit_ref),
                (inverse_hbm, inverse_ref),
                (qk_hbm, qk_ref),
                (v_hbm, v_ref),
                (turned_hbm, turned_ref),
                (states_hbm, states_ref),
                (cos_hbm, cos_ref),
                (sin_hbm, sin_ref),
                (own_hbm, own_ref),
            )
        )
    ]
    for load in loads:
        load.start()
    reached = everyone()
    greet(*reached)
    rate = decays(order_ref, heads)
    across = block_scales(lengths_ref, rate, group_rows, scale_ref, docs_col)
    docs_row[...] = row_docs(lengths_ref, group_rows)
    fold = group_weights(lengths_ref, rate, group_rows, True)
    greeted(*reached)
    moves = Moves(send, recv)
    swaps = [
        moves.go(far_ref, far_in, near["pair"]),
        moves.go(up_ref, up_in, near["cross"]),
        moves.go(down_ref, down_in, near["cross"]),
    ]

    def block_rows(b):
        return pl.ds(pl.multiple_of(b * SPAN, SPAN), SPAN)

    def q_cols(h):
        return pl.ds(h * KEY, KEY)

    def k_cols(h):
        return pl.ds((heads + h) * KEY, KEY)

    def v_cols(h):
        return pl.ds(h * VAL, VAL)

    for load in loads[:5]:
        load.wait()

    first_gate = 2 * heads * KEY + cols
    states = [Gather(moves, near, state_view(gathered, h)) for h in range(heads)]
    gains[...] = jnp.zeros_like(gains)
    kept = [
        pltpu.make_async_copy(
            grads.at[:, pl.ds(first_gate, cols)],
            grads_out.at[:, pl.ds(first_gate, cols)],
            keep_sem.at[0],
        ),
        pltpu.make_async_copy(
            grads.at[:, pl.ds(0, first_gate)], grads_out.at[:, pl.ds(0, first_gate)], keep_sem.at[1]
        ),
    ]
    for h in range(heads):
        gain = gain_ref[:, h * VAL : (h + 1) * VAL]

        def tile_back(i, total):
            at = pl.ds(pl.multiple_of(i * 128, 128), 128)
            grad = dot_nt(branch[at, :], out_weights[v_cols(h), :]).astype(BF).astype(F32)
            gate = gate_ref[at, v_cols(h)].astype(F32)
            sigma = 1.0 / (1.0 + jnp.exp(-gate))
            swish = gate * sigma
            unit = unit_ref[at, v_cols(h)].astype(F32)
            grads[at, pl.ds(first_gate + h * VAL, VAL)] = (
                grad * unit * gain * (sigma + swish * (1.0 - sigma))
            ).astype(BF)
            inner = grad * swish
            scaled = inner * gain
            first = jnp.mean(scaled, axis=-1, keepdims=True)
            second = jnp.mean(scaled * unit, axis=-1, keepdims=True)
            back[at, v_cols(h)] = (
                inverse_ref[at, h : h + 1] * (scaled - first - unit * second)
            ).astype(BF)
            return total + jnp.sum(inner * unit, axis=0, keepdims=True)

        gains[pl.ds(0, 1), v_cols(h)] = lax.fori_loop(
            0, group_rows // 128, tile_back, jnp.zeros((1, VAL), F32)
        )
        if h == 0:
            for load in loads[5:]:
                load.wait()
        total = jnp.zeros((KEY, VAL), F32)
        for b in reversed(range(blocks)):
            weighed = back[block_rows(b), v_cols(h)].astype(F32) * scale_ref[
                block_rows(b), h : h + 1
            ]
            term = dot_tn(qk_ref[block_rows(b), q_cols(h)], weighed.astype(BF))
            terms[b, pl.ds(h * KEY, KEY), :] = term
            total = across[h][b] * total + term
        gathered[0, pl.ds(h * KEY, KEY), :] = total.astype(BF)
        states[h].first()
    kept[0].start()

    def out_term(r):
        return dot_nn(turned_ref[...], branch[:, r * part : (r + 1) * part])

    outward = Scatter(
        moves, near, out_term, (odd_out, odd_in, out_far, in_far, out_near, in_near), wo_grad
    )

    def intra(h):
        @pl.loop(0, blocks)
        def _(b):
            first = pl.multiple_of(b * SPAN, SPAN)
            for tile in range(SPAN - 128, -1, -128):
                at = pl.ds(first + tile, 128)
                seen = pl.ds(first, tile + 128)
                mask = tile_decay(docs_col, docs_row, rate[h], first, tile, 128)
                query = qk_ref[at, q_cols(h)]
                key = qk_ref[seen, k_cols(h)]
                ret = back[at, v_cols(h)]
                probs = (dot_nt(query, key) * mask).astype(BF)
                score = (dot_nt(ret, v_ref[seen, v_cols(h)]) * mask).astype(BF)
                dqk[at, q_cols(h)] = dot_nn(score, key)
                to_keys = dot_tn(score, query)
                to_values = dot_tn(probs, ret)
                if tile == SPAN - 128:
                    dqk[seen, k_cols(h)] = to_keys
                    dv[seen, v_cols(h)] = to_values
                else:
                    dqk[seen, k_cols(h)] += to_keys
                    dv[seen, v_cols(h)] += to_values

    def finish_head(h):
        later = jnp.zeros((KEY, VAL), F32)
        for r in range(8):
            later = later + fold[h][r] * gathered[r, pl.ds(h * KEY, KEY), :].astype(F32)
        for b in reversed(range(blocks)):
            folded[b] = later.astype(BF)
            later = across[h][b] * later + terms[b, pl.ds(h * KEY, KEY), :]

        @pl.loop(0, group_rows // 128)
        def _(i):
            at = pl.ds(pl.multiple_of(i * 128, 128), 128)
            b = lax.div(i, SPAN // 128)
            reach = scale_ref[at, h : h + 1]
            leave = scale_ref[at, heads + h : heads + h + 1]
            state = states_ref[pl.ds(pl.multiple_of((h * blocks + b) * KEY, KEY), KEY), :]
            cosine, sine = cos_ref[at, :], sin_ref[at, :]
            for found, to in (
                (
                    dqk[at, q_cols(h)] + reach * dot_nt(back[at, v_cols(h)], state),
                    q_cols(h),
                ),
                (
                    dqk[at, k_cols(h)] + leave * dot_nt(v_ref[at, v_cols(h)], folded[b]),
                    k_cols(h),
                ),
            ):
                one, two = found[:, : KEY // 2], found[:, KEY // 2 :]
                grads[at, to] = jnp.concatenate(
                    [one * cosine + two * sine, two * cosine - one * sine], axis=1
                ).astype(BF)
            found = dv[at, v_cols(h)] + leave * dot_nn(qk_ref[at, k_cols(h)], folded[b])
            grads[at, pl.ds(2 * heads * KEY + h * VAL, VAL)] = found.astype(BF)

    intra(0)
    states[0].second()
    for i in (3, 1, 2, 0):
        outward.odd(i)
    for h in range(1, heads):
        states[h].second()
        intra(h)
    outward.far()
    states[0].third()
    for h in range(1, heads):
        states[h].third()
    states[0].done()
    finish_head(0)
    outward.close()
    for h in range(1, heads):
        states[h].done()
        finish_head(h)
    kept[1].start()
    swaps[0].wait_recv()
    for r, place in enumerate(xor_places(tok)):
        at = pl.ds(r * part, part)
        layer_out[:, pl.ds(pl.multiple_of(place * part, part), part)] = (
            own_ref[:, at] + far_in[:, at].astype(F32)
        ).astype(BF)
    outward.done()
    for swap_ in swaps[1:]:
        swap_.wait_recv()
    for copy in kept:
        copy.wait()
    moves.finish()


def recall(
    doc_lengths, head_order, gain, qk, v, gate, unit, inverse, states, cosine, sine, mixed_turned,
    branch, out_full, layer_own, far_out, up_far, down_far,
):
    group_rows, cols = v.shape
    heads = cols // VAL
    blocks = group_rows // SPAN
    width = branch.shape[1]
    part = width // 8
    piece = (cols, part)
    moves = 3 + 8 + 8 * heads
    struct = jax.ShapeDtypeStruct
    loaded = (
        out_full, branch, gate, unit, inverse, qk, v, mixed_turned, states, cosine, sine, layer_own
    )
    return pl.pallas_call(
        recall_kernel,
        out_shape=(
            struct(piece, F32),
            struct((8, cols), F32),
            struct(far_out.shape, BF),
            struct((group_rows, 3 * cols), BF),
            struct(up_far.shape, BF),
            struct(down_far.shape, BF),
        ),
        in_specs=[SMEM] * 2 + [VMEM] + [ANY] * 15,
        out_specs=[VMEM] * 3 + [ANY] * 3,
        scratch_shapes=[
            *[pltpu.VMEM(array.shape, array.dtype) for array in loaded],
            pltpu.VMEM(far_out.shape, BF),
            pltpu.VMEM((group_rows, 3 * cols), BF),
            pltpu.VMEM((group_rows, 1), jnp.int32),
            pltpu.VMEM((8, group_rows), jnp.int32),
            pltpu.VMEM((group_rows, 2 * heads), F32),
            pltpu.VMEM(v.shape, BF),
            pltpu.VMEM((blocks, heads * KEY, VAL), F32),
            pltpu.VMEM((8, heads * KEY, VAL), BF),
            pltpu.VMEM((blocks, KEY, VAL), BF),
            pltpu.VMEM((group_rows, 2 * heads * KEY), F32),
            pltpu.VMEM((group_rows, cols), F32),
            pltpu.VMEM((4,) + piece, BF),
            pltpu.VMEM((4,) + piece, BF),
            pltpu.VMEM(piece, BF),
            pltpu.VMEM((2, cols // 2, part), BF),
            pltpu.VMEM((2,) + piece, BF),
            pltpu.VMEM((2,) + piece, BF),
            pltpu.SemaphoreType.DMA((moves,)),
            pltpu.SemaphoreType.DMA((moves,)),
            pltpu.SemaphoreType.DMA((len(loaded),)),
            pltpu.SemaphoreType.DMA((2,)),
        ],
        compiler_params=pltpu.CompilerParams(
            collective_id=4, has_side_effects=True, vmem_limit_bytes=LIMIT
        ),
        cost_estimate=pl.CostEstimate(
            flops=20 << 30, bytes_accessed=40 << 20, transcendentals=0
        ),
    )(doc_lengths, head_order, gain[None, :], *loaded, far_out, up_far, down_far)


def norm_forward(values, gain):
    mean = jnp.mean(values, axis=-1, keepdims=True)
    centred = values - mean
    inverse = lax.rsqrt(jnp.mean(centred * centred, axis=-1, keepdims=True) + EPS)
    unit = centred * inverse
    return (unit * gain, unit, inverse)


def norm_backward(grad_out, unit, inverse, gain):
    scaled = grad_out * gain
    first = jnp.mean(scaled, axis=-1, keepdims=True)
    second = jnp.mean(scaled * unit, axis=-1, keepdims=True)
    return (inverse * (scaled - first - unit * second), jnp.sum(grad_out * unit, axis=0))


def doc_index(row_ids, starts):
    return jnp.sum((starts[None, :] <= row_ids[:, None]).astype(jnp.int32), axis=1) - 1


def doc_position(row_ids, starts):
    first = jnp.max(jnp.where(starts[None, :] <= row_ids[:, None], starts[None, :], 0), axis=1)
    return row_ids - first


def angles(position, half):
    freq = jnp.exp(-jnp.log(10000.0) * jnp.arange(half, dtype=F32) / half)
    turn = position.astype(F32)[:, None] * freq[None, :]
    return (jnp.cos(turn), jnp.sin(turn))


def rotate(values, cosine, sine):
    half = values.shape[-1] // 2
    first, second = (values[..., :half], values[..., half:])
    return jnp.concatenate(
        [first * cosine - second * sine, first * sine + second * cosine], axis=-1
    )


def unrotate(grads, cosine, sine):
    return rotate(grads, cosine, -sine)


def span_masks(doc_ids, before, log_decay):
    size = doc_ids.shape[0]
    place = jnp.arange(size, dtype=F32)
    lag = place[:, None] - place[None, :]
    same = (doc_ids[:, None] == doc_ids[None, :]) & (lag >= 0)
    decay = jnp.where(same, jnp.exp(jnp.maximum(lag, 0.0) * log_decay), 0.0)
    reach = jnp.where(doc_ids == before, jnp.exp((place + 1.0) * log_decay), 0.0)[:, None]
    leave = jnp.where(doc_ids == doc_ids[-1], jnp.exp((size - 1.0 - place) * log_decay), 0.0)[
        :, None
    ]
    across = jnp.where(doc_ids[-1] == before, jnp.exp(size * log_decay), 0.0)
    return (decay, reach, leave, across)


def gelu_slope(hidden_pre):
    return (
        0.5 * (1.0 + lax.erf(hidden_pre * SQRT_HALF))
        + hidden_pre * jnp.exp(-0.5 * hidden_pre * hidden_pre) * INV_ROOT_TWO_PI
    )


def plain(
    tokens,
    cotangent,
    doc_lengths,
    head_order,
    norm_gain,
    w_query,
    w_key,
    w_value,
    w_gate,
    group_gain,
    w_out,
    ffn_gain,
    w_up,
    w_down,
):
    heads = w_query.shape[1] // KEY
    head_count = lax.axis_size("head")
    tok_count = lax.axis_size("tok")
    z = lax.axis_index("head")
    tok = lax.axis_index("tok")
    rows = tokens.shape[0]
    group_rows = rows * head_count
    blocks = group_rows // SPAN
    width = tokens.shape[1]
    part = width // tok_count

    tokens_f = reorder(tokens).astype(F32)
    cot_own = reorder(cotangent)
    gain1 = reorder(norm_gain)
    gain2 = reorder(ffn_gain)
    normed1, unit1, inverse1 = norm_forward(tokens_f, gain1)
    qk = w_query.shape[1]
    vg = w_value.shape[1]
    up_two = jnp.concatenate([w_up, swap(w_up, "head", 2)], axis=1)
    down_two = jnp.concatenate([w_down, swap(w_down, "head", 2)], axis=0)
    up_full = tok_gather(up_two, 0)
    down_full = tok_gather(down_two, 1)
    cot_pair = jnp.concatenate([cot_own, swap(cot_own, "head", 1)], axis=0)

    ends = jnp.cumsum(doc_lengths)
    starts = ends - doc_lengths
    first_row = tok * group_rows
    row_ids = first_row + jnp.arange(group_rows, dtype=jnp.int32)
    doc_ids = doc_index(row_ids, starts)
    previous = doc_index(jnp.reshape(first_row - 1, (1,)), starts)[0]
    group_last = doc_index((jnp.arange(tok_count, dtype=jnp.int32) + 1) * group_rows - 1, starts)
    cosine, sine = angles(doc_position(row_ids, starts), KEY // 2)
    ranks = lax.dynamic_slice_in_dim(head_order, z * heads, heads)
    log_decay = jnp.log1p(-jnp.exp2(-(5.0 + ranks.astype(F32))))

    group = head_gather(normed1.astype(BF))
    qkvg_full = tok_gather(jnp.concatenate([w_query, w_key, w_value, w_gate], axis=1), 0)
    out_full = tok_gather(w_out, 1)
    projected = mm(group, qkvg_full)
    qk_rows = jnp.concatenate(
        [
            rotate(projected[:, h * KEY : (h + 1) * KEY], cosine, sine).astype(BF)
            for h in range(2 * heads)
        ],
        axis=1,
    )
    v_rows = projected[:, 2 * qk : 2 * qk + vg].astype(BF)
    gate = projected[:, 2 * qk + vg :]

    def head_of(array, head, size):
        return array[:, head * size : (head + 1) * size]

    def block_of(array, block):
        return array[block * SPAN : (block + 1) * SPAN]

    q, k, v, masks = [], [], [], []
    for h in range(heads):
        q.append(head_of(qk_rows, h, KEY))
        k.append(head_of(qk_rows, heads + h, KEY))
        v.append(head_of(v_rows, h, VAL))
        masks.append(
            [
                span_masks(
                    block_of(doc_ids, b),
                    previous if b == 0 else doc_ids[b * SPAN - 1],
                    log_decay[h],
                )
                for b in range(blocks)
            ]
        )

    group_order = jnp.arange(tok_count, dtype=jnp.int32)

    def weigh(lag, last, h):
        return jnp.where(
            (lag >= 0) & (group_last == last),
            jnp.exp(jnp.maximum(lag, 0).astype(F32) * group_rows * log_decay[h]),
            0.0,
        )

    ends_of = []
    added = []
    for h in range(heads):
        state = jnp.zeros((KEY, VAL), F32)
        terms = []
        for b in range(blocks):
            term = mm_tn(block_of(k[h], b), (block_of(v[h], b) * masks[h][b][2]).astype(BF))
            terms.append(term)
            state = masks[h][b][3] * state + term
        added.append(terms)
        ends_of.append(state.astype(BF))
    all_states = lax.all_gather(jnp.concatenate(ends_of, axis=0), "tok", axis=0)
    lag = tok - 1 - group_order
    states = []
    retained = []
    for h in range(heads):
        weights = weigh(lag, previous, h)
        state = jnp.sum(
            all_states[:, h * KEY : (h + 1) * KEY].astype(F32) * weights[:, None, None], axis=0
        )
        mine = []
        outs = []
        for b in range(blocks):
            mine.append(state.astype(BF))
            qb, kb, vb = block_of(q[h], b), block_of(k[h], b), block_of(v[h], b)
            decay, reach, leave, across = masks[h][b]
            probs = (mm_nt(qb, kb) * decay).astype(BF)
            outs.append(mm(probs, vb) + reach * mm(qb, mine[-1]))
            state = across * state + added[h][b]
        states.append(mine)
        retained.append(jnp.concatenate(outs, axis=0))

    mixed_parts, unit_g, inverse_g, grouped, swish, sigma = [], [], [], [], [], []
    for h in range(heads):
        g, u, i = norm_forward(retained[h], head_of(group_gain[None, :], h, VAL))
        gate_h = head_of(gate, h, VAL)
        s = jax.nn.sigmoid(gate_h)
        unit_g.append(u)
        inverse_g.append(i)
        grouped.append(g)
        sigma.append(s)
        swish.append(gate_h * s)
        mixed_parts.append((swish[-1] * g).astype(BF))
    mixed = jnp.concatenate(mixed_parts, axis=1)

    out_sum = head_scatter(lambda i: mm(rows_of(mixed, i, rows), out_full))
    resid = tokens_f + out_sum
    normed2, unit2, inverse2 = norm_forward(resid, gain2)
    lifted2 = normed2.astype(BF)
    lifted2_pair = jnp.concatenate([lifted2, swap(lifted2, "head", 1)], axis=0)
    hidden_pre = mm(lifted2_pair, up_full)
    hidden = jax.nn.gelu(hidden_pre, approximate=False).astype(BF)
    hidden_grad = mm_nt(cot_pair, down_full)
    pre_grad = (hidden_grad * gelu_slope(hidden_pre)).astype(BF)
    far_grad = mm_nt(pre_grad[rows:], up_full).astype(BF)
    lifted2_grad = mm_nt(pre_grad[:rows], up_full) + swap(far_grad, "head", 1).astype(F32)
    resid_part, ffn_gain_local = norm_backward(lifted2_grad, unit2, inverse2, gain2)
    resid_grad = cot_own.astype(F32) + resid_part
    branch_own = resid_grad.astype(BF)
    branch = head_gather(branch_own)

    far_out = mm(hidden[rows:], down_full).astype(BF)
    layer_out = reorder(
        (resid + mm(hidden[:rows], down_full) + swap(far_out, "head", 1).astype(F32)).astype(BF)
    )

    def piece(array, r):
        return array[:, r * part : (r + 1) * part]

    slots = range(tok_count)
    down_two_grad = tok_scatter([mm_tn(hidden, piece(cot_pair, r)) for r in slots])
    half = down_two_grad.shape[0] // 2
    w_down_grad = down_two_grad[:half] + swap(
        down_two_grad[half:].astype(BF), "head", 2
    ).astype(F32)
    up_two_grad = tok_scatter([mm_tn(piece(lifted2_pair, r), pre_grad) for r in slots])
    half = up_two_grad.shape[1] // 2
    w_up_grad = up_two_grad[:, :half] + swap(
        up_two_grad[:, half:].astype(BF), "head", 2
    ).astype(F32)

    mixed_grad = mm_nt(branch, out_full).astype(BF)
    w_out_grad = tok_scatter([mm_tn(mixed, piece(branch, r)) for r in slots])

    gate_parts, ret_grad, group_gain_parts = [], [], []
    for h in range(heads):
        head_grad = head_of(mixed_grad, h, VAL).astype(F32)
        gate_parts.append(
            (head_grad * grouped[h] * (sigma[h] + swish[h] * (1.0 - sigma[h]))).astype(BF)
        )
        back, gain_term = norm_backward(
            head_grad * swish[h], unit_g[h], inverse_g[h], head_of(group_gain[None, :], h, VAL)
        )
        ret_grad.append(back.astype(BF))
        group_gain_parts.append(gain_term)
    gate_grad = jnp.concatenate(gate_parts, axis=1)
    w_gate_grad = tok_scatter([mm_tn(piece(group, r), gate_grad) for r in slots])

    pending_of, pending_terms = [], []
    for h in range(heads):
        pending = jnp.zeros((KEY, VAL), F32)
        terms = [None] * blocks
        for b in reversed(range(blocks)):
            terms[b] = mm_tn(
                block_of(q[h], b), (block_of(ret_grad[h], b) * masks[h][b][1]).astype(BF)
            )
            pending = masks[h][b][3] * pending + terms[b]
        pending_terms.append(terms)
        pending_of.append(pending.astype(BF))
    all_pending = lax.all_gather(jnp.concatenate(pending_of, axis=0), "tok", axis=0)
    lag_back = group_order - 1 - tok
    shifted_last = doc_index(group_order * group_rows - 1, starts)
    q_parts, k_parts, v_parts = [], [], []
    for h in range(heads):
        weights = jnp.where(
            (lag_back >= 0) & (shifted_last == doc_ids[-1]),
            jnp.exp(jnp.maximum(lag_back, 0).astype(F32) * group_rows * log_decay[h]),
            0.0,
        )
        later = jnp.sum(
            all_pending[:, h * KEY : (h + 1) * KEY].astype(F32) * weights[:, None, None], axis=0
        )
        qg, kg, vg_ = [None] * blocks, [None] * blocks, [None] * blocks
        for b in reversed(range(blocks)):
            qb, kb, vb = block_of(q[h], b), block_of(k[h], b), block_of(v[h], b)
            rb = block_of(ret_grad[h], b)
            decay, reach, leave, across = masks[h][b]
            probs = (mm_nt(qb, kb) * decay).astype(BF)
            score_grad = (mm_nt(rb, vb) * decay).astype(BF)
            later_b = later.astype(BF)
            qg[b] = mm(score_grad, kb) + reach * mm_nt(rb, states[h][b])
            kg[b] = mm_tn(score_grad, qb) + leave * mm_nt(vb, later_b)
            vg_[b] = mm_tn(probs, rb) + leave * mm(kb, later_b)
            later = across * later + pending_terms[h][b]
        q_parts.append(unrotate(jnp.concatenate(qg, axis=0), cosine, sine).astype(BF))
        k_parts.append(unrotate(jnp.concatenate(kg, axis=0), cosine, sine).astype(BF))
        v_parts.append(jnp.concatenate(vg_, axis=0).astype(BF))
    all_grad = jnp.concatenate(q_parts + k_parts + v_parts + [gate_grad], axis=1)
    group_terms = jnp.concatenate(group_gain_parts, axis=0)
    ffn_terms = reorder(ffn_gain_local)
    row_grad = head_scatter(lambda i: mm_nt(rows_of(all_grad, i, rows), qkvg_full))
    input_part, norm_gain_local = norm_backward(row_grad, unit1, inverse1, gain1)
    tokens_grad = reorder(resid_grad + input_part)
    qkv_grad = all_grad[:, : 2 * qk + vg]
    w_qkv_grad = tok_scatter([mm_tn(piece(group, r), qkv_grad) for r in slots])
    w_query_grad = w_qkv_grad[:, :qk]
    w_key_grad = w_qkv_grad[:, qk : 2 * qk]
    w_value_grad = w_qkv_grad[:, 2 * qk :]
    group_gain_grad = sum_small(group_terms, "tok")
    ffn_sum = sum_small(sum_small(ffn_terms, "tok"), "head")
    norm_sum = sum_small(sum_small(reorder(norm_gain_local), "tok"), "head")
    return (
        layer_out,
        tokens_grad,
        norm_sum,
        w_query_grad,
        w_key_grad,
        w_value_grad,
        w_gate_grad,
        group_gain_grad,
        w_out_grad,
        ffn_sum,
        w_up_grad,
        w_down_grad,
    )


def fused(
    tokens,
    cotangent,
    doc_lengths,
    head_order,
    norm_gain,
    w_query,
    w_key,
    w_value,
    w_gate,
    group_gain,
    w_out,
    ffn_gain,
    w_up,
    w_down,
):
    turned, qkvg_full, out_full, qk_rows, v_rows, gate, cosine, sine = enter(
        tokens, norm_gain, doc_lengths, w_query, w_key, w_value, w_gate, w_out
    )
    resid, inverse_g, unit_g, states, cot_pair, mixed_turned, up_full, down_full = retain(
        doc_lengths, head_order, group_gain, qk_rows, v_rows, gate, tokens, out_full, cotangent,
        w_up, w_down,
    )
    (
        ffn_terms, up_own, up_far, down_own, down_far, layer_own, far_out, resid_grad, branch
    ) = feed_forward(resid, ffn_gain, cot_pair, up_full, down_full)
    w_out_grad, group_terms, layer_out, all_grad, up_in, down_in = recall(
        doc_lengths, head_order, group_gain, qk_rows, v_rows, gate, unit_g, inverse_g, states,
        cosine, sine, mixed_turned, branch, out_full, layer_own, far_out, up_far, down_far,
    )
    w_up_grad = up_own + up_in.astype(F32)
    w_down_grad = down_own + down_in.astype(F32)
    (
        w_query_grad, w_key_grad, w_value_grad, w_gate_grad, norm_sum, ffn_sum, group_sum, tokens_grad
    ) = depart(all_grad, qkvg_full, turned, tokens, resid_grad, norm_gain, ffn_terms, group_terms)
    return (
        layer_out,
        tokens_grad,
        norm_sum.reshape(-1),
        w_query_grad,
        w_key_grad,
        w_value_grad,
        w_gate_grad,
        group_sum.reshape(-1)[: group_gain.shape[0]],
        w_out_grad,
        ffn_sum.reshape(-1),
        w_up_grad,
        w_down_grad,
    )


def local(*arrays):
    return fused(*arrays) if paired() else plain(*arrays)


def solution(mesh):
    rows = P(("tok", "head"), None)
    inward = P("tok", "head")
    outward = P("head", "tok")
    return jax.shard_map(
        local,
        mesh=mesh,
        in_specs=(
            rows, rows, P(), P(), P(), inward, inward, inward, inward, P("head"),
            outward, P(), inward, outward,
        ),
        out_specs=(
            rows, rows, P(), inward, inward, inward, inward, P("head"),
            outward, P(), inward, outward,
        ),
        check_vma=False,
    )
```

```python
import jax
import jax.numpy as jnp
from jax import lax
from jax.experimental import pallas as pl
from jax.experimental.pallas import tpu as pltpu
from jax.sharding import PartitionSpec as P

KEY = 256
VAL = 512
SPAN = 512

EPS = 1e-05
SQRT_HALF = 0.7071067811865476
INV_ROOT_TWO_PI = 0.3989422804014327
BF = jnp.bfloat16
F32 = jnp.float32


def mm(left, right):
    return jnp.dot(left, right, preferred_element_type=F32)


def mm_nt(left, right):
    return lax.dot_general(left, right, (((1,), (1,)), ((), ())), preferred_element_type=F32)


def mm_tn(left, right):
    return lax.dot_general(left, right, (((0,), (0,)), ((), ())), preferred_element_type=F32)


def swap(array, axis, bit):
    count = lax.axis_size(axis)
    return lax.ppermute(array, axis, [(i, i ^ bit) for i in range(count)])


def shift(array):
    count = lax.axis_size("head")
    return lax.ppermute(array, "head", [(i, (i + 1) % count) for i in range(count)])


def paired():
    return lax.axis_size("tok") == 8


def reorder(array):
    if not paired():
        return array
    me = lax.axis_index("tok")
    width = array.shape[-1] // 8
    return jnp.concatenate(
        [
            lax.dynamic_slice_in_dim(array, (me ^ r) * width, width, array.ndim - 1)
            for r in range(8)
        ],
        axis=-1,
    )


def halves(array):
    half = array.shape[0] // 2
    return array[:half], array[half:]


def tok_gather(shard, axis):
    if not paired():
        return lax.all_gather(shard, "tok", axis=axis, tiled=True)
    along_x = swap(shard, "tok", 2)
    along_y = swap(shard, "tok", 4)
    far = jnp.concatenate(
        [swap(halves(along_x)[0], "tok", 4), swap(halves(along_y)[1], "tok", 2)], axis=0
    )
    own = [shard, along_x, along_y, far]
    pieces = []
    for piece in own:
        pieces += [piece, swap(piece, "tok", 1)]
    return jnp.concatenate(pieces, axis=axis)


def tok_scatter(pieces):
    pieces = [p.astype(BF) for p in pieces]
    if not paired():
        return lax.psum_scatter(jnp.stack(pieces), "tok", scatter_dimension=0).astype(F32)
    kept = [
        pieces[r].astype(F32) + swap(pieces[r + 1], "tok", 1).astype(F32) for r in (0, 2, 4, 6)
    ]
    zero, two, four, six = kept
    six_a, six_b = halves(six.astype(BF))
    two_a, two_b = halves(two)
    four_a, four_b = halves(four)
    four_a = four_a + swap(six_a, "tok", 2).astype(F32)
    two_b = two_b + swap(six_b, "tok", 4).astype(F32)
    two = jnp.concatenate([two_a, two_b], axis=0).astype(BF)
    four = jnp.concatenate([four_a, four_b], axis=0).astype(BF)
    return zero + swap(two, "tok", 2).astype(F32) + swap(four, "tok", 4).astype(F32)


def head_gather(rows):
    count = lax.axis_size("head")
    me = lax.axis_index("head")
    size = rows.shape[0]
    whole = jnp.zeros((count * size,) + rows.shape[1:], rows.dtype)
    whole = lax.dynamic_update_slice_in_dim(whole, rows, me * size, 0)
    for step in range(1, count):
        rows = shift(rows)
        source = lax.rem(me - step + count, count)
        whole = lax.dynamic_update_slice_in_dim(whole, rows, source * size, 0)
    return whole


def head_scatter(term):
    count = lax.axis_size("head")
    me = lax.axis_index("head")
    total = term(lax.rem(me + count - 1, count))
    for step in range(1, count):
        arrived = shift(total.astype(BF))
        owner = lax.rem(me + 2 * count - 1 - step, count)
        total = term(owner) + arrived.astype(F32)
    return total


def rows_of(array, index, size):
    return lax.dynamic_slice_in_dim(array, index * size, size, 0)


def sum_small(vector, axis):
    count = lax.axis_size(axis)
    bit = 1
    while bit < count:
        vector = vector + swap(vector, axis, bit)
        bit *= 2
    return vector


MESH = pl.DeviceIdType.MESH
ANY = pl.BlockSpec(memory_space=pl.ANY)
VMEM = pl.BlockSpec(memory_space=pltpu.VMEM)
SMEM = pl.BlockSpec(memory_space=pltpu.SMEM)
LIMIT = 60 * 1024 * 1024


def flipped(index, bit):
    return index + bit - 2 * bit * lax.rem(lax.div(index, bit), 2)


def peers():
    tok = lax.axis_index("tok")
    z = lax.axis_index("head")
    count = lax.axis_size("head")
    return {
        "core": {"tok": flipped(tok, 1), "head": z},
        "x": {"tok": flipped(tok, 2), "head": z},
        "y": {"tok": flipped(tok, 4), "head": z},
        "up": {"tok": tok, "head": lax.rem(z + 1, count)},
        "down": {"tok": tok, "head": lax.rem(z + count - 1, count)},
        "pair": {"tok": tok, "head": flipped(z, 1)},
        "cross": {"tok": tok, "head": flipped(z, 2)},
    }


def everyone():
    near = peers()
    tok = lax.axis_index("tok")
    z = lax.axis_index("head")
    count = lax.axis_size("head")
    others = [{"tok": tok, "head": lax.rem(z + step, count)} for step in range(1, count)]
    return [near["core"], near["x"], near["y"], *others]


def greet(*devices):
    barrier = pltpu.get_barrier_semaphore()
    for device in devices:
        pl.semaphore_signal(barrier, inc=1, device_id=device, device_id_type=MESH)


def greeted(*devices):
    pl.semaphore_wait(pltpu.get_barrier_semaphore(), len(devices))


def doc_starts(lengths):
    starts, total = [], 0
    for d in range(lengths.shape[0]):
        starts.append(total)
        total = total + lengths[d]
    return starts


def doc_at(row, starts):
    return sum((start <= row).astype(jnp.int32) for start in starts) - 1


def doc_first(row, starts):
    first = jnp.zeros_like(row)
    for start in starts:
        first = jnp.maximum(first, jnp.where(start <= row, start, 0))
    return first


def decays(order, heads):
    z = lax.axis_index("head")
    found = []
    for h in range(heads):
        rank = jnp.full((1, 1), order[z * heads + h], jnp.int32).astype(F32)
        found.append(jnp.log1p(-jnp.exp2(-(5.0 + rank))))
    return found


def block_scales(lengths, log_decay, group_rows, scale, docs):
    heads = len(log_decay)
    starts = doc_starts(lengths)
    first_row = lax.axis_index("tok") * group_rows
    across = [[] for _ in range(heads)]
    for b in range(group_rows // SPAN):
        at = pl.ds(b * SPAN, SPAN)
        low = first_row + b * SPAN
        place = lax.broadcasted_iota(jnp.int32, (SPAN, 1), 0)
        doc = doc_at(low + place, starts)
        docs[at, :] = doc
        before = doc_at(low - 1, starts)
        last = doc_at(low + SPAN - 1, starts)
        where = place.astype(F32)
        for h in range(heads):
            scale[at, h : h + 1] = jnp.where(
                doc == before, jnp.exp((where + 1.0) * log_decay[h]), 0.0
            )
            scale[at, heads + h : heads + h + 1] = jnp.where(
                doc == last, jnp.exp((SPAN - 1.0 - where) * log_decay[h]), 0.0
            )
            across[h].append(jnp.where(last == before, jnp.exp(SPAN * log_decay[h]), 0.0))
    return across


def row_docs(lengths, group_rows):
    starts = doc_starts(lengths)
    first_row = lax.axis_index("tok") * group_rows
    return doc_at(first_row + lax.broadcasted_iota(jnp.int32, (8, group_rows), 1), starts)


def group_weights(lengths, log_decay, group_rows, backward):
    starts = doc_starts(lengths)
    tok = lax.axis_index("tok")
    first_row = tok * group_rows
    found = [[] for _ in log_decay]
    for other in xor_places(tok):
        if backward:
            lag = other - 1 - tok
            same = doc_at(other * group_rows - 1, starts) == doc_at(
                first_row + group_rows - 1, starts
            )
        else:
            lag = tok - 1 - other
            same = doc_at((other + 1) * group_rows - 1, starts) == doc_at(first_row - 1, starts)
        amount = (jnp.maximum(lag, 0) * group_rows).astype(F32)
        for h, rate in enumerate(log_decay):
            found[h].append(jnp.where((lag >= 0) & same, jnp.exp(amount * rate), 0.0))
    return found


def state_view(gathered, h):
    def view(r, side=None):
        if side is None:
            return gathered.at[r, pl.ds(h * KEY, KEY), :]
        return gathered.at[r, pl.ds(h * KEY + side * (KEY // 2), KEY // 2), :]

    return view


class Moves:
    def __init__(self, send, recv):
        self.send, self.recv, self.made, self.over = send, recv, [], []

    def go(self, src, dst, device):
        n = len(self.made)
        copy = pltpu.make_async_remote_copy(
            src_ref=src,
            dst_ref=dst,
            send_sem=self.send.at[n],
            recv_sem=self.recv.at[n],
            device_id=device,
            device_id_type=MESH,
        )
        copy.start()
        self.made.append(copy)
        return copy

    def sent(self, copy):
        copy.wait_send()
        self.over.append(copy)

    def finish(self):
        for copy in self.made:
            if not any(copy is gone for gone in self.over):
                copy.wait_send()


class Gather:
    def __init__(self, moves, near, view):
        self.moves, self.near, self.view = moves, near, view

    def first(self):
        go, near, view = self.moves.go, self.near, self.view
        self.x = go(view(0), view(2), near["x"])
        self.y = go(view(0), view(4), near["y"])
        self.cores = [go(view(0), view(1), near["core"])]

    def second(self):
        go, near, view = self.moves.go, self.near, self.view
        self.x.wait_recv()
        self.far = [go(view(2, 0), view(6, 0), near["y"])]
        self.cores.append(go(view(2), view(3), near["core"]))
        self.y.wait_recv()
        self.far.append(go(view(4, 1), view(6, 1), near["x"]))
        self.cores.append(go(view(4), view(5), near["core"]))

    def third(self):
        go, near, view = self.moves.go, self.near, self.view
        for copy in self.far:
            copy.wait_recv()
        self.cores.append(go(view(6), view(7), near["core"]))

    def done(self):
        for copy in self.cores:
            copy.wait_recv()


def enter_kernel(
    tok_ref,
    gain_ref,
    lengths_ref,
    wq_ref,
    wk_ref,
    wv_ref,
    wg_ref,
    wo_ref,
    turned_out,
    weights_out,
    out_full,
    qk_hbm,
    v_hbm,
    gate_hbm,
    cos_hbm,
    sin_hbm,
    qk_out,
    v_out,
    gate_out,
    cos_ref,
    sin_ref,
    turned,
    group,
    weights,
    own_out,
    gain,
    send,
    recv,
    own_sem,
    keep_sem,
    rows_sem,
):
    near = peers()
    tok = lax.axis_index("tok")
    z = lax.axis_index("head")
    count = lax.axis_size("head")
    rows, width = tok_ref.shape
    part = width // 8
    cols = weights.shape[2]
    half = wq_ref.shape[1]

    own = [
        pltpu.make_async_copy(wq_ref, weights.at[0, pl.ds(0, part), pl.ds(0, half)], own_sem.at[0]),
        pltpu.make_async_copy(
            wk_ref, weights.at[0, pl.ds(0, part), pl.ds(half, half)], own_sem.at[1]
        ),
        pltpu.make_async_copy(wv_ref, weights.at[1, pl.ds(0, part), :], own_sem.at[2]),
        pltpu.make_async_copy(wg_ref, weights.at[2, pl.ds(0, part), :], own_sem.at[3]),
        pltpu.make_async_copy(wo_ref, own_out, own_sem.at[4]),
    ]
    for copy in own:
        copy.start()
    reached = everyone()
    greet(*reached)
    gain[...] = arranged(gain_ref, tok)
    moves = Moves(send, recv)

    def chunk_view(c):
        def view(r, side=None):
            if side is None:
                return weights.at[c, pl.ds(r * part, part), :]
            return weights.at[c, pl.ds(r * part + side * (part // 2), part // 2), :]

        return view

    def out_view(r, side=None):
        if r == 0:
            return own_out
        if side is None:
            return out_full.at[:, pl.ds(r * part, part)]
        size = out_full.shape[0] // 2
        return out_full.at[pl.ds(side * size, size), pl.ds(r * part, part)]

    chunks = [Gather(moves, near, chunk_view(c)) for c in range(3)]
    outward = Gather(moves, near, out_view)
    def lift(side):
        @pl.loop(side * (rows // 32), (side + 1) * (rows // 32))
        def _(i):
            at = pl.ds(pl.multiple_of(i * 16, 16), 16)
            values = arranged(tok_ref.at[at, :], tok).astype(F32)
            mean = jnp.mean(values, axis=-1, keepdims=True)
            centred = values - mean
            inverse = lax.rsqrt(jnp.mean(centred * centred, axis=-1, keepdims=True) + EPS)
            lifted = (centred * inverse * gain[...]).astype(BF)
            group[pl.ds(pl.multiple_of(z * rows + i * 16, 16), 16), :] = lifted

    def shard(step, side):
        owner = lax.rem(z - step + count, count)
        size = rows // 2
        return group.at[pl.ds(pl.multiple_of(owner * rows + side * size, size), size), :]

    ring = {}

    def pass_on(step, side):
        if step:
            ring[step - 1, side].wait_recv()
        if step < count - 1:
            ring[step, side] = moves.go(shard(step, side), shard(step, side), near["up"])

    def keep_rows(step):
        owner = lax.rem(z - step + count, count)
        at = pl.ds(pl.multiple_of(owner * rows, rows), rows)
        for n, (source, target) in enumerate(
            ((qk_out, qk_hbm), (v_out, v_hbm), (gate_out, gate_hbm))
        ):
            copy = pltpu.make_async_copy(
                source.at[at, :], target.at[at, :], rows_sem.at[3 * step + n]
            )
            copy.start()
            kept.append(copy)

    def project(c, steps, part_rows=None):
        first, number = steps
        offset, size = part_rows or (0, rows)

        @pl.loop(0, number * (cols // 256))
        def _(i):
            step = first + lax.div(i, cols // 256)
            tile = lax.rem(i, cols // 256)
            owner = lax.rem(z - step + count, count)
            at = pl.ds(pl.multiple_of(owner * rows + offset, size), size)
            to = pl.ds(pl.multiple_of(tile * 256, 256), 256)
            found = jnp.dot(group[at, :], weights[c, :, to], preferred_element_type=F32)
            if c == 0:
                cosine, sine = cos_ref[at, :], sin_ref[at, :]
                one, two = found[:, :128], found[:, 128:]
                qk_out[at, to] = jnp.concatenate(
                    [one * cosine - two * sine, one * sine + two * cosine], axis=1
                ).astype(BF)
            elif c == 1:
                v_out[at, to] = found.astype(BF)
            else:
                gate_out[at, to] = found.astype(BF)

    def turn(step, offset, size):
        owner = lax.rem(z - step + count, count)
        to = pl.ds(pl.multiple_of(owner * rows + offset, size), size)

        @pl.loop(0, width // 256)
        def _(i):
            at = pl.ds(pl.multiple_of(i * 256, 256), 256)
            turned[at, to] = group[to, at].T

    def keep_turned(step):
        owner = lax.rem(z - step + count, count)
        to = pl.ds(pl.multiple_of(owner * rows, rows), rows)
        copy = pltpu.make_async_copy(
            turned.at[:, to], turned_out.at[:, to], rows_sem.at[3 * count + step]
        )
        copy.start()
        kept.append(copy)

    def keep(c):
        copy = pltpu.make_async_copy(
            weights.at[c], weights_out.at[:, pl.ds(c * cols, cols)], keep_sem.at[c]
        )
        copy.start()
        kept.append(copy)

    lift(0)
    greeted(*reached)
    pass_on(0, 0)
    own[0].wait()
    own[1].wait()
    chunks[0].first()
    own[2].wait()
    chunks[1].first()
    lift(1)
    pass_on(0, 1)
    own[3].wait()
    own[4].wait()
    kept = [pltpu.make_async_copy(own_out, out_full.at[:, pl.ds(0, part)], keep_sem.at[4])]
    kept[0].start()
    group_rows = rows * count
    starts = doc_starts(lengths_ref)
    index = lax.broadcasted_iota(jnp.int32, (1, KEY // 2), 1).astype(F32)
    freq = jnp.exp(-jnp.log(10000.0) * index / (KEY // 2))

    @pl.loop(0, group_rows // 64)
    def _(i):
        at = pl.ds(pl.multiple_of(i * 64, 64), 64)
        row = tok * group_rows + i * 64 + lax.broadcasted_iota(jnp.int32, (64, KEY // 2), 0)
        turn = (row - doc_first(row, starts)).astype(F32) * freq
        cos_ref[at, :] = jnp.cos(turn)
        sin_ref[at, :] = jnp.sin(turn)

    for n, (source, target) in enumerate(((cos_ref, cos_hbm), (sin_ref, sin_hbm))):
        copy = pltpu.make_async_copy(source, target, keep_sem.at[5 + n])
        copy.start()
        kept.append(copy)

    chunks[0].second()
    chunks[2].first()
    pass_on(1, 0)
    chunks[1].second()
    outward.first()
    pass_on(1, 1)
    chunks[0].third()
    chunks[0].done()
    keep(0)
    project(0, (0, 2))
    pass_on(2, 0)
    for step in range(2):
        turn(step, 0, rows)
        keep_turned(step)
    chunks[2].second()
    pass_on(2, 1)
    chunks[1].third()
    chunks[1].done()
    keep(1)
    project(1, (0, 2))
    outward.second()
    project(0, (2, 1))
    project(1, (2, 1))
    turn(2, 0, rows)
    keep_turned(2)
    chunks[2].third()
    chunks[2].done()
    keep(2)
    project(2, (0, 3))
    for step in range(3):
        keep_rows(step)
    outward.third()
    pass_on(3, 0)
    turn(3, 0, rows // 2)
    for c in range(3):
        project(c, (3, 1), (0, rows // 2))
    pass_on(3, 1)
    turn(3, rows // 2, rows // 2)
    keep_turned(3)
    for c in range(3):
        project(c, (3, 1), (rows // 2, rows // 2))
    keep_rows(3)
    outward.done()
    for copy in kept:
        copy.wait()
    moves.finish()


def arranged(ref, tok):
    part = ref.shape[-1] // 8
    return jnp.concatenate(
        [ref[:, pl.ds(pl.multiple_of(place * part, part), part)] for place in xor_places(tok)],
        axis=1,
    )


def xor_places(tok):
    places = []
    for r in range(8):
        place = tok
        for bit in (1, 2, 4):
            if r & bit:
                place = flipped(place, bit)
        places.append(place)
    return places


def enter(tokens, gain, doc_lengths, w_query, w_key, w_value, w_gate, w_out):
    rows, width = tokens.shape
    group_rows = rows * lax.axis_size("head")
    cols = w_value.shape[1]
    moves = 4 * 8 + 6
    return pl.pallas_call(
        enter_kernel,
        out_shape=(
            jax.ShapeDtypeStruct((width, group_rows), BF),
            jax.ShapeDtypeStruct((width, 3 * cols), BF),
            jax.ShapeDtypeStruct((w_out.shape[0], width), BF),
            jax.ShapeDtypeStruct((group_rows, cols), BF),
            jax.ShapeDtypeStruct((group_rows, cols), BF),
            jax.ShapeDtypeStruct((group_rows, cols), BF),
            jax.ShapeDtypeStruct((group_rows, KEY // 2), F32),
            jax.ShapeDtypeStruct((group_rows, KEY // 2), F32),
        ),
        in_specs=[VMEM] * 2 + [SMEM] + [ANY] * 5,
        out_specs=[ANY] * 8,
        scratch_shapes=[
            *[pltpu.VMEM((group_rows, cols), BF)] * 3,
            *[pltpu.VMEM((group_rows, KEY // 2), F32)] * 2,
            pltpu.VMEM((width, group_rows), BF),
            pltpu.VMEM((group_rows, width), BF),
            pltpu.VMEM((3, width, cols), BF),
            pltpu.VMEM(w_out.shape, BF),
            pltpu.VMEM((1, width), F32),
            pltpu.SemaphoreType.DMA((moves,)),
            pltpu.SemaphoreType.DMA((moves,)),
            pltpu.SemaphoreType.DMA((5,)),
            pltpu.SemaphoreType.DMA((7,)),
            pltpu.SemaphoreType.DMA((16,)),
        ],
        compiler_params=pltpu.CompilerParams(
            collective_id=0, has_side_effects=True, vmem_limit_bytes=LIMIT
        ),
        cost_estimate=pl.CostEstimate(
            flops=2 * group_rows * width * 3 * cols, bytes_accessed=40 << 20, transcendentals=0
        ),
    )(tokens, gain[None, :], doc_lengths, w_query, w_key, w_value, w_gate, w_out)


class Scatter:
    def __init__(self, moves, near, term, buffers, result, before=None, ready=None):
        self.moves, self.near, self.term, self.result = moves, near, term, result
        self.odd_out, self.odd_in, self.far_out, self.far_in, self.near_out, self.near_in = buffers
        self.half = self.far_out.shape[0] // 2
        self.before, self.ready, self.frees = before, ready, None
        self.cores = {}

    def odd(self, i):
        if self.before is not None:
            if not self.cores:
                pl.semaphore_wait(self.ready, 1)
            self.moves.sent(self.before.cores[i])
        self.odd_out[i] = self.term(2 * i + 1).astype(BF)
        self.cores[i] = self.moves.go(self.odd_out.at[i], self.odd_in.at[i], self.near["core"])

    def folded(self, i):
        self.cores[i].wait_recv()
        return self.term(2 * i) + self.odd_in[i].astype(F32)

    def far(self):
        value = self.folded(3).astype(BF)
        if self.before is not None:
            for move in self.before.fars:
                self.moves.sent(move)
        self.far_out[...] = value
        self.fars = [
            self.moves.go(
                self.far_out.at[pl.ds(side * self.half, self.half), :],
                self.far_in.at[side],
                self.near[way],
            )
            for side, way in ((0, "x"), (1, "y"))
        ]

    def close(self):
        half = self.half
        self.nears = []
        for i, side, way in ((1, 1, "x"), (2, 0, "y")):
            value = self.folded(i)
            self.fars[side].wait_recv()
            helped = value[side * half : (side + 1) * half] + self.far_in[side].astype(F32)
            other = value[(1 - side) * half : (2 - side) * half]
            if self.before is not None:
                self.moves.sent(self.before.nears[i - 1])
            self.near_out[i - 1, pl.ds(side * half, half), :] = helped.astype(BF)
            self.near_out[i - 1, pl.ds((1 - side) * half, half), :] = other.astype(BF)
            self.nears.append(
                self.moves.go(self.near_out.at[i - 1], self.near_in.at[i - 1], self.near[way])
            )
        self.result[...] = self.folded(0)
        if self.frees is not None:
            pl.semaphore_signal(
                self.frees, inc=1, device_id=self.near["core"], device_id_type=MESH
            )

    def done(self):
        for i in range(2):
            self.nears[i].wait_recv()
        self.result[...] += self.near_in[0].astype(F32) + self.near_in[1].astype(F32)


class Beside:
    def __init__(self, left, right):
        self.refs, self.size = (left, right), left.shape[1]

    def __getitem__(self, index):
        return jnp.concatenate([ref[...] for ref in self.refs], axis=1)

    def __setitem__(self, index, value):
        for i, ref in enumerate(self.refs):
            ref[...] = value[:, i * self.size : (i + 1) * self.size]


class AllSum:
    def __init__(self, moves, vector, slots, others):
        self.moves, self.vector, self.slots, self.others = moves, vector, slots, others

    def start(self):
        self.made = [
            self.moves.go(self.vector, self.slots.at[n], device)
            for n, device in enumerate(self.others)
        ]

    def total(self):
        total = self.vector[...]
        for n, move in enumerate(self.made):
            move.wait_recv()
            total = total + self.slots[n]
        return total


def leave_kernel(
    grads_ref,
    weights_ref,
    turned_ref,
    tok_ref,
    resid_ref,
    gain_ref,
    ffn_ref,
    group_ref,
    wq_out,
    wk_out,
    wv_out,
    wg_out,
    norm_out,
    ffn_out,
    group_out,
    tokens_hbm,
    tokens_grad,
    units,
    spreads,
    grads,
    weights,
    turned,
    ring_out,
    ring_in,
    held,
    odd_out,
    odd_in,
    far_out,
    far_in,
    near_out,
    near_in,
    norm_vec,
    norm_vec2,
    norm_slots_z,
    norm_slots,
    ffn_vec,
    ffn_vec2,
    ffn_slots_z,
    ffn_slots,
    group_vec,
    group_slots,
    gain,
    send,
    recv,
    load_sem,
    free_sem,
):
    near = peers()
    tok = lax.axis_index("tok")
    z = lax.axis_index("head")
    count = lax.axis_size("head")
    rows, width = tok_ref.shape
    part = width // 8
    gain[...] = arranged(gain_ref, tok)
    cols = wv_out.shape[1]
    strip = width // 4

    def owned(step):
        owner = lax.rem(z + 2 * count - 1 - step, count)
        return pl.ds(pl.multiple_of(owner * rows, rows), rows)

    grad_loads = [
        pltpu.make_async_copy(
            grads_ref.at[owned(step), :], grads.at[owned(step), :], load_sem.at[step]
        )
        for step in range(count)
    ]
    strip_loads = [
        pltpu.make_async_copy(
            weights_ref.at[pl.ds(n * strip, strip), :],
            weights.at[pl.ds(n * strip, strip), :],
            load_sem.at[count + n],
        )
        for n in range(4)
    ]
    turned_load = pltpu.make_async_copy(turned_ref, turned, load_sem.at[count + 4])
    loads = [grad_loads[0], *strip_loads, *grad_loads[1:], turned_load]
    for load in loads:
        load.start()
    z_others = [{"tok": tok, "head": lax.rem(z + step, count)} for step in range(1, count)]
    tok_others = [{"tok": place, "head": z} for place in xor_places(tok)[1:]]
    greet(*z_others, *tok_others)
    gain[...] = arranged(gain_ref, tok)
    moves = Moves(send, recv)

    def ring_term(step, side):
        @pl.loop(side * (width // 512), (side + 1) * (width // 512))
        def _(i):
            to = pl.ds(pl.multiple_of(i * 256, 256), 256)
            held[:, to] = dot_nt(grads[owned(step), :], weights[to, :])

    ring = {}
    half = width // 2

    def ring_send(step, side):
        at = pl.ds(side * half, half)
        value = held[:, at]
        if step:
            ring[step - 1, side].wait_recv()
            value = value + ring_in[step - 1, :, at].astype(F32)
        ring_out[step, :, at] = value.astype(BF)
        ring[step, side] = moves.go(
            ring_out.at[step, :, at], ring_in.at[step, :, at], near["up"]
        )

    def chunk_term(c):
        def term(r):
            left = turned[pl.ds(r * part, part), :]
            return jnp.concatenate(
                [
                    jnp.dot(
                        left,
                        grads[:, c * cols + j * 256 : c * cols + (j + 1) * 256],
                        preferred_element_type=F32,
                    )
                    for j in range(cols // 256)
                ],
                axis=1,
            )

        return term

    def buffers(c):
        s = c % 2
        return (
            odd_out.at[s], odd_in.at[s], far_out.at[s], far_in.at[c], near_out.at[s], near_in.at[c]
        )

    scatters = [
        Scatter(moves, near, chunk_term(c), buffers(c), result)
        for c, result in enumerate((Beside(wq_out, wk_out), wv_out))
    ]
    scatters.append(
        Scatter(moves, near, chunk_term(2), buffers(2), wg_out, scatters[0], free_sem)
    )
    scatters[0].frees = free_sem

    def spread(ref, value):
        for n in range(ref.shape[1] // part):
            ref[:, n * part : (n + 1) * part] = value[n : n + 1, :]

    ffn_vec[...] = jnp.zeros_like(ffn_vec)
    group_vec[...] = jnp.zeros_like(group_vec)
    for r, place in enumerate(xor_places(tok)):
        ffn_vec[pl.ds(place, 1), :] = (
            ffn_ref[pl.ds(0, 1), r * part : (r + 1) * part]
            + ffn_ref[pl.ds(1, 1), r * part : (r + 1) * part]
        )
    for n in range(cols // part):
        group_vec[pl.ds(n, 1), :] = group_ref[pl.ds(0, 1), n * part : (n + 1) * part]
    ffn_z = AllSum(moves, ffn_vec, ffn_slots_z, z_others)
    group_tok = AllSum(moves, group_vec, group_slots, tok_others)
    grad_loads[0].wait()
    strip_loads[0].wait()
    strip_loads[1].wait()
    ring_term(0, 0)
    greeted(*z_others, *tok_others)
    ring_send(0, 0)
    strip_loads[2].wait()
    strip_loads[3].wait()
    ring_term(0, 1)
    ring_send(0, 1)
    for load in grad_loads[1:]:
        load.wait()
    turned_load.wait()
    for i in (3, 1, 2, 0):
        scatters[0].odd(i)
    for i in (3, 1):
        scatters[1].odd(i)
    scatters[0].far()
    ring_term(1, 0)
    ring_term(1, 1)
    ring_send(1, 0)
    for i in (2, 0):
        scatters[1].odd(i)
    scatters[1].far()
    ring_send(1, 1)
    scatters[0].close()
    ring_term(2, 0)
    ring_term(2, 1)
    for i in (3, 1):
        scatters[2].odd(i)
    ring_send(2, 0)
    for i in (2, 0):
        scatters[2].odd(i)
    scatters[2].far()
    scatters[1].close()
    ring_send(2, 1)
    scatters[0].done()
    ring_term(3, 0)
    ring_term(3, 1)
    scatters[2].close()
    size = 16

    @pl.loop(0, rows // size)
    def _(i):
        at = pl.ds(pl.multiple_of(i * size, size), size)
        values = arranged(tok_ref.at[at, :], tok).astype(F32)
        mean = jnp.mean(values, axis=-1, keepdims=True)
        centred = values - mean
        inverse = lax.rsqrt(jnp.mean(centred * centred, axis=-1, keepdims=True) + EPS)
        units[at, :] = centred * inverse
        spreads[at, :] = inverse

    scatters[1].done()
    scatters[2].done()
    for side in range(2):
        ring[2, side].wait_recv()
    ffn_z.start()
    group_tok.start()

    def block(i, total):
        at = pl.ds(pl.multiple_of(i * size, size), size)
        unit = units[at, :]
        grad = held[at, :] + ring_in[2, at, :].astype(F32)
        scaled = grad * gain[...]
        first = jnp.mean(scaled, axis=-1, keepdims=True)
        second = jnp.mean(scaled * unit, axis=-1, keepdims=True)
        found = resid_ref[at, :] + spreads[at, :] * (scaled - first - unit * second)
        for r, place in enumerate(xor_places(tok)):
            tokens_grad[at, pl.ds(pl.multiple_of(place * part, part), part)] = found[
                :, r * part : (r + 1) * part
            ]
        return total + jnp.sum(grad * unit, axis=0, keepdims=True)

    total = lax.fori_loop(0, rows // size, block, jnp.zeros((1, width), F32))
    keep = pltpu.make_async_copy(tokens_grad, tokens_hbm, load_sem.at[count + 5])
    keep.start()
    for r, place in enumerate(xor_places(tok)):
        norm_vec[pl.ds(place, 1), :] = total[:, r * part : (r + 1) * part]
    norm_z = AllSum(moves, norm_vec, norm_slots_z, z_others)
    norm_z.start()
    ffn_vec2[...] = ffn_z.total()
    ffn_tok = AllSum(moves, ffn_vec2, ffn_slots, tok_others)
    ffn_tok.start()
    norm_vec2[...] = norm_z.total()
    norm_tok = AllSum(moves, norm_vec2, norm_slots, tok_others)
    norm_tok.start()
    spread(group_out, group_tok.total())
    spread(ffn_out, ffn_tok.total())
    spread(norm_out, norm_tok.total())
    keep.wait()
    moves.finish()


def depart(grads, weights, turned, tokens, resid_grad, gain, ffn_terms, group_terms):
    rows, width = tokens.shape
    count = lax.axis_size("head")
    cols = grads.shape[1] // 3
    part = width // 8
    moves = 6 + 3 * 8 + 2 * (count - 1) + 3 * 7
    vector = (8, part)
    return pl.pallas_call(
        leave_kernel,
        out_shape=(
            jax.ShapeDtypeStruct((part, cols // 2), F32),
            jax.ShapeDtypeStruct((part, cols // 2), F32),
            jax.ShapeDtypeStruct((part, cols), F32),
            jax.ShapeDtypeStruct((part, cols), F32),
            jax.ShapeDtypeStruct((1, width), F32),
            jax.ShapeDtypeStruct((1, width), F32),
            jax.ShapeDtypeStruct((1, cols), F32),
            jax.ShapeDtypeStruct((rows, width), F32),
        ),
        in_specs=[ANY] * 3 + [VMEM] * 5,
        out_specs=[VMEM] * 7 + [ANY],
        scratch_shapes=[
            pltpu.VMEM((rows, width), F32),
            pltpu.VMEM((rows, width), F32),
            pltpu.VMEM((rows, 1), F32),
            pltpu.VMEM(grads.shape, BF),
            pltpu.VMEM(weights.shape, BF),
            pltpu.VMEM(turned.shape, BF),
            pltpu.VMEM((3, rows, width), BF),
            pltpu.VMEM((3, rows, width), BF),
            pltpu.VMEM((rows, width), F32),
            pltpu.VMEM((2, 4, part, cols), BF),
            pltpu.VMEM((2, 4, part, cols), BF),
            pltpu.VMEM((2, part, cols), BF),
            pltpu.VMEM((3, 2, part // 2, cols), BF),
            pltpu.VMEM((2, 2, part, cols), BF),
            pltpu.VMEM((3, 2, part, cols), BF),
            pltpu.VMEM(vector, F32),
            pltpu.VMEM(vector, F32),
            pltpu.VMEM((count - 1,) + vector, F32),
            pltpu.VMEM((7,) + vector, F32),
            pltpu.VMEM(vector, F32),
            pltpu.VMEM(vector, F32),
            pltpu.VMEM((count - 1,) + vector, F32),
            pltpu.VMEM((7,) + vector, F32),
            pltpu.VMEM(vector, F32),
            pltpu.VMEM((7,) + vector, F32),
            pltpu.VMEM((1, width), F32),
            pltpu.SemaphoreType.DMA((moves,)),
            pltpu.SemaphoreType.DMA((moves,)),
            pltpu.SemaphoreType.DMA((count + 6,)),
            pltpu.SemaphoreType.REGULAR,
        ],
        compiler_params=pltpu.CompilerParams(
            collective_id=1, has_side_effects=True, vmem_limit_bytes=LIMIT
        ),
        cost_estimate=pl.CostEstimate(
            flops=2 * grads.shape[0] * width * 5 * cols, bytes_accessed=40 << 20, transcendentals=0
        ),
    )(
        grads, weights, turned, tokens, resid_grad, gain[None, :], ffn_terms, group_terms
    )


def dot_nt(left, right):
    return lax.dot_general(left, right, (((1,), (1,)), ((), ())), preferred_element_type=F32)


def dot_tn(left, right):
    return lax.dot_general(left, right, (((0,), (0,)), ((), ())), preferred_element_type=F32)


def dot_nn(left, right):
    return jnp.dot(left, right, preferred_element_type=F32)


def tile_decay(docs_col, docs_row, log_decay, first, tile, top):
    size = tile + top
    shape = (top, size)
    lag = (
        lax.broadcasted_iota(jnp.int32, shape, 0)
        + tile
        - lax.broadcasted_iota(jnp.int32, shape, 1)
    )
    same = docs_col[pl.ds(first + tile, top), :] == docs_row[pl.ds(0, 1), pl.ds(first, size)]
    power = jnp.exp(jnp.maximum(lag, 0).astype(F32) * log_decay)
    return jnp.where(same & (lag >= 0), power, 0.0)


def retain_kernel(
    lengths_ref,
    order_ref,
    gain_ref,
    qk_ref,
    v_ref,
    wu_ref,
    wd_ref,
    gate_hbm,
    tok_hbm,
    cot_hbm,
    wo_ref,
    resid_out,
    inverse_out,
    unit_hbm,
    states_hbm,
    cot_out,
    turned_hbm,
    up_full,
    down_full,
    gate_ref,
    tok_ref,
    cot_ref,
    cot_rows,
    unit_out,
    states_out,
    cot_pair,
    mixed_turned,
    mixed_out,
    out_weights,
    retained,
    terms,
    folded,
    gathered,
    held,
    ring_out,
    ring_in,
    docs_col,
    docs_row,
    scale_ref,
    send,
    recv,
    own_sem,
):
    near = peers()
    tok = lax.axis_index("tok")
    z = lax.axis_index("head")
    count = lax.axis_size("head")
    rows, width = tok_hbm.shape
    group_rows = rows * count
    part = width // 8
    heads = v_ref.shape[1] // VAL
    blocks = group_rows // SPAN
    slice_ = wu_ref.shape[1]
    own = [
        pltpu.make_async_copy(
            wu_ref, up_full.at[pl.ds(0, part), pl.ds(0, slice_)], own_sem.at[0]
        ),
        pltpu.make_async_copy(
            wd_ref, down_full.at[pl.ds(0, slice_), pl.ds(0, part)], own_sem.at[1]
        ),
        pltpu.make_async_copy(wo_ref, out_weights, own_sem.at[2]),
        pltpu.make_async_copy(gate_hbm, gate_ref, own_sem.at[3]),
        pltpu.make_async_copy(tok_hbm, tok_ref, own_sem.at[4]),
        pltpu.make_async_copy(cot_hbm, cot_ref, own_sem.at[5]),
    ]
    keeps = [
        pltpu.make_async_copy(unit_out, unit_hbm, own_sem.at[7]),
        pltpu.make_async_copy(states_out, states_hbm, own_sem.at[8]),
        pltpu.make_async_copy(mixed_turned, turned_hbm, own_sem.at[9]),
        pltpu.make_async_copy(cot_pair, cot_out, own_sem.at[10]),
    ]
    for copy in own:
        copy.start()
    reached = everyone()
    greet(*reached)
    rate = decays(order_ref, heads)
    across = block_scales(lengths_ref, rate, group_rows, scale_ref, docs_col)
    docs_row[...] = row_docs(lengths_ref, group_rows)
    fold = group_weights(lengths_ref, rate, group_rows, False)
    greeted(*reached)
    moves = Moves(send, recv)
    far_up = moves.go(
        wu_ref, up_full.at[pl.ds(0, part), pl.ds(slice_, slice_)], near["cross"]
    )
    far_down = moves.go(
        wd_ref, down_full.at[pl.ds(slice_, slice_), pl.ds(0, part)], near["cross"]
    )

    def block_rows(b):
        return pl.ds(pl.multiple_of(b * SPAN, SPAN), SPAN)


    def q_cols(h):
        return pl.ds(h * KEY, KEY)

    def k_cols(h):
        return pl.ds((heads + h) * KEY, KEY)

    def v_cols(h):
        return pl.ds(h * VAL, VAL)

    def up_view(s):
        def view(r, side=None):
            if r == 0 and s == 0:
                return wu_ref
            if side is None:
                return up_full.at[pl.ds(r * part, part), pl.ds(s * slice_, slice_)]
            size = part // 2
            return up_full.at[
                pl.ds(r * part + side * size, size), pl.ds(s * slice_, slice_)
            ]

        return view

    def down_view(s):
        def view(r, side=None):
            if r == 0 and s == 0:
                return wd_ref
            if side is None:
                return down_full.at[pl.ds(s * slice_, slice_), pl.ds(r * part, part)]
            size = slice_ // 2
            return down_full.at[
                pl.ds(s * slice_ + side * size, size), pl.ds(r * part, part)
            ]

        return view

    wide = [
        Gather(moves, near, view) for view in (up_view(0), down_view(0), up_view(1), down_view(1))
    ]

    states = [Gather(moves, near, state_view(gathered, h)) for h in range(heads)]
    for h in range(heads):
        total = jnp.zeros((KEY, VAL), F32)
        for b in range(blocks):
            weighed = v_ref[block_rows(b), v_cols(h)].astype(F32) * scale_ref[
                block_rows(b), heads + h : heads + h + 1
            ]
            term = dot_tn(qk_ref[block_rows(b), k_cols(h)], weighed.astype(BF))
            terms[b, pl.ds(h * KEY, KEY), :] = term
            total = across[h][b] * total + term
        gathered[0, pl.ds(h * KEY, KEY), :] = total.astype(BF)
        states[h].first()
    wide[0].first()
    own[5].wait()
    cot_move = moves.go(cot_ref, cot_rows, near["pair"])

    def intra(h):
        @pl.loop(0, blocks)
        def _(b):
            first = pl.multiple_of(b * SPAN, SPAN)
            for tile in range(0, SPAN, 128):
                at = pl.ds(first + tile, 128)
                seen = pl.ds(first, tile + 128)
                scores = dot_nt(qk_ref[at, q_cols(h)], qk_ref[seen, k_cols(h)])
                mask = tile_decay(docs_col, docs_row, rate[h], first, tile, 128)
                probs = (scores * mask).astype(BF)
                retained[at, v_cols(h)] = dot_nn(probs, v_ref[seen, v_cols(h)])

    def finish_head(h):
        first = jnp.zeros((KEY, VAL), F32)
        for r in range(8):
            first = first + fold[h][r] * gathered[r, pl.ds(h * KEY, KEY), :].astype(F32)
        for b in range(blocks):
            folded[b] = first.astype(BF)
            states_out[pl.ds((h * blocks + b) * KEY, KEY), :] = first.astype(BF)
            first = across[h][b] * first + terms[b, pl.ds(h * KEY, KEY), :]

        @pl.loop(0, group_rows // 128)
        def _(i):
            at = pl.ds(pl.multiple_of(i * 128, 128), 128)
            b = lax.div(i, SPAN // 128)
            cross = dot_nn(qk_ref[at, q_cols(h)], folded[b])
            values = retained[at, v_cols(h)] + scale_ref[at, h : h + 1] * cross
            mean = jnp.mean(values, axis=-1, keepdims=True)
            centred = values - mean
            inverse = lax.rsqrt(jnp.mean(centred * centred, axis=-1, keepdims=True) + EPS)
            unit = centred * inverse
            gate = gate_ref[at, v_cols(h)].astype(F32)
            swish = gate / (1.0 + jnp.exp(-gate))
            unit_out[at, v_cols(h)] = unit.astype(BF)
            inverse_out[at, h : h + 1] = inverse
            mixed = (swish * unit * gain_ref[:, h * VAL : (h + 1) * VAL]).astype(BF)
            mixed_out[at, v_cols(h)] = mixed
            mixed_turned[v_cols(h), at] = mixed.T

    for h in range(heads):
        intra(h)
        states[h].second()
    wide[1].first()
    for h in range(heads):
        states[h].third()
    wide[0].second()
    own[3].wait()
    for h in range(heads):
        states[h].done()
        finish_head(h)
    for keep in keeps[:3]:
        keep.start()

    def ring_term(step, side):
        owner = lax.rem(z + 2 * count - 1 - step, count)
        at = pl.ds(pl.multiple_of(owner * rows, rows), rows)

        @pl.loop(side * (width // 512), (side + 1) * (width // 512))
        def _(i):
            to = pl.ds(pl.multiple_of(i * 256, 256), 256)
            held[:, to] = dot_nn(mixed_out[at, :], out_weights[:, to])

    ring = {}
    half = width // 2

    def ring_send(step, side):
        at = pl.ds(side * half, half)
        value = held[:, at]
        if step:
            ring[step - 1, side].wait_recv()
            value = value + ring_in[step - 1, :, at].astype(F32)
        ring_out[step, :, at] = value.astype(BF)
        ring[step, side] = moves.go(
            ring_out.at[step, :, at], ring_in.at[step, :, at], near["up"]
        )

    own[2].wait()
    for side in range(2):
        ring_term(0, side)
        ring_send(0, side)
    wide[1].second()
    ring_term(1, 0)
    ring_term(1, 1)
    far_up.wait_recv()
    wide[2].first()
    wide[0].third()
    ring_send(1, 0)
    far_down.wait_recv()
    wide[3].first()
    wide[1].third()
    ring_send(1, 1)
    ring_term(2, 0)
    ring_term(2, 1)
    wide[2].second()
    ring_send(2, 0)
    wide[3].second()
    ring_send(2, 1)
    ring_term(3, 0)
    ring_term(3, 1)
    wide[2].third()
    wide[3].third()
    own[4].wait()
    cot_move.wait_recv()
    for ref, first in ((cot_ref, 0), (cot_rows, rows)):
        for r, place in enumerate(xor_places(tok)):
            cot_pair[pl.ds(first, rows), pl.ds(r * part, part)] = ref[
                :, pl.ds(pl.multiple_of(place * part, part), part)
            ]
    keeps[3].start()
    for side in range(2):
        ring[2, side].wait_recv()
        for n in range(4):
            r = side * 4 + n
            place = xor_places(tok)[r]
            at = pl.ds(r * part, part)
            values = tok_ref[:, pl.ds(pl.multiple_of(place * part, part), part)].astype(F32)
            resid_out[:, at] = values + held[:, at] + ring_in[2, :, at].astype(F32)
    for gather in wide:
        gather.done()
    own[0].wait()
    own[1].wait()
    for keep in keeps:
        keep.wait()
    moves.finish()


def retain(
    doc_lengths, head_order, gain, qk, v, gate, tokens, out_full, cotangent, w_up, w_down
):
    rows, width = tokens.shape
    count = lax.axis_size("head")
    group_rows = rows * count
    heads = v.shape[1] // VAL
    blocks = group_rows // SPAN
    wide = 2 * w_up.shape[1]
    moves = 3 + (4 + heads) * 8 + 6
    struct = jax.ShapeDtypeStruct
    kept = (
        struct(v.shape, BF),
        struct((heads * blocks * KEY, VAL), BF),
        struct((2 * rows, width), BF),
        struct((heads * VAL, group_rows), BF),
    )
    return pl.pallas_call(
        retain_kernel,
        out_shape=(
            struct((rows, width), F32),
            struct((group_rows, heads), F32),
            *kept,
            struct((width, wide), BF),
            struct((wide, width), BF),
        ),
        in_specs=[SMEM] * 2 + [VMEM] * 5 + [ANY] * 4,
        out_specs=[VMEM] * 2 + [ANY] * 6,
        scratch_shapes=[
            pltpu.VMEM(gate.shape, BF),
            *[pltpu.VMEM(tokens.shape, BF)] * 3,
            *[pltpu.VMEM(array.shape, BF) for array in kept],
            pltpu.VMEM(v.shape, BF),
            pltpu.VMEM(out_full.shape, BF),
            pltpu.VMEM((group_rows, heads * VAL), F32),
            pltpu.VMEM((blocks, heads * KEY, VAL), F32),
            pltpu.VMEM((blocks, KEY, VAL), BF),
            pltpu.VMEM((8, heads * KEY, VAL), BF),
            pltpu.VMEM((rows, width), F32),
            pltpu.VMEM((3, rows, width), BF),
            pltpu.VMEM((3, rows, width), BF),
            pltpu.VMEM((group_rows, 1), jnp.int32),
            pltpu.VMEM((8, group_rows), jnp.int32),
            pltpu.VMEM((group_rows, 2 * heads), F32),
            pltpu.SemaphoreType.DMA((moves,)),
            pltpu.SemaphoreType.DMA((moves,)),
            pltpu.SemaphoreType.DMA((11,)),
        ],
        compiler_params=pltpu.CompilerParams(
            collective_id=2, has_side_effects=True, vmem_limit_bytes=LIMIT
        ),
        cost_estimate=pl.CostEstimate(
            flops=12 << 30, bytes_accessed=40 << 20, transcendentals=0
        ),
    )(
        doc_lengths, head_order, gain[None, :], qk, v, w_up, w_down, gate, tokens, cotangent,
        out_full,
    )


def feed_kernel(
    resid_ref,
    gain_ref,
    cot_ref,
    up_ref,
    down_ref,
    gain_out,
    up_own,
    up_far,
    down_own,
    down_far,
    layer_hbm,
    far_hbm,
    resid_hbm,
    branch,
    layer_out,
    far_out,
    resid_grad,
    up,
    down,
    lifted,
    cot,
    hidden,
    turned,
    pre,
    back_out,
    back_in,
    odd_out_d,
    odd_in_d,
    odd_out_u,
    odd_in_u,
    far_out_d,
    far_in_d,
    far_out_u,
    far_in_u,
    near_out_d,
    near_in_d,
    near_out_u,
    near_in_u,
    up_sum,
    down_sum,
    gain,
    send,
    recv,
    load_sem,
    free_sem,
):
    near = peers()
    z = lax.axis_index("head")
    count = lax.axis_size("head")
    rows, width = resid_ref.shape
    part = width // 8
    side_rows = rows // 2
    wide = up.shape[1]
    slice_ = wide // 2
    loads = [
        pltpu.make_async_copy(cot_ref, cot, load_sem.at[0]),
        pltpu.make_async_copy(up_ref, up, load_sem.at[1]),
        pltpu.make_async_copy(down_ref, down, load_sem.at[2]),
    ]
    for load in loads:
        load.start()
    reached = everyone()
    greet(*reached)
    gain[...] = arranged(gain_ref, lax.axis_index("tok"))
    moves = Moves(send, recv)
    size = 16

    pairs = []
    for side in range(2):

        @pl.loop(0, side_rows // size)
        def _(i):
            at = pl.ds(pl.multiple_of(side * side_rows + i * size, size), size)
            values = resid_ref[at, :]
            mean = jnp.mean(values, axis=-1, keepdims=True)
            centred = values - mean
            inverse = lax.rsqrt(jnp.mean(centred * centred, axis=-1, keepdims=True) + EPS)
            lifted[at, :] = (centred * inverse * gain[...]).astype(BF)

        if side == 0:
            greeted(*reached)
        pairs.append(
            moves.go(
                lifted.at[pl.ds(side * side_rows, side_rows), :],
                lifted.at[pl.ds(rows + side * side_rows, side_rows), :],
                near["pair"],
            )
        )

    def feed(first, number):
        @pl.loop(0, wide // 256)
        def _(i):
            to = pl.ds(pl.multiple_of(i * 256, 256), 256)
            at = pl.ds(first, number)
            hidden_pre = dot_nn(lifted[at, :], up[:, to])
            hidden_grad = dot_nt(cot[at, :], down[to, :])
            phi = 0.5 * (1.0 + lax.erf(hidden_pre * SQRT_HALF))
            made = (hidden_pre * phi).astype(BF)
            hidden[at, to] = made
            turned[to, at] = made.T
            slope = phi + hidden_pre * jnp.exp(-0.5 * hidden_pre * hidden_pre) * INV_ROOT_TWO_PI
            pre[at, to] = (hidden_grad * slope).astype(BF)

    for load in loads:
        load.wait()
    feed(0, rows)
    backs = []
    for side in range(2):
        if side:

            @pl.loop(0, width // 256)
            def _(i):
                to = pl.ds(pl.multiple_of(i * 256, 256), 256)
                resid_grad[:, to] = dot_nt(pre[pl.ds(0, rows), :], up[to, :])

        pairs[side].wait_recv()
        feed(rows + side * side_rows, side_rows)

        @pl.loop(0, width // 256)
        def _(i):
            to = pl.ds(pl.multiple_of(i * 256, 256), 256)
            found = dot_nt(pre[pl.ds(rows + side * side_rows, side_rows), :], up[to, :])
            back_out[pl.ds(side * side_rows, side_rows), to] = found.astype(BF)

        at = pl.ds(side * side_rows, side_rows)
        backs.append(moves.go(back_out.at[at, :], back_in.at[at, :], near["pair"]))

    def down_term(s):
        def term(r):
            return dot_nn(turned[pl.ds(s * slice_, slice_), :], cot[:, r * part : (r + 1) * part])

        return term

    def up_term(s):
        def term(r):
            return dot_tn(
                lifted[:, r * part : (r + 1) * part], pre[:, s * slice_ : (s + 1) * slice_]
            )

        return term

    down_sets = [
        (odd_out_d, odd_in_d, far_out_d, far_in_d.at[s], near_out_d, near_in_d.at[s])
        for s in range(2)
    ]
    up_sets = [
        (odd_out_u, odd_in_u, far_out_u, far_in_u.at[s], near_out_u, near_in_u.at[s])
        for s in range(2)
    ]
    sums = [
        Scatter(moves, near, down_term(0), down_sets[0], down_own),
        Scatter(moves, near, up_term(0), up_sets[0], up_own),
    ]
    sums += [
        Scatter(moves, near, down_term(1), down_sets[1], down_sum, sums[0], free_sem.at[0]),
        Scatter(moves, near, up_term(1), up_sets[1], up_sum, sums[1], free_sem.at[1]),
    ]
    sums[0].frees = free_sem.at[0]
    sums[1].frees = free_sem.at[1]

    ring = {}

    def shard(step, side):
        owner = lax.rem(z - step + count, count)
        first = pl.multiple_of(owner * rows + side * side_rows, side_rows)
        return branch.at[pl.ds(first, side_rows), :]

    def pass_on(step, side):
        if step:
            ring[step - 1, side].wait_recv()
        if step < count - 1:
            here = back_in.at[pl.ds(side * side_rows, side_rows), :] if step == 0 else shard(step, side)
            ring[step, side] = moves.go(here, shard(step, side), near["up"])

    def norm_back(side):
        backs[side].wait_recv()

        def block(i, total):
            at = pl.ds(pl.multiple_of(side * side_rows + i * size, size), size)
            values = resid_ref[at, :]
            mean = jnp.mean(values, axis=-1, keepdims=True)
            centred = values - mean
            inverse = lax.rsqrt(jnp.mean(centred * centred, axis=-1, keepdims=True) + EPS)
            unit = centred * inverse
            grad = resid_grad[at, :] + back_in[at, :].astype(F32)
            scaled = grad * gain[...]
            first = jnp.mean(scaled, axis=-1, keepdims=True)
            second = jnp.mean(scaled * unit, axis=-1, keepdims=True)
            found = cot[at, :].astype(F32) + inverse * (scaled - first - unit * second)
            resid_grad[at, :] = found
            back_in[at, :] = found.astype(BF)
            return total + jnp.sum(grad * unit, axis=0, keepdims=True)

        total = lax.fori_loop(0, side_rows // size, block, jnp.zeros((1, width), F32))
        gain_out[pl.ds(side, 1), :] = total

    norm_back(0)
    pass_on(0, 0)
    for i in (3, 1, 2, 0):
        sums[0].odd(i)
    for i in (3, 1):
        sums[1].odd(i)
    norm_back(1)
    pass_on(0, 1)
    mine = pltpu.make_async_copy(
        back_in, branch.at[pl.ds(pl.multiple_of(z * rows, rows), rows), :], load_sem.at[3]
    )
    mine.start()
    keeps = [pltpu.make_async_copy(resid_grad, resid_hbm, load_sem.at[4])]
    keeps[0].start()
    sums[0].far()
    for i in (2, 0):
        sums[1].odd(i)
    sums[1].far()
    pass_on(1, 0)
    sums[0].close()
    for i in (3, 1, 2, 0):
        sums[2].odd(i)
    sums[2].far()
    pass_on(1, 1)
    sums[1].close()
    for i in (3, 1, 2, 0):
        sums[3].odd(i)
    sums[3].far()
    pass_on(2, 0)
    sums[2].close()

    @pl.loop(0, width // 256)
    def _(i):
        to = pl.ds(pl.multiple_of(i * 256, 256), 256)
        layer_out[:, to] = resid_ref[:, to] + dot_nn(hidden[pl.ds(0, rows), :], down[:, to])

    keeps.append(pltpu.make_async_copy(layer_out, layer_hbm, load_sem.at[5]))
    keeps[-1].start()
    pass_on(2, 1)

    @pl.loop(0, width // 256)
    def _(i):
        to = pl.ds(pl.multiple_of(i * 256, 256), 256)
        far_out[:, to] = dot_nn(hidden[pl.ds(rows, rows), :], down[:, to]).astype(BF)

    keeps.append(pltpu.make_async_copy(far_out, far_hbm, load_sem.at[6]))
    keeps[-1].start()
    sums[0].done()
    sums[1].done()
    sums[3].close()
    pass_on(3, 0)
    sums[2].done()
    down_far[...] = down_sum[...].astype(BF)
    pass_on(3, 1)
    sums[3].done()
    up_far[...] = up_sum[...].astype(BF)
    mine.wait()
    for keep in keeps:
        keep.wait()
    moves.finish()


def feed_forward(resid, gain, cot_pair, up_full, down_full):
    rows, width = resid.shape
    count = lax.axis_size("head")
    part = width // 8
    wide = up_full.shape[1]
    slice_ = wide // 2
    moves = 4 + 4 * 8 + 6
    struct = jax.ShapeDtypeStruct
    down_piece = (slice_, part)
    up_piece = (part, slice_)

    def sets(piece):
        half = (piece[0] // 2, piece[1])
        return [
            pltpu.VMEM(piece, BF),
            pltpu.VMEM((2, 2) + half, BF),
        ]

    def nears(piece):
        return [pltpu.VMEM((2,) + piece, BF), pltpu.VMEM((2, 2) + piece, BF)]

    def odds(piece):
        return [pltpu.VMEM((4,) + piece, BF)] * 2

    return pl.pallas_call(
        feed_kernel,
        out_shape=(
            struct((8, width), F32),
            struct(up_piece, F32),
            struct(up_piece, BF),
            struct(down_piece, F32),
            struct(down_piece, BF),
            struct((rows, width), F32),
            struct((rows, width), BF),
            struct((rows, width), F32),
            struct((count * rows, width), BF),
        ),
        in_specs=[VMEM] * 2 + [ANY] * 3,
        out_specs=[VMEM] * 5 + [ANY] * 4,
        scratch_shapes=[
            pltpu.VMEM((rows, width), F32),
            pltpu.VMEM((rows, width), BF),
            pltpu.VMEM((rows, width), F32),
            pltpu.VMEM((width, wide), BF),
            pltpu.VMEM((wide, width), BF),
            pltpu.VMEM((2 * rows, width), BF),
            pltpu.VMEM((2 * rows, width), BF),
            pltpu.VMEM((2 * rows, wide), BF),
            pltpu.VMEM((wide, 2 * rows), BF),
            pltpu.VMEM((2 * rows, wide), BF),
            pltpu.VMEM((rows, width), BF),
            pltpu.VMEM((rows, width), BF),
            *odds(down_piece),
            *odds(up_piece),
            *sets(down_piece),
            *sets(up_piece),
            *nears(down_piece),
            *nears(up_piece),
            pltpu.VMEM(up_piece, F32),
            pltpu.VMEM(down_piece, F32),
            pltpu.VMEM((1, width), F32),
            pltpu.SemaphoreType.DMA((moves,)),
            pltpu.SemaphoreType.DMA((moves,)),
            pltpu.SemaphoreType.DMA((7,)),
            pltpu.SemaphoreType.REGULAR((2,)),
        ],
        compiler_params=pltpu.CompilerParams(
            collective_id=3, has_side_effects=True, vmem_limit_bytes=LIMIT
        ),
        cost_estimate=pl.CostEstimate(
            flops=26 << 30, bytes_accessed=40 << 20, transcendentals=0
        ),
    )(resid, gain[None, :], cot_pair, up_full, down_full)


def recall_kernel(
    lengths_ref,
    order_ref,
    gain_ref,
    wo_hbm,
    branch_hbm,
    gate_hbm,
    unit_hbm,
    inverse_hbm,
    qk_hbm,
    v_hbm,
    turned_hbm,
    states_hbm,
    cos_hbm,
    sin_hbm,
    own_hbm,
    far_ref,
    up_ref,
    down_ref,
    wo_grad,
    gains,
    layer_out,
    grads_out,
    up_in,
    down_in,
    out_weights,
    branch,
    gate_ref,
    unit_ref,
    inverse_ref,
    qk_ref,
    v_ref,
    turned_ref,
    states_ref,
    cos_ref,
    sin_ref,
    own_ref,
    far_in,
    grads,
    docs_col,
    docs_row,
    scale_ref,
    back,
    terms,
    gathered,
    folded,
    dqk,
    dv,
    odd_out,
    odd_in,
    out_far,
    in_far,
    out_near,
    in_near,
    send,
    recv,
    load_sem,
    keep_sem,
):
    near = peers()
    tok = lax.axis_index("tok")
    group_rows, cols = v_ref.shape
    heads = cols // VAL
    blocks = group_rows // SPAN
    width = branch.shape[1]
    part = width // 8
    loads = [
        pltpu.make_async_copy(source, target, load_sem.at[n])
        for n, (source, target) in enumerate(
            (
                (wo_hbm, out_weights),
                (branch_hbm, branch),
                (gate_hbm, gate_ref),
                (unit_hbm, unit_ref),
                (inverse_hbm, inverse_ref),
                (qk_hbm, qk_ref),
                (v_hbm, v_ref),
                (turned_hbm, turned_ref),
                (states_hbm, states_ref),
                (cos_hbm, cos_ref),
                (sin_hbm, sin_ref),
                (own_hbm, own_ref),
            )
        )
    ]
    for load in loads:
        load.start()
    reached = everyone()
    greet(*reached)
    rate = decays(order_ref, heads)
    across = block_scales(lengths_ref, rate, group_rows, scale_ref, docs_col)
    docs_row[...] = row_docs(lengths_ref, group_rows)
    fold = group_weights(lengths_ref, rate, group_rows, True)
    greeted(*reached)
    moves = Moves(send, recv)
    swaps = [
        moves.go(far_ref, far_in, near["pair"]),
        moves.go(up_ref, up_in, near["cross"]),
        moves.go(down_ref, down_in, near["cross"]),
    ]

    def block_rows(b):
        return pl.ds(pl.multiple_of(b * SPAN, SPAN), SPAN)

    def q_cols(h):
        return pl.ds(h * KEY, KEY)

    def k_cols(h):
        return pl.ds((heads + h) * KEY, KEY)

    def v_cols(h):
        return pl.ds(h * VAL, VAL)

    for load in loads[:5]:
        load.wait()

    first_gate = 2 * heads * KEY + cols
    states = [Gather(moves, near, state_view(gathered, h)) for h in range(heads)]
    gains[...] = jnp.zeros_like(gains)
    kept = [
        pltpu.make_async_copy(
            grads.at[:, pl.ds(first_gate, cols)],
            grads_out.at[:, pl.ds(first_gate, cols)],
            keep_sem.at[0],
        ),
        pltpu.make_async_copy(
            grads.at[:, pl.ds(0, first_gate)], grads_out.at[:, pl.ds(0, first_gate)], keep_sem.at[1]
        ),
    ]
    for h in range(heads):
        gain = gain_ref[:, h * VAL : (h + 1) * VAL]

        @pl.loop(0, group_rows // 256)
        def _(i):
            at = pl.ds(pl.multiple_of(i * 256, 256), 256)
            dv[at, v_cols(h)] = dot_nt(branch[at, :], out_weights[v_cols(h), :])

        def tile_back(i, total):
            at = pl.ds(pl.multiple_of(i * 16, 16), 16)
            grad = dv[at, v_cols(h)].astype(BF).astype(F32)
            gate = gate_ref[at, v_cols(h)].astype(F32)
            sigma = 1.0 / (1.0 + jnp.exp(-gate))
            swish = gate * sigma
            unit = unit_ref[at, v_cols(h)].astype(F32)
            grads[at, pl.ds(first_gate + h * VAL, VAL)] = (
                grad * unit * gain * (sigma + swish * (1.0 - sigma))
            ).astype(BF)
            inner = grad * swish
            scaled = inner * gain
            first = jnp.mean(scaled, axis=-1, keepdims=True)
            second = jnp.mean(scaled * unit, axis=-1, keepdims=True)
            back[at, v_cols(h)] = (
                inverse_ref[at, h : h + 1] * (scaled - first - unit * second)
            ).astype(BF)
            return total + jnp.sum(inner * unit, axis=0, keepdims=True)

        gains[pl.ds(0, 1), v_cols(h)] = lax.fori_loop(
            0, group_rows // 16, tile_back, jnp.zeros((1, VAL), F32), unroll=2
        )
        if h == 0:
            for load in loads[5:]:
                load.wait()
        total = jnp.zeros((KEY, VAL), F32)
        for b in reversed(range(blocks)):
            weighed = back[block_rows(b), v_cols(h)].astype(F32) * scale_ref[
                block_rows(b), h : h + 1
            ]
            term = dot_tn(qk_ref[block_rows(b), q_cols(h)], weighed.astype(BF))
            terms[b, pl.ds(h * KEY, KEY), :] = term
            total = across[h][b] * total + term
        gathered[0, pl.ds(h * KEY, KEY), :] = total.astype(BF)
        states[h].first()
    kept[0].start()

    def out_term(r):
        return dot_nn(turned_ref[...], branch[:, r * part : (r + 1) * part])

    outward = Scatter(
        moves, near, out_term, (odd_out, odd_in, out_far, in_far, out_near, in_near), wo_grad
    )

    def intra(h):
        @pl.loop(0, blocks)
        def _(b):
            first = pl.multiple_of(b * SPAN, SPAN)
            for tile in range(SPAN - 128, -1, -128):
                at = pl.ds(first + tile, 128)
                seen = pl.ds(first, tile + 128)
                mask = tile_decay(docs_col, docs_row, rate[h], first, tile, 128)
                query = qk_ref[at, q_cols(h)]
                key = qk_ref[seen, k_cols(h)]
                ret = back[at, v_cols(h)]
                probs = (dot_nt(query, key) * mask).astype(BF)
                score = (dot_nt(ret, v_ref[seen, v_cols(h)]) * mask).astype(BF)
                dqk[at, q_cols(h)] = dot_nn(score, key)
                to_keys = dot_tn(score, query)
                to_values = dot_tn(probs, ret)
                if tile == SPAN - 128:
                    dqk[seen, k_cols(h)] = to_keys
                    dv[seen, v_cols(h)] = to_values
                else:
                    dqk[seen, k_cols(h)] += to_keys
                    dv[seen, v_cols(h)] += to_values

    def finish_head(h):
        later = jnp.zeros((KEY, VAL), F32)
        for r in range(8):
            later = later + fold[h][r] * gathered[r, pl.ds(h * KEY, KEY), :].astype(F32)
        for b in reversed(range(blocks)):
            folded[b] = later.astype(BF)
            later = across[h][b] * later + terms[b, pl.ds(h * KEY, KEY), :]

        @pl.loop(0, group_rows // 128)
        def _(i):
            at = pl.ds(pl.multiple_of(i * 128, 128), 128)
            b = lax.div(i, SPAN // 128)
            reach = scale_ref[at, h : h + 1]
            leave = scale_ref[at, heads + h : heads + h + 1]
            state = states_ref[pl.ds(pl.multiple_of((h * blocks + b) * KEY, KEY), KEY), :]
            cosine, sine = cos_ref[at, :], sin_ref[at, :]
            for found, to in (
                (
                    dqk[at, q_cols(h)] + reach * dot_nt(back[at, v_cols(h)], state),
                    q_cols(h),
                ),
                (
                    dqk[at, k_cols(h)] + leave * dot_nt(v_ref[at, v_cols(h)], folded[b]),
                    k_cols(h),
                ),
            ):
                one, two = found[:, : KEY // 2], found[:, KEY // 2 :]
                grads[at, to] = jnp.concatenate(
                    [one * cosine + two * sine, two * cosine - one * sine], axis=1
                ).astype(BF)
            found = dv[at, v_cols(h)] + leave * dot_nn(qk_ref[at, k_cols(h)], folded[b])
            grads[at, pl.ds(2 * heads * KEY + h * VAL, VAL)] = found.astype(BF)

    intra(0)
    states[0].second()
    for i in (3, 1, 2, 0):
        outward.odd(i)
    for h in range(1, heads):
        states[h].second()
        intra(h)
    outward.far()
    states[0].third()
    for h in range(1, heads):
        states[h].third()
    states[0].done()
    finish_head(0)
    outward.close()
    for h in range(1, heads):
        states[h].done()
        finish_head(h)
    kept[1].start()
    swaps[0].wait_recv()
    for r, place in enumerate(xor_places(tok)):
        at = pl.ds(r * part, part)
        layer_out[:, pl.ds(pl.multiple_of(place * part, part), part)] = (
            own_ref[:, at] + far_in[:, at].astype(F32)
        ).astype(BF)
    outward.done()
    for swap_ in swaps[1:]:
        swap_.wait_recv()
    for copy in kept:
        copy.wait()
    moves.finish()


def recall(
    doc_lengths, head_order, gain, qk, v, gate, unit, inverse, states, cosine, sine, mixed_turned,
    branch, out_full, layer_own, far_out, up_far, down_far,
):
    group_rows, cols = v.shape
    heads = cols // VAL
    blocks = group_rows // SPAN
    width = branch.shape[1]
    part = width // 8
    piece = (cols, part)
    moves = 3 + 8 + 8 * heads
    struct = jax.ShapeDtypeStruct
    loaded = (
        out_full, branch, gate, unit, inverse, qk, v, mixed_turned, states, cosine, sine, layer_own
    )
    return pl.pallas_call(
        recall_kernel,
        out_shape=(
            struct(piece, F32),
            struct((8, cols), F32),
            struct(far_out.shape, BF),
            struct((group_rows, 3 * cols), BF),
            struct(up_far.shape, BF),
            struct(down_far.shape, BF),
        ),
        in_specs=[SMEM] * 2 + [VMEM] + [ANY] * 15,
        out_specs=[VMEM] * 3 + [ANY] * 3,
        scratch_shapes=[
            *[pltpu.VMEM(array.shape, array.dtype) for array in loaded],
            pltpu.VMEM(far_out.shape, BF),
            pltpu.VMEM((group_rows, 3 * cols), BF),
            pltpu.VMEM((group_rows, 1), jnp.int32),
            pltpu.VMEM((8, group_rows), jnp.int32),
            pltpu.VMEM((group_rows, 2 * heads), F32),
            pltpu.VMEM(v.shape, BF),
            pltpu.VMEM((blocks, heads * KEY, VAL), F32),
            pltpu.VMEM((8, heads * KEY, VAL), BF),
            pltpu.VMEM((blocks, KEY, VAL), BF),
            pltpu.VMEM((group_rows, 2 * heads * KEY), F32),
            pltpu.VMEM((group_rows, cols), F32),
            pltpu.VMEM((4,) + piece, BF),
            pltpu.VMEM((4,) + piece, BF),
            pltpu.VMEM(piece, BF),
            pltpu.VMEM((2, cols // 2, part), BF),
            pltpu.VMEM((2,) + piece, BF),
            pltpu.VMEM((2,) + piece, BF),
            pltpu.SemaphoreType.DMA((moves,)),
            pltpu.SemaphoreType.DMA((moves,)),
            pltpu.SemaphoreType.DMA((len(loaded),)),
            pltpu.SemaphoreType.DMA((2,)),
        ],
        compiler_params=pltpu.CompilerParams(
            collective_id=4, has_side_effects=True, vmem_limit_bytes=LIMIT
        ),
        cost_estimate=pl.CostEstimate(
            flops=20 << 30, bytes_accessed=40 << 20, transcendentals=0
        ),
    )(doc_lengths, head_order, gain[None, :], *loaded, far_out, up_far, down_far)


def norm_forward(values, gain):
    mean = jnp.mean(values, axis=-1, keepdims=True)
    centred = values - mean
    inverse = lax.rsqrt(jnp.mean(centred * centred, axis=-1, keepdims=True) + EPS)
    unit = centred * inverse
    return (unit * gain, unit, inverse)


def norm_backward(grad_out, unit, inverse, gain):
    scaled = grad_out * gain
    first = jnp.mean(scaled, axis=-1, keepdims=True)
    second = jnp.mean(scaled * unit, axis=-1, keepdims=True)
    return (inverse * (scaled - first - unit * second), jnp.sum(grad_out * unit, axis=0))


def doc_index(row_ids, starts):
    return jnp.sum((starts[None, :] <= row_ids[:, None]).astype(jnp.int32), axis=1) - 1


def doc_position(row_ids, starts):
    first = jnp.max(jnp.where(starts[None, :] <= row_ids[:, None], starts[None, :], 0), axis=1)
    return row_ids - first


def angles(position, half):
    freq = jnp.exp(-jnp.log(10000.0) * jnp.arange(half, dtype=F32) / half)
    turn = position.astype(F32)[:, None] * freq[None, :]
    return (jnp.cos(turn), jnp.sin(turn))


def rotate(values, cosine, sine):
    half = values.shape[-1] // 2
    first, second = (values[..., :half], values[..., half:])
    return jnp.concatenate(
        [first * cosine - second * sine, first * sine + second * cosine], axis=-1
    )


def unrotate(grads, cosine, sine):
    return rotate(grads, cosine, -sine)


def span_masks(doc_ids, before, log_decay):
    size = doc_ids.shape[0]
    place = jnp.arange(size, dtype=F32)
    lag = place[:, None] - place[None, :]
    same = (doc_ids[:, None] == doc_ids[None, :]) & (lag >= 0)
    decay = jnp.where(same, jnp.exp(jnp.maximum(lag, 0.0) * log_decay), 0.0)
    reach = jnp.where(doc_ids == before, jnp.exp((place + 1.0) * log_decay), 0.0)[:, None]
    leave = jnp.where(doc_ids == doc_ids[-1], jnp.exp((size - 1.0 - place) * log_decay), 0.0)[
        :, None
    ]
    across = jnp.where(doc_ids[-1] == before, jnp.exp(size * log_decay), 0.0)
    return (decay, reach, leave, across)


def gelu_slope(hidden_pre):
    return (
        0.5 * (1.0 + lax.erf(hidden_pre * SQRT_HALF))
        + hidden_pre * jnp.exp(-0.5 * hidden_pre * hidden_pre) * INV_ROOT_TWO_PI
    )


def plain(
    tokens,
    cotangent,
    doc_lengths,
    head_order,
    norm_gain,
    w_query,
    w_key,
    w_value,
    w_gate,
    group_gain,
    w_out,
    ffn_gain,
    w_up,
    w_down,
):
    heads = w_query.shape[1] // KEY
    head_count = lax.axis_size("head")
    tok_count = lax.axis_size("tok")
    z = lax.axis_index("head")
    tok = lax.axis_index("tok")
    rows = tokens.shape[0]
    group_rows = rows * head_count
    blocks = group_rows // SPAN
    width = tokens.shape[1]
    part = width // tok_count

    tokens_f = reorder(tokens).astype(F32)
    cot_own = reorder(cotangent)
    gain1 = reorder(norm_gain)
    gain2 = reorder(ffn_gain)
    normed1, unit1, inverse1 = norm_forward(tokens_f, gain1)
    qk = w_query.shape[1]
    vg = w_value.shape[1]
    up_two = jnp.concatenate([w_up, swap(w_up, "head", 2)], axis=1)
    down_two = jnp.concatenate([w_down, swap(w_down, "head", 2)], axis=0)
    up_full = tok_gather(up_two, 0)
    down_full = tok_gather(down_two, 1)
    cot_pair = jnp.concatenate([cot_own, swap(cot_own, "head", 1)], axis=0)

    ends = jnp.cumsum(doc_lengths)
    starts = ends - doc_lengths
    first_row = tok * group_rows
    row_ids = first_row + jnp.arange(group_rows, dtype=jnp.int32)
    doc_ids = doc_index(row_ids, starts)
    previous = doc_index(jnp.reshape(first_row - 1, (1,)), starts)[0]
    group_last = doc_index((jnp.arange(tok_count, dtype=jnp.int32) + 1) * group_rows - 1, starts)
    cosine, sine = angles(doc_position(row_ids, starts), KEY // 2)
    ranks = lax.dynamic_slice_in_dim(head_order, z * heads, heads)
    log_decay = jnp.log1p(-jnp.exp2(-(5.0 + ranks.astype(F32))))

    group = head_gather(normed1.astype(BF))
    qkvg_full = tok_gather(jnp.concatenate([w_query, w_key, w_value, w_gate], axis=1), 0)
    out_full = tok_gather(w_out, 1)
    projected = mm(group, qkvg_full)
    qk_rows = jnp.concatenate(
        [
            rotate(projected[:, h * KEY : (h + 1) * KEY], cosine, sine).astype(BF)
            for h in range(2 * heads)
        ],
        axis=1,
    )
    v_rows = projected[:, 2 * qk : 2 * qk + vg].astype(BF)
    gate = projected[:, 2 * qk + vg :]

    def head_of(array, head, size):
        return array[:, head * size : (head + 1) * size]

    def block_of(array, block):
        return array[block * SPAN : (block + 1) * SPAN]

    q, k, v, masks = [], [], [], []
    for h in range(heads):
        q.append(head_of(qk_rows, h, KEY))
        k.append(head_of(qk_rows, heads + h, KEY))
        v.append(head_of(v_rows, h, VAL))
        masks.append(
            [
                span_masks(
                    block_of(doc_ids, b),
                    previous if b == 0 else doc_ids[b * SPAN - 1],
                    log_decay[h],
                )
                for b in range(blocks)
            ]
        )

    group_order = jnp.arange(tok_count, dtype=jnp.int32)

    def weigh(lag, last, h):
        return jnp.where(
            (lag >= 0) & (group_last == last),
            jnp.exp(jnp.maximum(lag, 0).astype(F32) * group_rows * log_decay[h]),
            0.0,
        )

    ends_of = []
    added = []
    for h in range(heads):
        state = jnp.zeros((KEY, VAL), F32)
        terms = []
        for b in range(blocks):
            term = mm_tn(block_of(k[h], b), (block_of(v[h], b) * masks[h][b][2]).astype(BF))
            terms.append(term)
            state = masks[h][b][3] * state + term
        added.append(terms)
        ends_of.append(state.astype(BF))
    all_states = lax.all_gather(jnp.concatenate(ends_of, axis=0), "tok", axis=0)
    lag = tok - 1 - group_order
    states = []
    retained = []
    for h in range(heads):
        weights = weigh(lag, previous, h)
        state = jnp.sum(
            all_states[:, h * KEY : (h + 1) * KEY].astype(F32) * weights[:, None, None], axis=0
        )
        mine = []
        outs = []
        for b in range(blocks):
            mine.append(state.astype(BF))
            qb, kb, vb = block_of(q[h], b), block_of(k[h], b), block_of(v[h], b)
            decay, reach, leave, across = masks[h][b]
            probs = (mm_nt(qb, kb) * decay).astype(BF)
            outs.append(mm(probs, vb) + reach * mm(qb, mine[-1]))
            state = across * state + added[h][b]
        states.append(mine)
        retained.append(jnp.concatenate(outs, axis=0))

    mixed_parts, unit_g, inverse_g, grouped, swish, sigma = [], [], [], [], [], []
    for h in range(heads):
        g, u, i = norm_forward(retained[h], head_of(group_gain[None, :], h, VAL))
        gate_h = head_of(gate, h, VAL)
        s = jax.nn.sigmoid(gate_h)
        unit_g.append(u)
        inverse_g.append(i)
        grouped.append(g)
        sigma.append(s)
        swish.append(gate_h * s)
        mixed_parts.append((swish[-1] * g).astype(BF))
    mixed = jnp.concatenate(mixed_parts, axis=1)

    out_sum = head_scatter(lambda i: mm(rows_of(mixed, i, rows), out_full))
    resid = tokens_f + out_sum
    normed2, unit2, inverse2 = norm_forward(resid, gain2)
    lifted2 = normed2.astype(BF)
    lifted2_pair = jnp.concatenate([lifted2, swap(lifted2, "head", 1)], axis=0)
    hidden_pre = mm(lifted2_pair, up_full)
    hidden = jax.nn.gelu(hidden_pre, approximate=False).astype(BF)
    hidden_grad = mm_nt(cot_pair, down_full)
    pre_grad = (hidden_grad * gelu_slope(hidden_pre)).astype(BF)
    far_grad = mm_nt(pre_grad[rows:], up_full).astype(BF)
    lifted2_grad = mm_nt(pre_grad[:rows], up_full) + swap(far_grad, "head", 1).astype(F32)
    resid_part, ffn_gain_local = norm_backward(lifted2_grad, unit2, inverse2, gain2)
    resid_grad = cot_own.astype(F32) + resid_part
    branch_own = resid_grad.astype(BF)
    branch = head_gather(branch_own)

    far_out = mm(hidden[rows:], down_full).astype(BF)
    layer_out = reorder(
        (resid + mm(hidden[:rows], down_full) + swap(far_out, "head", 1).astype(F32)).astype(BF)
    )

    def piece(array, r):
        return array[:, r * part : (r + 1) * part]

    slots = range(tok_count)
    down_two_grad = tok_scatter([mm_tn(hidden, piece(cot_pair, r)) for r in slots])
    half = down_two_grad.shape[0] // 2
    w_down_grad = down_two_grad[:half] + swap(
        down_two_grad[half:].astype(BF), "head", 2
    ).astype(F32)
    up_two_grad = tok_scatter([mm_tn(piece(lifted2_pair, r), pre_grad) for r in slots])
    half = up_two_grad.shape[1] // 2
    w_up_grad = up_two_grad[:, :half] + swap(
        up_two_grad[:, half:].astype(BF), "head", 2
    ).astype(F32)

    mixed_grad = mm_nt(branch, out_full).astype(BF)
    w_out_grad = tok_scatter([mm_tn(mixed, piece(branch, r)) for r in slots])

    gate_parts, ret_grad, group_gain_parts = [], [], []
    for h in range(heads):
        head_grad = head_of(mixed_grad, h, VAL).astype(F32)
        gate_parts.append(
            (head_grad * grouped[h] * (sigma[h] + swish[h] * (1.0 - sigma[h]))).astype(BF)
        )
        back, gain_term = norm_backward(
            head_grad * swish[h], unit_g[h], inverse_g[h], head_of(group_gain[None, :], h, VAL)
        )
        ret_grad.append(back.astype(BF))
        group_gain_parts.append(gain_term)
    gate_grad = jnp.concatenate(gate_parts, axis=1)
    w_gate_grad = tok_scatter([mm_tn(piece(group, r), gate_grad) for r in slots])

    pending_of, pending_terms = [], []
    for h in range(heads):
        pending = jnp.zeros((KEY, VAL), F32)
        terms = [None] * blocks
        for b in reversed(range(blocks)):
            terms[b] = mm_tn(
                block_of(q[h], b), (block_of(ret_grad[h], b) * masks[h][b][1]).astype(BF)
            )
            pending = masks[h][b][3] * pending + terms[b]
        pending_terms.append(terms)
        pending_of.append(pending.astype(BF))
    all_pending = lax.all_gather(jnp.concatenate(pending_of, axis=0), "tok", axis=0)
    lag_back = group_order - 1 - tok
    shifted_last = doc_index(group_order * group_rows - 1, starts)
    q_parts, k_parts, v_parts = [], [], []
    for h in range(heads):
        weights = jnp.where(
            (lag_back >= 0) & (shifted_last == doc_ids[-1]),
            jnp.exp(jnp.maximum(lag_back, 0).astype(F32) * group_rows * log_decay[h]),
            0.0,
        )
        later = jnp.sum(
            all_pending[:, h * KEY : (h + 1) * KEY].astype(F32) * weights[:, None, None], axis=0
        )
        qg, kg, vg_ = [None] * blocks, [None] * blocks, [None] * blocks
        for b in reversed(range(blocks)):
            qb, kb, vb = block_of(q[h], b), block_of(k[h], b), block_of(v[h], b)
            rb = block_of(ret_grad[h], b)
            decay, reach, leave, across = masks[h][b]
            probs = (mm_nt(qb, kb) * decay).astype(BF)
            score_grad = (mm_nt(rb, vb) * decay).astype(BF)
            later_b = later.astype(BF)
            qg[b] = mm(score_grad, kb) + reach * mm_nt(rb, states[h][b])
            kg[b] = mm_tn(score_grad, qb) + leave * mm_nt(vb, later_b)
            vg_[b] = mm_tn(probs, rb) + leave * mm(kb, later_b)
            later = across * later + pending_terms[h][b]
        q_parts.append(unrotate(jnp.concatenate(qg, axis=0), cosine, sine).astype(BF))
        k_parts.append(unrotate(jnp.concatenate(kg, axis=0), cosine, sine).astype(BF))
        v_parts.append(jnp.concatenate(vg_, axis=0).astype(BF))
    all_grad = jnp.concatenate(q_parts + k_parts + v_parts + [gate_grad], axis=1)
    group_terms = jnp.concatenate(group_gain_parts, axis=0)
    ffn_terms = reorder(ffn_gain_local)
    row_grad = head_scatter(lambda i: mm_nt(rows_of(all_grad, i, rows), qkvg_full))
    input_part, norm_gain_local = norm_backward(row_grad, unit1, inverse1, gain1)
    tokens_grad = reorder(resid_grad + input_part)
    qkv_grad = all_grad[:, : 2 * qk + vg]
    w_qkv_grad = tok_scatter([mm_tn(piece(group, r), qkv_grad) for r in slots])
    w_query_grad = w_qkv_grad[:, :qk]
    w_key_grad = w_qkv_grad[:, qk : 2 * qk]
    w_value_grad = w_qkv_grad[:, 2 * qk :]
    group_gain_grad = sum_small(group_terms, "tok")
    ffn_sum = sum_small(sum_small(ffn_terms, "tok"), "head")
    norm_sum = sum_small(sum_small(reorder(norm_gain_local), "tok"), "head")
    return (
        layer_out,
        tokens_grad,
        norm_sum,
        w_query_grad,
        w_key_grad,
        w_value_grad,
        w_gate_grad,
        group_gain_grad,
        w_out_grad,
        ffn_sum,
        w_up_grad,
        w_down_grad,
    )


def fused(
    tokens,
    cotangent,
    doc_lengths,
    head_order,
    norm_gain,
    w_query,
    w_key,
    w_value,
    w_gate,
    group_gain,
    w_out,
    ffn_gain,
    w_up,
    w_down,
):
    turned, qkvg_full, out_full, qk_rows, v_rows, gate, cosine, sine = enter(
        tokens, norm_gain, doc_lengths, w_query, w_key, w_value, w_gate, w_out
    )
    resid, inverse_g, unit_g, states, cot_pair, mixed_turned, up_full, down_full = retain(
        doc_lengths, head_order, group_gain, qk_rows, v_rows, gate, tokens, out_full, cotangent,
        w_up, w_down,
    )
    (
        ffn_terms, up_own, up_far, down_own, down_far, layer_own, far_out, resid_grad, branch
    ) = feed_forward(resid, ffn_gain, cot_pair, up_full, down_full)
    w_out_grad, group_terms, layer_out, all_grad, up_in, down_in = recall(
        doc_lengths, head_order, group_gain, qk_rows, v_rows, gate, unit_g, inverse_g, states,
        cosine, sine, mixed_turned, branch, out_full, layer_own, far_out, up_far, down_far,
    )
    w_up_grad = up_own + up_in.astype(F32)
    w_down_grad = down_own + down_in.astype(F32)
    (
        w_query_grad, w_key_grad, w_value_grad, w_gate_grad, norm_sum, ffn_sum, group_sum, tokens_grad
    ) = depart(all_grad, qkvg_full, turned, tokens, resid_grad, norm_gain, ffn_terms, group_terms)
    return (
        layer_out,
        tokens_grad,
        norm_sum.reshape(-1),
        w_query_grad,
        w_key_grad,
        w_value_grad,
        w_gate_grad,
        group_sum.reshape(-1),
        w_out_grad,
        ffn_sum.reshape(-1),
        w_up_grad,
        w_down_grad,
    )


def local(*arrays):
    return fused(*arrays) if paired() else plain(*arrays)


def solution(mesh):
    rows = P(("tok", "head"), None)
    inward = P("tok", "head")
    outward = P("head", "tok")
    return jax.shard_map(
        local,
        mesh=mesh,
        in_specs=(
            rows, rows, P(), P(), P(), inward, inward, inward, inward, P("head"),
            outward, P(), inward, outward,
        ),
        out_specs=(
            rows, rows, P(), inward, inward, inward, inward, P("head"),
            outward, P(), inward, outward,
        ),
        check_vma=False,
    )
```
